32 devices in a mesh: member: 8 (over z, core), band: 4 (over y, x).
Axes of the slice: x: 2, y: 2, z: 4, core: 2. Of those that a mesh axis runs over, the one named last changes fastest.
Arguments:
- ensemble: bfloat16 [8, 2, 16, 16, 1440], P('member', None, None, 'band'), may hold values from -6 to 6
- member_weight: float32 [8], replicated, may hold values from 0.5 to 2
- member_of_slot: int32 [8], P('member'), may hold values from 0 to 7, each once
- halfwidth: int32 [16], replicated, may hold values from 1 to 4, as said below
- static_root: float32 [16, 16], replicated, may hold values from -1.5 to 1.5
- innovation: bfloat16 [2, 16, 16, 1440], P(None, None, 'band'), may hold values from -6 to 6
- precision: bfloat16 [16, 16, 1440], P(None, 'band'), may hold values from 0.1 to 3
Outputs:
- control_members: float32 [8, 16, 16, 1440], P('member', None, 'band')
- control_static: float32 [16, 16, 1440], P(None, 'band')
- increment: float32 [2, 16, 16, 1440], P(None, 'member', 'band')
The draws below stay inside these ranges and needn't reach their ends.
Inputs may be any that keep to these rules, and one draw needn't show every extreme that they name: `member_of_slot`: each member appears in exactly one slot. `halfwidth`: some level has a half-width of exactly 4.
All inputs are finite; a program needn't handle non-finite values.
Results may differ from the reference program's by a relative error of at most 0.0062.
Values may be sent and summed in bfloat16 or wider, within the bound.
No kernel may reach another device: no remote copies, remote signals or barrier semaphores. Data moves between devices by JAX's collectives and lax.ppermute only.
A program may use at most 64 MiB of HBM per device.

```python
import math
import jax
import jax.numpy as jnp
from jax import lax

LEV = 16
LON = 1440
TSLOT = 2
ITERS = 2
HMAX = 4
LREACH = 18
MEMBERS = 8
LAT = 16


def draw_halfwidth(key, part):
    first_key = jax.random.fold_in(key, 11)
    second_key = jax.random.fold_in(key, 12)
    widths = jax.random.randint(first_key, (LEV,), 1, HMAX + 1, dtype=jnp.int32)
    chosen = jax.random.randint(second_key, (), 0, LEV, dtype=jnp.int32)
    return jnp.where(jnp.arange(LEV, dtype=jnp.int32) == chosen, HMAX, widths).astype(jnp.int32)


def draw_precision(key, part):
    uniform_draw = jax.random.uniform(jax.random.fold_in(key, 21), (LEV, LAT, LON), jnp.float32)
    base = jnp.exp(jnp.log(0.1) * (1.0 - uniform_draw))
    latitude = jnp.arange(LAT, dtype=jnp.float32)[None, :, None]
    factor = 1.0 + 2.0 * latitude / max(LAT - 1, 1)
    return (base * factor).astype(jnp.bfloat16)


def steps_of(rng, extent, shards, smallest, top_value):
    level, own = 1.0, jax.random.fold_in(rng, 6)
    for axis_at, parts in shards:
        steps = jnp.exp(jax.random.uniform(jax.random.fold_in(own, axis_at), (parts,), jnp.float32, smallest / len(shards), top_value / len(shards)))
        level = level * jnp.repeat(steps, extent[axis_at] // parts).reshape([-1 if axis == axis_at else 1 for axis in range(len(extent))])
    return level


def normal_values(stream_key, dims, spread, limit, cuts=(), kind=jnp.bfloat16):
    values = jax.random.normal(stream_key, dims, jnp.float32) * spread
    if len(cuts) > 0:
        values = steps_of(stream_key, dims, cuts, -0.22, 0.18) * values
    return jnp.clip(values, min=-limit, max=limit).astype(kind)


def setup_inputs(seed: int = 0) -> dict:
    arg_keys = jax.random.split(jax.random.key(seed), 8)
    return {
        "ensemble": normal_values(arg_keys[0], (MEMBERS, TSLOT, LEV, LAT, LON), 1.0, 6.0, ((0, 8), (3, 4))),
        "member_weight": jnp.clip(jnp.exp(jax.random.uniform(arg_keys[1], (MEMBERS,), jnp.float32, math.log(0.5), math.log(2.0))), 0.5, 2.0),
        "member_of_slot": jax.random.permutation(arg_keys[2], MEMBERS).astype(jnp.int32),
        "halfwidth": draw_halfwidth(jax.random.fold_in(arg_keys[7], 71), 0),
        "static_root": normal_values(arg_keys[4], (LEV, LEV), LEV ** -0.5, 1.5, (), jnp.float32),
        "innovation": normal_values(arg_keys[5], (TSLOT, LEV, LAT, LON), 1.0, 6.0, ((2, 4),)),
        "precision": draw_precision(jax.random.fold_in(arg_keys[7], 71), 0),
    }


ensemble_share = 0.8
static_share = 0.6
length_scale = 6.0

def lon_kernel(reach, width):
    rows_index = jnp.arange(width + 2 * reach, dtype=jnp.int32)[:, None]
    cols_index = jnp.arange(width, dtype=jnp.int32)[None, :]
    distance = jnp.abs(rows_index - reach - cols_index).astype(jnp.float32)
    values = jnp.exp(-0.5 * (distance / length_scale) ** 2) / (length_scale * math.sqrt(2.0 * math.pi))
    return jnp.where(distance <= reach, values, jnp.zeros_like(values)).astype(jnp.bfloat16)

def smooth_longitude(field, reach, blocks):
    width = field.shape[-1] // blocks
    pieces = field.reshape(field.shape[:-1] + (blocks, width))
    before = jnp.roll(pieces, 1, axis=-2)[..., width - reach:]
    after = jnp.roll(pieces, -1, axis=-2)[..., :reach]
    window = jnp.concatenate([before, pieces, after], axis=-1)
    kernel = lon_kernel(reach, width)
    result = jnp.einsum('...bm,mo->...bo', window.astype(jnp.float32), kernel.astype(jnp.float32))
    return result.reshape(field.shape).astype(jnp.bfloat16)

def taper_weights(halfwidth, reach):
    offsets = jnp.abs(jnp.arange(-reach, reach + 1, dtype=jnp.int32)).astype(jnp.float32)
    spans = halfwidth.astype(jnp.float32)[:, None] + 1.0
    return jnp.maximum(1.0 - offsets[None, :] / spans, 0.0) / spans

def localize(field, taper):
    smoothed = smooth_longitude(field.astype(jnp.bfloat16), LREACH, LON // LREACH)
    padded = jnp.pad(smoothed, ((0, 0), (HMAX, HMAX), (0, 0)))
    row_count = field.shape[1]
    summed = jnp.zeros(field.shape, jnp.float32)
    for offset in range(2 * HMAX + 1):
        summed = summed + taper[:, offset][:, None, None] * padded[:, offset:offset + row_count, :].astype(jnp.float32)
    return summed

def forward(control_members, control_static, scaled, ensemble, taper, static_root):

    def add_member(running, items):
        weight, member_field, control = items
        localized = localize(control, taper)
        return (running + weight * member_field.astype(jnp.float32) * localized[None], None)
    start = jnp.zeros((TSLOT, LEV, LAT, LON), jnp.float32)
    summed, _ = lax.scan(add_member, start, (scaled, ensemble, control_members))
    static = jnp.einsum('lq,qyx->lyx', static_root, control_static, precision=lax.Precision.HIGHEST)
    return ensemble_share * summed + static_share * static[None]

def adjoint(weighted, scaled, ensemble, taper, static_root):

    def one_member(items):
        weight, member_field = items
        folded = weight * lax.optimization_barrier(jnp.sum(member_field.astype(jnp.float32) * weighted, axis=0))
        return ensemble_share * localize(folded, taper)
    grad_members = lax.map(one_member, (scaled, ensemble))
    grad_static = static_share * jnp.einsum('ql,qyx->lyx', static_root, lax.optimization_barrier(jnp.sum(weighted, axis=0)), precision=lax.Precision.HIGHEST)
    return (grad_members, grad_static)

def reference(ensemble, member_weight, member_of_slot, halfwidth, static_root, innovation, precision):
    scaled = member_weight[member_of_slot]
    taper = taper_weights(halfwidth, HMAX)
    precise = precision.astype(jnp.float32)
    res_members, res_static = adjoint(precise[None] * innovation.astype(jnp.float32), scaled, ensemble, taper, static_root)
    dir_members, dir_static = (res_members, res_static)
    sol_members = jnp.zeros_like(res_members)
    sol_static = jnp.zeros_like(res_static)
    increment = jnp.zeros((TSLOT, LEV, LAT, LON), jnp.float32)
    norm_now = jnp.sum(res_members * res_members) + jnp.sum(res_static * res_static)
    for iteration in range(ITERS):
        image = forward(dir_members, dir_static, scaled, ensemble, taper, static_root)
        hes_members, hes_static = adjoint(precise[None] * image, scaled, ensemble, taper, static_root)
        hes_members = dir_members + hes_members
        hes_static = dir_static + hes_static
        alpha = norm_now / (jnp.sum(dir_members * hes_members) + jnp.sum(dir_static * hes_static))
        sol_members = sol_members + alpha * dir_members
        sol_static = sol_static + alpha * dir_static
        increment = increment + alpha * image
        res_members = res_members - alpha * hes_members
        res_static = res_static - alpha * hes_static
        norm_next = jnp.sum(res_members * res_members) + jnp.sum(res_static * res_static)
        ratio = norm_next / norm_now
        dir_members = res_members + ratio * dir_members
        dir_static = res_static + ratio * dir_static
        norm_now = norm_next
    return (sol_members, sol_static, increment)
```

```python
import math

import jax
import jax.numpy as jnp
from jax import lax
from jax.experimental import pallas as pl
from jax.experimental.pallas import tpu as pltpu
from jax.sharding import PartitionSpec as P

HMAX = 4
LREACH = 18
REACHES = 4
LANES = 128
BOTH = ("member", "band")

ensemble_share = 0.8
static_share = 0.6
length_scale = 6.0


def round_up(value, step):
    return -(-value // step) * step


def with_halo(block, dim, width):
    count = lax.axis_size("band")
    forward = [(i, i + 1) for i in range(count - 1)]
    backward = [(target, source) for source, target in forward]
    low = lax.ppermute(
        lax.slice_in_dim(block, block.shape[dim] - width, None, axis=dim), "band", forward
    )
    high = lax.ppermute(lax.slice_in_dim(block, 0, width, axis=dim), "band", backward)
    return jnp.concatenate([low, block, high], axis=dim)


def kernel_values(distance):
    values = jnp.exp(-0.5 * (distance / length_scale) ** 2) / (
        length_scale * math.sqrt(2.0 * math.pi)
    )
    return jnp.where(distance <= LREACH, values, jnp.zeros_like(values)).astype(jnp.bfloat16)


def lon_kernel(reach, width):
    rows_index = jnp.arange(width + 2 * reach, dtype=jnp.int32)[:, None]
    cols_index = jnp.arange(width, dtype=jnp.int32)[None, :]
    return kernel_values(jnp.abs(rows_index - reach - cols_index).astype(jnp.float32))


def ring_kernel(width, padded):
    rows_index = jnp.arange(padded, dtype=jnp.int32)[:, None]
    cols_index = jnp.arange(padded, dtype=jnp.int32)[None, :]
    apart = jnp.abs(rows_index - cols_index)
    distance = jnp.minimum(apart, width - apart).astype(jnp.float32)
    inside = (rows_index < width) & (cols_index < width)
    return jnp.where(inside, kernel_values(distance), 0).astype(jnp.bfloat16)


def smooth_longitude(field, reach, blocks):
    width = field.shape[-1] // blocks
    pieces = field.reshape(field.shape[:-1] + (blocks, width))
    before = jnp.roll(pieces, 1, axis=-2)[..., width - reach :]
    after = jnp.roll(pieces, -1, axis=-2)[..., :reach]
    window = jnp.concatenate([before, pieces, after], axis=-1)
    kernel = lon_kernel(reach, width)
    result = jnp.einsum("...bm,mo->...bo", window, kernel, preferred_element_type=jnp.float32)
    return result.reshape(field.shape).astype(jnp.bfloat16)


def taper_weights(halfwidth, reach):
    offsets = jnp.abs(jnp.arange(-reach, reach + 1, dtype=jnp.int32)).astype(jnp.float32)
    spans = halfwidth.astype(jnp.float32)[:, None] + 1.0
    return jnp.maximum(1.0 - offsets[None, :] / spans, 0.0) / spans


def localize(field, taper):
    smoothed = smooth_longitude(field.astype(jnp.bfloat16), LREACH, 3)
    padded = with_halo(smoothed, 1, HMAX)
    row_count = field.shape[1]
    summed = jnp.zeros(field.shape, jnp.float32)
    for offset in range(2 * HMAX + 1):
        summed = summed + taper[:, offset][:, None, None] * padded[
            :, offset : offset + row_count, :
        ].astype(jnp.float32)
    return summed


def taper_matrix(halfwidth, bands, rows, copies):
    levels = halfwidth.shape[0]
    per_copy = bands * levels * rows
    index = jnp.arange(copies * per_copy, dtype=jnp.int32)
    copy = index // per_copy
    band = index // (levels * rows) % bands
    level = index // rows % levels
    latitude = band * rows + index % rows
    spans = halfwidth.astype(jnp.float32)[level][:, None] + 1.0
    apart = jnp.abs(latitude[:, None] - latitude[None, :]).astype(jnp.float32)
    same = (copy[:, None] == copy[None, :]) & (level[:, None] == level[None, :])
    near = jnp.maximum(1.0 - apart / spans, 0.0) / spans
    full = jnp.where(same, near, 0.0)
    high = full.astype(jnp.bfloat16)
    low = (full - high.astype(jnp.float32)).astype(jnp.bfloat16)
    return jnp.stack([high, low])


def windows(field, count, halo, padded, fill):
    lon = field.shape[-1]
    share = lon // count
    ring = jnp.concatenate([field[..., lon - halo :], field, field[..., :halo]], axis=-1)
    tail = jnp.broadcast_to(fill, field.shape[:-1] + (padded - share - 2 * halo,)).astype(field.dtype)
    pieces = []
    for piece in range(count):
        start = piece * share
        pieces.append(
            jnp.concatenate(
                [ring[..., start + halo : start + 2 * halo + share], ring[..., start : start + halo], tail],
                axis=-1,
            )
        )
    return jnp.stack(pieces)


def exchange_bands(blocks):
    count = blocks.shape[0]
    if count > 8:
        return lax.all_to_all(blocks, "band", 0, 0, tiled=True)
    here = lax.axis_index("band")
    arrived = [lax.dynamic_index_in_dim(blocks, here, 0, keepdims=False)]
    for shift in range(1, count):
        outgoing = lax.dynamic_index_in_dim(blocks, lax.rem(here + shift, count), 0, keepdims=False)
        arrived.append(
            lax.ppermute(outgoing, "band", [(i, (i + shift) % count) for i in range(count)])
        )
    ordered = []
    for source in range(count):
        block = arrived[0]
        for shift in range(1, count):
            block = jnp.where(lax.rem(here - source + count, count) == shift, arrived[shift], block)
        ordered.append(block)
    return jnp.stack(ordered)


def spread(field, ring, taper):
    copies = taper.shape[1]
    smoothed = jnp.dot(field.astype(jnp.bfloat16), ring, preferred_element_type=jnp.float32)
    smoothed = smoothed.astype(jnp.bfloat16)
    parts = []
    for start in range(0, field.shape[0], copies):
        part = smoothed[start : start + copies]
        parts.append(
            jnp.dot(taper[0], part, preferred_element_type=jnp.float32)
            + jnp.dot(taper[1], part, preferred_element_type=jnp.float32)
        )
    return parts[0] if len(parts) == 1 else jnp.concatenate(parts, axis=0)


def load_members(stacked, weight, members, bands, slots, width):
    own = stacked.shape[1] // slots
    stacked = stacked.astype(jnp.float32)
    which = stacked[:, :1, width : width + 1]
    scale = jnp.zeros(which.shape, jnp.float32)
    for member in range(members):
        scale = scale + jnp.where(which == member, weight[member], 0.0)
    shape = (members, bands * own, stacked.shape[-1])
    return [
        (scale * stacked[:, slot * own : (slot + 1) * own]).reshape(shape) for slot in range(slots)
    ]


def solution(mesh):
    members, bands = mesh.shape["member"], mesh.shape["band"]

    def first_half(slots, width, kept, weight, stacked, fields, ring, taper, out_ref, image_ref, grad_ref):
        scaled = load_members(stacked[...], weight, members, bands, slots, width)
        rows, padded = scaled[0].shape[1:]
        own = rows // bands
        fields = fields[...].astype(jnp.float32)

        def field(index):
            return fields[:, index * own : (index + 1) * own].reshape(rows, padded)

        precise, static = field(slots), field(slots + 1)

        def fold(weighted):
            total = scaled[0] * weighted[0][None]
            for slot in range(1, slots):
                total = total + scaled[slot] * weighted[slot][None]
            return total.reshape(members * rows, padded)

        grad = ensemble_share * spread(fold([precise * field(t) for t in range(slots)]), ring[...], taper)
        local = spread(grad, ring[...], taper).reshape(members, rows, padded)
        image = [ensemble_share * jnp.sum(scaled[t] * local, axis=0) for t in range(slots)]
        weighted = [precise * (image[t] + static) for t in range(slots)]
        grad = ensemble_share * spread(fold(weighted), ring[...], taper)
        grad_ref[...] = grad.astype(jnp.bfloat16)
        total = weighted[0]
        for t in range(1, slots):
            total = total + weighted[t]
        grad = grad[:, :kept].reshape(members, bands, own, kept)
        total = total[:, :kept].reshape(bands, own, kept)
        for member in range(members):
            for band in range(bands):
                out_ref[member * bands + band] = jnp.concatenate(
                    [grad[member, band], total[band]], axis=0
                ).astype(jnp.bfloat16)
        for t in range(slots):
            image_ref[:, t * own : (t + 1) * own] = image[t][:, :kept].reshape(bands, own, kept)

    def second_half(slots, width, kept, weight, stacked, grad, ring, taper, image_ref):
        scaled = load_members(stacked[...], weight, members, bands, slots, width)
        rows, padded = scaled[0].shape[1:]
        own = rows // bands
        local = spread(grad[...], ring[...], taper).reshape(members, rows, padded)
        for t in range(slots):
            image = ensemble_share * jnp.sum(scaled[t] * local, axis=0)
            image_ref[:, t * own : (t + 1) * own] = image[:, :kept].reshape(bands, own, kept)

    def shards(ensemble, member_weight, member_of_slot, halfwidth, static_root, innovation, precision):
        _, slots, levels, rows, lon = ensemble.shape
        level_share, lon_share = levels // members, lon // bands
        own = level_share * rows
        halo = REACHES * LREACH
        width = lon_share + 2 * halo
        padded = round_up(width + 1, LANES)
        kept = min(padded, round_up(lon_share, LANES))
        first_level = lax.axis_index("member") * level_share
        highest = lax.Precision.HIGHEST
        vmem = pl.BlockSpec(memory_space=pltpu.VMEM)
        smem = pl.BlockSpec(memory_space=pltpu.SMEM)
        params = pltpu.CompilerParams(vmem_limit_bytes=48 * 1024 * 1024)

        def own_levels(field, axis):
            return lax.dynamic_slice_in_dim(field, first_level, level_share, axis)

        pieces = windows(
            ensemble[0], bands, halo, padded, member_of_slot.astype(jnp.bfloat16)[0]
        ).reshape(bands, slots, members, own, padded)
        pieces = jnp.transpose(pieces, (2, 0, 1, 3, 4)).reshape(members * bands, slots * own, padded)
        stacked = lax.all_to_all(pieces, BOTH, 0, 0, tiled=True)

        precise = precision.astype(jnp.float32)
        weighted = precise[None] * innovation.astype(jnp.float32)
        total = jnp.sum(weighted, axis=0)
        pulled = static_share * jnp.einsum("ql,qyx->lyx", static_root, total, precision=highest)
        own_root = own_levels(static_root, 0)
        static = static_share * jnp.einsum("lq,qyx->lyx", own_root, pulled, precision=highest)
        fields = jnp.concatenate(
            [
                own_levels(innovation, 1),
                own_levels(precision, 0)[None],
                static.astype(jnp.bfloat16)[None],
            ]
        ).reshape((slots + 2) * own, lon)
        fields = exchange_bands(windows(fields, bands, halo, padded, jnp.zeros((), jnp.bfloat16)))

        picker = (member_of_slot[0] == jnp.arange(member_weight.shape[0], dtype=jnp.int32)).astype(
            jnp.float32
        )
        scale = jnp.sum(picker * member_weight)
        folded = scale * jnp.sum(ensemble[0].astype(jnp.float32) * weighted, axis=0)
        grad_first = ensemble_share * localize(folded, taper_weights(halfwidth, HMAX))

        ring = ring_kernel(width, padded)
        per_member = bands * own
        copies = members
        while copies > 1 and (copies * per_member > 256 or members % copies):
            copies -= 1
        taper = taper_matrix(own_levels(halfwidth, 0), bands, rows, copies)

        out, image_first, grad = pl.pallas_call(
            lambda *refs: first_half(slots, width, kept, *refs),
            out_shape=(
                jax.ShapeDtypeStruct((members * bands, 2 * own, kept), jnp.bfloat16),
                jax.ShapeDtypeStruct((bands, slots * own, kept), jnp.float32),
                jax.ShapeDtypeStruct((members * per_member, padded), jnp.bfloat16),
            ),
            in_specs=[smem, vmem, vmem, vmem, vmem],
            out_specs=(vmem, vmem, vmem),
            compiler_params=params,
            name="first_half",
        )(member_weight, stacked, fields, ring, taper)
        back = lax.all_to_all(out, BOTH, 0, 0, tiled=True)
        image_second = pl.pallas_call(
            lambda *refs: second_half(slots, width, kept, *refs),
            out_shape=jax.ShapeDtypeStruct((bands, slots * own, kept), jnp.float32),
            in_specs=[smem, vmem, vmem, vmem, vmem],
            out_specs=vmem,
            compiler_params=params,
            name="second_half",
        )(member_weight, stacked, grad, ring, taper)
        images = exchange_bands(jnp.concatenate([image_first, image_second], axis=1))

        def join(blocks, lead):
            return jnp.concatenate(
                [blocks[(slice(None),) * lead + (band, Ellipsis, slice(0, lon_share))] for band in range(bands)],
                axis=-1,
            )

        images = join(images, 0).reshape(2, slots, level_share, rows, lon)
        back = join(back.reshape(members, bands, 2, level_share, rows, kept), 1).astype(jnp.float32)
        grad_second = back[:, 0].reshape(levels, rows, lon)
        total = back[:, 1].reshape(levels, rows, lon)
        pulled_second = static_share * jnp.einsum("ql,qyx->lyx", static_root, total, precision=highest)
        static_second = static_share * jnp.einsum("lq,qyx->lyx", own_root, pulled_second, precision=highest)
        image_first = images[0] + static[None]
        image_second = images[1] + static_second[None]

        own_precise = own_levels(precise, 0)[None]
        own_weighted = own_levels(weighted, 1)
        weighted_first = own_precise * image_first
        sums = jnp.stack(
            [
                jnp.sum(own_weighted * image_first),
                jnp.sum(weighted_first * image_first),
                jnp.sum(weighted_first * image_second),
                jnp.sum(own_precise * image_second * image_second),
            ]
        )
        sums = jnp.broadcast_to(jnp.pad(sums, (0, LANES - 4))[None], (members * bands, LANES))
        sums = jnp.sum(lax.all_to_all(sums, BOTH, 0, 0, tiled=True), axis=0)
        first_norm, first_image, cross, second_image = sums[0], sums[1], sums[2], sums[3]
        alpha = first_norm / (first_norm + first_image)
        ratio = first_image / first_norm
        next_norm = alpha * alpha * jnp.maximum(cross - ratio * first_image, 0.0)
        beta = next_norm / first_norm
        spread_image = second_image - 2.0 * ratio * cross + ratio * ratio * first_image
        curvature = next_norm + alpha * alpha * spread_image - beta * next_norm / alpha
        alpha_next = jnp.clip(next_norm / curvature, 0.0, 1.0)
        on_first = alpha + alpha_next * (1.0 - alpha + beta)
        on_second = -alpha * alpha_next
        return (
            (on_first * grad_first + on_second * grad_second)[None],
            on_first * pulled + on_second * pulled_second,
            on_first * image_first + on_second * image_second,
        )

    return jax.shard_map(
        shards,
        mesh=mesh,
        in_specs=(
            P("member", None, None, "band", None),
            P(),
            P("member"),
            P(),
            P(),
            P(None, None, "band", None),
            P(None, "band", None),
        ),
        out_specs=(
            P("member", None, "band", None),
            P(None, "band", None),
            P(None, "member", "band", None),
        ),
        check_vma=False,
    )
```

```python
import math

import jax
import jax.numpy as jnp
from jax import lax
from jax.experimental import pallas as pl
from jax.experimental.pallas import tpu as pltpu
from jax.sharding import PartitionSpec as P

HMAX = 4
LREACH = 18
REACHES = 4
LANES = 128
BOTH = ("member", "band")

ensemble_share = 0.8
static_share = 0.6
length_scale = 6.0


def round_up(value, step):
    return -(-value // step) * step


def neighbours(block):
    count = lax.axis_size("band")
    forward = [(i, i + 1) for i in range(count - 1)]
    backward = [(target, source) for source, target in forward]
    return lax.ppermute(block, "band", forward), lax.ppermute(block, "band", backward)


def kernel_values(distance):
    values = jnp.exp(-0.5 * (distance / length_scale) ** 2) / (
        length_scale * math.sqrt(2.0 * math.pi)
    )
    return jnp.where(distance <= LREACH, values, jnp.zeros_like(values)).astype(jnp.bfloat16)


def lon_kernel(reach, width):
    rows_index = jnp.arange(width + 2 * reach, dtype=jnp.int32)[:, None]
    cols_index = jnp.arange(width, dtype=jnp.int32)[None, :]
    return kernel_values(jnp.abs(rows_index - reach - cols_index).astype(jnp.float32))


def ring_kernel(width, padded):
    rows_index = jnp.arange(padded, dtype=jnp.int32)[:, None]
    cols_index = jnp.arange(padded, dtype=jnp.int32)[None, :]
    apart = jnp.abs(rows_index - cols_index)
    distance = jnp.minimum(apart, width - apart).astype(jnp.float32)
    inside = (rows_index < width) & (cols_index < width)
    return jnp.where(inside, kernel_values(distance), 0).astype(jnp.bfloat16)


def smooth_longitude(field, reach, blocks):
    width = field.shape[-1] // blocks
    pieces = field.reshape(field.shape[:-1] + (blocks, width))
    before = jnp.roll(pieces, 1, axis=-2)[..., width - reach :]
    after = jnp.roll(pieces, -1, axis=-2)[..., :reach]
    window = jnp.concatenate([before, pieces, after], axis=-1)
    kernel = lon_kernel(reach, width)
    result = jnp.einsum("...bm,mo->...bo", window, kernel, preferred_element_type=jnp.float32)
    return result.reshape(field.shape).astype(jnp.bfloat16)


def halves(full):
    high = full.astype(jnp.bfloat16)
    low = (full - high.astype(jnp.float32)).astype(jnp.bfloat16)
    return jnp.stack([high, low])


def halo_taper(halfwidth, rows):
    levels = halfwidth.shape[0]
    own = levels * rows
    target = jnp.arange(own, dtype=jnp.int32)[:, None]
    source = jnp.arange(3 * own, dtype=jnp.int32)[None, :]
    spans = jnp.repeat(halfwidth.astype(jnp.float32), rows)[:, None] + 1.0
    shift = (source // own - 1) * rows + source % rows - target % rows
    same = source // rows % levels == target // rows
    near = jnp.maximum(1.0 - jnp.abs(shift).astype(jnp.float32) / spans, 0.0) / spans
    return halves(jnp.where(same, near, 0.0))


def each_row(matrix, rows):
    same = jnp.eye(rows, dtype=jnp.float32)
    wide = matrix[:, None, :, None] * same[None, :, None, :]
    return wide.reshape(matrix.shape[0] * rows, matrix.shape[1] * rows)


def exact_dot(matrix, field):
    return jnp.dot(
        matrix, field, precision=lax.Precision.HIGHEST, preferred_element_type=jnp.float32
    )


def taper_matrix(halfwidth, bands, rows, copies):
    levels = halfwidth.shape[0]
    per_copy = bands * levels * rows
    index = jnp.arange(copies * per_copy, dtype=jnp.int32)
    copy = index // per_copy
    band = index // (levels * rows) % bands
    level = index // rows % levels
    latitude = band * rows + index % rows
    spans = halfwidth.astype(jnp.float32)[level][:, None] + 1.0
    apart = jnp.abs(latitude[:, None] - latitude[None, :]).astype(jnp.float32)
    same = (copy[:, None] == copy[None, :]) & (level[:, None] == level[None, :])
    near = jnp.maximum(1.0 - apart / spans, 0.0) / spans
    return halves(jnp.where(same, near, 0.0))


def windows(field, count, halo, padded, fill):
    lon = field.shape[-1]
    share = lon // count
    ring = jnp.concatenate([field[..., lon - halo :], field, field[..., :halo]], axis=-1)
    tail = jnp.broadcast_to(fill, field.shape[:-1] + (padded - share - 2 * halo,)).astype(field.dtype)
    pieces = []
    for piece in range(count):
        start = piece * share
        pieces.append(
            jnp.concatenate(
                [ring[..., start + halo : start + 2 * halo + share], ring[..., start : start + halo], tail],
                axis=-1,
            )
        )
    return jnp.stack(pieces)


def exchange_bands(blocks):
    count = blocks.shape[0]
    if count > 8:
        return lax.all_to_all(blocks, "band", 0, 0, tiled=True)
    here = lax.axis_index("band")
    arrived = [lax.dynamic_index_in_dim(blocks, here, 0, keepdims=False)]
    for shift in range(1, count):
        outgoing = lax.dynamic_index_in_dim(blocks, lax.rem(here + shift, count), 0, keepdims=False)
        arrived.append(
            lax.ppermute(outgoing, "band", [(i, (i + shift) % count) for i in range(count)])
        )
    ordered = []
    for source in range(count):
        block = arrived[0]
        for shift in range(1, count):
            block = jnp.where(lax.rem(here - source + count, count) == shift, arrived[shift], block)
        ordered.append(block)
    return jnp.stack(ordered)


def spread(field, ring, taper):
    copies = taper.shape[1]
    smoothed = jnp.dot(field.astype(jnp.bfloat16), ring, preferred_element_type=jnp.float32)
    smoothed = smoothed.astype(jnp.bfloat16)
    parts = []
    for start in range(0, field.shape[0], copies):
        part = smoothed[start : start + copies]
        parts.append(
            jnp.dot(taper[0], part, preferred_element_type=jnp.float32)
            + jnp.dot(taper[1], part, preferred_element_type=jnp.float32)
        )
    return parts[0] if len(parts) == 1 else jnp.concatenate(parts, axis=0)


def load_members(stacked, weight, members, bands, slots, width):
    own = stacked.shape[1] // slots
    stacked = stacked.astype(jnp.float32)
    which = stacked[:, :1, width : width + 1]
    scale = jnp.zeros(which.shape, jnp.float32)
    for member in range(members):
        scale = scale + jnp.where(which == member, weight[member], 0.0)
    shape = (members, bands * own, stacked.shape[-1])
    return [
        (scale * stacked[:, slot * own : (slot + 1) * own]).reshape(shape) for slot in range(slots)
    ]


def solution(mesh):
    members, bands = mesh.shape["member"], mesh.shape["band"]

    def first_half(slots, width, kept, weight, stacked, fields, ring, taper, out_ref, image_ref, grad_ref):
        scaled = load_members(stacked[...], weight, members, bands, slots, width)
        rows, padded = scaled[0].shape[1:]
        own = rows // bands
        fields = fields[...].astype(jnp.float32)

        def field(index):
            return fields[:, index * own : (index + 1) * own].reshape(rows, padded)

        precise, static = field(slots), field(slots + 1)

        def fold(weighted):
            total = scaled[0] * weighted[0][None]
            for slot in range(1, slots):
                total = total + scaled[slot] * weighted[slot][None]
            return total.reshape(members * rows, padded)

        grad = ensemble_share * spread(fold([precise * field(t) for t in range(slots)]), ring[...], taper)
        local = spread(grad, ring[...], taper).reshape(members, rows, padded)
        image = [ensemble_share * jnp.sum(scaled[t] * local, axis=0) for t in range(slots)]
        weighted = [precise * (image[t] + static) for t in range(slots)]
        grad = ensemble_share * spread(fold(weighted), ring[...], taper)
        grad_ref[...] = grad.astype(jnp.bfloat16)
        total = weighted[0]
        for t in range(1, slots):
            total = total + weighted[t]
        grad = grad[:, :kept].reshape(members, bands, own, kept)
        total = total[:, :kept].reshape(bands, own, kept)
        for member in range(members):
            for band in range(bands):
                out_ref[member * bands + band] = jnp.concatenate(
                    [grad[member, band], total[band]], axis=0
                ).astype(jnp.bfloat16)
        for t in range(slots):
            image_ref[:, t * own : (t + 1) * own] = image[t][:, :kept].reshape(bands, own, kept)

    def second_half(slots, width, kept, weight, stacked, grad, ring, taper, image_ref):
        scaled = load_members(stacked[...], weight, members, bands, slots, width)
        rows, padded = scaled[0].shape[1:]
        own = rows // bands
        local = spread(grad[...], ring[...], taper).reshape(members, rows, padded)
        for t in range(slots):
            image = ensemble_share * jnp.sum(scaled[t] * local, axis=0)
            image_ref[:, t * own : (t + 1) * own] = image[:, :kept].reshape(bands, own, kept)

    def first_gradient(below, here, above, taper, grad_ref):
        stacked = jnp.concatenate([below[...], here[...], above[...]], axis=0)
        grad_ref[...] = ensemble_share * (
            jnp.dot(taper[0], stacked, preferred_element_type=jnp.float32)
            + jnp.dot(taper[1], stacked, preferred_element_type=jnp.float32)
        )

    def total_piece(back, band, own):
        kept = back.shape[-1]
        pieces = [back[member * bands + band, own:].astype(jnp.float32) for member in range(members)]
        return jnp.concatenate(pieces, axis=0).reshape(members * own, kept)

    def inner_products(slots, lon_share, back, images, fields, static, mixing, sums_ref):
        own, kept = static.shape[1:]
        inside = lax.broadcasted_iota(jnp.int32, (own, kept), 1) < lon_share
        sums = [jnp.zeros((own, kept), jnp.float32) for _ in range(4)]
        for band in range(bands):
            second_static = exact_dot(mixing[...], total_piece(back, band, own))
            field = fields[band, :, :kept].astype(jnp.float32)
            precise = field[slots * own : (slots + 1) * own]
            for t in range(slots):
                first = images[band, t * own : (t + 1) * own] + static[band]
                second = images[band, (slots + t) * own : (slots + t + 1) * own] + second_static
                weighted = precise * first
                sums[0] = sums[0] + precise * field[t * own : (t + 1) * own] * first
                sums[1] = sums[1] + weighted * first
                sums[2] = sums[2] + weighted * second
                sums[3] = sums[3] + precise * second * second
        lane = lax.broadcasted_iota(jnp.int32, (1, LANES), 1)
        row = jnp.zeros((1, LANES), jnp.float32)
        for index, part in enumerate(sums):
            part = jnp.where(inside, part, 0.0)
            part = jnp.sum(jnp.sum(part, axis=0, keepdims=True), axis=1, keepdims=True)
            row = row + jnp.where(lane == index, part, 0.0)
        sums_ref[...] = jnp.broadcast_to(row, sums_ref.shape)

    def join(slots, lon_share, back, images, static, mixing, pulling, grad_ref, pulled_ref, image_ref):
        own = static.shape[1]
        for band in range(bands):
            place = slice(band * lon_share, (band + 1) * lon_share)
            total = total_piece(back, band, own)
            second_static = exact_dot(mixing[...], total)
            pulled_ref[:, place] = exact_dot(pulling[...], total)[:, :lon_share]
            grad = jnp.concatenate(
                [back[member * bands + band, :own].astype(jnp.float32) for member in range(members)], axis=0
            )
            grad_ref[:, place] = grad[:, :lon_share]
            for t in range(slots):
                first = images[band, t * own : (t + 1) * own] + static[band]
                second = images[band, (slots + t) * own : (slots + t + 1) * own] + second_static
                image_ref[t * own : (t + 1) * own, place] = first[:, :lon_share]
                image_ref[(slots + t) * own : (slots + t + 1) * own, place] = second[:, :lon_share]

    def finish(slots, sums, grad_first, grad_second, pulled_first, pulled_second, images, member_ref, static_ref, image_ref):
        total = jnp.sum(sums[...], axis=0, keepdims=True)
        lane = lax.broadcasted_iota(jnp.int32, total.shape, 1)
        first_norm, first_image, cross, second_image = [
            jnp.sum(jnp.where(lane == index, total, 0.0), axis=1, keepdims=True) for index in range(4)
        ]
        alpha = first_norm / (first_norm + first_image)
        ratio = first_image / first_norm
        next_norm = alpha * alpha * jnp.maximum(cross - ratio * first_image, 0.0)
        beta = next_norm / first_norm
        apart = second_image - 2.0 * ratio * cross + ratio * ratio * first_image
        curvature = next_norm + alpha * alpha * apart - beta * next_norm / alpha
        alpha_next = jnp.clip(next_norm / curvature, 0.0, 1.0)
        on_first = alpha + alpha_next * (1.0 - alpha + beta)
        on_second = -alpha * alpha_next
        levels, rows = static_ref.shape[:2]
        member = on_first * grad_first[...] + on_second * grad_second[...]
        static = on_first * pulled_first[...] + on_second * pulled_second[...]
        for level in range(levels):
            place = slice(level * rows, (level + 1) * rows)
            member_ref[0, level] = member[place]
            static_ref[level] = static[place]
        half = images.shape[0] // 2
        image = on_first * images[:half] + on_second * images[half:]
        level_share = image_ref.shape[1]
        for t in range(slots):
            for level in range(level_share):
                start = (t * level_share + level) * rows
                image_ref[t, level] = image[start : start + rows]

    def shards(ensemble, member_weight, member_of_slot, halfwidth, static_root, innovation, precision):
        _, slots, levels, rows, lon = ensemble.shape
        level_share, lon_share = levels // members, lon // bands
        own = level_share * rows
        halo = REACHES * LREACH
        width = lon_share + 2 * halo
        padded = round_up(width + 1, LANES)
        kept = min(padded, round_up(lon_share, LANES))
        vmem = pl.BlockSpec(memory_space=pltpu.VMEM)
        smem = pl.BlockSpec(memory_space=pltpu.SMEM)

        def call(body, name, shapes, specs, *operands, flops=0):
            return pl.pallas_call(
                body,
                out_shape=tuple(jax.ShapeDtypeStruct(shape, kind) for shape, kind in shapes),
                in_specs=specs,
                out_specs=(vmem,) * len(shapes),
                compiler_params=pltpu.CompilerParams(vmem_limit_bytes=48 * 1024 * 1024),
                cost_estimate=pl.CostEstimate(flops=flops, bytes_accessed=1 << 20, transcendentals=0),
                name=name,
            )(*operands)

        pieces = windows(
            ensemble[0], bands, halo, padded, member_of_slot.astype(jnp.bfloat16)[0]
        ).reshape(bands, slots, members, own, padded)
        pieces = jnp.transpose(pieces, (2, 0, 1, 3, 4)).reshape(members * bands, slots * own, padded)
        pieces, ensemble, member_weight, member_of_slot, halfwidth, static_root, innovation, precision = (
            lax.optimization_barrier(
                (pieces, ensemble, member_weight, member_of_slot, halfwidth, static_root, innovation, precision)
            )
        )
        stacked = lax.all_to_all(pieces, BOTH, 0, 0, tiled=True)

        first_level = lax.axis_index("member") * level_share

        def own_levels(field, axis):
            return lax.dynamic_slice_in_dim(field, first_level, level_share, axis)

        innovation = innovation.reshape(slots, levels * rows, lon)
        precision = precision.reshape(levels * rows, lon)
        weighted = precision.astype(jnp.float32)[None] * innovation.astype(jnp.float32)
        total = jnp.sum(weighted, axis=0)
        pulling = each_row(static_share * static_root.T, rows)
        own_root = each_row(static_share * own_levels(static_root, 0), rows)
        mixing = exact_dot(own_root, pulling)
        pulled = exact_dot(pulling, total)
        static = exact_dot(own_root, pulled)

        def own_rows(field, axis):
            return lax.dynamic_slice_in_dim(field, first_level * rows, own, axis)

        fields = jnp.concatenate(
            [own_rows(innovation, 1), own_rows(precision, 0)[None], static.astype(jnp.bfloat16)[None]]
        ).reshape((slots + 2) * own, lon)
        here_fields = windows(fields, bands, halo, padded, jnp.zeros((), jnp.bfloat16))
        fields = exchange_bands(here_fields)
        static = jnp.pad(
            jnp.transpose(static.reshape(own, bands, lon_share), (1, 0, 2)),
            ((0, 0), (0, 0), (0, kept - lon_share)),
        )

        picker = (member_of_slot[0] == jnp.arange(member_weight.shape[0], dtype=jnp.int32)).astype(
            jnp.float32
        )
        scale = jnp.sum(picker * member_weight)
        folded = scale * jnp.sum(
            ensemble.reshape(slots, levels * rows, lon).astype(jnp.float32) * weighted, axis=0
        )
        smoothed = smooth_longitude(folded.astype(jnp.bfloat16), LREACH, 3)
        below, above = neighbours(smoothed)
        (grad_first,) = call(
            first_gradient,
            "first_gradient",
            [((levels * rows, lon), jnp.float32)],
            [vmem] * 4,
            below,
            smoothed,
            above,
            halo_taper(halfwidth, rows),
        )

        ring = ring_kernel(width, padded)
        per_member = bands * own
        copies = members
        while copies > 1 and (copies * per_member > 256 or members % copies):
            copies -= 1
        taper = taper_matrix(own_levels(halfwidth, 0), bands, rows, copies)

        out, image_first, grad = call(
            lambda *refs: first_half(slots, width, kept, *refs),
            "first_half",
            [
                ((members * bands, 2 * own, kept), jnp.bfloat16),
                ((bands, slots * own, kept), jnp.float32),
                ((members * per_member, padded), jnp.bfloat16),
            ],
            [smem, vmem, vmem, vmem, vmem],
            member_weight,
            stacked,
            fields,
            ring,
            taper,
            flops=10**9,
        )
        back = lax.all_to_all(out, BOTH, 0, 0, tiled=True)
        (image_second,) = call(
            lambda *refs: second_half(slots, width, kept, *refs),
            "second_half",
            [((bands, slots * own, kept), jnp.float32)],
            [smem, vmem, vmem, vmem, vmem],
            member_weight,
            stacked,
            grad,
            ring,
            taper,
            flops=10**9,
        )
        images = exchange_bands(jnp.concatenate([image_first, image_second], axis=1))

        (sums,) = call(
            lambda *refs: inner_products(slots, lon_share, *refs),
            "inner_products",
            [((members * bands, LANES), jnp.float32)],
            [vmem] * 5,
            back,
            images,
            here_fields,
            static,
            mixing,
        )
        sums = lax.all_to_all(sums, BOTH, 0, 0, tiled=True)
        grad_second, pulled_second, images = call(
            lambda *refs: join(slots, lon_share, *refs),
            "join",
            [
                ((levels * rows, lon), jnp.float32),
                ((levels * rows, lon), jnp.float32),
                ((2 * slots * own, lon), jnp.float32),
            ],
            [vmem] * 5,
            back,
            images,
            static,
            mixing,
            pulling,
            flops=10**9,
        )
        return call(
            lambda *refs: finish(slots, *refs),
            "finish",
            [
                ((1, levels, rows, lon), jnp.float32),
                ((levels, rows, lon), jnp.float32),
                ((slots, level_share, rows, lon), jnp.float32),
            ],
            [vmem] * 6,
            sums,
            grad_first,
            grad_second,
            pulled,
            pulled_second,
            images,
        )

    return jax.shard_map(
        shards,
        mesh=mesh,
        in_specs=(
            P("member", None, None, "band", None),
            P(),
            P("member"),
            P(),
            P(),
            P(None, None, "band", None),
            P(None, "band", None),
        ),
        out_specs=(
            P("member", None, "band", None),
            P(None, "band", None),
            P(None, "member", "band", None),
        ),
        check_vma=False,
    )
```

```python
import math

import jax
import jax.numpy as jnp
from jax import lax
from jax.experimental import pallas as pl
from jax.experimental.pallas import tpu as pltpu
from jax.sharding import PartitionSpec as P

HMAX = 4
LREACH = 18
REACHES = 4
LANES = 128
BOTH = ("member", "band")

ensemble_share = 0.8
static_share = 0.6
length_scale = 6.0


def round_up(value, step):
    return -(-value // step) * step


def neighbours(block):
    count = lax.axis_size("band")
    forward = [(i, i + 1) for i in range(count - 1)]
    backward = [(target, source) for source, target in forward]
    return lax.ppermute(block, "band", forward), lax.ppermute(block, "band", backward)


def kernel_values(distance):
    values = jnp.exp(-0.5 * (distance / length_scale) ** 2) / (
        length_scale * math.sqrt(2.0 * math.pi)
    )
    return jnp.where(distance <= LREACH, values, jnp.zeros_like(values)).astype(jnp.bfloat16)


def lon_kernel(reach, width):
    rows_index = jnp.arange(width + 2 * reach, dtype=jnp.int32)[:, None]
    cols_index = jnp.arange(width, dtype=jnp.int32)[None, :]
    return kernel_values(jnp.abs(rows_index - reach - cols_index).astype(jnp.float32))


def ring_kernel(width, padded):
    rows_index = jnp.arange(padded, dtype=jnp.int32)[:, None]
    cols_index = jnp.arange(padded, dtype=jnp.int32)[None, :]
    apart = jnp.abs(rows_index - cols_index)
    distance = jnp.minimum(apart, width - apart).astype(jnp.float32)
    inside = (rows_index < width) & (cols_index < width)
    return jnp.where(inside, kernel_values(distance), 0).astype(jnp.bfloat16)


def halves(full):
    high = full.astype(jnp.bfloat16)
    low = (full - high.astype(jnp.float32)).astype(jnp.bfloat16)
    return jnp.stack([high, low])


def halo_taper(halfwidth, rows):
    levels = halfwidth.shape[0]
    own = levels * rows
    target = jnp.arange(own, dtype=jnp.int32)[:, None]
    source = jnp.arange(3 * own, dtype=jnp.int32)[None, :]
    spans = jnp.repeat(halfwidth.astype(jnp.float32), rows)[:, None] + 1.0
    shift = (source // own - 1) * rows + source % rows - target % rows
    same = source // rows % levels == target // rows
    near = jnp.maximum(1.0 - jnp.abs(shift).astype(jnp.float32) / spans, 0.0) / spans
    return halves(jnp.where(same, near, 0.0))


def each_row(matrix, rows):
    same = jnp.eye(rows, dtype=jnp.float32)
    wide = matrix[:, None, :, None] * same[None, :, None, :]
    return wide.reshape(matrix.shape[0] * rows, matrix.shape[1] * rows)


def exact_dot(matrix, field):
    return jnp.dot(
        matrix, field, precision=lax.Precision.HIGHEST, preferred_element_type=jnp.float32
    )


def taper_matrix(halfwidth, bands, rows, copies):
    levels = halfwidth.shape[0]
    per_copy = bands * levels * rows
    index = jnp.arange(copies * per_copy, dtype=jnp.int32)
    copy = index // per_copy
    band = index // (levels * rows) % bands
    level = index // rows % levels
    latitude = band * rows + index % rows
    spans = halfwidth.astype(jnp.float32)[level][:, None] + 1.0
    apart = jnp.abs(latitude[:, None] - latitude[None, :]).astype(jnp.float32)
    same = (copy[:, None] == copy[None, :]) & (level[:, None] == level[None, :])
    near = jnp.maximum(1.0 - apart / spans, 0.0) / spans
    return halves(jnp.where(same, near, 0.0))


def windows(field, count, halo, padded, fill):
    lon = field.shape[-1]
    share = lon // count
    ring = jnp.concatenate([field[..., lon - halo :], field, field[..., :halo]], axis=-1)
    tail = jnp.broadcast_to(fill, field.shape[:-1] + (padded - share - 2 * halo,)).astype(field.dtype)
    pieces = []
    for piece in range(count):
        start = piece * share
        pieces.append(
            jnp.concatenate(
                [ring[..., start + halo : start + 2 * halo + share], ring[..., start : start + halo], tail],
                axis=-1,
            )
        )
    return jnp.stack(pieces)


def exchange_bands(blocks):
    count = blocks.shape[0]
    if count > 8:
        return lax.all_to_all(blocks, "band", 0, 0, tiled=True)
    here = lax.axis_index("band")
    arrived = [lax.dynamic_index_in_dim(blocks, here, 0, keepdims=False)]
    for shift in range(1, count):
        outgoing = lax.dynamic_index_in_dim(blocks, lax.rem(here + shift, count), 0, keepdims=False)
        arrived.append(
            lax.ppermute(outgoing, "band", [(i, (i + shift) % count) for i in range(count)])
        )
    ordered = []
    for source in range(count):
        block = arrived[0]
        for shift in range(1, count):
            block = jnp.where(lax.rem(here - source + count, count) == shift, arrived[shift], block)
        ordered.append(block)
    return jnp.stack(ordered)


def spread(field, ring, taper):
    copies = taper.shape[1]
    smoothed = jnp.dot(field.astype(jnp.bfloat16), ring, preferred_element_type=jnp.float32)
    smoothed = smoothed.astype(jnp.bfloat16)
    parts = []
    for start in range(0, field.shape[0], copies):
        part = smoothed[start : start + copies]
        parts.append(
            jnp.dot(taper[0], part, preferred_element_type=jnp.float32)
            + jnp.dot(taper[1], part, preferred_element_type=jnp.float32)
        )
    return parts[0] if len(parts) == 1 else jnp.concatenate(parts, axis=0)


def load_members(stacked, weight, members, bands, slots, width):
    own = stacked.shape[1] // slots
    stacked = stacked.astype(jnp.float32)
    which = stacked[:, :1, width : width + 1]
    scale = jnp.zeros(which.shape, jnp.float32)
    for member in range(members):
        scale = scale + jnp.where(which == member, weight[member], 0.0)
    shape = (members, bands * own, stacked.shape[-1])
    return [
        (scale * stacked[:, slot * own : (slot + 1) * own]).reshape(shape) for slot in range(slots)
    ]


def solution(mesh):
    members, bands = mesh.shape["member"], mesh.shape["band"]

    def first_half(slots, width, kept, weight, stacked, fields, ring, taper, out_ref, image_ref, grad_ref):
        scaled = load_members(stacked[...], weight, members, bands, slots, width)
        rows, padded = scaled[0].shape[1:]
        own = rows // bands
        fields = fields[...].astype(jnp.float32)

        def field(index):
            return fields[:, index * own : (index + 1) * own].reshape(rows, padded)

        precise, static = field(slots), field(slots + 1)

        def fold(weighted):
            total = scaled[0] * weighted[0][None]
            for slot in range(1, slots):
                total = total + scaled[slot] * weighted[slot][None]
            return total.reshape(members * rows, padded)

        grad = ensemble_share * spread(fold([precise * field(t) for t in range(slots)]), ring[...], taper)
        local = spread(grad, ring[...], taper).reshape(members, rows, padded)
        image = [ensemble_share * jnp.sum(scaled[t] * local, axis=0) for t in range(slots)]
        weighted = [precise * (image[t] + static) for t in range(slots)]
        grad = ensemble_share * spread(fold(weighted), ring[...], taper)
        grad_ref[...] = grad.astype(jnp.bfloat16)
        total = weighted[0]
        for t in range(1, slots):
            total = total + weighted[t]
        grad = grad[:, :kept].reshape(members, bands, own, kept)
        total = total[:, :kept].reshape(bands, own, kept)
        for member in range(members):
            for band in range(bands):
                out_ref[member * bands + band] = jnp.concatenate(
                    [grad[member, band], total[band]], axis=0
                ).astype(jnp.bfloat16)
        for t in range(slots):
            image_ref[:, t * own : (t + 1) * own] = image[t][:, :kept].reshape(bands, own, kept)

    def second_half(slots, width, kept, weight, stacked, grad, ring, taper, image_ref):
        scaled = load_members(stacked[...], weight, members, bands, slots, width)
        rows, padded = scaled[0].shape[1:]
        own = rows // bands
        local = spread(grad[...], ring[...], taper).reshape(members, rows, padded)
        for t in range(slots):
            image = ensemble_share * jnp.sum(scaled[t] * local, axis=0)
            image_ref[:, t * own : (t + 1) * own] = image[:, :kept].reshape(bands, own, kept)

    def pack(slots, levels, rows, halo, marks, ensemble, out_ref):
        values = ensemble[...].astype(jnp.float32)
        lon = values.shape[1]
        share, own = lon // bands, levels // members * rows
        tail = out_ref.shape[2] - share - 2 * halo
        mark = jnp.full((values.shape[0], tail), marks[0], jnp.int32).astype(jnp.float32)
        for band in range(bands):
            start = band * share
            parts = [values[:, start : min(lon, start + share + halo)]]
            if start + share + halo > lon:
                parts.append(values[:, : start + share + halo - lon])
            if start < halo:
                parts.append(values[:, lon - halo + start :])
            parts += [values[:, max(start - halo, 0) : start]] if start else []
            window = jnp.concatenate(parts + [mark], axis=1)
            for member in range(members):
                picked = [
                    window[slot * levels * rows + member * own : slot * levels * rows + (member + 1) * own]
                    for slot in range(slots)
                ]
                out_ref[member * bands + band] = jnp.concatenate(picked, axis=0).astype(jnp.bfloat16)

    def fold_smooth(slots, scale, ensemble, innovation, precision, kernel, out_ref):
        count, lon = precision.shape
        precise = precision[...].astype(jnp.float32)
        total = jnp.zeros((count, lon), jnp.float32)
        for t in range(slots):
            place = slice(t * count, (t + 1) * count)
            weighted = precise * innovation[place].astype(jnp.float32)
            total = total + ensemble[place].astype(jnp.float32) * weighted
        total = scale[0] * total
        width = kernel.shape[1]
        margin = (kernel.shape[0] - width) // 2
        steps = -(-lon // width)
        after = steps * width + margin - lon
        ring = jnp.concatenate([total[:, lon - margin :], total, total[:, :after]], axis=1)
        ring = ring.astype(jnp.bfloat16)
        for step in range(steps):
            start, stop = step * width, min(lon, (step + 1) * width)
            piece = jnp.dot(
                ring[:, start : start + kernel.shape[0]], kernel[...], preferred_element_type=jnp.float32
            )
            out_ref[:, start:stop] = piece[:, : stop - start].astype(jnp.bfloat16)

    def first_gradient(below, here, above, taper, grad_ref):
        stacked = jnp.concatenate([below[...], here[...], above[...]], axis=0)
        grad_ref[...] = ensemble_share * (
            jnp.dot(taper[0], stacked, preferred_element_type=jnp.float32)
            + jnp.dot(taper[1], stacked, preferred_element_type=jnp.float32)
        )

    def total_piece(back, band, own):
        kept = back.shape[-1]
        pieces = [back[member * bands + band, own:].astype(jnp.float32) for member in range(members)]
        return jnp.concatenate(pieces, axis=0).reshape(members * own, kept)

    def inner_products(slots, lon_share, back, images, fields, static, mixing, sums_ref):
        own, kept = static.shape[1:]
        inside = lax.broadcasted_iota(jnp.int32, (own, kept), 1) < lon_share
        sums = [jnp.zeros((own, kept), jnp.float32) for _ in range(4)]
        for band in range(bands):
            second_static = exact_dot(mixing[...], total_piece(back, band, own))
            field = fields[band, :, :kept].astype(jnp.float32)
            precise = field[slots * own : (slots + 1) * own]
            for t in range(slots):
                first = images[band, t * own : (t + 1) * own] + static[band]
                second = images[band, (slots + t) * own : (slots + t + 1) * own] + second_static
                weighted = precise * first
                sums[0] = sums[0] + precise * field[t * own : (t + 1) * own] * first
                sums[1] = sums[1] + weighted * first
                sums[2] = sums[2] + weighted * second
                sums[3] = sums[3] + precise * second * second
        lane = lax.broadcasted_iota(jnp.int32, (1, LANES), 1)
        row = jnp.zeros((1, LANES), jnp.float32)
        for index, part in enumerate(sums):
            part = jnp.where(inside, part, 0.0)
            part = jnp.sum(jnp.sum(part, axis=0, keepdims=True), axis=1, keepdims=True)
            row = row + jnp.where(lane == index, part, 0.0)
        sums_ref[...] = jnp.broadcast_to(row, sums_ref.shape)

    def join(slots, lon_share, back, images, static, mixing, pulling, grad_ref, pulled_ref, image_ref):
        own = static.shape[1]
        for band in range(bands):
            place = slice(band * lon_share, (band + 1) * lon_share)
            total = total_piece(back, band, own)
            second_static = exact_dot(mixing[...], total)
            pulled_ref[:, place] = exact_dot(pulling[...], total)[:, :lon_share]
            grad = jnp.concatenate(
                [back[member * bands + band, :own].astype(jnp.float32) for member in range(members)], axis=0
            )
            grad_ref[:, place] = grad[:, :lon_share]
            for t in range(slots):
                first = images[band, t * own : (t + 1) * own] + static[band]
                second = images[band, (slots + t) * own : (slots + t + 1) * own] + second_static
                image_ref[t * own : (t + 1) * own, place] = first[:, :lon_share]
                image_ref[(slots + t) * own : (slots + t + 1) * own, place] = second[:, :lon_share]

    def finish(slots, sums, grad_first, grad_second, pulled_first, pulled_second, images, member_ref, static_ref, image_ref):
        total = jnp.sum(sums[...], axis=0, keepdims=True)
        lane = lax.broadcasted_iota(jnp.int32, total.shape, 1)
        first_norm, first_image, cross, second_image = [
            jnp.sum(jnp.where(lane == index, total, 0.0), axis=1, keepdims=True) for index in range(4)
        ]
        alpha = first_norm / (first_norm + first_image)
        ratio = first_image / first_norm
        next_norm = alpha * alpha * jnp.maximum(cross - ratio * first_image, 0.0)
        beta = next_norm / first_norm
        apart = second_image - 2.0 * ratio * cross + ratio * ratio * first_image
        curvature = next_norm + alpha * alpha * apart - beta * next_norm / alpha
        alpha_next = jnp.clip(next_norm / curvature, 0.0, 1.0)
        on_first = alpha + alpha_next * (1.0 - alpha + beta)
        on_second = -alpha * alpha_next
        levels, rows = static_ref.shape[:2]
        member = on_first * grad_first[...] + on_second * grad_second[...]
        static = on_first * pulled_first[...] + on_second * pulled_second[...]
        for level in range(levels):
            place = slice(level * rows, (level + 1) * rows)
            member_ref[0, level] = member[place]
            static_ref[level] = static[place]
        half = images.shape[0] // 2
        image = on_first * images[:half] + on_second * images[half:]
        level_share = image_ref.shape[1]
        for t in range(slots):
            for level in range(level_share):
                start = (t * level_share + level) * rows
                image_ref[t, level] = image[start : start + rows]

    def shards(ensemble, member_weight, member_of_slot, halfwidth, static_root, innovation, precision):
        _, slots, levels, rows, lon = ensemble.shape
        level_share, lon_share = levels // members, lon // bands
        own = level_share * rows
        halo = REACHES * LREACH
        width = lon_share + 2 * halo
        padded = round_up(width + 1, LANES)
        kept = min(padded, round_up(lon_share, LANES))
        vmem = pl.BlockSpec(memory_space=pltpu.VMEM)
        smem = pl.BlockSpec(memory_space=pltpu.SMEM)

        def call(body, name, shapes, specs, *operands, flops=0):
            return pl.pallas_call(
                body,
                out_shape=tuple(jax.ShapeDtypeStruct(shape, kind) for shape, kind in shapes),
                in_specs=specs,
                out_specs=(vmem,) * len(shapes),
                compiler_params=pltpu.CompilerParams(vmem_limit_bytes=48 * 1024 * 1024),
                cost_estimate=pl.CostEstimate(flops=flops, bytes_accessed=1 << 20, transcendentals=0),
                name=name,
            )(*operands)

        ensemble = ensemble.reshape(slots * levels * rows, lon)
        (pieces,) = call(
            lambda *refs: pack(slots, levels, rows, halo, *refs),
            "pack",
            [((members * bands, slots * own, padded), jnp.bfloat16)],
            [smem, vmem],
            member_of_slot,
            ensemble,
        )
        pieces, ensemble, member_weight, member_of_slot, halfwidth, static_root, innovation, precision = (
            lax.optimization_barrier(
                (pieces, ensemble, member_weight, member_of_slot, halfwidth, static_root, innovation, precision)
            )
        )
        stacked = lax.all_to_all(pieces, BOTH, 0, 0, tiled=True)

        first_level = lax.axis_index("member") * level_share

        def own_levels(field, axis):
            return lax.dynamic_slice_in_dim(field, first_level, level_share, axis)

        innovation = innovation.reshape(slots, levels * rows, lon)
        precision = precision.reshape(levels * rows, lon)
        weighted = precision.astype(jnp.float32)[None] * innovation.astype(jnp.float32)
        total = jnp.sum(weighted, axis=0)
        pulling = each_row(static_share * static_root.T, rows)
        own_root = each_row(static_share * own_levels(static_root, 0), rows)
        mixing = exact_dot(own_root, pulling)
        pulled = exact_dot(pulling, total)
        static = exact_dot(own_root, pulled)

        def own_rows(field, axis):
            return lax.dynamic_slice_in_dim(field, first_level * rows, own, axis)

        fields = jnp.concatenate(
            [own_rows(innovation, 1), own_rows(precision, 0)[None], static.astype(jnp.bfloat16)[None]]
        ).reshape((slots + 2) * own, lon)
        here_fields = windows(fields, bands, halo, padded, jnp.zeros((), jnp.bfloat16))
        fields = exchange_bands(here_fields)
        static = jnp.pad(
            jnp.transpose(static.reshape(own, bands, lon_share), (1, 0, 2)),
            ((0, 0), (0, 0), (0, kept - lon_share)),
        )

        ring = ring_kernel(width, padded)
        per_member = bands * own
        copies = members
        while copies > 1 and (copies * per_member > 256 or members % copies):
            copies -= 1
        taper = taper_matrix(own_levels(halfwidth, 0), bands, rows, copies)

        out, image_first, grad = call(
            lambda *refs: first_half(slots, width, kept, *refs),
            "first_half",
            [
                ((members * bands, 2 * own, kept), jnp.bfloat16),
                ((bands, slots * own, kept), jnp.float32),
                ((members * per_member, padded), jnp.bfloat16),
            ],
            [smem, vmem, vmem, vmem, vmem],
            member_weight,
            stacked,
            fields,
            ring,
            taper,
            flops=10**9,
        )
        back = lax.all_to_all(out, BOTH, 0, 0, tiled=True)
        (image_second,) = call(
            lambda *refs: second_half(slots, width, kept, *refs),
            "second_half",
            [((bands, slots * own, kept), jnp.float32)],
            [smem, vmem, vmem, vmem, vmem],
            member_weight,
            stacked,
            grad,
            ring,
            taper,
            flops=10**9,
        )
        images = exchange_bands(jnp.concatenate([image_first, image_second], axis=1))

        image_second, ensemble, innovation, precision = lax.optimization_barrier(
            (image_second, ensemble, innovation, precision)
        )
        picker = member_of_slot == jnp.arange(member_weight.shape[0], dtype=jnp.int32)
        scale = jnp.sum(picker.astype(jnp.float32) * member_weight, keepdims=True)
        (smoothed,) = call(
            lambda *refs: fold_smooth(slots, *refs),
            "fold_smooth",
            [((levels * rows, lon), jnp.bfloat16)],
            [smem, vmem, vmem, vmem, vmem],
            scale,
            ensemble,
            innovation.reshape(slots * levels * rows, lon),
            precision,
            lon_kernel(LANES, 2 * LANES),
        )
        below, above = neighbours(smoothed)

        (sums,) = call(
            lambda *refs: inner_products(slots, lon_share, *refs),
            "inner_products",
            [((members * bands, LANES), jnp.float32)],
            [vmem] * 5,
            back,
            images,
            here_fields,
            static,
            mixing,
        )
        sums, below, smoothed, above = lax.optimization_barrier((sums, below, smoothed, above))
        sums = lax.all_to_all(sums, BOTH, 0, 0, tiled=True)
        grad_second, pulled_second, images = call(
            lambda *refs: join(slots, lon_share, *refs),
            "join",
            [
                ((levels * rows, lon), jnp.float32),
                ((levels * rows, lon), jnp.float32),
                ((2 * slots * own, lon), jnp.float32),
            ],
            [vmem] * 5,
            back,
            images,
            static,
            mixing,
            pulling,
            flops=10**9,
        )
        (grad_first,) = call(
            first_gradient,
            "first_gradient",
            [((levels * rows, lon), jnp.float32)],
            [vmem] * 4,
            below,
            smoothed,
            above,
            halo_taper(halfwidth, rows),
            flops=10**9,
        )
        return call(
            lambda *refs: finish(slots, *refs),
            "finish",
            [
                ((1, levels, rows, lon), jnp.float32),
                ((levels, rows, lon), jnp.float32),
                ((slots, level_share, rows, lon), jnp.float32),
            ],
            [vmem] * 6,
            sums,
            grad_first,
            grad_second,
            pulled,
            pulled_second,
            images,
        )

    return jax.shard_map(
        shards,
        mesh=mesh,
        in_specs=(
            P("member", None, None, "band", None),
            P(),
            P("member"),
            P(),
            P(),
            P(None, None, "band", None),
            P(None, "band", None),
        ),
        out_specs=(
            P("member", None, "band", None),
            P(None, "band", None),
            P(None, "member", "band", None),
        ),
        check_vma=False,
    )
```

```python
import math

import jax
import jax.numpy as jnp
import numpy as np
from jax import lax
from jax.experimental import pallas as pl
from jax.experimental.pallas import tpu as pltpu
from jax.sharding import PartitionSpec as P

HMAX = 4
LREACH = 18
REACHES = 4
LANES = 128
FEW = 8
BOTH = ("member", "band")

ensemble_share = 0.8
static_share = 0.6
length_scale = 6.0


def round_up(value, step):
    return -(-value // step) * step


def lon_weights(distance):
    distance = distance.astype(np.float32)
    values = np.exp(np.float32(-0.5) * (distance / np.float32(length_scale)) ** 2)
    values = values / np.float32(length_scale * math.sqrt(2.0 * math.pi))
    return jnp.asarray(np.where(distance <= LREACH, values, 0.0), jnp.bfloat16)


def lon_kernel(reach, width):
    return lon_weights(np.abs(np.arange(width + 2 * reach)[:, None] - reach - np.arange(width)[None]))


def ring_kernel(width, padded):
    apart = np.abs(np.arange(padded)[:, None] - np.arange(padded)[None])
    inside = (np.arange(padded)[:, None] < width) & (np.arange(padded)[None] < width)
    return lon_weights(np.where(inside, np.minimum(apart, width - apart), 2 * LREACH))


def halves(full):
    high = full.astype(jnp.bfloat16)
    return high, (full - high.astype(jnp.float32)).astype(jnp.bfloat16)


def near(apart, spans):
    return jnp.maximum(1.0 - apart / spans, 0.0) / spans


def row_apart(bands, held, rows, copies):
    index = np.arange(copies * bands * held * rows)
    latitude = index // (held * rows) % bands * rows + index % rows
    level = index // rows % held
    copy = index // (bands * held * rows)
    same = (copy[:, None] == copy[None]) & (level[:, None] == level[None])
    apart = np.where(same, np.abs(latitude[:, None] - latitude[None]), 1000)
    return apart.astype(np.float32), level[:, None].astype(np.float32)


def halo_apart(levels, rows):
    own = levels * rows
    target, source = np.arange(own)[:, None], np.arange(3 * own)[None]
    shift = (source // own - 1) * rows + source % rows - target % rows
    same = source // rows % levels == target // rows
    level = (target // rows).astype(np.float32)
    return np.where(same, np.abs(shift), 1000).astype(np.float32), level


def each_row(matrix, rows):
    same = jnp.eye(rows, dtype=jnp.float32)
    wide = matrix[:, None, :, None] * same[None, :, None, :]
    return wide.reshape(matrix.shape[0] * rows, matrix.shape[1] * rows)


def exact_dot(matrix, field):
    return jnp.dot(
        matrix, field, precision=lax.Precision.HIGHEST, preferred_element_type=jnp.float32
    )


def window(values, band, share, halo, tail):
    lon = values.shape[1]
    start = band * share
    stop = start + share + halo
    parts = [values[:, start : min(lon, stop)]]
    if stop > lon:
        parts.append(values[:, : stop - lon])
    if start < halo:
        parts.append(values[:, lon - halo + start :])
    if start:
        parts.append(values[:, max(start - halo, 0) : start])
    return jnp.concatenate(parts + [tail], axis=1)


def spread(field, ring, taper):
    copies = taper.shape[1]
    smoothed = jnp.dot(field.astype(jnp.bfloat16), ring, preferred_element_type=jnp.float32)
    smoothed = smoothed.astype(jnp.bfloat16)
    parts = []
    for start in range(0, field.shape[0], copies):
        part = smoothed[start : start + copies]
        parts.append(
            jnp.dot(taper[0], part, preferred_element_type=jnp.float32)
            + jnp.dot(taper[1], part, preferred_element_type=jnp.float32)
        )
    return parts[0] if len(parts) == 1 else jnp.concatenate(parts, axis=0)


def solution(mesh):
    members, bands = mesh.shape["member"], mesh.shape["band"]
    groups = 2 if members % 2 == 0 else 1
    fellows = members // groups
    few = bands <= FEW

    def shards(ensemble, member_weight, member_of_slot, halfwidth, static_root, innovation, precision):
        _, slots, levels, rows, lon = ensemble.shape
        level_share, lon_share = levels // members, lon // bands
        own = level_share * rows
        held = groups * own
        halo = REACHES * LREACH
        width = lon_share + 2 * halo
        padded = round_up(width + 1, LANES)
        kept = min(padded, round_up(lon_share, LANES))
        per_member = bands * held
        copies = fellows
        while copies > 1 and (copies * per_member > 256 or fellows % copies):
            copies -= 1
        arrays = slots + 2
        vmem = pl.BlockSpec(memory_space=pltpu.VMEM)
        smem = pl.BlockSpec(memory_space=pltpu.SMEM)
        limit = min(48, max(14, 24 * fellows * bands * slots * held * padded // 2**20)) * 2**20

        def call(body, shapes, scalars, operands, scratch=(), flops=0):
            return pl.pallas_call(
                body,
                out_shape=tuple(jax.ShapeDtypeStruct(shape, kind) for shape, kind in shapes),
                in_specs=[smem] * len(scalars) + [vmem] * len(operands),
                out_specs=(vmem,) * len(shapes),
                scratch_shapes=[pltpu.VMEM(shape, kind) for shape, kind in scratch],
                compiler_params=pltpu.CompilerParams(vmem_limit_bytes=limit),
                cost_estimate=pl.CostEstimate(flops=flops, bytes_accessed=0, transcendentals=0),
                name=body.__name__,
            )(*scalars, *operands)

        f32, bf16 = jnp.float32, jnp.bfloat16

        def position(here):
            return lax.div(here[0], fellows), lax.rem(here[0], fellows), here[1]

        def level_of(group, fellow, share):
            return (group * fellows + fellow) * level_share + share

        def shifted(place, shift, count):
            return lax.rem(place + shift + count, count)

        def load_members(weight, stacked):
            stacked = stacked[...].astype(f32)
            which = stacked[:, :1, width : width + 1]
            scale = jnp.zeros(which.shape, f32)
            for member in range(members):
                scale = scale + jnp.where(which == member, weight[member], 0.0)
            shape = (fellows, per_member, padded)
            return [
                (scale * stacked[:, slot * held : (slot + 1) * held]).reshape(shape)
                for slot in range(slots)
            ]

        def fold(scaled, weighted):
            total = scaled[0] * weighted[0][None]
            for slot in range(1, slots):
                total = total + scaled[slot] * weighted[slot][None]
            return total.reshape(fellows * per_member, padded)

        def images_of(scaled, grad, ring, taper):
            local = spread(grad, ring, taper).reshape(fellows, per_member, padded)
            return [ensemble_share * jnp.sum(scaled[t] * local, axis=0) for t in range(slots)]

        def pack(marks, ensemble, out):
            values = jnp.concatenate(
                [ensemble[0, t, level].astype(f32) for t in range(slots) for level in range(levels)],
                axis=0,
            )
            tail = jnp.full((values.shape[0], padded - width), marks[0], jnp.int32).astype(f32)
            for band in range(bands):
                piece = window(values, band, lon_share, halo, tail)
                for fellow in range(fellows):
                    picked = []
                    for t in range(slots):
                        for group in range(groups):
                            start = (t * levels + level_of(group, fellow, 0)) * rows
                            picked.append(piece[start : start + own])
                    out[fellow * bands + band] = jnp.concatenate(picked, axis=0).astype(bf16)

        def observe(here, widths, innovation, precision, pulling, root, apart, level, *refs):
            outs, (pieces, pulled, mixing, taper, static, mixed, spans) = refs[:-7], refs[-7:]
            group_here, fellow_here, band_here = position(here)
            total = []
            for at in range(levels):
                precise = precision[at].astype(f32)
                part = precise * innovation[0, at].astype(f32)
                for t in range(1, slots):
                    part = part + precise * innovation[t, at].astype(f32)
                total.append(part)
            back = exact_dot(pulling[...], jnp.concatenate(total, axis=0))
            pulled[...] = back
            forth = exact_dot(root[...], back)
            both = exact_dot(root[...], pulling[...])
            for at in range(levels):
                static[at] = forth[at * rows : (at + 1) * rows]
                mixed[at] = both[at * rows : (at + 1) * rows]

            def of_levels(picked):
                parts = [innovation[t, at].astype(f32) for t in range(slots) for at in picked]
                parts += [precision[at].astype(f32) for at in picked] + [static[at] for at in picked]
                return jnp.concatenate(parts, axis=0)

            picked = [level_of(group_here, fellow_here, share) for share in range(level_share)]
            mixing[...] = jnp.concatenate([mixed[at] for at in picked], axis=0)
            values = of_levels(picked)
            tail = jnp.zeros((values.shape[0], padded - width), f32)
            for band in range(bands):
                pieces[band] = window(values, band, lon_share, halo, tail)[:, :kept]

            picked = [
                level_of(group, fellow_here, share)
                for group in range(groups)
                for share in range(level_share)
            ]
            values = of_levels(picked)
            tail = jnp.zeros((values.shape[0], padded - width), f32)
            for band in range(bands):
                piece = window(values, band, lon_share, halo, tail).astype(bf16)
                if few:
                    spans[band] = piece
                else:
                    outs[0][band] = piece
            if few:
                for shift in range(bands):
                    outs[shift][...] = spans[shifted(band_here, shift, bands)]
            span = jnp.ones(level.shape, f32)
            for at, which in enumerate(picked):
                span = span + jnp.where(level[...] == at, widths[which].astype(f32), 0.0)
            taper[0], taper[1] = halves(near(apart[...], span))

        def first_image(here, weight, stacked, ring, taper, *refs):
            blocks, (part, send, fields, spans) = refs[:-4], refs[-4:]
            _, _, band_here = position(here)
            if few:
                for shift in range(bands):
                    spans[shifted(band_here, -shift, bands)] = blocks[shift][...]
                values = spans[...]
            else:
                values = blocks[0][...]
            field = []
            for index in range(arrays):
                piece = values[:, index * held : (index + 1) * held].reshape(per_member, padded)
                fields[index] = piece
                field.append(piece.astype(f32))
            scaled = load_members(weight, stacked)
            weighted = [field[slots] * field[t] for t in range(slots)]
            grad = ensemble_share * spread(fold(scaled, weighted), ring[...], taper)
            for t, image in enumerate(images_of(scaled, grad, ring[...], taper)):
                part[t] = image
                send[t] = image.astype(bf16)

        def second_gradient(here, weight, stacked, ring, taper, part, fields, *refs):
            others, (out, image_out, grad_out) = refs[:-3], refs[-3:]
            scaled = load_members(weight, stacked)
            precise, static = fields[slots].astype(f32), fields[slots + 1].astype(f32)
            weighted, total = [], jnp.zeros((per_member, padded), f32)
            for t in range(slots):
                image = part[t]
                for other in others:
                    image = image + other[t].astype(f32)
                image_out[t] = image[:, :kept].reshape(bands, groups, own, kept)
                weighted.append(precise * (image + static))
                total = total + weighted[t]
            grad = ensemble_share * spread(fold(scaled, weighted), ring[...], taper)
            grad_out[...] = grad.astype(bf16)
            grad = grad[:, :kept].reshape(fellows, bands, held, kept)
            total = total[:, :kept].reshape(bands, held, kept)
            for fellow in range(fellows):
                for band in range(bands):
                    out[fellow * bands + band] = jnp.concatenate(
                        [grad[fellow, band], total[band]], axis=0
                    ).astype(bf16)

        def second_image(here, weight, stacked, ring, taper, first, grad, *refs):
            outs, second = refs[:-1], refs[-1]
            group_here, _, band_here = position(here)
            scaled = load_members(weight, stacked)
            for t, image in enumerate(images_of(scaled, grad[...], ring[...], taper)):
                second[t] = image[:, :kept].reshape(bands, groups, own, kept)
            for apart in range(groups):
                for shift in range(bands):
                    if few:
                        group, band = shifted(group_here, apart, groups), shifted(band_here, shift, bands)
                        out = outs[apart * bands + shift]
                    else:
                        group, band, out = apart, shift, outs[0].at[apart, shift]
                    for t in range(slots):
                        out[t * own : (t + 1) * own] = second[t, band, group]
                    if not few or apart == 0:
                        for t in range(slots):
                            image = first[t, band, group]
                            if not few:
                                image = jnp.where(group_here == group, image, 0.0)
                            out[(slots + t) * own : (slots + t + 1) * own] = image

        def fold_smooth(marks, weight, ensemble, innovation, precision, kernel, out):
            total = []
            for at in range(levels):
                precise = precision[at].astype(f32)
                part = jnp.zeros((rows, lon), f32)
                for t in range(slots):
                    weighted = precise * innovation[t, at].astype(f32)
                    part = part + ensemble[0, t, at].astype(f32) * weighted
                total.append(part)
            total = weight[marks[0]] * jnp.concatenate(total, axis=0)
            step = kernel.shape[1]
            margin = (kernel.shape[0] - step) // 2
            steps = -(-lon // step)
            after = steps * step + margin - lon
            ring = jnp.concatenate([total[:, lon - margin :], total, total[:, :after]], axis=1)
            ring = ring.astype(bf16)
            for start in range(0, lon, step):
                stop = min(lon, start + step)
                piece = jnp.dot(
                    ring[:, start : start + kernel.shape[0]], kernel[...], preferred_element_type=f32
                )
                out[:, start:stop] = piece[:, : stop - start].astype(bf16)

        def first_gradient(widths, below, middle, above, apart, level, grad):
            span = jnp.ones(level.shape, f32)
            for at in range(levels):
                span = span + jnp.where(level[...] == at, widths[at].astype(f32), 0.0)
            high, low = halves(near(apart[...], span))
            stacked = jnp.concatenate([below[...], middle[...], above[...]], axis=0)
            grad[...] = ensemble_share * (
                jnp.dot(high, stacked, preferred_element_type=f32)
                + jnp.dot(low, stacked, preferred_element_type=f32)
            )

        def by_level(back, band, start):
            parts = []
            for group in range(groups):
                for fellow in range(fellows):
                    at = start + group * own
                    parts.append(back[fellow * bands + band, at : at + own].astype(f32))
            return jnp.concatenate(parts, axis=0)

        def gather_images(here, blocks, images):
            _, _, band_here = position(here)
            half = slots * own
            for shift in range(bands):
                if few:
                    place = shifted(band_here, -shift, bands)
                    second, first = blocks[shift][:half], blocks[shift][half:]
                    for apart in range(1, groups):
                        second = second + blocks[apart * bands + shift][...]
                else:
                    place = shift
                    second, first = blocks[0][0, shift, :half], blocks[0][0, shift, half:]
                    for group in range(1, groups):
                        second = second + blocks[0][group, shift, :half]
                        first = first + blocks[0][group, shift, half:]
                images[place, :half] = second
                images[place, half:] = first

        def inner_products(here, back, pieces, mixing, *refs):
            blocks, (sums, images) = refs[:-2], refs[-2:]
            gather_images(here, blocks, images)
            inside = lax.broadcasted_iota(jnp.int32, (own, kept), 1) < lon_share
            parts = [jnp.zeros((own, kept), f32) for _ in range(4)]
            for band in range(bands):
                second_static = exact_dot(mixing[...], by_level(back, band, held))
                field = pieces[band]
                precise = field[slots * own : (slots + 1) * own]
                first_static = field[(slots + 1) * own :]
                for t in range(slots):
                    second = images[band, t * own : (t + 1) * own] + second_static
                    first = images[band, (slots + t) * own : (slots + t + 1) * own] + first_static
                    weighted = precise * first
                    parts[0] = parts[0] + precise * field[t * own : (t + 1) * own] * first
                    parts[1] = parts[1] + weighted * first
                    parts[2] = parts[2] + weighted * second
                    parts[3] = parts[3] + precise * second * second
            lane = lax.broadcasted_iota(jnp.int32, (1, LANES), 1)
            row = jnp.zeros((1, LANES), f32)
            for index, part in enumerate(parts):
                part = jnp.where(inside, part, 0.0)
                part = jnp.sum(jnp.sum(part, axis=0, keepdims=True), axis=1, keepdims=True)
                row = row + jnp.where(lane == index, part, 0.0)
            sums[...] = jnp.broadcast_to(row, sums.shape)

        def join(here, back, pieces, mixing, pulling, *refs):
            blocks, (grad, pulled, image, images) = refs[:-4], refs[-4:]
            gather_images(here, blocks, images)
            for band in range(bands):
                place = slice(band * lon_share, (band + 1) * lon_share)
                total = by_level(back, band, held)
                second_static = exact_dot(mixing[...], total)
                pulled[:, place] = exact_dot(pulling[...], total)[:, :lon_share]
                grad[:, place] = by_level(back, band, 0)[:, :lon_share]
                first_static = pieces[band, (slots + 1) * own :]
                for t in range(2 * slots):
                    part = images[band, t * own : (t + 1) * own]
                    part = part + (second_static if t < slots else first_static)
                    image[t * own : (t + 1) * own, place] = part[:, :lon_share]

        def finish(sums, grad_first, grad_second, pulled_first, pulled_second, images, *outs):
            member_out, static_out, image_out = outs
            total = jnp.sum(sums[...], axis=0, keepdims=True)
            lane = lax.broadcasted_iota(jnp.int32, total.shape, 1)
            first_norm, first_image, cross, second_image = [
                jnp.sum(jnp.where(lane == index, total, 0.0), axis=1, keepdims=True)
                for index in range(4)
            ]
            alpha = first_norm / (first_norm + first_image)
            ratio = first_image / first_norm
            next_norm = alpha * alpha * jnp.maximum(cross - ratio * first_image, 0.0)
            beta = next_norm / first_norm
            apart = second_image - 2.0 * ratio * cross + ratio * ratio * first_image
            curvature = next_norm + alpha * alpha * apart - beta * next_norm / alpha
            alpha_next = jnp.clip(next_norm / curvature, 0.0, 1.0)
            on_first = alpha + alpha_next * (1.0 - alpha + beta)
            on_second = -alpha * alpha_next
            member = on_first * grad_first[...] + on_second * grad_second[...]
            static = on_first * pulled_first[...] + on_second * pulled_second[...]
            for level in range(levels):
                place = slice(level * rows, (level + 1) * rows)
                member_out[0, level] = member[place]
                static_out[level] = static[place]
            half = slots * own
            image = on_first * images[half:] + on_second * images[:half]
            for t in range(slots):
                for level in range(level_share):
                    start = (t * level_share + level) * rows
                    image_out[t, level] = image[start : start + rows]

        def trade(blocks, shifts):
            arrived = []
            for block, (apart, shift) in zip(blocks, shifts):
                if (apart, shift) == (0, 0):
                    arrived.append(block)
                    continue
                moves = []
                for member in range(members):
                    group, fellow = divmod(member, fellows)
                    target = (group + apart) % groups * fellows + fellow
                    for band in range(bands):
                        moves.append((member * bands + band, target * bands + (band + shift) % bands))
                arrived.append(lax.ppermute(block, BOTH, moves))
            return arrived

        group_devices = [
            [group * fellows * bands + at for at in range(fellows * bands)] for group in range(groups)
        ]

        def across_group(blocks):
            return lax.all_to_all(blocks, BOTH, 0, 0, tiled=True, axis_index_groups=group_devices)

        here = jnp.stack([lax.axis_index("member"), lax.axis_index("band")]).astype(jnp.int32)

        (pieces,) = call(
            pack,
            [((fellows * bands, slots * held, padded), bf16)],
            [member_of_slot],
            [ensemble],
        )
        pieces, ensemble, innovation, precision, static_root = lax.optimization_barrier(
            (pieces, ensemble, innovation, precision, static_root)
        )
        stacked = across_group(pieces)

        pulling = each_row(static_share * static_root.T, rows)
        root = each_row(static_share * static_root, rows)
        apart, level = row_apart(bands, groups * level_share, rows, copies)
        block = (arrays * held, padded)
        results = call(
            observe,
            ([(block, bf16)] * bands if few else [((bands,) + block, bf16)])
            + [
                ((bands, arrays * own, kept), f32),
                ((levels * rows, lon), f32),
                ((own, levels * rows), f32),
                ((2,) + apart.shape, bf16),
            ],
            [here, halfwidth],
            [innovation, precision, pulling, root, jnp.asarray(apart), jnp.asarray(level)],
            scratch=[
                ((levels, rows, lon), f32),
                ((levels, rows, levels * rows), f32),
                ((bands,) + block, bf16),
            ],
        )
        blocks, (own_pieces, pulled, mixing, taper) = results[:-4], results[-4:]
        if few:
            blocks = trade(blocks, [(0, shift) for shift in range(bands)])
        else:
            blocks = [lax.all_to_all(blocks[0], "band", 0, 0, tiled=True)]
        ring = ring_kernel(width, padded)

        part, send, fields = call(
            first_image,
            [
                ((slots, per_member, padded), f32),
                ((slots, per_member, padded), bf16),
                ((arrays, per_member, padded), bf16),
            ],
            [here, member_weight],
            [stacked, ring, taper, *blocks],
            scratch=[((bands,) + block, bf16)],
        )
        others = trade([send] * (groups - 1), [(apart, 0) for apart in range(1, groups)])

        send, ensemble, innovation, precision = lax.optimization_barrier(
            (send, ensemble, innovation, precision)
        )
        (smoothed,) = call(
            fold_smooth,
            [((levels * rows, lon), bf16)],
            [member_of_slot, member_weight],
            [ensemble, innovation, precision, lon_kernel(LANES, 2 * LANES)],
        )
        up = [(at, at + 1) for at in range(bands - 1)]
        below = lax.ppermute(smoothed, "band", up)
        above = lax.ppermute(smoothed, "band", [(target, source) for source, target in up])

        out, image_first, grad = call(
            second_gradient,
            [
                ((fellows * bands, 2 * held, kept), bf16),
                ((slots, bands, groups, own, kept), f32),
                ((fellows * per_member, padded), bf16),
            ],
            [here, member_weight],
            [stacked, ring, taper, part, fields, *others],
        )
        back = across_group(out)
        half = (slots * own, kept)
        full = (2 * slots * own, kept)
        if few:
            shapes = [(full, f32)] * bands + [(half, f32)] * ((groups - 1) * bands)
        else:
            shapes = [((groups, bands) + full, f32)]
        images = call(
            second_image,
            shapes,
            [here, member_weight],
            [stacked, ring, taper, image_first, grad],
            scratch=[((slots, bands, groups, own, kept), f32)],
            flops=10**9,
        )
        if few:
            images = trade(
                images, [(apart, shift) for apart in range(groups) for shift in range(bands)]
            )
        else:
            same_fellow = [
                [(group * fellows + fellow) * bands + band for group in range(groups) for band in range(bands)]
                for fellow in range(fellows)
            ]
            flat = images[0].reshape((groups * bands,) + full)
            flat = lax.all_to_all(flat, BOTH, 0, 0, tiled=True, axis_index_groups=same_fellow)
            images = [flat.reshape((groups, bands) + full)]

        gathered = [((bands,) + full, f32)]
        (sums,) = call(
            inner_products,
            [((members * bands, LANES), f32)],
            [here],
            [back, own_pieces, mixing, *images],
            scratch=gathered,
        )
        sums, smoothed = lax.optimization_barrier((sums, smoothed))
        sums = lax.all_to_all(sums, BOTH, 0, 0, tiled=True)
        grad_second, pulled_second, images = call(
            join,
            [((levels * rows, lon), f32), ((levels * rows, lon), f32), ((2 * slots * own, lon), f32)],
            [here],
            [back, own_pieces, mixing, pulling, *images],
            scratch=gathered,
            flops=10**9,
        )
        apart, level = halo_apart(levels, rows)
        (grad_first,) = call(
            first_gradient,
            [((levels * rows, lon), f32)],
            [halfwidth],
            [below, smoothed, above, jnp.asarray(apart), jnp.asarray(level)],
            flops=10**9,
        )
        return call(
            finish,
            [
                ((1, levels, rows, lon), f32),
                ((levels, rows, lon), f32),
                ((slots, level_share, rows, lon), f32),
            ],
            [],
            [sums, grad_first, grad_second, pulled, pulled_second, images],
        )

    return jax.shard_map(
        shards,
        mesh=mesh,
        in_specs=(
            P("member", None, None, "band", None),
            P(),
            P("member"),
            P(),
            P(),
            P(None, None, "band", None),
            P(None, "band", None),
        ),
        out_specs=(
            P("member", None, "band", None),
            P(None, "band", None),
            P(None, "member", "band", None),
        ),
        check_vma=False,
    )
```

```python
import math

import jax
import jax.numpy as jnp
import numpy as np
from jax import lax
from jax.experimental import pallas as pl
from jax.experimental.pallas import tpu as pltpu
from jax.sharding import PartitionSpec as P

HMAX = 4
LREACH = 18
REACHES = 4
LANES = 128
FEW = 8
SUMS = 4
PARTS = 3
BOTH = ("member", "band")

ensemble_share = 0.8
static_share = 0.6
length_scale = 6.0


def round_up(value, step):
    return -(-value // step) * step


def lon_weights(distance):
    distance = distance.astype(np.float32)
    values = np.exp(np.float32(-0.5) * (distance / np.float32(length_scale)) ** 2)
    values = values / np.float32(length_scale * math.sqrt(2.0 * math.pi))
    return jnp.asarray(np.where(distance <= LREACH, values, 0.0), jnp.bfloat16)


def lon_kernel(reach, width):
    return lon_weights(np.abs(np.arange(width + 2 * reach)[:, None] - reach - np.arange(width)[None]))


def ring_kernel(width, padded):
    apart = np.abs(np.arange(padded)[:, None] - np.arange(padded)[None])
    inside = (np.arange(padded)[:, None] < width) & (np.arange(padded)[None] < width)
    return lon_weights(np.where(inside, np.minimum(apart, width - apart), 2 * LREACH))


def halves(full):
    high = full.astype(jnp.bfloat16)
    return high, (full - high.astype(jnp.float32)).astype(jnp.bfloat16)


def near(apart, spans):
    return jnp.maximum(1.0 - apart / spans, 0.0) / spans


def row_apart(bands, held, rows, copies):
    index = np.arange(copies * bands * held * rows)
    latitude = index // (held * rows) % bands * rows + index % rows
    level = index // rows % held
    copy = index // (bands * held * rows)
    same = (copy[:, None] == copy[None]) & (level[:, None] == level[None])
    apart = np.where(same, np.abs(latitude[:, None] - latitude[None]), 1000)
    return apart.astype(np.float32), level[:, None].astype(np.float32)


def halo_apart(levels, rows):
    own = levels * rows
    target, source = np.arange(own)[:, None], np.arange(3 * own)[None]
    shift = (source // own - 1) * rows + source % rows - target % rows
    same = source // rows % levels == target // rows
    level = (target // rows).astype(np.float32)
    return np.where(same, np.abs(shift), 1000).astype(np.float32), level


def each_row(matrix, rows):
    same = jnp.eye(rows, dtype=jnp.float32)
    wide = matrix[:, None, :, None] * same[None, :, None, :]
    return wide.reshape(matrix.shape[0] * rows, matrix.shape[1] * rows)


def exact_dot(matrix, field):
    return jnp.dot(
        matrix, field, precision=lax.Precision.HIGHEST, preferred_element_type=jnp.float32
    )


def window(values, band, share, halo, tail):
    lon = values.shape[1]
    start = band * share
    stop = start + share + halo
    parts = [values[:, start : min(lon, stop)]]
    if stop > lon:
        parts.append(values[:, : stop - lon])
    if start < halo:
        parts.append(values[:, lon - halo + start :])
    if start:
        parts.append(values[:, max(start - halo, 0) : start])
    return jnp.concatenate(parts + [tail], axis=1)


def spread(field, ring, taper):
    copies = taper.shape[1]
    smoothed = jnp.dot(field.astype(jnp.bfloat16), ring, preferred_element_type=jnp.float32)
    smoothed = smoothed.astype(jnp.bfloat16)
    parts = []
    for start in range(0, field.shape[0], copies):
        part = smoothed[start : start + copies]
        parts.append(
            jnp.dot(taper[0], part, preferred_element_type=jnp.float32)
            + jnp.dot(taper[1], part, preferred_element_type=jnp.float32)
        )
    return parts[0] if len(parts) == 1 else jnp.concatenate(parts, axis=0)


def solution(mesh):
    members, bands = mesh.shape["member"], mesh.shape["band"]
    few = bands <= FEW

    def shards(ensemble, member_weight, member_of_slot, halfwidth, static_root, innovation, precision):
        _, slots, levels, rows, lon = ensemble.shape
        level_share, lon_share = levels // members, lon // bands
        own = level_share * rows
        halo = REACHES * LREACH
        width = lon_share + 2 * halo
        padded = round_up(width + 1, LANES)
        kept = round_up(lon_share + SUMS * PARTS, LANES)
        per_member = bands * own
        copies = members
        while copies > 1 and (copies * per_member > 256 or members % copies):
            copies -= 1
        arrays = slots + 2
        everything = levels * rows
        traded = everything + 4 * slots * own
        vmem = pl.BlockSpec(memory_space=pltpu.VMEM)
        smem = pl.BlockSpec(memory_space=pltpu.SMEM)
        limit = min(48, max(14, 24 * members * bands * slots * own * padded // 2**20)) * 2**20

        def call(body, shapes, scalars, operands, scratch=(), flops=0):
            return pl.pallas_call(
                body,
                out_shape=tuple(jax.ShapeDtypeStruct(shape, kind) for shape, kind in shapes),
                in_specs=[smem] * len(scalars) + [vmem] * len(operands),
                out_specs=(vmem,) * len(shapes),
                scratch_shapes=[pltpu.VMEM(shape, kind) for shape, kind in scratch],
                compiler_params=pltpu.CompilerParams(vmem_limit_bytes=limit),
                cost_estimate=pl.CostEstimate(flops=flops, bytes_accessed=0, transcendentals=0),
                name=body.__name__,
            )(*scalars, *operands)

        f32, bf16 = jnp.float32, jnp.bfloat16

        def shifted(place, shift):
            return lax.rem(place + shift + bands, bands)

        def load_members(weight, stacked):
            stacked = stacked[...].astype(f32)
            which = stacked[:, :1, width : width + 1]
            scale = jnp.zeros(which.shape, f32)
            for member in range(members):
                scale = scale + jnp.where(which == member, weight[member], 0.0)
            shape = (members, per_member, padded)
            return [
                (scale * stacked[:, slot * own : (slot + 1) * own]).reshape(shape)
                for slot in range(slots)
            ]

        def fold(scaled, weighted):
            total = scaled[0] * weighted[0][None]
            for slot in range(1, slots):
                total = total + scaled[slot] * weighted[slot][None]
            return total.reshape(members * per_member, padded)

        def images_of(scaled, grad, ring, taper):
            local = spread(grad, ring, taper).reshape(members, per_member, padded)
            return [ensemble_share * jnp.sum(scaled[t] * local, axis=0) for t in range(slots)]

        def pack(marks, ensemble, out):
            values = jnp.concatenate(
                [ensemble[0, t, level].astype(f32) for t in range(slots) for level in range(levels)],
                axis=0,
            )
            tail = jnp.full((values.shape[0], padded - width), marks[0], jnp.int32).astype(f32)
            for band in range(bands):
                piece = window(values, band, lon_share, halo, tail)
                for member in range(members):
                    picked = []
                    for t in range(slots):
                        start = t * everything + member * own
                        picked.append(piece[start : start + own])
                    out[member * bands + band] = jnp.concatenate(picked, axis=0).astype(bf16)

        def observe(here, widths, innovation, precision, pulling, root, apart, level, *refs):
            outs, (own_static, pulled, mixing, taper, static, mixed, spans) = refs[:-7], refs[-7:]
            total = []
            for at in range(levels):
                precise = precision[at].astype(f32)
                part = precise * innovation[0, at].astype(f32)
                for t in range(1, slots):
                    part = part + precise * innovation[t, at].astype(f32)
                total.append(part)
            back = exact_dot(pulling[...], jnp.concatenate(total, axis=0))
            pulled[...] = back
            forth = exact_dot(root[...], back)
            both = exact_dot(root[...], pulling[...])
            for at in range(levels):
                static[at] = forth[at * rows : (at + 1) * rows]
                mixed[at] = both[at * rows : (at + 1) * rows]
            picked = [here[0] * level_share + share for share in range(level_share)]
            mixing[...] = jnp.concatenate([mixed[at] for at in picked], axis=0)
            parts = [innovation[t, at].astype(f32) for t in range(slots) for at in picked]
            parts += [precision[at].astype(f32) for at in picked] + [static[at] for at in picked]
            values = jnp.concatenate(parts, axis=0)
            tail = jnp.zeros((values.shape[0], padded - width), f32)
            for band in range(bands):
                piece = window(values, band, lon_share, halo, tail)
                own_static[band] = piece[(slots + 1) * own :, :kept]
                if few:
                    spans[band] = piece.astype(bf16)
                else:
                    outs[0][band] = piece.astype(bf16)
            if few:
                for shift in range(bands):
                    outs[shift][...] = spans[shifted(here[1], shift)]
            span = jnp.ones(level.shape, f32)
            for at, which in enumerate(picked):
                span = span + jnp.where(level[...] == at, widths[which].astype(f32), 0.0)
            taper[0], taper[1] = halves(near(apart[...], span))

        def first_half(here, weight, stacked, ring, taper, *refs):
            blocks, (total_out, grad_out, full_out, image_out, fields, spans) = refs[:-6], refs[-6:]
            if few:
                for shift in range(bands):
                    spans[shifted(here[1], -shift)] = blocks[shift][...]
                values = spans[...]
            else:
                values = blocks[0][...]
            field = []
            for index in range(arrays):
                piece = values[:, index * own : (index + 1) * own].astype(f32)
                piece = piece.reshape(per_member, padded)
                fields[index] = piece[:, :kept]
                field.append(piece)
            precise, static = field[slots], field[slots + 1]
            scaled = load_members(weight, stacked)
            weighted = [precise * field[t] for t in range(slots)]
            grad = ensemble_share * spread(fold(scaled, weighted), ring[...], taper)
            total = jnp.zeros((per_member, padded), f32)
            weighted = []
            for t, image in enumerate(images_of(scaled, grad, ring[...], taper)):
                image_out[t] = image[:, :kept]
                weighted.append(precise * (image + static))
                total = total + weighted[t]
            total = total[:, :kept].astype(bf16)
            for member in range(members):
                total_out[member] = total
            grad = (ensemble_share * spread(fold(scaled, weighted), ring[...], taper)).astype(bf16)
            full_out[...] = grad
            grad_out[...] = grad[:, :kept].reshape(members * bands, own, kept)

        def second_image(weight, stacked, ring, taper, grad, image_out):
            scaled = load_members(weight, stacked)
            for t, image in enumerate(images_of(scaled, grad[...], ring[...], taper)):
                image_out[t] = image[:, :kept]

        def combine(here, total, grad, first, second, fields, mixing, *refs):
            outs, (out, spans) = refs[:-2], refs[-2:]
            mixed, precise, static = [], fields[slots], fields[slots + 1]
            for band in range(bands):
                place = slice(band * own, (band + 1) * own)
                every = jnp.concatenate([total[member, place].astype(f32) for member in range(members)], axis=0)
                mixed.append(exact_dot(mixing[...], every))
                spans[band, :everything] = every.astype(bf16)
            mixed = jnp.concatenate(mixed, axis=0)
            sums = [jnp.zeros((per_member, kept), f32) for _ in range(SUMS)]
            for t in range(slots):
                image = second[t] + mixed
                whole = first[t] + static
                weighted = precise * whole
                sums[0] = sums[0] + precise * fields[t] * whole
                sums[1] = sums[1] + weighted * whole
                sums[2] = sums[2] + weighted * image
                sums[3] = sums[3] + precise * image * image
                for which, values in enumerate((first[t], image)):
                    for half, part in enumerate(halves(values)):
                        at = everything + ((half * 2 + which) * slots + t) * own
                        for band in range(bands):
                            spans[band, at : at + own] = part[band * own : (band + 1) * own]
            for shift in range(bands):
                if few:
                    outs[shift][...] = spans[shifted(here[1], shift)]
                else:
                    outs[0][shift] = spans[shift]
            inside = lax.broadcasted_iota(jnp.int32, (per_member, kept), 1) < lon_share
            lane = lax.broadcasted_iota(jnp.int32, (1, kept), 1) - lon_share
            row = jnp.zeros((1, kept), f32)
            for index, part in enumerate(sums):
                part = jnp.where(inside, part, 0.0)
                part = jnp.sum(jnp.sum(part, axis=0, keepdims=True), axis=1, keepdims=True)
                for piece in range(PARTS):
                    high = part.astype(bf16).astype(f32)
                    row = row + jnp.where(lane == PARTS * index + piece, high, 0.0)
                    part = part - high
            shape = (own, kept)
            lane = lax.broadcasted_iota(jnp.int32, shape, 1)
            row = jnp.broadcast_to(row, shape)
            for block in range(members * bands):
                out[block] = jnp.where(lane < lon_share, grad[block].astype(f32), row).astype(bf16)

        def fold_smooth(marks, weight, ensemble, innovation, precision, kernel, out):
            total = []
            for at in range(levels):
                precise = precision[at].astype(f32)
                part = jnp.zeros((rows, lon), f32)
                for t in range(slots):
                    weighted = precise * innovation[t, at].astype(f32)
                    part = part + ensemble[0, t, at].astype(f32) * weighted
                total.append(part)
            total = weight[marks[0]] * jnp.concatenate(total, axis=0)
            step = kernel.shape[1]
            margin = (kernel.shape[0] - step) // 2
            steps = -(-lon // step)
            after = steps * step + margin - lon
            ring = jnp.concatenate([total[:, lon - margin :], total, total[:, :after]], axis=1)
            ring = ring.astype(bf16)
            for start in range(0, lon, step):
                stop = min(lon, start + step)
                piece = jnp.dot(
                    ring[:, start : start + kernel.shape[0]], kernel[...], preferred_element_type=f32
                )
                out[:, start:stop] = piece[:, : stop - start].astype(bf16)

        def first_gradient(widths, below, middle, above, apart, level, grad):
            span = jnp.ones(level.shape, f32)
            for at in range(levels):
                span = span + jnp.where(level[...] == at, widths[at].astype(f32), 0.0)
            high, low = halves(near(apart[...], span))
            stacked = jnp.concatenate([below[...], middle[...], above[...]], axis=0)
            grad[...] = ensemble_share * (
                jnp.dot(high, stacked, preferred_element_type=f32)
                + jnp.dot(low, stacked, preferred_element_type=f32)
            )

        def join(here, own_static, pulling, *refs):
            blocks, (pulled, images, spans) = refs[:-3], refs[-3:]
            for shift in range(bands):
                if few:
                    spans[shifted(here[1], -shift)] = blocks[shift][...]
                else:
                    spans[shift] = blocks[0][shift]
            size = 2 * slots * own
            for band in range(bands):
                place = slice(band * lon_share, (band + 1) * lon_share)
                every = spans[band, :everything].astype(f32)
                pulled[:, place] = exact_dot(pulling[...], every)[:, :lon_share]
                both = spans[band, everything : everything + size].astype(f32)
                both = both + spans[band, everything + size :].astype(f32)
                static = own_static[band]
                for t in range(slots):
                    at = slice(t * own, (t + 1) * own)
                    images[at, place] = (both[at] + static)[:, :lon_share]
                images[slots * own :, place] = both[slots * own :, :lon_share]

        def finish(back, grad_first, pulled_first, pulled_second, images, *refs):
            member_out, static_out, image_out, second = refs
            total = back[0, :1].astype(f32)
            for block in range(1, members * bands):
                total = total + back[block, :1].astype(f32)
            lane = lax.broadcasted_iota(jnp.int32, total.shape, 1) - lon_share
            first_norm, first_image, cross, second_image = [
                jnp.sum(
                    jnp.where((lane >= PARTS * index) & (lane < PARTS * (index + 1)), total, 0.0),
                    axis=1,
                    keepdims=True,
                )
                for index in range(SUMS)
            ]
            alpha = first_norm / (first_norm + first_image)
            ratio = first_image / first_norm
            next_norm = alpha * alpha * jnp.maximum(cross - ratio * first_image, 0.0)
            beta = next_norm / first_norm
            apart = second_image - 2.0 * ratio * cross + ratio * ratio * first_image
            curvature = next_norm + alpha * alpha * apart - beta * next_norm / alpha
            alpha_next = jnp.clip(next_norm / curvature, 0.0, 1.0)
            on_first = alpha + alpha_next * (1.0 - alpha + beta)
            on_second = -alpha * alpha_next
            for band in range(bands):
                grad = jnp.concatenate(
                    [back[member * bands + band].astype(f32) for member in range(members)], axis=0
                )
                second[:, band * lon_share : (band + 1) * lon_share] = grad[:, :lon_share]
            member = on_first * grad_first[...] + on_second * second[...]
            static = on_first * pulled_first[...] + on_second * pulled_second[...]
            for level in range(levels):
                place = slice(level * rows, (level + 1) * rows)
                member_out[0, level] = member[place]
                static_out[level] = static[place]
            half = slots * own
            image = on_first * images[:half] + on_second * images[half:]
            for t in range(slots):
                for level in range(level_share):
                    start = (t * level_share + level) * rows
                    image_out[t, level] = image[start : start + rows]

        def trade(blocks):
            if not few:
                return [lax.all_to_all(blocks[0], "band", 0, 0, tiled=True)]
            return [blocks[0]] + [
                lax.ppermute(blocks[shift], "band", [(at, (at + shift) % bands) for at in range(bands)])
                for shift in range(1, bands)
            ]

        def tradable(shape, kind):
            return [(shape, kind)] * bands if few else [((bands,) + shape, kind)]

        here = jnp.stack([lax.axis_index("member"), lax.axis_index("band")]).astype(jnp.int32)

        (pieces,) = call(
            pack, [((members * bands, slots * own, padded), bf16)], [member_of_slot], [ensemble]
        )
        pieces, ensemble, innovation, precision, static_root = lax.optimization_barrier(
            (pieces, ensemble, innovation, precision, static_root)
        )
        stacked = lax.all_to_all(pieces, BOTH, 0, 0, tiled=True)

        pulling = each_row(static_share * static_root.T, rows)
        root = each_row(static_share * static_root, rows)
        apart, level = row_apart(bands, level_share, rows, copies)
        block = (arrays * own, padded)
        results = call(
            observe,
            tradable(block, bf16)
            + [
                ((bands, own, kept), f32),
                ((everything, lon), f32),
                ((own, everything), f32),
                ((2,) + apart.shape, bf16),
            ],
            [here, halfwidth],
            [innovation, precision, pulling, root, jnp.asarray(apart), jnp.asarray(level)],
            scratch=[((levels, rows, lon), f32), ((levels, rows, everything), f32), ((bands,) + block, bf16)],
        )
        blocks, (own_static, pulled, mixing, taper) = trade(results[:-4]), results[-4:]
        ring = ring_kernel(width, padded)

        total, grad, full, image_first, fields = call(
            first_half,
            [
                ((members, per_member, kept), bf16),
                ((members * bands, own, kept), bf16),
                ((members * per_member, padded), bf16),
                ((slots, per_member, kept), f32),
                ((arrays, per_member, kept), f32),
            ],
            [here, member_weight],
            [stacked, ring, taper, *blocks],
            scratch=[((bands,) + block, bf16)],
        )
        total = lax.all_to_all(total, "member", 0, 0, tiled=True)
        (image_second,) = call(
            second_image,
            [((slots, per_member, kept), f32)],
            [member_weight],
            [stacked, ring, taper, full],
            flops=10**9,
        )

        image_second, ensemble, innovation, precision = lax.optimization_barrier(
            (image_second, ensemble, innovation, precision)
        )
        (smoothed,) = call(
            fold_smooth,
            [((everything, lon), bf16)],
            [member_of_slot, member_weight],
            [ensemble, innovation, precision, lon_kernel(LANES, 2 * LANES)],
        )
        up = [(at, at + 1) for at in range(bands - 1)]
        below = lax.ppermute(smoothed, "band", up)
        above = lax.ppermute(smoothed, "band", [(target, source) for source, target in up])

        results = call(
            combine,
            tradable((traded, kept), bf16) + [((members * bands, own, kept), bf16)],
            [here],
            [total, grad, image_first, image_second, fields, mixing],
            scratch=[((bands, traded, kept), bf16)],
        )
        back = lax.all_to_all(results[-1], BOTH, 0, 0, tiled=True)
        blocks = trade(results[:-1])
        pulled_second, images = call(
            join,
            [((everything, lon), f32), ((2 * slots * own, lon), f32)],
            [here],
            [own_static, pulling, *blocks],
            scratch=[((bands, traded, kept), bf16)],
        )
        apart, level = halo_apart(levels, rows)
        (grad_first,) = call(
            first_gradient,
            [((everything, lon), f32)],
            [halfwidth],
            [below, smoothed, above, jnp.asarray(apart), jnp.asarray(level)],
        )
        return call(
            finish,
            [
                ((1, levels, rows, lon), f32),
                ((levels, rows, lon), f32),
                ((slots, level_share, rows, lon), f32),
            ],
            [],
            [back, grad_first, pulled, pulled_second, images],
            scratch=[((everything, lon), f32)],
        )

    return jax.shard_map(
        shards,
        mesh=mesh,
        in_specs=(
            P("member", None, None, "band", None),
            P(),
            P("member"),
            P(),
            P(),
            P(None, None, "band", None),
            P(None, "band", None),
        ),
        out_specs=(
            P("member", None, "band", None),
            P(None, "band", None),
            P(None, "member", "band", None),
        ),
        check_vma=False,
    )
```

```python
import math

import jax
import jax.numpy as jnp
import numpy as np
from jax import lax
from jax.experimental import pallas as pl
from jax.experimental.pallas import tpu as pltpu
from jax.sharding import PartitionSpec as P

HMAX = 4
LREACH = 18
REACHES = 4
LANES = 128
FEW = 8
SUMS = 4
PARTS = 3
BOTH = ("member", "band")

ensemble_share = 0.8
static_share = 0.6
length_scale = 6.0


def round_up(value, step):
    return -(-value // step) * step


def lon_weights(distance):
    distance = distance.astype(np.float32)
    values = np.exp(np.float32(-0.5) * (distance / np.float32(length_scale)) ** 2)
    values = values / np.float32(length_scale * math.sqrt(2.0 * math.pi))
    return jnp.asarray(np.where(distance <= LREACH, values, 0.0), jnp.bfloat16)


def lon_kernel(reach, width):
    return lon_weights(np.abs(np.arange(width + 2 * reach)[:, None] - reach - np.arange(width)[None]))


def ring_kernel(width, padded):
    apart = np.abs(np.arange(padded)[:, None] - np.arange(padded)[None])
    inside = (np.arange(padded)[:, None] < width) & (np.arange(padded)[None] < width)
    return lon_weights(np.where(inside, np.minimum(apart, width - apart), 2 * LREACH))


def halves(full):
    high = full.astype(jnp.bfloat16)
    return high, (full - high.astype(jnp.float32)).astype(jnp.bfloat16)


def near(apart, spans):
    return jnp.maximum(spans - apart, 0.0).astype(jnp.bfloat16)


def row_apart(bands, held, rows, copies):
    index = np.arange(copies * bands * held * rows)
    latitude = index // (held * rows) % bands * rows + index % rows
    level = index // rows % held
    copy = index // (bands * held * rows)
    same = (copy[:, None] == copy[None]) & (level[:, None] == level[None])
    apart = np.where(same, np.abs(latitude[:, None] - latitude[None]), 1000)
    return apart.astype(np.float32), level[:, None].astype(np.float32)


def halo_apart(levels, rows):
    own = levels * rows
    target, source = np.arange(own)[:, None], np.arange(3 * own)[None]
    shift = (source // own - 1) * rows + source % rows - target % rows
    same = source // rows % levels == target // rows
    level = (target // rows).astype(np.float32)
    return np.where(same, np.abs(shift), 1000).astype(np.float32), level


def row_levels(levels, rows):
    index = np.arange(levels * rows)
    level = index[:, None] // rows == np.arange(levels)[None]
    place = index[:, None] % rows == index[None] % rows
    return level.astype(np.float32), place.astype(np.float32)


def exact_dot(matrix, field):
    return jnp.dot(
        matrix, field, precision=lax.Precision.HIGHEST, preferred_element_type=jnp.float32
    )


def parts_dot(matrix, field):
    count, parts = matrix.shape[0], []
    for _ in range(PARTS):
        part = matrix.astype(jnp.bfloat16).astype(jnp.float32)
        parts.append(part)
        matrix = matrix - part
    stacked = jnp.concatenate(parts, axis=0).astype(jnp.bfloat16)
    products = jnp.dot(stacked, field, preferred_element_type=jnp.float32)
    total = products[:count]
    for index in range(1, PARTS):
        total = total + products[index * count : (index + 1) * count]
    return total


def window(values, band, share, halo, tail):
    lon = values.shape[1]
    start = band * share
    stop = start + share + halo
    parts = [values[:, start : min(lon, stop)]]
    if stop > lon:
        parts.append(values[:, : stop - lon])
    if start < halo:
        parts.append(values[:, lon - halo + start :])
    if start:
        parts.append(values[:, max(start - halo, 0) : start])
    return jnp.concatenate(parts + [tail], axis=1)


def spread(field, ring, taper, factor):
    copies = taper.shape[0]
    smoothed = jnp.dot(field.astype(jnp.bfloat16), ring, preferred_element_type=jnp.float32)
    smoothed = smoothed.astype(jnp.bfloat16)
    parts = []
    for start in range(0, field.shape[0], copies):
        part = smoothed[start : start + copies]
        parts.append(factor * jnp.dot(taper, part, preferred_element_type=jnp.float32))
    return parts[0] if len(parts) == 1 else jnp.concatenate(parts, axis=0)


def solution(mesh):
    members, bands = mesh.shape["member"], mesh.shape["band"]
    few = bands <= FEW

    def shards(ensemble, member_weight, member_of_slot, halfwidth, static_root, innovation, precision):
        _, slots, levels, rows, lon = ensemble.shape
        level_share, lon_share = levels // members, lon // bands
        own = level_share * rows
        halo = REACHES * LREACH
        width = lon_share + 2 * halo
        padded = round_up(width + 1, LANES)
        kept = round_up(lon_share + SUMS * PARTS, LANES)
        per_member = bands * own
        copies = members
        while copies > 1 and (copies * per_member > 256 or members % copies):
            copies -= 1
        arrays = slots + 2
        everything = levels * rows
        traded = everything + 4 * slots * own
        vmem = pl.BlockSpec(memory_space=pltpu.VMEM)
        smem = pl.BlockSpec(memory_space=pltpu.SMEM)
        limit = min(48, max(14, 24 * members * bands * slots * own * padded // 2**20)) * 2**20

        def call(body, shapes, scalars, operands, scratch=(), flops=0):
            return pl.pallas_call(
                body,
                out_shape=tuple(jax.ShapeDtypeStruct(shape, kind) for shape, kind in shapes),
                in_specs=[smem] * len(scalars) + [vmem] * len(operands),
                out_specs=(vmem,) * len(shapes),
                scratch_shapes=[pltpu.VMEM(shape, kind) for shape, kind in scratch],
                compiler_params=pltpu.CompilerParams(vmem_limit_bytes=limit),
                cost_estimate=pl.CostEstimate(flops=flops, bytes_accessed=0, transcendentals=0),
                name=body.__name__,
            )(*scalars, *operands)

        f32, bf16 = jnp.float32, jnp.bfloat16

        def shifted(place, shift):
            return lax.rem(place + shift + bands, bands)

        def load_members(weight, stacked):
            stacked = stacked[...].astype(f32)
            which = stacked[:, :1, width : width + 1]
            scale = jnp.zeros(which.shape, f32)
            for member in range(members):
                scale = scale + jnp.where(which == member, weight[member], 0.0)
            shape = (members, per_member, padded)
            return [
                (scale * stacked[:, slot * own : (slot + 1) * own]).reshape(shape)
                for slot in range(slots)
            ]

        def fold(scaled, weighted):
            total = scaled[0] * weighted[0][None]
            for slot in range(1, slots):
                total = total + scaled[slot] * weighted[slot][None]
            return total.reshape(members * per_member, padded)

        def images_of(scaled, grad, ring, taper, factor):
            local = spread(grad, ring, taper, factor).reshape(members, per_member, padded)
            return [jnp.sum(scaled[t] * local, axis=0) for t in range(slots)]

        def pack(marks, ensemble, out, arrived, packed, in_sems, out_sems):
            def incoming(t):
                return pltpu.make_async_copy(ensemble.at[0, t], arrived.at[t], in_sems.at[t])

            def outgoing(member):
                place = pl.ds(member * bands, bands)
                return pltpu.make_async_copy(packed.at[place], out.at[place], out_sems.at[member])

            for t in range(slots):
                incoming(t).start()
            tail = jnp.full((slots * own, padded - width), marks[0], jnp.int32).astype(f32)
            for t in range(slots):
                incoming(t).wait()
            for member in range(members):
                picked = range(member * level_share, (member + 1) * level_share)
                values = [arrived[t, at].astype(f32) for t in range(slots) for at in picked]
                values = jnp.concatenate(values, axis=0)
                for band in range(bands):
                    piece = window(values, band, lon_share, halo, tail)
                    packed[member * bands + band] = piece.astype(bf16)
                outgoing(member).start()
            for member in range(members):
                outgoing(member).wait()

        def observe(here, widths, weight, innovation, precision, root, of_level, same, apart, level, *refs):
            outs, (own_static, pulled, mixing, pulling, taper, factor, static, mixed, spans) = refs[:-9], refs[-9:]
            total = []
            for at in range(levels):
                precise = precision[at].astype(f32)
                part = precise * innovation[0, at].astype(f32)
                for t in range(1, slots):
                    part = part + precise * innovation[t, at].astype(f32)
                total.append(part)
            out_of = lax.dot_general(
                exact_dot(of_level[...], static_share * root[...]),
                of_level[...],
                (((1,), (1,)), ((), ())),
                precision=lax.Precision.HIGHEST,
                preferred_element_type=f32,
            )
            out_of = out_of * same[...]
            into = out_of.T
            pulling[...] = into
            back = exact_dot(into, jnp.concatenate(total, axis=0))
            pulled[...] = back
            forth = exact_dot(out_of, back)
            both = exact_dot(out_of, into)
            for at in range(levels):
                static[at] = forth[at * rows : (at + 1) * rows]
                mixed[at] = both[at * rows : (at + 1) * rows]
            picked = [here[0] * level_share + share for share in range(level_share)]
            mixing[...] = jnp.concatenate([mixed[at] for at in picked], axis=0)
            parts = [innovation[t, at].astype(f32) for t in range(slots) for at in picked]
            parts += [precision[at].astype(f32) for at in picked] + [static[at] for at in picked]
            values = jnp.concatenate(parts, axis=0)
            tail = jnp.zeros((values.shape[0], padded - width), f32)
            for band in range(bands):
                piece = window(values, band, lon_share, halo, tail)
                own_static[band] = piece[(slots + 1) * own :, :kept]
                if few:
                    spans[band] = piece.astype(bf16)
                else:
                    outs[0][band] = piece.astype(bf16)
            if few:
                for shift in range(bands):
                    outs[shift][...] = spans[shifted(here[1], shift)]
            span = jnp.ones(level.shape, f32)
            for at, which in enumerate(picked):
                span = span + jnp.where(level[...] == at, widths[which].astype(f32), 0.0)
            taper[...] = near(apart[...], span)
            factor[...] = ensemble_share / (span * span)

        def first_half(here, weight, stacked, ring, taper, factor, *refs):
            blocks, (total_out, weighted_out, image_out, fields, spans) = refs[:-5], refs[-5:]
            if few:
                for shift in range(bands):
                    spans[shifted(here[1], -shift)] = blocks[shift][...]
                values = spans[...]
            else:
                values = blocks[0][...]
            field = []
            for index in range(arrays):
                piece = values[:, index * own : (index + 1) * own].astype(f32)
                piece = piece.reshape(per_member, padded)
                fields[index] = piece[:, :kept]
                field.append(piece)
            precise, static = field[slots], field[slots + 1]
            scaled = load_members(weight, stacked)
            weighted = [precise * field[t] for t in range(slots)]
            grad = spread(fold(scaled, weighted), ring[...], taper[...], factor[...])
            total = jnp.zeros((per_member, padded), f32)
            for t, image in enumerate(images_of(scaled, grad, ring[...], taper[...], factor[...])):
                image_out[t] = image[:, :kept]
                image = precise * (image + static)
                weighted_out[t] = image
                total = total + image
            total = total[:, :kept].astype(bf16)
            for member in range(members):
                total_out[member] = total

        def store_halves(spans, start, slot, values):
            for half, part in enumerate(halves(values)):
                at = start + (half * slots + slot) * own
                for band in range(bands):
                    spans[band, at : at + own] = part[band * own : (band + 1) * own]

        def deal(here, spans, outs):
            for shift in range(bands):
                if few:
                    outs[shift][...] = spans[shifted(here[1], shift)]
                else:
                    outs[0][shift] = spans[shift]

        def second_half(weight, stacked, ring, taper, factor, weighted, grad_out, image_out):
            scaled = load_members(weight, stacked)
            grad = fold(scaled, [weighted[t] for t in range(slots)])
            grad = spread(grad, ring[...], taper[...], factor[...]).astype(bf16)
            grad_out[...] = grad[:, :kept].reshape(members * bands, own, kept)
            for t, image in enumerate(images_of(scaled, grad, ring[...], taper[...], factor[...])):
                image_out[t] = image[:, :kept]

        def combine(here, total, grad, first, second, fields, mixing, *refs):
            outs, (out, spans) = refs[:-2], refs[-2:]
            mixed, precise, static = [], fields[slots], fields[slots + 1]
            for band in range(bands):
                place = slice(band * own, (band + 1) * own)
                every = jnp.concatenate([total[member, place].astype(f32) for member in range(members)], axis=0)
                every = every.astype(bf16)
                mixed.append(parts_dot(mixing[...], every))
                spans[band, :everything] = every
            mixed = jnp.concatenate(mixed, axis=0)
            sums = [jnp.zeros((per_member, kept), f32) for _ in range(SUMS)]
            for t in range(slots):
                image = second[t] + mixed
                whole = first[t] + static
                weighted = precise * whole
                sums[0] = sums[0] + precise * fields[t] * whole
                sums[1] = sums[1] + weighted * whole
                sums[2] = sums[2] + weighted * image
                sums[3] = sums[3] + precise * image * image
                store_halves(spans, everything, t, first[t])
                store_halves(spans, everything + 2 * slots * own, t, image)
            deal(here, spans, outs)
            inside = lax.broadcasted_iota(jnp.int32, (per_member, kept), 1) < lon_share
            lane = lax.broadcasted_iota(jnp.int32, (1, kept), 1) - lon_share
            row = jnp.zeros((1, kept), f32)
            for index, part in enumerate(sums):
                part = jnp.where(inside, part, 0.0)
                part = jnp.sum(jnp.sum(part, axis=0, keepdims=True), axis=1, keepdims=True)
                for piece in range(PARTS):
                    high = part.astype(bf16).astype(f32)
                    row = row + jnp.where(lane == PARTS * index + piece, high, 0.0)
                    part = part - high
            shape = (own, kept)
            lane = lax.broadcasted_iota(jnp.int32, shape, 1)
            row = jnp.broadcast_to(row, shape)
            for block in range(members * bands):
                out[block] = jnp.where(lane < lon_share, grad[block].astype(f32), row).astype(bf16)

        def fold_smooth(marks, weight, ensemble, innovation, precision, kernel, out):
            total = []
            for at in range(levels):
                precise = precision[at].astype(f32)
                part = jnp.zeros((rows, lon), f32)
                for t in range(slots):
                    weighted = precise * innovation[t, at].astype(f32)
                    part = part + ensemble[0, t, at].astype(f32) * weighted
                total.append(part)
            total = weight[marks[0]] * jnp.concatenate(total, axis=0)
            step = kernel.shape[1]
            margin = (kernel.shape[0] - step) // 2
            steps = -(-lon // step)
            after = steps * step + margin - lon
            ring = jnp.concatenate([total[:, lon - margin :], total, total[:, :after]], axis=1)
            ring = ring.astype(bf16)
            for start in range(0, lon, step):
                stop = min(lon, start + step)
                piece = jnp.dot(
                    ring[:, start : start + kernel.shape[0]], kernel[...], preferred_element_type=f32
                )
                out[:, start:stop] = piece[:, : stop - start].astype(bf16)

        def first_gradient(widths, below, middle, above, apart, level, grad):
            span = jnp.ones(level.shape, f32)
            for at in range(levels):
                span = span + jnp.where(level[...] == at, widths[at].astype(f32), 0.0)
            stacked = jnp.concatenate([below[...], middle[...], above[...]], axis=0)
            summed = jnp.dot(near(apart[...], span), stacked, preferred_element_type=f32)
            grad[...] = ensemble_share / (span * span) * summed

        def join(here, own_static, pulling, *refs):
            blocks, (pulled, images, spans) = refs[:-3], refs[-3:]
            for shift in range(bands):
                if few:
                    spans[shifted(here[1], -shift)] = blocks[shift][...]
                else:
                    spans[shift] = blocks[0][shift]
            size = slots * own
            for band in range(bands):
                place = slice(band * lon_share, (band + 1) * lon_share)
                pulled[:, place] = parts_dot(pulling[...], spans[band, :everything])[:, :lon_share]
                parts = spans[band, everything:].astype(f32)
                first = parts[:size] + parts[size : 2 * size]
                second = parts[2 * size : 3 * size] + parts[3 * size :]
                static = own_static[band]
                for t in range(slots):
                    at = slice(t * own, (t + 1) * own)
                    images[at, place] = (first[at] + static)[:, :lon_share]
                images[size:, place] = second[:, :lon_share]

        def finish(back, grad_first, pulled_first, pulled_second, images, *refs):
            member_out, static_out, image_out, second = refs
            total = back[0, :1].astype(f32)
            for block in range(1, members * bands):
                total = total + back[block, :1].astype(f32)
            lane = lax.broadcasted_iota(jnp.int32, total.shape, 1) - lon_share
            first_norm, first_image, cross, second_image = [
                jnp.sum(
                    jnp.where((lane >= PARTS * index) & (lane < PARTS * (index + 1)), total, 0.0),
                    axis=1,
                    keepdims=True,
                )
                for index in range(SUMS)
            ]
            alpha = first_norm / (first_norm + first_image)
            ratio = first_image / first_norm
            next_norm = alpha * alpha * jnp.maximum(cross - ratio * first_image, 0.0)
            beta = next_norm / first_norm
            apart = second_image - 2.0 * ratio * cross + ratio * ratio * first_image
            curvature = next_norm + alpha * alpha * apart - beta * next_norm / alpha
            alpha_next = jnp.clip(next_norm / curvature, 0.0, 1.0)
            on_first = alpha + alpha_next * (1.0 - alpha + beta)
            on_second = -alpha * alpha_next
            for band in range(bands):
                grad = jnp.concatenate(
                    [back[member * bands + band].astype(f32) for member in range(members)], axis=0
                )
                second[:, band * lon_share : (band + 1) * lon_share] = grad[:, :lon_share]
            member = on_first * grad_first[...] + on_second * second[...]
            static = on_first * pulled_first[...] + on_second * pulled_second[...]
            for level in range(levels):
                place = slice(level * rows, (level + 1) * rows)
                member_out[0, level] = member[place]
                static_out[level] = static[place]
            half = slots * own
            image = on_first * images[:half] + on_second * images[half:]
            for t in range(slots):
                for level in range(level_share):
                    start = (t * level_share + level) * rows
                    image_out[t, level] = image[start : start + rows]

        def trade(blocks):
            if not few:
                return [lax.all_to_all(blocks[0], "band", 0, 0, tiled=True)]
            return [blocks[0]] + [
                lax.ppermute(blocks[shift], "band", [(at, (at + shift) % bands) for at in range(bands)])
                for shift in range(1, bands)
            ]

        def tradable(shape, kind):
            return [(shape, kind)] * bands if few else [((bands,) + shape, kind)]

        here = jnp.stack([lax.axis_index("member"), lax.axis_index("band")]).astype(jnp.int32)

        block = (members * bands, slots * own, padded)
        pieces = pl.pallas_call(
            pack,
            out_shape=jax.ShapeDtypeStruct(block, bf16),
            in_specs=[smem, pl.BlockSpec(memory_space=pltpu.HBM)],
            out_specs=pl.BlockSpec(memory_space=pltpu.HBM),
            scratch_shapes=[
                pltpu.VMEM((slots, levels, rows, lon), bf16),
                pltpu.VMEM(block, bf16),
                pltpu.SemaphoreType.DMA((slots,)),
                pltpu.SemaphoreType.DMA((members,)),
            ],
            compiler_params=pltpu.CompilerParams(vmem_limit_bytes=60 * 2**20),
            name="pack",
        )(member_of_slot, ensemble)
        pieces, ensemble, innovation, precision, static_root = lax.optimization_barrier(
            (pieces, ensemble, innovation, precision, static_root)
        )
        stacked = lax.all_to_all(pieces, BOTH, 0, 0, tiled=True)

        of_level, same = row_levels(levels, rows)
        apart, level = row_apart(bands, level_share, rows, copies)
        block = (arrays * own, padded)
        results = call(
            observe,
            tradable(block, bf16)
            + [
                ((bands, own, kept), f32),
                ((everything, lon), f32),
                ((own, everything), f32),
                ((everything, everything), f32),
                (apart.shape, bf16),
                (level.shape, f32),
            ],
            [here, halfwidth, member_weight],
            [innovation, precision, static_root]
            + [jnp.asarray(table) for table in (of_level, same, apart, level)],
            scratch=[((levels, rows, lon), f32), ((levels, rows, everything), f32), ((bands,) + block, bf16)],
        )
        blocks = trade(results[:-6])
        own_static, pulled, mixing, pulling, taper, factor = results[-6:]
        own_static, ensemble, innovation, precision = lax.optimization_barrier(
            (own_static, ensemble, innovation, precision)
        )
        (smoothed,) = call(
            fold_smooth,
            [((everything, lon), bf16)],
            [member_of_slot, member_weight],
            [ensemble, innovation, precision, lon_kernel(LANES, 2 * LANES)],
        )
        up = [(at, at + 1) for at in range(bands - 1)]
        below = lax.ppermute(smoothed, "band", up)
        above = lax.ppermute(smoothed, "band", [(target, source) for source, target in up])

        ring, above = lax.optimization_barrier((ring_kernel(width, padded), above))
        total, weighted, image_first, fields = call(
            first_half,
            [
                ((members, per_member, kept), bf16),
                ((slots, per_member, padded), f32),
                ((slots, per_member, kept), f32),
                ((arrays, per_member, kept), f32),
            ],
            [here, member_weight],
            [stacked, ring, taper, factor, *blocks],
            scratch=[((bands,) + block, bf16)],
        )
        total = lax.all_to_all(total, "member", 0, 0, tiled=True)
        grad, image_second = call(
            second_half,
            [((members * bands, own, kept), bf16), ((slots, per_member, kept), f32)],
            [member_weight],
            [stacked, ring, taper, factor, weighted],
            flops=10**9,
        )

        results = call(
            combine,
            tradable((traded, kept), bf16) + [((members * bands, own, kept), bf16)],
            [here],
            [total, grad, image_first, image_second, fields, mixing],
            scratch=[((bands, traded, kept), bf16)],
        )
        gradients, below = lax.optimization_barrier((results[-1], below))
        back = lax.all_to_all(gradients, BOTH, 0, 0, tiled=True)
        blocks = trade(results[:-1])
        pulled_second, images = call(
            join,
            [((everything, lon), f32), ((2 * slots * own, lon), f32)],
            [here],
            [own_static, pulling, *blocks],
            scratch=[((bands, traded, kept), bf16)],
        )
        apart, level = halo_apart(levels, rows)
        (grad_first,) = call(
            first_gradient,
            [((everything, lon), f32)],
            [halfwidth],
            [below, smoothed, above, jnp.asarray(apart), jnp.asarray(level)],
        )
        return call(
            finish,
            [
                ((1, levels, rows, lon), f32),
                ((levels, rows, lon), f32),
                ((slots, level_share, rows, lon), f32),
            ],
            [],
            [back, grad_first, pulled, pulled_second, images],
            scratch=[((everything, lon), f32)],
        )

    return jax.shard_map(
        shards,
        mesh=mesh,
        in_specs=(
            P("member", None, None, "band", None),
            P(),
            P("member"),
            P(),
            P(),
            P(None, None, "band", None),
            P(None, "band", None),
        ),
        out_specs=(
            P("member", None, "band", None),
            P(None, "band", None),
            P(None, "member", "band", None),
        ),
        check_vma=False,
    )
```

```python
import math

import jax
import jax.numpy as jnp
import numpy as np
from jax import lax
from jax.experimental import pallas as pl
from jax.experimental.pallas import tpu as pltpu
from jax.sharding import PartitionSpec as P

HMAX = 4
LREACH = 18
REACHES = 4
LANES = 128
FEW = 8
SUMS = 4
PARTS = 3
BOTH = ("member", "band")

ensemble_share = 0.8
static_share = 0.6
length_scale = 6.0


def round_up(value, step):
    return -(-value // step) * step


def lon_weights(distance):
    distance = distance.astype(np.float32)
    values = np.exp(np.float32(-0.5) * (distance / np.float32(length_scale)) ** 2)
    values = values / np.float32(length_scale * math.sqrt(2.0 * math.pi))
    return jnp.asarray(np.where(distance <= LREACH, values, 0.0), jnp.bfloat16)


def ring_kernel(width, padded):
    apart = np.abs(np.arange(padded)[:, None] - np.arange(padded)[None])
    inside = (np.arange(padded)[:, None] < width) & (np.arange(padded)[None] < width)
    return lon_weights(np.where(inside, np.minimum(apart, width - apart), 2 * LREACH))


def near(apart, spans):
    return jnp.maximum(spans - apart, 0.0).astype(jnp.bfloat16)


def row_apart(bands, held, rows, copies):
    index = np.arange(copies * bands * held * rows)
    latitude = index // (held * rows) % bands * rows + index % rows
    level = index // rows % held
    copy = index // (bands * held * rows)
    same = (copy[:, None] == copy[None]) & (level[:, None] == level[None])
    apart = np.where(same, np.abs(latitude[:, None] - latitude[None]), 1000)
    return apart.astype(np.float32), level[:, None].astype(np.float32)


def row_levels(levels, rows):
    index = np.arange(levels * rows)
    level = index[:, None] // rows == np.arange(levels)[None]
    place = index[:, None] % rows == index[None] % rows
    return level.astype(np.float32), place.astype(np.float32)


def exact_dot(matrix, field):
    return jnp.dot(
        matrix, field, precision=lax.Precision.HIGHEST, preferred_element_type=jnp.float32
    )


def parts_dot(matrix, field):
    count, parts = matrix.shape[0], []
    for _ in range(PARTS):
        part = matrix.astype(jnp.bfloat16).astype(jnp.float32)
        parts.append(part)
        matrix = matrix - part
    stacked = jnp.concatenate(parts, axis=0).astype(jnp.bfloat16)
    products = jnp.dot(stacked, field, preferred_element_type=jnp.float32)
    total = products[:count]
    for index in range(1, PARTS):
        total = total + products[index * count : (index + 1) * count]
    return total


def window(values, band, share, halo, tail):
    lon = values.shape[1]
    start = band * share
    stop = start + share + halo
    parts = [values[:, start : min(lon, stop)]]
    if stop > lon:
        parts.append(values[:, : stop - lon])
    if start < halo:
        parts.append(values[:, lon - halo + start :])
    if start:
        parts.append(values[:, max(start - halo, 0) : start])
    return jnp.concatenate(parts + [tail], axis=1)


def spread(field, ring, taper, factor):
    copies = taper.shape[0]
    smoothed = jnp.dot(field.astype(jnp.bfloat16), ring, preferred_element_type=jnp.float32)
    smoothed = smoothed.astype(jnp.bfloat16)
    parts = []
    for start in range(0, field.shape[0], copies):
        part = smoothed[start : start + copies]
        parts.append(factor * jnp.dot(taper, part, preferred_element_type=jnp.float32))
    return parts[0] if len(parts) == 1 else jnp.concatenate(parts, axis=0)


def solution(mesh):
    members, bands = mesh.shape["member"], mesh.shape["band"]
    few = bands <= FEW

    def shards(ensemble, member_weight, member_of_slot, halfwidth, static_root, innovation, precision):
        _, slots, levels, rows, lon = ensemble.shape
        level_share, lon_share = levels // members, lon // bands
        own = level_share * rows
        halo = REACHES * LREACH
        width = lon_share + 2 * halo
        padded = round_up(width + 1, LANES)
        kept = round_up(lon_share + SUMS * PARTS, LANES)
        per_member = bands * own
        copies = members
        while copies > 1 and (copies * per_member > 256 or members % copies):
            copies -= 1
        arrays = slots + 2
        everything = levels * rows
        traded = everything + 2 * slots * own
        vmem = pl.BlockSpec(memory_space=pltpu.VMEM)
        smem = pl.BlockSpec(memory_space=pltpu.SMEM)
        limit = min(48, max(14, 24 * members * bands * slots * own * padded // 2**20)) * 2**20

        def call(body, shapes, scalars, operands, scratch=(), flops=0):
            return pl.pallas_call(
                body,
                out_shape=tuple(jax.ShapeDtypeStruct(shape, kind) for shape, kind in shapes),
                in_specs=[smem] * len(scalars) + [vmem] * len(operands),
                out_specs=(vmem,) * len(shapes),
                scratch_shapes=[pltpu.VMEM(shape, kind) for shape, kind in scratch],
                compiler_params=pltpu.CompilerParams(vmem_limit_bytes=limit),
                cost_estimate=pl.CostEstimate(flops=flops, bytes_accessed=0, transcendentals=0),
                name=body.__name__,
            )(*scalars, *operands)

        f32, bf16 = jnp.float32, jnp.bfloat16

        def shifted(place, shift):
            return lax.rem(place + shift + bands, bands)

        def load_members(weight, stacked):
            stacked = stacked[...].astype(f32)
            which = stacked[:, :1, width : width + 1]
            scale = jnp.zeros(which.shape, f32)
            for member in range(members):
                scale = scale + jnp.where(which == member, weight[member], 0.0)
            shape = (members, per_member, padded)
            return [
                (scale * stacked[:, slot * own : (slot + 1) * own]).reshape(shape)
                for slot in range(slots)
            ]

        def fold(scaled, weighted):
            total = scaled[0] * weighted[0][None]
            for slot in range(1, slots):
                total = total + scaled[slot] * weighted[slot][None]
            return total.reshape(members * per_member, padded)

        def images_of(scaled, grad, ring, taper, factor):
            local = spread(grad, ring, taper, factor).reshape(members, per_member, padded)
            return [jnp.sum(scaled[t] * local, axis=0) for t in range(slots)]

        def pack(marks, ensemble, out, arrived, packed, in_sems, out_sems):
            def incoming(t):
                return pltpu.make_async_copy(ensemble.at[0, t], arrived.at[t], in_sems.at[t])

            def outgoing(member):
                place = pl.ds(member * bands, bands)
                return pltpu.make_async_copy(packed.at[place], out.at[place], out_sems.at[member])

            for t in range(slots):
                incoming(t).start()
            tail = jnp.full((slots * own, padded - width), marks[0], jnp.int32).astype(f32)
            for t in range(slots):
                incoming(t).wait()
            for member in range(members):
                picked = range(member * level_share, (member + 1) * level_share)
                values = [arrived[t, at].astype(f32) for t in range(slots) for at in picked]
                values = jnp.concatenate(values, axis=0)
                for band in range(bands):
                    piece = window(values, band, lon_share, halo, tail)
                    packed[member * bands + band] = piece.astype(bf16)
                outgoing(member).start()
            for member in range(members):
                outgoing(member).wait()

        def observe(here, widths, weight, innovation, precision, root, of_level, same, apart, level, *refs):
            outs, (own_static, pulled, mixing, pulling, taper, factor, static, mixed, spans) = refs[:-9], refs[-9:]
            total = []
            for at in range(levels):
                precise = precision[at].astype(f32)
                part = precise * innovation[0, at].astype(f32)
                for t in range(1, slots):
                    part = part + precise * innovation[t, at].astype(f32)
                total.append(part)
            out_of = lax.dot_general(
                exact_dot(of_level[...], static_share * root[...]),
                of_level[...],
                (((1,), (1,)), ((), ())),
                precision=lax.Precision.HIGHEST,
                preferred_element_type=f32,
            )
            out_of = out_of * same[...]
            into = out_of.T
            pulling[...] = into
            back = exact_dot(into, jnp.concatenate(total, axis=0))
            pulled[...] = back
            forth = exact_dot(out_of, back)
            both = exact_dot(out_of, into)
            for at in range(levels):
                static[at] = forth[at * rows : (at + 1) * rows]
                mixed[at] = both[at * rows : (at + 1) * rows]
            picked = [here[0] * level_share + share for share in range(level_share)]
            mixing[...] = jnp.concatenate([mixed[at] for at in picked], axis=0)
            parts = [innovation[t, at].astype(f32) for t in range(slots) for at in picked]
            parts += [precision[at].astype(f32) for at in picked] + [static[at] for at in picked]
            values = jnp.concatenate(parts, axis=0)
            tail = jnp.zeros((values.shape[0], padded - width), f32)
            for band in range(bands):
                piece = window(values, band, lon_share, halo, tail)
                own_static[band] = piece[(slots + 1) * own :, :kept]
                if few:
                    spans[band] = piece.astype(bf16)
                else:
                    outs[0][band] = piece.astype(bf16)
            if few:
                for shift in range(bands):
                    outs[shift][...] = spans[shifted(here[1], shift)]
            span = jnp.ones(level.shape, f32)
            for at, which in enumerate(picked):
                span = span + jnp.where(level[...] == at, widths[which].astype(f32), 0.0)
            taper[...] = near(apart[...], span)
            factor[...] = ensemble_share / (span * span)

        def first_half(here, weight, stacked, ring, taper, factor, *refs):
            blocks, (total_out, weighted_out, grad_out, image_out, fields, spans) = refs[:-6], refs[-6:]
            if few:
                for shift in range(bands):
                    spans[shifted(here[1], -shift)] = blocks[shift][...]
                values = spans[...]
            else:
                values = blocks[0][...]
            field = []
            for index in range(arrays):
                piece = values[:, index * own : (index + 1) * own].astype(f32)
                piece = piece.reshape(per_member, padded)
                fields[index] = piece[:, :kept]
                field.append(piece)
            precise, static = field[slots], field[slots + 1]
            scaled = load_members(weight, stacked)
            weighted = [precise * field[t] for t in range(slots)]
            grad = spread(fold(scaled, weighted), ring[...], taper[...], factor[...])
            grad_out[...] = grad[:, :kept]
            total = jnp.zeros((per_member, padded), f32)
            for t, image in enumerate(images_of(scaled, grad, ring[...], taper[...], factor[...])):
                image_out[t] = image[:, :kept]
                image = precise * (image + static)
                weighted_out[t] = image
                total = total + image
            total = total[:, :kept].astype(bf16)
            for member in range(members):
                total_out[member] = total

        def inner(first, second):
            inside = lax.broadcasted_iota(jnp.int32, first.shape, 1) < lon_share
            product = jnp.where(inside, first * second, 0.0)
            return jnp.sum(jnp.sum(product, axis=0, keepdims=True), axis=1, keepdims=True)

        def closest(first, second):
            norm = inner(first, first)
            ratio = inner(first, second) / jnp.where(norm > 0.0, norm, 1.0)
            return ratio.astype(bf16).astype(f32)

        def deal(here, spans, outs):
            for shift in range(bands):
                if few:
                    outs[shift][...] = spans[shifted(here[1], shift)]
                else:
                    outs[0][shift] = spans[shift]

        def second_half(weight, stacked, ring, taper, factor, weighted, first, pair_out, image_out):
            scaled = load_members(weight, stacked)
            grad = fold(scaled, [weighted[t] for t in range(slots)])
            grad = spread(grad, ring[...], taper[...], factor[...])
            for t, image in enumerate(images_of(scaled, grad, ring[...], taper[...], factor[...])):
                image_out[t] = image[:, :kept]
            first, second = first[...], grad[:, :kept]
            ratio = closest(first, second)
            shape = (members * bands, own, kept)
            second = (second - ratio * first).reshape(shape)
            lane = lax.broadcasted_iota(jnp.int32, shape, 2)
            second = jnp.where(lane < lon_share, second, ratio.reshape(1, 1, 1))
            pair_out[:, :own] = first.reshape(shape).astype(bf16)
            pair_out[:, own:] = second.astype(bf16)

        def combine(here, total, pairs, first, second, fields, mixing, *refs):
            outs, (out, spans) = refs[:-2], refs[-2:]
            lane = lax.broadcasted_iota(jnp.int32, (1, kept), 1) - lon_share
            mixed, precise, static = [], fields[slots], fields[slots + 1]
            for band in range(bands):
                place = slice(band * own, (band + 1) * own)
                every = jnp.concatenate([total[member, place].astype(f32) for member in range(members)], axis=0)
                every = every.astype(bf16)
                mixed.append(parts_dot(mixing[...], every))
                spans[band, :everything] = every
            mixed = jnp.concatenate(mixed, axis=0)
            images = [second[t] + mixed for t in range(slots)]
            sums = [jnp.zeros((per_member, kept), f32) for _ in range(SUMS)]
            for t, image in enumerate(images):
                whole = first[t] + static
                weighted = precise * whole
                sums[0] = sums[0] + precise * fields[t] * whole
                sums[1] = sums[1] + weighted * whole
                sums[2] = sums[2] + weighted * image
                sums[3] = sums[3] + precise * image * image
            ratio = closest(
                jnp.concatenate([first[t] for t in range(slots)], axis=0), jnp.concatenate(images, axis=0)
            )
            for which in range(2):
                for t, image in enumerate(images):
                    image = jnp.where(lane < 0, image - ratio * first[t], ratio) if which else first[t]
                    image = image.astype(bf16)
                    at = everything + (which * slots + t) * own
                    for band in range(bands):
                        spans[band, at : at + own] = image[band * own : (band + 1) * own]
            deal(here, spans, outs)
            row = jnp.zeros((1, kept), f32)
            for index, part in enumerate(sums):
                part = jnp.where(lane < 0, part, 0.0)
                part = jnp.sum(jnp.sum(part, axis=0, keepdims=True), axis=1, keepdims=True)
                for piece in range(PARTS):
                    high = part.astype(bf16).astype(f32)
                    row = row + jnp.where(lane == PARTS * index + piece, high, 0.0)
                    part = part - high
            shape = (2 * own, kept)
            lane = lax.broadcasted_iota(jnp.int32, shape, 1)
            sender = lax.broadcasted_iota(jnp.int32, shape, 0) < own
            row = jnp.broadcast_to(row, shape)
            for block in range(members * bands):
                values = pairs[block].astype(f32)
                out[block] = jnp.where((lane >= lon_share) & sender, row, values).astype(bf16)

        def join(here, own_static, pulling, *refs):
            blocks, (pulled, images, spans) = refs[:-3], refs[-3:]
            for shift in range(bands):
                if few:
                    spans[shifted(here[1], -shift)] = blocks[shift][...]
                else:
                    spans[shift] = blocks[0][shift]
            size = slots * own
            for band in range(bands):
                place = slice(band * lon_share, (band + 1) * lon_share)
                pulled[:, place] = parts_dot(pulling[...], spans[band, :everything])[:, :lon_share]
                parts = spans[band, everything:].astype(f32)
                first = parts[:size]
                second = parts[size:] + parts[size : size + 1, lon_share : lon_share + 1] * first
                static = own_static[band]
                for t in range(slots):
                    at = slice(t * own, (t + 1) * own)
                    images[at, place] = (first[at] + static)[:, :lon_share]
                images[size:, place] = second[:, :lon_share]

        def finish(back, pulled_first, pulled_second, images, *refs):
            member_out, static_out, image_out, member = refs
            total = back[0, :1].astype(f32)
            for block in range(1, members * bands):
                total = total + back[block, :1].astype(f32)
            lane = lax.broadcasted_iota(jnp.int32, total.shape, 1) - lon_share
            first_norm, first_image, cross, second_image = [
                jnp.sum(
                    jnp.where((lane >= PARTS * index) & (lane < PARTS * (index + 1)), total, 0.0),
                    axis=1,
                    keepdims=True,
                )
                for index in range(SUMS)
            ]
            alpha = first_norm / (first_norm + first_image)
            ratio = first_image / first_norm
            next_norm = alpha * alpha * jnp.maximum(cross - ratio * first_image, 0.0)
            beta = next_norm / first_norm
            apart = second_image - 2.0 * ratio * cross + ratio * ratio * first_image
            curvature = next_norm + alpha * alpha * apart - beta * next_norm / alpha
            alpha_next = jnp.clip(next_norm / curvature, 0.0, 1.0)
            on_first = alpha + alpha_next * (1.0 - alpha + beta)
            on_second = -alpha * alpha_next
            for band in range(bands):
                parts = []
                for source in range(members):
                    first = back[source * bands + band, :own].astype(f32)
                    second = back[source * bands + band, own:].astype(f32)
                    ratio = second[:1, lon_share : lon_share + 1]
                    parts.append((on_first + on_second * ratio) * first + on_second * second)
                piece = jnp.concatenate(parts, axis=0)
                member[:, band * lon_share : (band + 1) * lon_share] = piece[:, :lon_share]
            static = on_first * pulled_first[...] + on_second * pulled_second[...]
            for level in range(levels):
                place = slice(level * rows, (level + 1) * rows)
                member_out[0, level] = member[place]
                static_out[level] = static[place]
            half = slots * own
            image = on_first * images[:half] + on_second * images[half:]
            for t in range(slots):
                for level in range(level_share):
                    start = (t * level_share + level) * rows
                    image_out[t, level] = image[start : start + rows]

        def trade(blocks):
            if not few:
                return [lax.all_to_all(blocks[0], "band", 0, 0, tiled=True)]
            return [blocks[0]] + [
                lax.ppermute(blocks[shift], "band", [(at, (at + shift) % bands) for at in range(bands)])
                for shift in range(1, bands)
            ]

        def tradable(shape, kind):
            return [(shape, kind)] * bands if few else [((bands,) + shape, kind)]

        here = jnp.stack([lax.axis_index("member"), lax.axis_index("band")]).astype(jnp.int32)

        block = (members * bands, slots * own, padded)
        pieces = pl.pallas_call(
            pack,
            out_shape=jax.ShapeDtypeStruct(block, bf16),
            in_specs=[smem, pl.BlockSpec(memory_space=pltpu.HBM)],
            out_specs=pl.BlockSpec(memory_space=pltpu.HBM),
            scratch_shapes=[
                pltpu.VMEM((slots, levels, rows, lon), bf16),
                pltpu.VMEM(block, bf16),
                pltpu.SemaphoreType.DMA((slots,)),
                pltpu.SemaphoreType.DMA((members,)),
            ],
            compiler_params=pltpu.CompilerParams(vmem_limit_bytes=60 * 2**20),
            name="pack",
        )(member_of_slot, ensemble)
        pieces, innovation, precision, static_root = lax.optimization_barrier(
            (pieces, innovation, precision, static_root)
        )
        stacked = lax.all_to_all(pieces, BOTH, 0, 0, tiled=True)

        of_level, same = row_levels(levels, rows)
        apart, level = row_apart(bands, level_share, rows, copies)
        block = (arrays * own, padded)
        results = call(
            observe,
            tradable(block, bf16)
            + [
                ((bands, own, kept), f32),
                ((everything, lon), f32),
                ((own, everything), f32),
                ((everything, everything), f32),
                (apart.shape, bf16),
                (level.shape, f32),
            ],
            [here, halfwidth, member_weight],
            [innovation, precision, static_root]
            + [jnp.asarray(table) for table in (of_level, same, apart, level)],
            scratch=[((levels, rows, lon), f32), ((levels, rows, everything), f32), ((bands,) + block, bf16)],
        )
        blocks = trade(results[:-6])
        own_static, pulled, mixing, pulling, taper, factor = results[-6:]
        ring = ring_kernel(width, padded)

        total, weighted, grad_first, image_first, fields = call(
            first_half,
            [
                ((members, per_member, kept), bf16),
                ((slots, per_member, padded), f32),
                ((members * per_member, kept), f32),
                ((slots, per_member, kept), f32),
                ((arrays, per_member, kept), f32),
            ],
            [here, member_weight],
            [stacked, ring, taper, factor, *blocks],
            scratch=[((bands,) + block, bf16)],
        )
        total = lax.all_to_all(total, "member", 0, 0, tiled=True)
        pairs, image_second = call(
            second_half,
            [((members * bands, 2 * own, kept), bf16), ((slots, per_member, kept), f32)],
            [member_weight],
            [stacked, ring, taper, factor, weighted, grad_first],
            flops=10**9,
        )

        results = call(
            combine,
            tradable((traded, kept), bf16) + [((members * bands, 2 * own, kept), bf16)],
            [here],
            [total, pairs, image_first, image_second, fields, mixing],
            scratch=[((bands, traded, kept), bf16)],
        )
        back = lax.all_to_all(results[-1], BOTH, 0, 0, tiled=True)
        blocks = trade(results[:-1])
        pulled_second, images = call(
            join,
            [((everything, lon), f32), ((2 * slots * own, lon), f32)],
            [here],
            [own_static, pulling, *blocks],
            scratch=[((bands, traded, kept), bf16)],
        )
        return call(
            finish,
            [
                ((1, levels, rows, lon), f32),
                ((levels, rows, lon), f32),
                ((slots, level_share, rows, lon), f32),
            ],
            [],
            [back, pulled, pulled_second, images],
            scratch=[((everything, lon), f32)],
        )

    return jax.shard_map(
        shards,
        mesh=mesh,
        in_specs=(
            P("member", None, None, "band", None),
            P(),
            P("member"),
            P(),
            P(),
            P(None, None, "band", None),
            P(None, "band", None),
        ),
        out_specs=(
            P("member", None, "band", None),
            P(None, "band", None),
            P(None, "member", "band", None),
        ),
        check_vma=False,
    )
```

```python
import math

import jax
import jax.numpy as jnp
import numpy as np
from jax import lax
from jax.experimental import pallas as pl
from jax.experimental.pallas import tpu as pltpu
from jax.sharding import PartitionSpec as P

HMAX = 4
LREACH = 18
REACHES = 4
LANES = 128
FEW = 8
SUMS = 4
PARTS = 3
BOTH = ("member", "band")

ensemble_share = 0.8
static_share = 0.6
length_scale = 6.0


def round_up(value, step):
    return -(-value // step) * step


def lon_weights(distance):
    distance = distance.astype(np.float32)
    values = np.exp(np.float32(-0.5) * (distance / np.float32(length_scale)) ** 2)
    values = values / np.float32(length_scale * math.sqrt(2.0 * math.pi))
    return jnp.asarray(np.where(distance <= LREACH, values, 0.0), jnp.bfloat16)


def ring_kernel(width, padded):
    apart = np.abs(np.arange(padded)[:, None] - np.arange(padded)[None])
    inside = (np.arange(padded)[:, None] < width) & (np.arange(padded)[None] < width)
    return lon_weights(np.where(inside, np.minimum(apart, width - apart), 2 * LREACH))


def near(apart, spans):
    return jnp.maximum(spans - apart, 0.0).astype(jnp.bfloat16)


def row_apart(bands, held, rows, copies):
    index = np.arange(copies * bands * held * rows)
    latitude = index // (held * rows) % bands * rows + index % rows
    level = index // rows % held
    copy = index // (bands * held * rows)
    same = (copy[:, None] == copy[None]) & (level[:, None] == level[None])
    apart = np.where(same, np.abs(latitude[:, None] - latitude[None]), 1000)
    return apart.astype(np.float32), level[:, None].astype(np.float32)


def row_levels(levels, rows):
    index = np.arange(levels * rows)
    level = index[:, None] // rows == np.arange(levels)[None]
    place = index[:, None] % rows == index[None] % rows
    return level.astype(np.float32), place.astype(np.float32)


def exact_dot(matrix, field):
    return jnp.dot(
        matrix, field, precision=lax.Precision.HIGHEST, preferred_element_type=jnp.float32
    )


def parts_dot(matrix, field):
    count, parts = matrix.shape[0], []
    for _ in range(PARTS):
        part = matrix.astype(jnp.bfloat16).astype(jnp.float32)
        parts.append(part)
        matrix = matrix - part
    stacked = jnp.concatenate(parts, axis=0).astype(jnp.bfloat16)
    products = jnp.dot(stacked, field, preferred_element_type=jnp.float32)
    total = products[:count]
    for index in range(1, PARTS):
        total = total + products[index * count : (index + 1) * count]
    return total


def window(values, band, share, halo, tail):
    lon = values.shape[1]
    start = band * share
    stop = start + share + halo
    parts = [values[:, start : min(lon, stop)]]
    if stop > lon:
        parts.append(values[:, : stop - lon])
    if start < halo:
        parts.append(values[:, lon - halo + start :])
    if start:
        parts.append(values[:, max(start - halo, 0) : start])
    return jnp.concatenate(parts + [tail], axis=1)


def spread(field, ring, taper, factor):
    copies = taper.shape[0]
    smoothed = jnp.dot(field.astype(jnp.bfloat16), ring, preferred_element_type=jnp.float32)
    smoothed = smoothed.astype(jnp.bfloat16)
    parts = []
    for start in range(0, field.shape[0], copies):
        part = smoothed[start : start + copies]
        parts.append(jnp.dot(taper, part, preferred_element_type=jnp.float32))
    return factor * (parts[0] if len(parts) == 1 else jnp.concatenate(parts, axis=0))


def solution(mesh):
    members, bands = mesh.shape["member"], mesh.shape["band"]
    few = bands <= FEW
    paired = members % 2 == 0 and members // 2 <= FEW

    def shards(ensemble, member_weight, member_of_slot, halfwidth, static_root, innovation, precision):
        _, slots, levels, rows, lon = ensemble.shape
        level_share, lon_share = levels // members, lon // bands
        own = level_share * rows
        halo = REACHES * LREACH
        width = lon_share + 2 * halo
        padded = round_up(width + 1, LANES)
        kept = round_up(lon_share + SUMS * PARTS, LANES)
        per_member = bands * own
        copies = members
        while copies > 1 and (copies * per_member > 256 or members % copies):
            copies -= 1
        arrays = slots + 2
        everything = levels * rows
        traded = everything + 2 * slots * own
        vmem = pl.BlockSpec(memory_space=pltpu.VMEM)
        smem = pl.BlockSpec(memory_space=pltpu.SMEM)
        limit = min(48, max(14, 24 * members * bands * slots * own * padded // 2**20)) * 2**20

        def call(body, shapes, scalars, operands, scratch=(), flops=0):
            return pl.pallas_call(
                body,
                out_shape=tuple(jax.ShapeDtypeStruct(shape, kind) for shape, kind in shapes),
                in_specs=[smem] * len(scalars) + [vmem] * len(operands),
                out_specs=(vmem,) * len(shapes),
                scratch_shapes=[pltpu.VMEM(shape, kind) for shape, kind in scratch],
                compiler_params=pltpu.CompilerParams(vmem_limit_bytes=limit),
                cost_estimate=pl.CostEstimate(flops=flops, bytes_accessed=0, transcendentals=0),
                name=body.__name__,
            )(*scalars, *operands)

        f32, bf16 = jnp.float32, jnp.bfloat16

        def chosen(turn, blocks, sign):
            if not few:
                return [blocks[0][band] for band in range(bands)]
            turned = []
            for band in range(bands):
                value = blocks[0]
                for shift in range(1, bands):
                    value = jnp.where(turn == (band - sign * shift) % bands, blocks[shift], value)
                turned.append(value)
            return turned

        def load_members(weights, stacked, factor):
            shape = (members, per_member, padded)
            values = stacked[...].astype(f32)
            ensemble = [
                values[:, slot * own : (slot + 1) * own].reshape(shape) for slot in range(slots)
            ]
            which = ensemble[0][:, :1, width : width + 1]
            scale = jnp.zeros(which.shape, f32)
            for member in range(members):
                weight = weights[member : member + 1, :1].reshape(1, 1, 1)
                scale = scale + jnp.where(which == member, weight, 0.0)
            scale = jnp.broadcast_to(scale, (members, per_member, 1))
            return ensemble, scale.reshape(members * per_member, 1) * factor

        def fold(ensemble, weighted):
            total = ensemble[0] * weighted[0][None]
            for slot in range(1, slots):
                total = total + ensemble[slot] * weighted[slot][None]
            return total.reshape(members * per_member, padded)

        def images_of(ensemble, grad, ring, taper, factor):
            local = spread(grad, ring, taper, factor).reshape(members, per_member, padded)
            return [jnp.sum(ensemble[t] * local, axis=0) for t in range(slots)]

        def pack(slot, ensemble, out, marks, arrived, packed, mark_sem, in_sems, out_sems):
            def incoming(t):
                return pltpu.make_async_copy(ensemble.at[0, t], arrived.at[t], in_sems.at[t])

            def outgoing(member):
                place = pl.ds(member * bands, bands)
                return pltpu.make_async_copy(packed.at[place], out.at[place], out_sems.at[member])

            mark = pltpu.make_async_copy(slot, marks, mark_sem)
            mark.start()
            for t in range(slots):
                incoming(t).start()
            mark.wait()
            tail = jnp.full((slots * own, padded - width), marks[0], jnp.int32).astype(f32).astype(bf16)
            for t in range(slots):
                incoming(t).wait()
            for member in range(members):
                picked = range(member * level_share, (member + 1) * level_share)
                values = [arrived[t, at].astype(f32) for t in range(slots) for at in picked]
                values = jnp.concatenate(values, axis=0).astype(bf16)
                for band in range(bands):
                    packed[member * bands + band] = window(values, band, lon_share, halo, tail)
                outgoing(member).start()
            for member in range(members):
                outgoing(member).wait()

        def observe(here, widths, weight, innovation, precision, root, of_level, same, apart, level, *refs):
            outs, results, (static, mixed, pulls) = refs[:-11], refs[-11:-3], refs[-3:]
            own_static, pulled, mixing, pulling, taper, factor, weights, turn = results
            turn[...] = jnp.full((1, LANES), here[1], jnp.int32)
            for member in range(members):
                weights[member : member + 1] = jnp.full((1, LANES), weight[member], f32)
            total = []
            for at in range(levels):
                precise = precision[at].astype(f32)
                part = precise * innovation[0, at].astype(f32)
                for t in range(1, slots):
                    part = part + precise * innovation[t, at].astype(f32)
                total.append(part)
            out_of = lax.dot_general(
                exact_dot(of_level[...], static_share * root[...]),
                of_level[...],
                (((1,), (1,)), ((), ())),
                precision=lax.Precision.HIGHEST,
                preferred_element_type=f32,
            )
            out_of = out_of * same[...]
            into = out_of.T
            back = exact_dot(into, jnp.concatenate(total, axis=0))
            pulled[...] = back
            forth = exact_dot(out_of, back)
            both = exact_dot(out_of, into)
            for at in range(levels):
                static[at] = forth[at * rows : (at + 1) * rows]
                mixed[at] = both[at * rows : (at + 1) * rows]
                pulls[at] = out_of[at * rows : (at + 1) * rows]
            picked = [here[0] * level_share + share for share in range(level_share)]
            arriving = [
                member * level_share + share
                for _, _, member in arrivals(here[0])
                for share in range(level_share)
            ]
            pulling[...] = jnp.concatenate([pulls[at] for at in arriving], axis=0).T
            column = lax.broadcasted_iota(jnp.int32, (everything, own), 0)
            own_column = here[0] * own + lax.broadcasted_iota(jnp.int32, (everything, own), 1)
            mixing[...] = exact_dot(
                jnp.concatenate([mixed[at] for at in arriving], axis=0), (column == own_column).astype(f32)
            ).T
            parts = [innovation[t, at].astype(f32) for t in range(slots) for at in picked]
            parts += [precision[at].astype(f32) for at in picked] + [static[at] for at in picked]
            values = jnp.concatenate(parts, axis=0)
            tail = jnp.zeros((values.shape[0], padded - width), f32)
            pieces = [window(values, band, lon_share, halo, tail) for band in range(bands)]
            for band, piece in enumerate(pieces):
                own_static[band] = piece[(slots + 1) * own :, :kept]
            deal(turn[:, :1], pieces, outs)
            span = jnp.ones(level.shape, f32)
            for at, which in enumerate(picked):
                span = span + jnp.where(level[...] == at, widths[which].astype(f32), 0.0)
            taper[...] = near(apart[...], span[: apart.shape[0]])
            factor[...] = ensemble_share / (span * span)

        def first_half(weights, turn, stacked, ring, taper, factor, *refs):
            blocks, (total_out, weighted_out, grad_out, image_out, fields) = refs[:-5], refs[-5:]
            if few:
                blocks = [block[...].astype(f32) for block in blocks]
            values = jnp.stack(chosen(turn[:, :1], blocks, -1)).astype(f32)
            field = []
            for index in range(arrays):
                piece = values[:, index * own : (index + 1) * own].reshape(per_member, padded)
                fields[index] = piece[:, :kept]
                field.append(piece)
            precise, static = field[slots], field[slots + 1]
            ensemble, factors = load_members(weights, stacked, factor[...])
            weighted = [precise * field[t] for t in range(slots)]
            grad = spread(fold(ensemble, weighted), ring[...], taper[...], factors)
            grad_out[...] = grad[:, :kept]
            total = jnp.zeros((per_member, padded), f32)
            for t, image in enumerate(images_of(ensemble, grad, ring[...], taper[...], factors)):
                image_out[t] = image[:, :kept]
                image = precise * (image + static)
                weighted_out[t] = image
                total = total + image
            total_out[...] = total[:, :kept].astype(bf16)

        def inner(first, second):
            inside = lax.broadcasted_iota(jnp.int32, first.shape, 1) < lon_share
            product = jnp.where(inside, first * second, 0.0)
            return jnp.sum(jnp.sum(product, axis=0, keepdims=True), axis=1, keepdims=True)

        def closest(first, second):
            norm = inner(first, first)
            ratio = inner(first, second) / jnp.where(norm > 0.0, norm, 1.0)
            return ratio.astype(bf16).astype(f32)

        def deal(turn, pieces, outs):
            if not few:
                for band, piece in enumerate(pieces):
                    outs[0][band] = piece.astype(bf16)
                return
            for shift in range(bands):
                value = pieces[0]
                for band in range(1, bands):
                    value = jnp.where(turn == (band - shift) % bands, pieces[band], value)
                outs[shift][...] = value.astype(bf16)

        def second_half(weights, stacked, ring, taper, factor, weighted, first, pair_out, image_out):
            ensemble, factors = load_members(weights, stacked, factor[...])
            grad = fold(ensemble, [weighted[t] for t in range(slots)])
            grad = spread(grad, ring[...], taper[...], factors)
            for t, image in enumerate(images_of(ensemble, grad, ring[...], taper[...], factors)):
                image_out[t] = image[:, :kept]
            first, second = first[...], grad[:, :kept]
            ratio = closest(first, second)
            shape = (members * bands, own, kept)
            second = (second - ratio * first).reshape(shape)
            lane = lax.broadcasted_iota(jnp.int32, shape, 2)
            second = jnp.where(lane < lon_share, second, ratio.reshape(1, 1, 1))
            pair_out[:, :own] = first.reshape(shape).astype(bf16)
            pair_out[:, own:] = second.astype(bf16)

        def combine(pairs, first, second, fields, mixing, *refs):
            blocks, (out, image_out) = refs[:-2], refs[-2:]
            lane = lax.broadcasted_iota(jnp.int32, (1, kept), 1) - lon_share
            every = [
                jnp.concatenate(
                    [
                        blocks[block][shift, band * own : (band + 1) * own].astype(f32)
                        for block, shift, _ in arrivals(0)
                    ],
                    axis=0,
                )
                for band in range(bands)
            ]
            mixed = parts_dot(mixing[...], jnp.concatenate(every, axis=1).astype(bf16))
            mixed = jnp.concatenate(
                [mixed[:, band * kept : (band + 1) * kept] for band in range(bands)], axis=0
            )
            precise, static = fields[slots], fields[slots + 1]
            sums = [jnp.zeros((per_member, kept), f32) for _ in range(SUMS)]
            for t in range(slots):
                image = second[t] + mixed
                image_out[t] = image
                whole = first[t] + static
                weighted = precise * whole
                sums[0] = sums[0] + precise * fields[t] * whole
                sums[1] = sums[1] + weighted * whole
                sums[2] = sums[2] + weighted * image
                sums[3] = sums[3] + precise * image * image
            row = jnp.zeros((1, kept), f32)
            for index, part in enumerate(sums):
                part = jnp.sum(jnp.where(lane < 0, part, 0.0), axis=0, keepdims=True)
                part = jnp.sum(part, axis=1, keepdims=True)
                for piece in range(PARTS):
                    high = part.astype(bf16).astype(f32)
                    row = row + jnp.where(lane == PARTS * index + piece, high, 0.0)
                    part = part - high
            row = jnp.broadcast_to(row, (own, kept))
            lane = lax.broadcasted_iota(jnp.int32, (own, kept), 1)
            for block in range(members * bands):
                values = pairs[block].astype(f32)
                values = [jnp.where(lane < lon_share, values[:own], row), values[own:]]
                out[block] = jnp.concatenate(values, axis=0).astype(bf16)

        def hand_out(turn, first, second, *refs):
            blocks, outs = refs[: len(totals)], refs[len(totals) :]
            lane = lax.broadcasted_iota(jnp.int32, (1, kept), 1)
            ratio = closest(
                jnp.concatenate([first[t] for t in range(slots)], axis=0),
                jnp.concatenate([second[t] for t in range(slots)], axis=0),
            )
            rest = [
                jnp.where(lane < lon_share, second[t] - ratio * first[t], ratio) for t in range(slots)
            ]
            images = [first[t] for t in range(slots)] + rest
            pieces = []
            for band in range(bands):
                place = slice(band * own, (band + 1) * own)
                parts = [blocks[block][shift, place].astype(f32) for block, shift, _ in arrivals(0)]
                pieces.append(jnp.concatenate(parts + [image[place] for image in images], axis=0))
            deal(turn[:, :1], pieces, outs)

        def join(turn, own_static, pulling, *refs):
            blocks, (pulled, images) = refs[:-2], refs[-2:]
            if few:
                blocks = [block[...].astype(f32) for block in blocks]
            pieces = chosen(turn[:, :1], blocks, -1)
            size = slots * own
            for band in range(bands):
                place = slice(band * lon_share, (band + 1) * lon_share)
                piece = pieces[band].astype(f32)
                every = piece[:everything].astype(bf16)
                pulled[:, place] = parts_dot(pulling[...], every)[:, :lon_share]
                parts = piece[everything:]
                first = parts[:size]
                second = parts[size:] + parts[size : size + 1, lon_share : lon_share + 1] * first
                static = own_static[band]
                for t in range(slots):
                    at = slice(t * own, (t + 1) * own)
                    images[at, place] = (first[at] + static)[:, :lon_share]
                images[size:, place] = second[:, :lon_share]

        def finish(back, pulled_first, pulled_second, images, *refs):
            (member_out, static_out, image_out), (member, static, image, sems) = refs[:3], refs[3:]

            def outgoing(index, source, target):
                return pltpu.make_async_copy(source, target, sems.at[index])

            def outgoing_member(index):
                place = pl.ds(index * level_share, level_share)
                return outgoing(index, member.at[place], member_out.at[0, place])

            static_copy = outgoing(members, static, static_out)
            image_copy = outgoing(members + 1, image, image_out)
            total = back[0, :1].astype(f32)
            for block in range(1, members * bands):
                total = total + back[block, :1].astype(f32)
            lane = lax.broadcasted_iota(jnp.int32, total.shape, 1) - lon_share
            first_norm, first_image, cross, second_image = [
                jnp.sum(
                    jnp.where((lane >= PARTS * index) & (lane < PARTS * (index + 1)), total, 0.0),
                    axis=1,
                    keepdims=True,
                )
                for index in range(SUMS)
            ]
            alpha = first_norm / (first_norm + first_image)
            ratio = first_image / first_norm
            next_norm = alpha * alpha * jnp.maximum(cross - ratio * first_image, 0.0)
            beta = next_norm / first_norm
            apart = second_image - 2.0 * ratio * cross + ratio * ratio * first_image
            curvature = next_norm + alpha * alpha * apart - beta * next_norm / alpha
            alpha_next = jnp.clip(next_norm / curvature, 0.0, 1.0)
            on_first = alpha + alpha_next * (1.0 - alpha + beta)
            on_second = -alpha * alpha_next
            values = on_first * pulled_first[...] + on_second * pulled_second[...]
            for level in range(levels):
                static[level] = values[level * rows : (level + 1) * rows]
            static_copy.start()
            half = slots * own
            values = on_first * images[:half] + on_second * images[half:]
            for t in range(slots):
                for level in range(level_share):
                    start = (t * level_share + level) * rows
                    image[t, level] = values[start : start + rows]
            image_copy.start()
            for source in range(members):
                parts = []
                for band in range(bands):
                    both = back[source * bands + band].astype(f32)
                    first, second = both[:own], both[own:]
                    ratio = second[:1, lon_share : lon_share + 1]
                    values = (on_first + on_second * ratio) * first + on_second * second
                    parts.append(values[:, :lon_share])
                values = jnp.concatenate(parts, axis=1)
                for share in range(level_share):
                    member[source * level_share + share] = values[share * rows : (share + 1) * rows]
                outgoing_member(source).start()
            static_copy.wait()
            image_copy.wait()
            for source in range(members):
                outgoing_member(source).wait()

        def trade(blocks):
            if not few:
                return [lax.all_to_all(blocks[0], "band", 0, 0, tiled=True)]
            return [blocks[0]] + [
                lax.ppermute(blocks[shift], "band", [(at, (at + shift) % bands) for at in range(bands)])
                for shift in range(1, bands)
            ]

        def around(block, beside):
            if not paired:
                return [lax.all_gather(block, "member")], beside
            here = [block] + [
                lax.ppermute(block, "member", [(at, (at + 2 * shift) % members) for at in range(members)])
                for shift in range(1, members // 2)
            ]
            here, beside = lax.optimization_barrier((jnp.stack(here), beside))
            return [here, lax.ppermute(here, "member", [(at, at ^ 1) for at in range(members)])], beside

        def arrivals(here):
            if not paired:
                return [(0, member, member) for member in range(members)]
            other = here + 1 - 2 * lax.rem(here, 2)
            return [
                (block, shift, lax.rem(source + members - 2 * shift, members))
                for block, source in enumerate((here, other))
                for shift in range(members // 2)
            ]

        def tradable(shape, kind):
            return [(shape, kind)] * bands if few else [((bands,) + shape, kind)]

        here = jnp.stack([lax.axis_index("member"), lax.axis_index("band")]).astype(jnp.int32)

        block = (members * bands, slots * own, padded)
        pieces = pl.pallas_call(
            pack,
            out_shape=jax.ShapeDtypeStruct(block, bf16),
            in_specs=[pl.BlockSpec(memory_space=pltpu.HBM)] * 2,
            out_specs=pl.BlockSpec(memory_space=pltpu.HBM),
            scratch_shapes=[
                pltpu.SMEM((1,), jnp.int32),
                pltpu.VMEM((slots, levels, rows, lon), bf16),
                pltpu.VMEM(block, bf16),
                pltpu.SemaphoreType.DMA,
                pltpu.SemaphoreType.DMA((slots,)),
                pltpu.SemaphoreType.DMA((members,)),
            ],
            compiler_params=pltpu.CompilerParams(vmem_limit_bytes=60 * 2**20),
            name="pack",
        )(member_of_slot, ensemble)
        pieces, innovation, precision, static_root = lax.optimization_barrier(
            (pieces, innovation, precision, static_root)
        )
        stacked = lax.all_to_all(pieces, BOTH, 0, 0, tiled=True)

        of_level, same = row_levels(levels, rows)
        apart, level = row_apart(bands, level_share, rows, copies)
        every_level = np.tile(level, (members // copies, 1))
        block = (arrays * own, padded)
        results = call(
            observe,
            tradable(block, bf16)
            + [
                ((bands, own, kept), f32),
                ((everything, lon), f32),
                ((own, everything), f32),
                ((everything, everything), f32),
                (apart.shape, bf16),
                (every_level.shape, f32),
                ((members, LANES), f32),
                ((1, LANES), jnp.int32),
            ],
            [here, halfwidth, member_weight],
            [innovation, precision, static_root]
            + [jnp.asarray(table) for table in (of_level, same, apart, every_level)],
            scratch=[((levels, rows, lon), f32)] + [((levels, rows, everything), f32)] * 2,
        )
        blocks = trade(results[:-8])
        own_static, pulled, mixing, pulling, taper, factor, weights, turn = results[-8:]
        ring = ring_kernel(width, padded)

        total, weighted, grad_first, image_first, fields = call(
            first_half,
            [
                ((per_member, kept), bf16),
                ((slots, per_member, padded), f32),
                ((members * per_member, kept), f32),
                ((slots, per_member, kept), f32),
                ((arrays, per_member, kept), f32),
            ],
            [],
            [weights, turn, stacked, ring, taper, factor, *blocks],
        )
        pairs, image_second = call(
            second_half,
            [((members * bands, 2 * own, kept), bf16), ((slots, per_member, kept), f32)],
            [],
            [weights, stacked, ring, taper, factor, weighted, grad_first],
            flops=10**9,
        )
        totals, image_second = around(total, image_second)

        pairs, image_second = call(
            combine,
            [((members * bands, 2 * own, kept), bf16), ((slots, per_member, kept), f32)],
            [],
            [pairs, image_first, image_second, fields, mixing, *totals],
        )
        back = lax.all_to_all(pairs, BOTH, 0, 0, tiled=True)
        blocks = call(
            hand_out,
            tradable((traded, kept), bf16),
            [],
            [turn, image_first, image_second, *totals],
        )
        blocks = trade(blocks)
        pulled_second, images = call(
            join,
            [((everything, lon), f32), ((2 * slots * own, lon), f32)],
            [],
            [turn, own_static, pulling, *blocks],
        )
        return pl.pallas_call(
            finish,
            out_shape=(
                jax.ShapeDtypeStruct((1, levels, rows, lon), f32),
                jax.ShapeDtypeStruct((levels, rows, lon), f32),
                jax.ShapeDtypeStruct((slots, level_share, rows, lon), f32),
            ),
            in_specs=[vmem] * 4,
            out_specs=(pl.BlockSpec(memory_space=pltpu.HBM),) * 3,
            scratch_shapes=[
                pltpu.VMEM((levels, rows, lon), f32),
                pltpu.VMEM((levels, rows, lon), f32),
                pltpu.VMEM((slots, level_share, rows, lon), f32),
                pltpu.SemaphoreType.DMA((members + 2,)),
            ],
            compiler_params=pltpu.CompilerParams(vmem_limit_bytes=limit),
            name="finish",
        )(back, pulled, pulled_second, images)

    return jax.shard_map(
        shards,
        mesh=mesh,
        in_specs=(
            P("member", None, None, "band", None),
            P(),
            P("member"),
            P(),
            P(),
            P(None, None, "band", None),
            P(None, "band", None),
        ),
        out_specs=(
            P("member", None, "band", None),
            P(None, "band", None),
            P(None, "member", "band", None),
        ),
        check_vma=False,
    )
```

```python
import math

import jax
import jax.numpy as jnp
import numpy as np
from jax import lax
from jax.experimental import pallas as pl
from jax.experimental.pallas import tpu as pltpu
from jax.sharding import PartitionSpec as P

HMAX = 4
LREACH = 18
REACHES = 4
LANES = 128
FEW = 8
SUMS = 4
PARTS = 3
BOTH = ("member", "band")

ensemble_share = 0.8
static_share = 0.6
length_scale = 6.0


def round_up(value, step):
    return -(-value // step) * step


def lon_weights(distance):
    distance = distance.astype(np.float32)
    values = np.exp(np.float32(-0.5) * (distance / np.float32(length_scale)) ** 2)
    values = values / np.float32(length_scale * math.sqrt(2.0 * math.pi))
    return jnp.asarray(np.where(distance <= LREACH, values, 0.0), jnp.bfloat16)


def ring_kernel(width, padded):
    apart = np.abs(np.arange(padded)[:, None] - np.arange(padded)[None])
    inside = (np.arange(padded)[:, None] < width) & (np.arange(padded)[None] < width)
    return lon_weights(np.where(inside, np.minimum(apart, width - apart), 2 * LREACH))


def near(apart, spans):
    return jnp.maximum(spans - apart, 0.0).astype(jnp.bfloat16)


def row_apart(bands, held, rows, copies):
    index = np.arange(copies * bands * held * rows)
    latitude = index // (held * rows) % bands * rows + index % rows
    level = index // rows % held
    copy = index // (bands * held * rows)
    same = (copy[:, None] == copy[None]) & (level[:, None] == level[None])
    apart = np.where(same, np.abs(latitude[:, None] - latitude[None]), 1000)
    return apart.astype(np.float32), level[:, None].astype(np.float32)


def row_levels(levels, rows):
    index = np.arange(levels * rows)
    level = index[:, None] // rows == np.arange(levels)[None]
    place = index[:, None] % rows == index[None] % rows
    return level.astype(np.float32), place.astype(np.float32)


def exact_dot(matrix, field):
    return jnp.dot(
        matrix, field, precision=lax.Precision.HIGHEST, preferred_element_type=jnp.float32
    )


def parts_dot(matrix, field):
    count, parts = matrix.shape[0], []
    for _ in range(PARTS):
        part = matrix.astype(jnp.bfloat16).astype(jnp.float32)
        parts.append(part)
        matrix = matrix - part
    stacked = jnp.concatenate(parts, axis=0).astype(jnp.bfloat16)
    products = jnp.dot(stacked, field, preferred_element_type=jnp.float32)
    total = products[:count]
    for index in range(1, PARTS):
        total = total + products[index * count : (index + 1) * count]
    return total


def window(values, band, share, halo, tail):
    lon = values.shape[1]
    start = band * share
    stop = start + share + halo
    parts = [values[:, start : min(lon, stop)]]
    if stop > lon:
        parts.append(values[:, : stop - lon])
    if start < halo:
        parts.append(values[:, lon - halo + start :])
    if start:
        parts.append(values[:, max(start - halo, 0) : start])
    return jnp.concatenate(parts + [tail], axis=1)


def spread(field, ring, taper, factor):
    copies = taper.shape[0]
    smoothed = jnp.dot(field.astype(jnp.bfloat16), ring, preferred_element_type=jnp.float32)
    smoothed = smoothed.astype(jnp.bfloat16)
    parts = []
    for start in range(0, field.shape[0], copies):
        part = smoothed[start : start + copies]
        parts.append(jnp.dot(taper, part, preferred_element_type=jnp.float32))
    return factor * (parts[0] if len(parts) == 1 else jnp.concatenate(parts, axis=0))


def solution(mesh):
    members, bands = mesh.shape["member"], mesh.shape["band"]
    few = bands <= FEW
    paired = members % 2 == 0 and members // 2 <= FEW

    def shards(ensemble, member_weight, member_of_slot, halfwidth, static_root, innovation, precision):
        _, slots, levels, rows, lon = ensemble.shape
        level_share, lon_share = levels // members, lon // bands
        own = level_share * rows
        halo = REACHES * LREACH
        width = lon_share + 2 * halo
        padded = round_up(width + 1, LANES)
        kept = round_up(lon_share + SUMS * PARTS, LANES)
        per_member = bands * own
        copies = members
        while copies > 1 and (copies * per_member > 256 or members % copies):
            copies -= 1
        arrays = slots + 2
        everything = levels * rows
        traded = everything + 2 * slots * own
        vmem = pl.BlockSpec(memory_space=pltpu.VMEM)
        smem = pl.BlockSpec(memory_space=pltpu.SMEM)
        limit = min(48, max(14, 24 * members * bands * slots * own * padded // 2**20)) * 2**20

        def call(body, shapes, scalars, operands, scratch=(), flops=0):
            return pl.pallas_call(
                body,
                out_shape=tuple(jax.ShapeDtypeStruct(shape, kind) for shape, kind in shapes),
                in_specs=[smem] * len(scalars) + [vmem] * len(operands),
                out_specs=(vmem,) * len(shapes),
                scratch_shapes=[pltpu.VMEM(shape, kind) for shape, kind in scratch],
                compiler_params=pltpu.CompilerParams(vmem_limit_bytes=limit),
                cost_estimate=pl.CostEstimate(flops=flops, bytes_accessed=0, transcendentals=0),
                name=body.__name__,
            )(*scalars, *operands)

        f32, bf16 = jnp.float32, jnp.bfloat16

        def chosen(turn, blocks, sign):
            if not few:
                return [blocks[0][band] for band in range(bands)]
            turned = []
            for band in range(bands):
                value = blocks[0]
                for shift in range(1, bands):
                    value = jnp.where(turn == (band - sign * shift) % bands, blocks[shift], value)
                turned.append(value)
            return turned

        def load_members(weights, stacked):
            shape = (members, per_member, padded)
            values = stacked[...].astype(f32)
            ensemble = [
                values[:, slot * own : (slot + 1) * own].reshape(shape) for slot in range(slots)
            ]
            which = ensemble[0][:, :1, width : width + 1]
            scale = jnp.zeros(which.shape, f32)
            for member in range(members):
                weight = weights[member : member + 1, :1].reshape(1, 1, 1)
                scale = scale + jnp.where(which == member, weight, 0.0)
            scale = jnp.broadcast_to(scale, (members, per_member, 1))
            return ensemble, scale.reshape(members * per_member, 1)

        def fold(ensemble, scale, weighted):
            total = ensemble[0] * weighted[0][None]
            for slot in range(1, slots):
                total = total + ensemble[slot] * weighted[slot][None]
            return scale * total.reshape(members * per_member, padded)

        def images_of(ensemble, grad, ring, taper, factor):
            local = spread(grad, ring, taper, factor).reshape(members, per_member, padded)
            return [jnp.sum(ensemble[t] * local, axis=0) for t in range(slots)]

        def pack(slot, ensemble, out, marks, arrived, packed, mark_sem, in_sems, out_sems):
            def incoming(t):
                return pltpu.make_async_copy(ensemble.at[0, t], arrived.at[t], in_sems.at[t])

            def outgoing(member):
                place = pl.ds(member * bands, bands)
                return pltpu.make_async_copy(packed.at[place], out.at[place], out_sems.at[member])

            mark = pltpu.make_async_copy(slot, marks, mark_sem)
            mark.start()
            for t in range(slots):
                incoming(t).start()
            mark.wait()
            tail = jnp.full((slots * own, padded - width), marks[0], jnp.int32).astype(f32).astype(bf16)
            for t in range(slots):
                incoming(t).wait()
            for member in range(members):
                picked = range(member * level_share, (member + 1) * level_share)
                values = [arrived[t, at].astype(f32) for t in range(slots) for at in picked]
                values = jnp.concatenate(values, axis=0).astype(bf16)
                for band in range(bands):
                    packed[member * bands + band] = window(values, band, lon_share, halo, tail)
                outgoing(member).start()
            for member in range(members):
                outgoing(member).wait()

        def observe(here, widths, weight, innovation, precision, root, of_level, same, apart, level, *refs):
            outs, results, (static, mixed, pulls) = refs[:-11], refs[-11:-3], refs[-3:]
            own_static, pulled, mixing, pulling, taper, factor, weights, turn = results
            turn[...] = jnp.full((1, LANES), here[1], jnp.int32)
            for member in range(members):
                weights[member : member + 1] = jnp.full((1, LANES), weight[member], f32)
            total = []
            for at in range(levels):
                precise = precision[at].astype(f32)
                part = precise * innovation[0, at].astype(f32)
                for t in range(1, slots):
                    part = part + precise * innovation[t, at].astype(f32)
                total.append(part)
            out_of = lax.dot_general(
                exact_dot(of_level[...], static_share * root[...]),
                of_level[...],
                (((1,), (1,)), ((), ())),
                precision=lax.Precision.HIGHEST,
                preferred_element_type=f32,
            )
            out_of = out_of * same[...]
            into = out_of.T
            back = exact_dot(into, jnp.concatenate(total, axis=0))
            pulled[...] = back
            forth = exact_dot(out_of, back)
            both = exact_dot(out_of, into)
            for at in range(levels):
                static[at] = forth[at * rows : (at + 1) * rows]
                mixed[at] = both[at * rows : (at + 1) * rows]
                pulls[at] = out_of[at * rows : (at + 1) * rows]
            picked = [here[0] * level_share + share for share in range(level_share)]
            arriving = [
                member * level_share + share
                for _, _, member in arrivals(here[0])
                for share in range(level_share)
            ]
            pulling[...] = jnp.concatenate([pulls[at] for at in arriving], axis=0).T
            column = lax.broadcasted_iota(jnp.int32, (everything, own), 0)
            own_column = here[0] * own + lax.broadcasted_iota(jnp.int32, (everything, own), 1)
            mixing[...] = exact_dot(
                jnp.concatenate([mixed[at] for at in arriving], axis=0), (column == own_column).astype(f32)
            ).T
            parts = [innovation[t, at].astype(f32) for t in range(slots) for at in picked]
            parts += [precision[at].astype(f32) for at in picked] + [static[at] for at in picked]
            values = jnp.concatenate(parts, axis=0)
            tail = jnp.zeros((values.shape[0], padded - width), f32)
            pieces = [window(values, band, lon_share, halo, tail) for band in range(bands)]
            for band, piece in enumerate(pieces):
                own_static[band] = piece[(slots + 1) * own :, :kept]
            deal(turn[:, :1], pieces, outs)
            span = jnp.ones(level.shape, f32)
            for at, which in enumerate(picked):
                span = span + jnp.where(level[...] == at, widths[which].astype(f32), 0.0)
            taper[...] = near(apart[...], span[: apart.shape[0]])
            factor[...] = ensemble_share / (span * span)

        def first_half(weights, turn, stacked, ring, taper, factor, *refs):
            blocks, (total_out, weighted_out, grad_out, image_out, fields) = refs[:-5], refs[-5:]
            if few:
                blocks = [block[...].astype(f32) for block in blocks]
            values = jnp.stack(chosen(turn[:, :1], blocks, -1)).astype(f32)
            field = []
            for index in range(arrays):
                piece = values[:, index * own : (index + 1) * own].reshape(per_member, padded)
                fields[index] = piece[:, :kept]
                field.append(piece)
            precise, static = field[slots], field[slots + 1]
            ensemble, scale = load_members(weights, stacked)
            weighted = [precise * field[t] for t in range(slots)]
            grad = spread(fold(ensemble, scale, weighted), ring[...], taper[...], factor[...])
            grad_out[...] = grad[:, :kept]
            total = jnp.zeros((per_member, padded), f32)
            for t, image in enumerate(images_of(ensemble, grad, ring[...], taper[...], scale * factor[...])):
                image_out[t] = image[:, :kept]
                image = precise * (image + static)
                weighted_out[t] = image
                total = total + image
            total_out[...] = total[:, :kept].astype(bf16)

        def inner(first, second):
            inside = lax.broadcasted_iota(jnp.int32, first.shape, 1) < lon_share
            product = jnp.where(inside, first * second, 0.0)
            return jnp.sum(jnp.sum(product, axis=0, keepdims=True), axis=1, keepdims=True)

        def closest(first, second):
            norm = inner(first, first)
            ratio = inner(first, second) / jnp.where(norm > 0.0, norm, 1.0)
            return ratio.astype(bf16).astype(f32)

        def deal(turn, pieces, outs):
            if not few:
                for band, piece in enumerate(pieces):
                    outs[0][band] = piece.astype(bf16)
                return
            for shift in range(bands):
                value = pieces[0]
                for band in range(1, bands):
                    value = jnp.where(turn == (band - shift) % bands, pieces[band], value)
                outs[shift][...] = value.astype(bf16)

        def second_half(weights, stacked, ring, taper, factor, weighted, first, pair_out, image_out):
            ensemble, scale = load_members(weights, stacked)
            grad = fold(ensemble, scale, [weighted[t] for t in range(slots)])
            grad = spread(grad, ring[...], taper[...], factor[...])
            for t, image in enumerate(images_of(ensemble, grad, ring[...], taper[...], scale * factor[...])):
                image_out[t] = image[:, :kept]
            first, second = first[...], grad[:, :kept]
            ratio = closest(first, second)
            shape = (members * bands, own, kept)
            second = (second - ratio * first).reshape(shape)
            lane = lax.broadcasted_iota(jnp.int32, shape, 2)
            second = jnp.where(lane < lon_share, second, ratio.reshape(1, 1, 1))
            pair_out[:, :own] = first.reshape(shape).astype(bf16)
            pair_out[:, own:] = second.astype(bf16)

        def combine(pairs, first, second, fields, mixing, *refs):
            blocks, (out, image_out) = refs[:-2], refs[-2:]
            lane = lax.broadcasted_iota(jnp.int32, (1, kept), 1) - lon_share
            every = [
                jnp.concatenate(
                    [
                        blocks[block][shift, band * own : (band + 1) * own].astype(f32)
                        for block, shift, _ in arrivals(0)
                    ],
                    axis=0,
                )
                for band in range(bands)
            ]
            mixed = parts_dot(mixing[...], jnp.concatenate(every, axis=1).astype(bf16))
            mixed = jnp.concatenate(
                [mixed[:, band * kept : (band + 1) * kept] for band in range(bands)], axis=0
            )
            precise, static = fields[slots], fields[slots + 1]
            sums = [jnp.zeros((per_member, kept), f32) for _ in range(SUMS)]
            for t in range(slots):
                image = second[t] + mixed
                image_out[t] = image
                whole = first[t] + static
                weighted = precise * whole
                sums[0] = sums[0] + precise * fields[t] * whole
                sums[1] = sums[1] + weighted * whole
                sums[2] = sums[2] + weighted * image
                sums[3] = sums[3] + precise * image * image
            row = jnp.zeros((1, kept), f32)
            for index, part in enumerate(sums):
                part = jnp.sum(jnp.where(lane < 0, part, 0.0), axis=0, keepdims=True)
                part = jnp.sum(part, axis=1, keepdims=True)
                for piece in range(PARTS):
                    high = part.astype(bf16).astype(f32)
                    row = row + jnp.where(lane == PARTS * index + piece, high, 0.0)
                    part = part - high
            row = jnp.broadcast_to(row, (own, kept))
            lane = lax.broadcasted_iota(jnp.int32, (own, kept), 1)
            for block in range(members * bands):
                values = pairs[block].astype(f32)
                values = [jnp.where(lane < lon_share, values[:own], row), values[own:]]
                out[block] = jnp.concatenate(values, axis=0).astype(bf16)

        def hand_out(turn, first, second, *refs):
            blocks, outs = refs[: len(totals)], refs[len(totals) :]
            lane = lax.broadcasted_iota(jnp.int32, (1, kept), 1)
            ratio = closest(
                jnp.concatenate([first[t] for t in range(slots)], axis=0),
                jnp.concatenate([second[t] for t in range(slots)], axis=0),
            )
            rest = [
                jnp.where(lane < lon_share, second[t] - ratio * first[t], ratio) for t in range(slots)
            ]
            images = [first[t] for t in range(slots)] + rest
            pieces = []
            for band in range(bands):
                place = slice(band * own, (band + 1) * own)
                parts = [blocks[block][shift, place].astype(f32) for block, shift, _ in arrivals(0)]
                pieces.append(jnp.concatenate(parts + [image[place] for image in images], axis=0))
            deal(turn[:, :1], pieces, outs)

        def join(turn, own_static, pulling, *refs):
            blocks, (pulled, images) = refs[:-2], refs[-2:]
            if few:
                blocks = [block[...].astype(f32) for block in blocks]
            pieces = chosen(turn[:, :1], blocks, -1)
            size = slots * own
            for band in range(bands):
                place = slice(band * lon_share, (band + 1) * lon_share)
                piece = pieces[band].astype(f32)
                every = piece[:everything].astype(bf16)
                pulled[:, place] = parts_dot(pulling[...], every)[:, :lon_share]
                parts = piece[everything:]
                first = parts[:size]
                second = parts[size:] + parts[size : size + 1, lon_share : lon_share + 1] * first
                static = own_static[band]
                for t in range(slots):
                    at = slice(t * own, (t + 1) * own)
                    images[at, place] = (first[at] + static)[:, :lon_share]
                images[size:, place] = second[:, :lon_share]

        def finish(back, pulled_first, pulled_second, images, *refs):
            (member_out, static_out, image_out), (member, static, image, sems) = refs[:3], refs[3:]

            def outgoing(index, source, target):
                return pltpu.make_async_copy(source, target, sems.at[index])

            def outgoing_member(index):
                place = pl.ds(index * level_share, level_share)
                return outgoing(index, member.at[place], member_out.at[0, place])

            static_copy = outgoing(members, static, static_out)
            image_copy = outgoing(members + 1, image, image_out)
            total = back[0, :1].astype(f32)
            for block in range(1, members * bands):
                total = total + back[block, :1].astype(f32)
            lane = lax.broadcasted_iota(jnp.int32, total.shape, 1) - lon_share
            first_norm, first_image, cross, second_image = [
                jnp.sum(
                    jnp.where((lane >= PARTS * index) & (lane < PARTS * (index + 1)), total, 0.0),
                    axis=1,
                    keepdims=True,
                )
                for index in range(SUMS)
            ]
            alpha = first_norm / (first_norm + first_image)
            ratio = first_image / first_norm
            next_norm = alpha * alpha * jnp.maximum(cross - ratio * first_image, 0.0)
            beta = next_norm / first_norm
            apart = second_image - 2.0 * ratio * cross + ratio * ratio * first_image
            curvature = next_norm + alpha * alpha * apart - beta * next_norm / alpha
            alpha_next = jnp.clip(next_norm / curvature, 0.0, 1.0)
            on_first = alpha + alpha_next * (1.0 - alpha + beta)
            on_second = -alpha * alpha_next
            values = on_first * pulled_first[...] + on_second * pulled_second[...]
            for level in range(levels):
                static[level] = values[level * rows : (level + 1) * rows]
            static_copy.start()
            half = slots * own
            values = on_first * images[:half] + on_second * images[half:]
            for t in range(slots):
                for level in range(level_share):
                    start = (t * level_share + level) * rows
                    image[t, level] = values[start : start + rows]
            image_copy.start()
            for source in range(members):
                parts = []
                for band in range(bands):
                    both = back[source * bands + band].astype(f32)
                    first, second = both[:own], both[own:]
                    ratio = second[:1, lon_share : lon_share + 1]
                    values = (on_first + on_second * ratio) * first + on_second * second
                    parts.append(values[:, :lon_share])
                values = jnp.concatenate(parts, axis=1)
                for share in range(level_share):
                    member[source * level_share + share] = values[share * rows : (share + 1) * rows]
                outgoing_member(source).start()
            static_copy.wait()
            image_copy.wait()
            for source in range(members):
                outgoing_member(source).wait()

        def trade(blocks):
            if not few:
                return [lax.all_to_all(blocks[0], "band", 0, 0, tiled=True)]
            return [blocks[0]] + [
                lax.ppermute(blocks[shift], "band", [(at, (at + shift) % bands) for at in range(bands)])
                for shift in range(1, bands)
            ]

        def around(block, beside):
            if not paired:
                return [lax.all_gather(block, "member")], beside
            here = [block] + [
                lax.ppermute(block, "member", [(at, (at + 2 * shift) % members) for at in range(members)])
                for shift in range(1, members // 2)
            ]
            here, beside = lax.optimization_barrier((jnp.stack(here), beside))
            return [here, lax.ppermute(here, "member", [(at, at ^ 1) for at in range(members)])], beside

        def arrivals(here):
            if not paired:
                return [(0, member, member) for member in range(members)]
            other = here + 1 - 2 * lax.rem(here, 2)
            return [
                (block, shift, lax.rem(source + members - 2 * shift, members))
                for block, source in enumerate((here, other))
                for shift in range(members // 2)
            ]

        def tradable(shape, kind):
            return [(shape, kind)] * bands if few else [((bands,) + shape, kind)]

        here = jnp.stack([lax.axis_index("member"), lax.axis_index("band")]).astype(jnp.int32)

        block = (members * bands, slots * own, padded)
        pieces = pl.pallas_call(
            pack,
            out_shape=jax.ShapeDtypeStruct(block, bf16),
            in_specs=[pl.BlockSpec(memory_space=pltpu.HBM)] * 2,
            out_specs=pl.BlockSpec(memory_space=pltpu.HBM),
            scratch_shapes=[
                pltpu.SMEM((1,), jnp.int32),
                pltpu.VMEM((slots, levels, rows, lon), bf16),
                pltpu.VMEM(block, bf16),
                pltpu.SemaphoreType.DMA,
                pltpu.SemaphoreType.DMA((slots,)),
                pltpu.SemaphoreType.DMA((members,)),
            ],
            compiler_params=pltpu.CompilerParams(vmem_limit_bytes=60 * 2**20),
            name="pack",
        )(member_of_slot, ensemble)
        pieces, innovation, precision, static_root = lax.optimization_barrier(
            (pieces, innovation, precision, static_root)
        )
        stacked = lax.all_to_all(pieces, BOTH, 0, 0, tiled=True)

        of_level, same = row_levels(levels, rows)
        apart, level = row_apart(bands, level_share, rows, copies)
        every_level = np.tile(level, (members // copies, 1))
        block = (arrays * own, padded)
        results = call(
            observe,
            tradable(block, bf16)
            + [
                ((bands, own, kept), f32),
                ((everything, lon), f32),
                ((own, everything), f32),
                ((everything, everything), f32),
                (apart.shape, bf16),
                (every_level.shape, f32),
                ((members, LANES), f32),
                ((1, LANES), jnp.int32),
            ],
            [here, halfwidth, member_weight],
            [innovation, precision, static_root]
            + [jnp.asarray(table) for table in (of_level, same, apart, every_level)],
            scratch=[((levels, rows, lon), f32)] + [((levels, rows, everything), f32)] * 2,
        )
        blocks = trade(results[:-8])
        own_static, pulled, mixing, pulling, taper, factor, weights, turn = results[-8:]
        ring = ring_kernel(width, padded)

        total, weighted, grad_first, image_first, fields = call(
            first_half,
            [
                ((per_member, kept), bf16),
                ((slots, per_member, padded), f32),
                ((members * per_member, kept), f32),
                ((slots, per_member, kept), f32),
                ((arrays, per_member, kept), f32),
            ],
            [],
            [weights, turn, stacked, ring, taper, factor, *blocks],
        )
        pairs, image_second = call(
            second_half,
            [((members * bands, 2 * own, kept), bf16), ((slots, per_member, kept), f32)],
            [],
            [weights, stacked, ring, taper, factor, weighted, grad_first],
            flops=10**9,
        )
        totals, image_second = around(total, image_second)

        pairs, image_second = call(
            combine,
            [((members * bands, 2 * own, kept), bf16), ((slots, per_member, kept), f32)],
            [],
            [pairs, image_first, image_second, fields, mixing, *totals],
        )
        back = lax.all_to_all(pairs, BOTH, 0, 0, tiled=True)
        blocks = call(
            hand_out,
            tradable((traded, kept), bf16),
            [],
            [turn, image_first, image_second, *totals],
        )
        blocks = trade(blocks)
        pulled_second, images = call(
            join,
            [((everything, lon), f32), ((2 * slots * own, lon), f32)],
            [],
            [turn, own_static, pulling, *blocks],
        )
        return pl.pallas_call(
            finish,
            out_shape=(
                jax.ShapeDtypeStruct((1, levels, rows, lon), f32),
                jax.ShapeDtypeStruct((levels, rows, lon), f32),
                jax.ShapeDtypeStruct((slots, level_share, rows, lon), f32),
            ),
            in_specs=[vmem] * 4,
            out_specs=(pl.BlockSpec(memory_space=pltpu.HBM),) * 3,
            scratch_shapes=[
                pltpu.VMEM((levels, rows, lon), f32),
                pltpu.VMEM((levels, rows, lon), f32),
                pltpu.VMEM((slots, level_share, rows, lon), f32),
                pltpu.SemaphoreType.DMA((members + 2,)),
            ],
            compiler_params=pltpu.CompilerParams(vmem_limit_bytes=limit),
            name="finish",
        )(back, pulled, pulled_second, images)

    return jax.shard_map(
        shards,
        mesh=mesh,
        in_specs=(
            P("member", None, None, "band", None),
            P(),
            P("member"),
            P(),
            P(),
            P(None, None, "band", None),
            P(None, "band", None),
        ),
        out_specs=(
            P("member", None, "band", None),
            P(None, "band", None),
            P(None, "member", "band", None),
        ),
        check_vma=False,
    )
```

```python
import math

import jax
import jax.numpy as jnp
import numpy as np
from jax import lax
from jax.experimental import pallas as pl
from jax.experimental.pallas import tpu as pltpu
from jax.sharding import PartitionSpec as P

HMAX = 4
LREACH = 18
REACHES = 4
LANES = 128
FEW = 8
SUMS = 4
PARTS = 3
BOTH = ("member", "band")

ensemble_share = 0.8
static_share = 0.6
length_scale = 6.0


def round_up(value, step):
    return -(-value // step) * step


def lon_weights(distance):
    distance = distance.astype(np.float32)
    values = np.exp(np.float32(-0.5) * (distance / np.float32(length_scale)) ** 2)
    values = values / np.float32(length_scale * math.sqrt(2.0 * math.pi))
    return jnp.asarray(np.where(distance <= LREACH, values, 0.0), jnp.bfloat16)


def lon_kernel(reach, width):
    return lon_weights(np.abs(np.arange(width + 2 * reach)[:, None] - reach - np.arange(width)[None]))


def ring_kernel(width, padded):
    apart = np.abs(np.arange(padded)[:, None] - np.arange(padded)[None])
    inside = (np.arange(padded)[:, None] < width) & (np.arange(padded)[None] < width)
    return lon_weights(np.where(inside, np.minimum(apart, width - apart), 2 * LREACH))


def near(apart, spans):
    return jnp.maximum(spans - apart, 0.0).astype(jnp.bfloat16)


def row_apart(bands, held, rows, copies):
    index = np.arange(copies * bands * held * rows)
    latitude = index // (held * rows) % bands * rows + index % rows
    level = index // rows % held
    copy = index // (bands * held * rows)
    same = (copy[:, None] == copy[None]) & (level[:, None] == level[None])
    apart = np.where(same, np.abs(latitude[:, None] - latitude[None]), 1000)
    return apart.astype(np.float32), level[:, None].astype(np.float32)


def halo_apart(levels, rows):
    own = levels * rows
    target, source = np.arange(own)[:, None], np.arange(3 * own)[None]
    shift = (source // own - 1) * rows + source % rows - target % rows
    same = source // rows % levels == target // rows
    return np.where(same, np.abs(shift), 1000).astype(np.float32)


def row_levels(levels, rows):
    index = np.arange(levels * rows)
    level = index[:, None] // rows == np.arange(levels)[None]
    place = index[:, None] % rows == index[None] % rows
    return level.astype(np.float32), place.astype(np.float32)


def partner(at, step, count, sign):
    if count & (count - 1):
        return (at + sign * step) % count
    return at ^ step


def exact_dot(matrix, field):
    return jnp.dot(
        matrix, field, precision=lax.Precision.HIGHEST, preferred_element_type=jnp.float32
    )


def parts_dot(matrix, field):
    count, parts = matrix.shape[0], []
    for _ in range(PARTS):
        part = matrix.astype(jnp.bfloat16).astype(jnp.float32)
        parts.append(part)
        matrix = matrix - part
    stacked = jnp.concatenate(parts, axis=0).astype(jnp.bfloat16)
    products = jnp.dot(stacked, field, preferred_element_type=jnp.float32)
    total = products[:count]
    for index in range(1, PARTS):
        total = total + products[index * count : (index + 1) * count]
    return total


def window(values, band, share, halo, tail):
    lon = values.shape[1]
    start = band * share
    stop = start + share + halo
    parts = [values[:, start : min(lon, stop)]]
    if stop > lon:
        parts.append(values[:, : stop - lon])
    if start < halo:
        parts.append(values[:, lon - halo + start :])
    if start:
        parts.append(values[:, max(start - halo, 0) : start])
    return jnp.concatenate(parts + [tail], axis=1)


def spread(field, ring, taper, factor):
    copies = taper.shape[0]
    smoothed = jnp.dot(field.astype(jnp.bfloat16), ring, preferred_element_type=jnp.float32)
    smoothed = smoothed.astype(jnp.bfloat16)
    parts = []
    for start in range(0, field.shape[0], copies):
        part = smoothed[start : start + copies]
        parts.append(jnp.dot(taper, part, preferred_element_type=jnp.float32))
    return factor * (parts[0] if len(parts) == 1 else jnp.concatenate(parts, axis=0))


def solution(mesh):
    members, bands = mesh.shape["member"], mesh.shape["band"]
    few = bands <= FEW
    paired = members % 2 == 0 and members // 2 <= FEW

    def shards(ensemble, member_weight, member_of_slot, halfwidth, static_root, innovation, precision):
        _, slots, levels, rows, lon = ensemble.shape
        level_share, lon_share = levels // members, lon // bands
        own = level_share * rows
        halo = REACHES * LREACH
        width = lon_share + 2 * halo
        padded = round_up(width + 1, LANES)
        kept = round_up(lon_share + SUMS * PARTS, LANES)
        per_member = bands * own
        copies = members
        while copies > 1 and (copies * per_member > 256 or members % copies):
            copies -= 1
        arrays = slots + 2
        everything = levels * rows
        traded = everything + 2 * slots * own
        vmem = pl.BlockSpec(memory_space=pltpu.VMEM)
        smem = pl.BlockSpec(memory_space=pltpu.SMEM)
        limit = min(48, max(14, 24 * members * bands * slots * own * padded // 2**20)) * 2**20

        def call(body, shapes, scalars, operands, scratch=(), flops=0):
            return pl.pallas_call(
                body,
                out_shape=tuple(jax.ShapeDtypeStruct(shape, kind) for shape, kind in shapes),
                in_specs=[smem] * len(scalars) + [vmem] * len(operands),
                out_specs=(vmem,) * len(shapes),
                scratch_shapes=[pltpu.VMEM(shape, kind) for shape, kind in scratch],
                compiler_params=pltpu.CompilerParams(vmem_limit_bytes=limit),
                cost_estimate=pl.CostEstimate(flops=flops, bytes_accessed=0, transcendentals=0),
                name=body.__name__,
            )(*scalars, *operands)

        f32, bf16 = jnp.float32, jnp.bfloat16

        def fold_smooth(own_weight, ensemble, innovation, precision, kernel, out):
            total = []
            for at in range(levels):
                precise = precision[at].astype(f32)
                part = jnp.zeros((rows, lon), f32)
                for t in range(slots):
                    weighted = precise * innovation[t, at].astype(f32)
                    part = part + ensemble[0, t, at].astype(f32) * weighted
                total.append(part)
            total = own_weight[:, :1] * jnp.concatenate(total, axis=0)
            step = kernel.shape[1]
            margin = (kernel.shape[0] - step) // 2
            steps = -(-lon // step)
            after = steps * step + margin - lon
            ring = jnp.concatenate([total[:, lon - margin :], total, total[:, :after]], axis=1)
            ring = ring.astype(bf16)
            for start in range(0, lon, step):
                stop = min(lon, start + step)
                piece = jnp.dot(
                    ring[:, start : start + kernel.shape[0]], kernel[...], preferred_element_type=f32
                )
                out[:, start:stop] = piece[:, : stop - start].astype(bf16)

        def first_gradient(turn, row_span, below, middle, above, apart, grad):
            span = row_span[:, :1]
            odd = jnp.full((everything, 1), 1, jnp.int32) * lax.rem(turn[:, :1], 2) == 1
            even_pair, odd_pair = below[...].astype(f32), above[...].astype(f32)
            low = jnp.where(odd, even_pair, odd_pair).astype(bf16)
            high = jnp.where(odd, odd_pair, even_pair).astype(bf16)
            stacked = jnp.concatenate([low, middle[...], high], axis=0)
            summed = jnp.dot(near(apart[...], span), stacked, preferred_element_type=f32)
            grad[...] = ensemble_share / (span * span) * summed

        def chosen(turn, blocks, sign):
            if not few:
                return [blocks[0][band] for band in range(bands)]
            turned = []
            for band in range(bands):
                value = blocks[0]
                for shift in range(1, bands):
                    value = jnp.where(turn == partner(band, shift, bands, -sign), blocks[shift], value)
                turned.append(value)
            return turned

        def load_members(weights, stacked):
            shape = (members, per_member, padded)
            values = stacked[...].astype(f32)
            ensemble = [
                values[:, slot * own : (slot + 1) * own].reshape(shape) for slot in range(slots)
            ]
            which = ensemble[0][:, :1, width : width + 1]
            scale = jnp.zeros(which.shape, f32)
            for member in range(members):
                weight = weights[member : member + 1, :1].reshape(1, 1, 1)
                scale = scale + jnp.where(which == member, weight, 0.0)
            scale = jnp.broadcast_to(scale, (members, per_member, 1))
            return ensemble, scale.reshape(members * per_member, 1)

        def fold(ensemble, scale, weighted):
            total = ensemble[0] * weighted[0][None]
            for slot in range(1, slots):
                total = total + ensemble[slot] * weighted[slot][None]
            return scale * total.reshape(members * per_member, padded)

        def images_of(ensemble, grad, ring, taper, factor):
            local = spread(grad, ring, taper, factor).reshape(members, per_member, padded)
            return [jnp.sum(ensemble[t] * local, axis=0) for t in range(slots)]

        def pack(slot, ensemble, out, marks, arrived, packed, mark_sem, in_sems, out_sems):
            def incoming(t):
                return pltpu.make_async_copy(ensemble.at[0, t], arrived.at[t], in_sems.at[t])

            def outgoing(member):
                place = pl.ds(member * bands, bands)
                return pltpu.make_async_copy(packed.at[place], out.at[place], out_sems.at[member])

            mark = pltpu.make_async_copy(slot, marks, mark_sem)
            mark.start()
            for t in range(slots):
                incoming(t).start()
            mark.wait()
            tail = jnp.full((slots * own, padded - width), marks[0], jnp.int32).astype(f32).astype(bf16)
            for t in range(slots):
                incoming(t).wait()
            for member in range(members):
                picked = range(member * level_share, (member + 1) * level_share)
                values = [arrived[t, at].astype(f32) for t in range(slots) for at in picked]
                values = jnp.concatenate(values, axis=0).astype(bf16)
                for band in range(bands):
                    packed[member * bands + band] = window(values, band, lon_share, halo, tail)
                outgoing(member).start()
            for member in range(members):
                outgoing(member).wait()

        def observe(here, widths, weight, marks, innovation, precision, root, of_level, same, apart, level, *refs):
            outs, results, (static, mixed, pulls) = refs[:-13], refs[-13:-3], refs[-3:]
            own_static, pulled, mixing, pulling, taper, factor, weights, turn, own_weight, row_span = results
            own_weight[...] = jnp.full((1, LANES), weight[marks[0]], f32)
            for at in range(levels):
                row_span[at * rows : (at + 1) * rows] = jnp.full((rows, LANES), widths[at].astype(f32) + 1.0, f32)
            turn[...] = jnp.full((1, LANES), here[1], jnp.int32)
            for member in range(members):
                weights[member : member + 1] = jnp.full((1, LANES), weight[member], f32)
            total = []
            for at in range(levels):
                precise = precision[at].astype(f32)
                part = precise * innovation[0, at].astype(f32)
                for t in range(1, slots):
                    part = part + precise * innovation[t, at].astype(f32)
                total.append(part)
            out_of = lax.dot_general(
                exact_dot(of_level[...], static_share * root[...]),
                of_level[...],
                (((1,), (1,)), ((), ())),
                precision=lax.Precision.HIGHEST,
                preferred_element_type=f32,
            )
            out_of = out_of * same[...]
            into = out_of.T
            back = exact_dot(into, jnp.concatenate(total, axis=0))
            pulled[...] = back
            forth = exact_dot(out_of, back)
            both = exact_dot(out_of, into)
            for at in range(levels):
                static[at] = forth[at * rows : (at + 1) * rows]
                mixed[at] = both[at * rows : (at + 1) * rows]
                pulls[at] = out_of[at * rows : (at + 1) * rows]
            picked = [here[0] * level_share + share for share in range(level_share)]
            arriving = [
                member * level_share + share
                for _, _, member in arrivals(here[0])
                for share in range(level_share)
            ]
            pulling[...] = jnp.concatenate([pulls[at] for at in arriving], axis=0).T
            column = lax.broadcasted_iota(jnp.int32, (everything, own), 0)
            own_column = here[0] * own + lax.broadcasted_iota(jnp.int32, (everything, own), 1)
            mixing[...] = exact_dot(
                jnp.concatenate([mixed[at] for at in arriving], axis=0), (column == own_column).astype(f32)
            ).T
            parts = [innovation[t, at].astype(f32) for t in range(slots) for at in picked]
            parts += [precision[at].astype(f32) for at in picked] + [static[at] for at in picked]
            values = jnp.concatenate(parts, axis=0)
            tail = jnp.zeros((values.shape[0], padded - width), f32)
            pieces = [window(values, band, lon_share, halo, tail) for band in range(bands)]
            for band, piece in enumerate(pieces):
                own_static[band] = piece[(slots + 1) * own :, :kept]
            deal(turn[:, :1], pieces, outs)
            span = jnp.ones(level.shape, f32)
            for at, which in enumerate(picked):
                span = span + jnp.where(level[...] == at, widths[which].astype(f32), 0.0)
            taper[...] = near(apart[...], span[: apart.shape[0]])
            factor[...] = ensemble_share / (span * span)

        def first_half(weights, turn, stacked, ring, taper, factor, *refs):
            blocks, (total_out, weighted_out, image_out, fields) = refs[:-4], refs[-4:]
            if few:
                blocks = [block[...].astype(f32) for block in blocks]
            values = jnp.stack(chosen(turn[:, :1], blocks, -1)).astype(f32)
            field = []
            for index in range(arrays):
                piece = values[:, index * own : (index + 1) * own].reshape(per_member, padded)
                fields[index] = piece[:, :kept]
                field.append(piece)
            precise, static = field[slots], field[slots + 1]
            ensemble, scale = load_members(weights, stacked)
            weighted = [precise * field[t] for t in range(slots)]
            grad = spread(fold(ensemble, scale, weighted), ring[...], taper[...], factor[...])
            total = jnp.zeros((per_member, padded), f32)
            for t, image in enumerate(images_of(ensemble, grad, ring[...], taper[...], scale * factor[...])):
                image_out[t] = image[:, :kept]
                image = precise * (image + static)
                weighted_out[t] = image
                total = total + image
            total_out[...] = total[:, :kept].astype(bf16)

        def inner(first, second):
            inside = lax.broadcasted_iota(jnp.int32, first.shape, 1) < lon_share
            product = jnp.where(inside, first * second, 0.0)
            return jnp.sum(jnp.sum(product, axis=0, keepdims=True), axis=1, keepdims=True)

        def closest(first, second):
            norm = inner(first, first)
            ratio = inner(first, second) / jnp.where(norm > 0.0, norm, 1.0)
            return ratio.astype(bf16).astype(f32)

        def deal(turn, pieces, outs):
            if not few:
                for band, piece in enumerate(pieces):
                    outs[0][band] = piece.astype(bf16)
                return
            for shift in range(bands):
                value = pieces[0]
                for band in range(1, bands):
                    value = jnp.where(turn == partner(band, shift, bands, -1), pieces[band], value)
                outs[shift][...] = value.astype(bf16)

        def second_half(weights, stacked, ring, taper, factor, weighted, grad_out, image_out):
            ensemble, scale = load_members(weights, stacked)
            grad = fold(ensemble, scale, [weighted[t] for t in range(slots)])
            grad = spread(grad, ring[...], taper[...], factor[...])
            for t, image in enumerate(images_of(ensemble, grad, ring[...], taper[...], scale * factor[...])):
                image_out[t] = image[:, :kept]
            grad_out[...] = grad[:, :kept].reshape(members * bands, own, kept).astype(bf16)

        def combine(grad, first, second, fields, mixing, *refs):
            blocks, (out, image_out) = refs[:-2], refs[-2:]
            lane = lax.broadcasted_iota(jnp.int32, (1, kept), 1) - lon_share
            every = [
                jnp.concatenate(
                    [
                        blocks[block][shift, band * own : (band + 1) * own].astype(f32)
                        for block, shift, _ in arrivals(0)
                    ],
                    axis=0,
                )
                for band in range(bands)
            ]
            mixed = parts_dot(mixing[...], jnp.concatenate(every, axis=1).astype(bf16))
            mixed = jnp.concatenate(
                [mixed[:, band * kept : (band + 1) * kept] for band in range(bands)], axis=0
            )
            precise, static = fields[slots], fields[slots + 1]
            sums = [jnp.zeros((per_member, kept), f32) for _ in range(SUMS)]
            for t in range(slots):
                image = second[t] + mixed
                image_out[t] = image
                whole = first[t] + static
                weighted = precise * whole
                sums[0] = sums[0] + precise * fields[t] * whole
                sums[1] = sums[1] + weighted * whole
                sums[2] = sums[2] + weighted * image
                sums[3] = sums[3] + precise * image * image
            row = jnp.zeros((1, kept), f32)
            for index, part in enumerate(sums):
                part = jnp.sum(jnp.where(lane < 0, part, 0.0), axis=0, keepdims=True)
                part = jnp.sum(part, axis=1, keepdims=True)
                for piece in range(PARTS):
                    high = part.astype(bf16).astype(f32)
                    row = row + jnp.where(lane == PARTS * index + piece, high, 0.0)
                    part = part - high
            row = jnp.broadcast_to(row, (own, kept))
            lane = lax.broadcasted_iota(jnp.int32, (own, kept), 1)
            for block in range(members * bands):
                out[block] = jnp.where(lane < lon_share, grad[block].astype(f32), row).astype(bf16)

        def hand_out(turn, first, second, *refs):
            blocks, outs = refs[: len(totals)], refs[len(totals) :]
            lane = lax.broadcasted_iota(jnp.int32, (1, kept), 1)
            ratio = closest(
                jnp.concatenate([first[t] for t in range(slots)], axis=0),
                jnp.concatenate([second[t] for t in range(slots)], axis=0),
            )
            rest = [
                jnp.where(lane < lon_share, second[t] - ratio * first[t], ratio) for t in range(slots)
            ]
            images = [first[t] for t in range(slots)] + rest
            pieces = []
            for band in range(bands):
                place = slice(band * own, (band + 1) * own)
                parts = [blocks[block][shift, place].astype(f32) for block, shift, _ in arrivals(0)]
                pieces.append(jnp.concatenate(parts + [image[place] for image in images], axis=0))
            deal(turn[:, :1], pieces, outs)

        def join(turn, own_static, pulling, *refs):
            blocks, (pulled, images) = refs[:-2], refs[-2:]
            if few:
                blocks = [block[...].astype(f32) for block in blocks]
            pieces = chosen(turn[:, :1], blocks, -1)
            size = slots * own
            for band in range(bands):
                place = slice(band * lon_share, (band + 1) * lon_share)
                piece = pieces[band].astype(f32)
                every = piece[:everything].astype(bf16)
                pulled[:, place] = parts_dot(pulling[...], every)[:, :lon_share]
                parts = piece[everything:]
                first = parts[:size]
                second = parts[size:] + parts[size : size + 1, lon_share : lon_share + 1] * first
                static = own_static[band]
                for t in range(slots):
                    at = slice(t * own, (t + 1) * own)
                    images[at, place] = (first[at] + static)[:, :lon_share]
                images[size:, place] = second[:, :lon_share]

        def finish(back, grad_first, pulled_first, pulled_second, images, *refs):
            (member_out, static_out, image_out), (member, static, image, sems) = refs[:3], refs[3:]

            def outgoing(index, source, target):
                return pltpu.make_async_copy(source, target, sems.at[index])

            def outgoing_member(index):
                place = pl.ds(index * level_share, level_share)
                return outgoing(index, member.at[place], member_out.at[0, place])

            static_copy = outgoing(members, static, static_out)
            image_copy = outgoing(members + 1, image, image_out)
            total = back[0, :1].astype(f32)
            for block in range(1, members * bands):
                total = total + back[block, :1].astype(f32)
            lane = lax.broadcasted_iota(jnp.int32, total.shape, 1) - lon_share
            first_norm, first_image, cross, second_image = [
                jnp.sum(
                    jnp.where((lane >= PARTS * index) & (lane < PARTS * (index + 1)), total, 0.0),
                    axis=1,
                    keepdims=True,
                )
                for index in range(SUMS)
            ]
            alpha = first_norm / (first_norm + first_image)
            ratio = first_image / first_norm
            next_norm = alpha * alpha * jnp.maximum(cross - ratio * first_image, 0.0)
            beta = next_norm / first_norm
            apart = second_image - 2.0 * ratio * cross + ratio * ratio * first_image
            curvature = next_norm + alpha * alpha * apart - beta * next_norm / alpha
            alpha_next = jnp.clip(next_norm / curvature, 0.0, 1.0)
            on_first = alpha + alpha_next * (1.0 - alpha + beta)
            on_second = -alpha * alpha_next
            values = on_first * pulled_first[...] + on_second * pulled_second[...]
            for level in range(levels):
                static[level] = values[level * rows : (level + 1) * rows]
            static_copy.start()
            half = slots * own
            values = on_first * images[:half] + on_second * images[half:]
            for t in range(slots):
                for level in range(level_share):
                    start = (t * level_share + level) * rows
                    image[t, level] = values[start : start + rows]
            image_copy.start()
            for source in range(members):
                parts = [
                    back[source * bands + band].astype(f32)[:, :lon_share] for band in range(bands)
                ]
                values = on_second * jnp.concatenate(parts, axis=1)
                values = values + on_first * grad_first[source * own : (source + 1) * own]
                for share in range(level_share):
                    member[source * level_share + share] = values[share * rows : (share + 1) * rows]
                outgoing_member(source).start()
            static_copy.wait()
            image_copy.wait()
            for source in range(members):
                outgoing_member(source).wait()

        def trade(blocks):
            if not few:
                return [lax.all_to_all(blocks[0], "band", 0, 0, tiled=True)]
            return [blocks[0]] + [
                lax.ppermute(
                    blocks[shift], "band", [(at, partner(at, shift, bands, 1)) for at in range(bands)]
                )
                for shift in range(1, bands)
            ]

        def around(block, beside):
            if not paired:
                return [lax.all_gather(block, "member")], beside
            here = [block] + [
                lax.ppermute(
                    block,
                    "member",
                    [(at, 2 * partner(at // 2, shift, members // 2, 1) + at % 2) for at in range(members)],
                )
                for shift in range(1, members // 2)
            ]
            here, beside = lax.optimization_barrier((jnp.stack(here), beside))
            return [here, lax.ppermute(here, "member", [(at, at ^ 1) for at in range(members)])], beside

        def arrivals(here):
            if not paired:
                return [(0, member, member) for member in range(members)]
            chip, core = lax.div(here, 2), lax.rem(here, 2)
            ring = (members // 2) & (members // 2 - 1)
            return [
                (
                    block,
                    shift,
                    2 * (lax.rem(chip + members // 2 - shift, members // 2) if ring else chip ^ shift) + side,
                )
                for block, side in enumerate((core, 1 - core))
                for shift in range(members // 2)
            ]

        def tradable(shape, kind):
            return [(shape, kind)] * bands if few else [((bands,) + shape, kind)]

        here = jnp.stack([lax.axis_index("member"), lax.axis_index("band")]).astype(jnp.int32)

        block = (members * bands, slots * own, padded)
        pieces = pl.pallas_call(
            pack,
            out_shape=jax.ShapeDtypeStruct(block, bf16),
            in_specs=[pl.BlockSpec(memory_space=pltpu.HBM)] * 2,
            out_specs=pl.BlockSpec(memory_space=pltpu.HBM),
            scratch_shapes=[
                pltpu.SMEM((1,), jnp.int32),
                pltpu.VMEM((slots, levels, rows, lon), bf16),
                pltpu.VMEM(block, bf16),
                pltpu.SemaphoreType.DMA,
                pltpu.SemaphoreType.DMA((slots,)),
                pltpu.SemaphoreType.DMA((members,)),
            ],
            compiler_params=pltpu.CompilerParams(vmem_limit_bytes=60 * 2**20),
            name="pack",
        )(member_of_slot, ensemble)
        pieces, ensemble, innovation, precision, static_root = lax.optimization_barrier(
            (pieces, ensemble, innovation, precision, static_root)
        )
        stacked = lax.all_to_all(pieces, BOTH, 0, 0, tiled=True)

        of_level, same = row_levels(levels, rows)
        apart, level = row_apart(bands, level_share, rows, copies)
        every_level = np.tile(level, (members // copies, 1))
        block = (arrays * own, padded)
        results = call(
            observe,
            tradable(block, bf16)
            + [
                ((bands, own, kept), f32),
                ((everything, lon), f32),
                ((own, everything), f32),
                ((everything, everything), f32),
                (apart.shape, bf16),
                (every_level.shape, f32),
                ((members, LANES), f32),
                ((1, LANES), jnp.int32),
                ((1, LANES), f32),
                ((everything, LANES), f32),
            ],
            [here, halfwidth, member_weight, member_of_slot],
            [innovation, precision, static_root]
            + [jnp.asarray(table) for table in (of_level, same, apart, every_level)],
            scratch=[((levels, rows, lon), f32)] + [((levels, rows, everything), f32)] * 2,
        )
        blocks = trade(results[:-10])
        own_static, pulled, mixing, pulling, taper, factor, weights, turn, own_weight, row_span = results[-10:]
        blocks, ensemble, innovation, precision = lax.optimization_barrier(
            (blocks, ensemble, innovation, precision)
        )
        (smoothed,) = call(
            fold_smooth,
            [((everything, lon), bf16)],
            [],
            [own_weight, ensemble, innovation, precision, lon_kernel(LANES, 2 * LANES)],
        )
        pairs = [(at, at + 1) for at in range(bands - 1)]
        below, above = [
            lax.ppermute(smoothed, "band", pairs[start::2] + [(to, at) for at, to in pairs[start::2]])
            for start in range(2)
        ]
        ring = ring_kernel(width, padded)

        total, weighted, image_first, fields = call(
            first_half,
            [
                ((per_member, kept), bf16),
                ((slots, per_member, padded), f32),
                ((slots, per_member, kept), f32),
                ((arrays, per_member, kept), f32),
            ],
            [],
            [weights, turn, stacked, ring, taper, factor, *blocks],
        )
        grad, image_second = call(
            second_half,
            [((members * bands, own, kept), bf16), ((slots, per_member, kept), f32)],
            [],
            [weights, stacked, ring, taper, factor, weighted],
            flops=10**9,
        )
        totals, (image_second, below, above) = around(total, (image_second, below, above))

        grad, image_second = call(
            combine,
            [((members * bands, own, kept), bf16), ((slots, per_member, kept), f32)],
            [],
            [grad, image_first, image_second, fields, mixing, *totals],
        )
        back = lax.all_to_all(grad, BOTH, 0, 0, tiled=True)
        blocks = call(
            hand_out,
            tradable((traded, kept), bf16),
            [],
            [turn, image_first, image_second, *totals],
        )
        blocks = trade(blocks)
        pulled_second, images = call(
            join,
            [((everything, lon), f32), ((2 * slots * own, lon), f32)],
            [],
            [turn, own_static, pulling, *blocks],
        )
        (grad_first,) = call(
            first_gradient,
            [((everything, lon), f32)],
            [],
            [turn, row_span, below, smoothed, above, jnp.asarray(halo_apart(levels, rows))],
        )
        return pl.pallas_call(
            finish,
            out_shape=(
                jax.ShapeDtypeStruct((1, levels, rows, lon), f32),
                jax.ShapeDtypeStruct((levels, rows, lon), f32),
                jax.ShapeDtypeStruct((slots, level_share, rows, lon), f32),
            ),
            in_specs=[vmem] * 5,
            out_specs=(pl.BlockSpec(memory_space=pltpu.HBM),) * 3,
            scratch_shapes=[
                pltpu.VMEM((levels, rows, lon), f32),
                pltpu.VMEM((levels, rows, lon), f32),
                pltpu.VMEM((slots, level_share, rows, lon), f32),
                pltpu.SemaphoreType.DMA((members + 2,)),
            ],
            compiler_params=pltpu.CompilerParams(vmem_limit_bytes=limit),
            name="finish",
        )(back, grad_first, pulled, pulled_second, images)

    return jax.shard_map(
        shards,
        mesh=mesh,
        in_specs=(
            P("member", None, None, "band", None),
            P(),
            P("member"),
            P(),
            P(),
            P(None, None, "band", None),
            P(None, "band", None),
        ),
        out_specs=(
            P("member", None, "band", None),
            P(None, "band", None),
            P(None, "member", "band", None),
        ),
        check_vma=False,
    )
```

```python
import math

import jax
import jax.numpy as jnp
import numpy as np
from jax import lax
from jax.experimental import pallas as pl
from jax.experimental.pallas import tpu as pltpu
from jax.sharding import PartitionSpec as P

HMAX = 4
LREACH = 18
REACHES = 4
LANES = 128
FEW = 8
SUMS = 4
PARTS = 3
BOTH = ("member", "band")

ensemble_share = 0.8
static_share = 0.6
length_scale = 6.0


def round_up(value, step):
    return -(-value // step) * step


def lon_weights(distance):
    distance = distance.astype(np.float32)
    values = np.exp(np.float32(-0.5) * (distance / np.float32(length_scale)) ** 2)
    values = values / np.float32(length_scale * math.sqrt(2.0 * math.pi))
    return jnp.asarray(np.where(distance <= LREACH, values, 0.0), jnp.bfloat16)


def lon_kernel(reach, width):
    return lon_weights(np.abs(np.arange(width + 2 * reach)[:, None] - reach - np.arange(width)[None]))


def ring_kernel(width, padded):
    apart = np.abs(np.arange(padded)[:, None] - np.arange(padded)[None])
    inside = (np.arange(padded)[:, None] < width) & (np.arange(padded)[None] < width)
    return lon_weights(np.where(inside, np.minimum(apart, width - apart), 2 * LREACH))


def near(apart, spans):
    return jnp.maximum(spans - apart, 0.0).astype(jnp.bfloat16)


def row_apart(bands, held, rows, copies):
    index = np.arange(copies * bands * held * rows)
    latitude = index // (held * rows) % bands * rows + index % rows
    level = index // rows % held
    copy = index // (bands * held * rows)
    same = (copy[:, None] == copy[None]) & (level[:, None] == level[None])
    apart = np.where(same, np.abs(latitude[:, None] - latitude[None]), 1000)
    return apart.astype(np.float32), level[:, None].astype(np.float32)


def halo_apart(levels, rows):
    own = levels * rows
    target, source = np.arange(own)[:, None], np.arange(3 * own)[None]
    shift = (source // own - 1) * rows + source % rows - target % rows
    same = source // rows % levels == target // rows
    return np.where(same, np.abs(shift), 1000).astype(np.float32)


def row_levels(levels, rows):
    index = np.arange(levels * rows)
    level = index[:, None] // rows == np.arange(levels)[None]
    place = index[:, None] % rows == index[None] % rows
    return level.astype(np.float32), place.astype(np.float32)


def partner(at, step, count, sign):
    if count & (count - 1):
        return (at + sign * step) % count
    return at ^ step


def exact_dot(matrix, field):
    return jnp.dot(
        matrix, field, precision=lax.Precision.HIGHEST, preferred_element_type=jnp.float32
    )


def parts_dot(matrix, field):
    count, parts = matrix.shape[0], []
    for _ in range(PARTS):
        part = matrix.astype(jnp.bfloat16).astype(jnp.float32)
        parts.append(part)
        matrix = matrix - part
    stacked = jnp.concatenate(parts, axis=0).astype(jnp.bfloat16)
    products = jnp.dot(stacked, field, preferred_element_type=jnp.float32)
    total = products[:count]
    for index in range(1, PARTS):
        total = total + products[index * count : (index + 1) * count]
    return total


def window(values, band, share, halo, tail):
    lon = values.shape[1]
    start = band * share
    stop = start + share + halo
    parts = [values[:, start : min(lon, stop)]]
    if stop > lon:
        parts.append(values[:, : stop - lon])
    if start < halo:
        parts.append(values[:, lon - halo + start :])
    if start:
        parts.append(values[:, max(start - halo, 0) : start])
    return jnp.concatenate(parts + [tail], axis=1)


def spread(field, ring, taper, factor):
    copies = taper.shape[0]
    smoothed = jnp.dot(field.astype(jnp.bfloat16), ring, preferred_element_type=jnp.float32)
    smoothed = smoothed.astype(jnp.bfloat16)
    parts = []
    for start in range(0, field.shape[0], copies):
        part = smoothed[start : start + copies]
        parts.append(jnp.dot(taper, part, preferred_element_type=jnp.float32))
    return factor * (parts[0] if len(parts) == 1 else jnp.concatenate(parts, axis=0))


def solution(mesh):
    members, bands = mesh.shape["member"], mesh.shape["band"]
    few = bands <= FEW
    paired = members % 2 == 0 and members // 2 <= FEW

    def shards(ensemble, member_weight, member_of_slot, halfwidth, static_root, innovation, precision):
        _, slots, levels, rows, lon = ensemble.shape
        level_share, lon_share = levels // members, lon // bands
        own = level_share * rows
        halo = REACHES * LREACH
        width = lon_share + 2 * halo
        padded = round_up(width + 1, LANES)
        kept = round_up(lon_share + SUMS * PARTS, LANES)
        per_member = bands * own
        copies = members
        while copies > 1 and (copies * per_member > 256 or members % copies):
            copies -= 1
        arrays = slots + 2
        everything = levels * rows
        traded = everything + 2 * slots * own
        vmem = pl.BlockSpec(memory_space=pltpu.VMEM)
        smem = pl.BlockSpec(memory_space=pltpu.SMEM)
        limit = min(48, max(14, 24 * members * bands * slots * own * padded // 2**20)) * 2**20

        def call(body, shapes, scalars, operands, scratch=(), flops=0):
            return pl.pallas_call(
                body,
                out_shape=tuple(jax.ShapeDtypeStruct(shape, kind) for shape, kind in shapes),
                in_specs=[smem] * len(scalars) + [vmem] * len(operands),
                out_specs=(vmem,) * len(shapes),
                scratch_shapes=[pltpu.VMEM(shape, kind) for shape, kind in scratch],
                compiler_params=pltpu.CompilerParams(vmem_limit_bytes=limit),
                cost_estimate=pl.CostEstimate(flops=flops, bytes_accessed=0, transcendentals=0),
                name=body.__name__,
            )(*scalars, *operands)

        f32, bf16 = jnp.float32, jnp.bfloat16

        def fold_smooth(own_weight, ensemble, innovation, precision, kernel, out):
            total = []
            for at in range(levels):
                precise = precision[at].astype(f32)
                part = jnp.zeros((rows, lon), f32)
                for t in range(slots):
                    weighted = precise * innovation[t, at].astype(f32)
                    part = part + ensemble[0, t, at].astype(f32) * weighted
                total.append(part)
            total = own_weight[:, :1] * jnp.concatenate(total, axis=0)
            step = kernel.shape[1]
            margin = (kernel.shape[0] - step) // 2
            steps = -(-lon // step)
            after = steps * step + margin - lon
            ring = jnp.concatenate([total[:, lon - margin :], total, total[:, :after]], axis=1)
            ring = ring.astype(bf16)
            for start in range(0, lon, step):
                stop = min(lon, start + step)
                piece = jnp.dot(
                    ring[:, start : start + kernel.shape[0]], kernel[...], preferred_element_type=f32
                )
                out[:, start:stop] = piece[:, : stop - start].astype(bf16)

        def first_gradient(turn, row_span, below, middle, above, apart, grad):
            span = row_span[:, :1]
            odd = jnp.full((everything, 1), 1, jnp.int32) * lax.rem(turn[:, :1], 2) == 1
            even_pair, odd_pair = below[...].astype(f32), above[...].astype(f32)
            low = jnp.where(odd, even_pair, odd_pair).astype(bf16)
            high = jnp.where(odd, odd_pair, even_pair).astype(bf16)
            stacked = jnp.concatenate([low, middle[...], high], axis=0)
            summed = jnp.dot(near(apart[...], span), stacked, preferred_element_type=f32)
            grad[...] = ensemble_share / (span * span) * summed

        def chosen(turn, blocks, sign):
            if not few:
                return [blocks[0][band] for band in range(bands)]
            turned = []
            for band in range(bands):
                value = blocks[0]
                for shift in range(1, bands):
                    value = jnp.where(turn == partner(band, shift, bands, -sign), blocks[shift], value)
                turned.append(value)
            return turned

        def load_members(weights, stacked):
            shape = (members, per_member, padded)
            values = stacked[...].astype(f32)
            ensemble = [
                values[:, slot * own : (slot + 1) * own].reshape(shape) for slot in range(slots)
            ]
            which = ensemble[0][:, :1, width : width + 1]
            scale = jnp.zeros(which.shape, f32)
            for member in range(members):
                weight = weights[member : member + 1, :1].reshape(1, 1, 1)
                scale = scale + jnp.where(which == member, weight, 0.0)
            scale = jnp.broadcast_to(scale, (members, per_member, 1))
            return ensemble, scale.reshape(members * per_member, 1)

        def fold(ensemble, scale, weighted):
            total = ensemble[0] * weighted[0][None]
            for slot in range(1, slots):
                total = total + ensemble[slot] * weighted[slot][None]
            return scale * total.reshape(members * per_member, padded)

        def images_of(ensemble, grad, ring, taper, factor):
            local = spread(grad, ring, taper, factor).reshape(members, per_member, padded)
            return [jnp.sum(ensemble[t] * local, axis=0) for t in range(slots)]

        def pack(slot, ensemble, out, marks, arrived, packed, mark_sem, in_sems, out_sems):
            def incoming(t):
                return pltpu.make_async_copy(ensemble.at[0, t], arrived.at[t], in_sems.at[t])

            def outgoing(member):
                place = pl.ds(member * bands, bands)
                return pltpu.make_async_copy(packed.at[place], out.at[place], out_sems.at[member])

            mark = pltpu.make_async_copy(slot, marks, mark_sem)
            mark.start()
            for t in range(slots):
                incoming(t).start()
            mark.wait()
            tail = jnp.full((slots * own, padded - width), marks[0], jnp.int32).astype(f32).astype(bf16)
            for t in range(slots):
                incoming(t).wait()
            for member in range(members):
                picked = range(member * level_share, (member + 1) * level_share)
                values = [arrived[t, at].astype(f32) for t in range(slots) for at in picked]
                values = jnp.concatenate(values, axis=0).astype(bf16)
                for band in range(bands):
                    packed[member * bands + band] = window(values, band, lon_share, halo, tail)
                outgoing(member).start()
            for member in range(members):
                outgoing(member).wait()

        def rows_between(root, of_level, same):
            wide = lax.dot_general(
                exact_dot(of_level, static_share * root),
                of_level,
                (((1,), (1,)), ((), ())),
                precision=lax.Precision.HIGHEST,
                preferred_element_type=f32,
            )
            return wide * same

        def observe(place, turn, innovation, precision, root, of_level, same, *refs):
            outs, (own_static, pulled) = refs[:-2], refs[-2:]
            out_of = rows_between(root[...], of_level[...], same[...])
            row = lax.broadcasted_iota(jnp.int32, (own, everything), 0)
            column = lax.broadcasted_iota(jnp.int32, (own, everything), 1)
            picker = (column == place[:, :1] * own + row).astype(f32)
            out_of_own = exact_dot(picker, out_of)
            precise = jnp.concatenate([precision[at].astype(f32) for at in range(levels)], axis=0)
            innovations = [
                jnp.concatenate([innovation[t, at].astype(f32) for at in range(levels)], axis=0)
                for t in range(slots)
            ]
            total = precise * innovations[0]
            for t in range(1, slots):
                total = total + precise * innovations[t]
            high = total.astype(bf16)
            low = (total - high.astype(f32)).astype(bf16)
            into = out_of.T
            back = parts_dot(into, high) + jnp.dot(into.astype(bf16), low, preferred_element_type=f32)
            pulled[...] = back
            values = [
                jnp.dot(picker.astype(bf16), field.astype(bf16), preferred_element_type=f32)
                for field in innovations + [precise]
            ]
            values = jnp.concatenate(values + [exact_dot(out_of_own, back)], axis=0)
            tail = jnp.zeros((values.shape[0], padded - width), f32)
            pieces = [window(values, band, lon_share, halo, tail) for band in range(bands)]
            for band, piece in enumerate(pieces):
                own_static[band] = piece[(slots + 1) * own :, :kept]
            deal(turn[:, :1], pieces, outs)

        def prepare(here, widths, weight, marks, root, of_level, same, apart, level, *refs):
            mixing, pulling, taper, factor, weights, own_weight, row_span, mixed, pulls = refs
            for member in range(members):
                weights[member : member + 1] = jnp.full((1, LANES), weight[member], f32)
            own_weight[...] = jnp.full((1, LANES), weight[marks[0]], f32)
            for at in range(levels):
                row_span[at * rows : (at + 1) * rows] = jnp.full(
                    (rows, LANES), widths[at].astype(f32) + 1.0, f32
                )
            out_of = rows_between(root[...], of_level[...], same[...])
            both = exact_dot(out_of, out_of.T)
            for at in range(levels):
                mixed[at] = both[at * rows : (at + 1) * rows]
                pulls[at] = out_of[at * rows : (at + 1) * rows]
            arriving = [
                member * level_share + share
                for _, _, member in arrivals(here[0])
                for share in range(level_share)
            ]
            pulling[...] = jnp.concatenate([pulls[at] for at in arriving], axis=0).T
            column = lax.broadcasted_iota(jnp.int32, (everything, own), 0)
            own_column = here[0] * own + lax.broadcasted_iota(jnp.int32, (everything, own), 1)
            mixing[...] = exact_dot(
                jnp.concatenate([mixed[at] for at in arriving], axis=0), (column == own_column).astype(f32)
            ).T
            span = jnp.ones(level.shape, f32)
            for share in range(level_share):
                which = here[0] * level_share + share
                span = span + jnp.where(level[...] == share, widths[which].astype(f32), 0.0)
            taper[...] = near(apart[...], span[: apart.shape[0]])
            factor[...] = ensemble_share / (span * span)

        def first_half(weights, turn, stacked, ring, taper, factor, *refs):
            blocks, (total_out, weighted_out, image_out, fields) = refs[:-4], refs[-4:]
            if few:
                blocks = [block[...].astype(f32) for block in blocks]
            values = jnp.stack(chosen(turn[:, :1], blocks, -1)).astype(f32)
            field = []
            for index in range(arrays):
                piece = values[:, index * own : (index + 1) * own].reshape(per_member, padded)
                fields[index] = piece[:, :kept]
                field.append(piece)
            precise, static = field[slots], field[slots + 1]
            ensemble, scale = load_members(weights, stacked)
            weighted = [precise * field[t] for t in range(slots)]
            grad = spread(fold(ensemble, scale, weighted), ring[...], taper[...], factor[...])
            total = jnp.zeros((per_member, padded), f32)
            for t, image in enumerate(images_of(ensemble, grad, ring[...], taper[...], scale * factor[...])):
                image_out[t] = image[:, :kept]
                image = precise * (image + static)
                weighted_out[t] = image
                total = total + image
            total_out[...] = total[:, :kept].astype(bf16)

        def inner(first, second):
            inside = lax.broadcasted_iota(jnp.int32, first.shape, 1) < lon_share
            product = jnp.where(inside, first * second, 0.0)
            return jnp.sum(jnp.sum(product, axis=0, keepdims=True), axis=1, keepdims=True)

        def closest(first, second):
            norm = inner(first, first)
            ratio = inner(first, second) / jnp.where(norm > 0.0, norm, 1.0)
            return ratio.astype(bf16).astype(f32)

        def deal(turn, pieces, outs):
            if not few:
                for band, piece in enumerate(pieces):
                    outs[0][band] = piece.astype(bf16)
                return
            for shift in range(bands):
                value = pieces[0]
                for band in range(1, bands):
                    value = jnp.where(turn == partner(band, shift, bands, -1), pieces[band], value)
                outs[shift][...] = value.astype(bf16)

        def second_half(weights, stacked, ring, taper, factor, weighted, grad_out, image_out):
            ensemble, scale = load_members(weights, stacked)
            grad = fold(ensemble, scale, [weighted[t] for t in range(slots)])
            grad = spread(grad, ring[...], taper[...], factor[...])
            for t, image in enumerate(images_of(ensemble, grad, ring[...], taper[...], scale * factor[...])):
                image_out[t] = image[:, :kept]
            grad_out[...] = grad[:, :kept].reshape(members * bands, own, kept).astype(bf16)

        def combine(grad, first, second, fields, mixing, *refs):
            blocks, (out, image_out) = refs[:-2], refs[-2:]
            lane = lax.broadcasted_iota(jnp.int32, (1, kept), 1) - lon_share
            every = [
                jnp.concatenate(
                    [
                        blocks[block][shift, band * own : (band + 1) * own].astype(f32)
                        for block, shift, _ in arrivals(0)
                    ],
                    axis=0,
                )
                for band in range(bands)
            ]
            mixed = parts_dot(mixing[...], jnp.concatenate(every, axis=1).astype(bf16))
            mixed = jnp.concatenate(
                [mixed[:, band * kept : (band + 1) * kept] for band in range(bands)], axis=0
            )
            precise, static = fields[slots], fields[slots + 1]
            sums = [jnp.zeros((per_member, kept), f32) for _ in range(SUMS)]
            for t in range(slots):
                image = second[t] + mixed
                image_out[t] = image
                whole = first[t] + static
                weighted = precise * whole
                sums[0] = sums[0] + precise * fields[t] * whole
                sums[1] = sums[1] + weighted * whole
                sums[2] = sums[2] + weighted * image
                sums[3] = sums[3] + precise * image * image
            row = jnp.zeros((1, kept), f32)
            for index, part in enumerate(sums):
                part = jnp.sum(jnp.where(lane < 0, part, 0.0), axis=0, keepdims=True)
                part = jnp.sum(part, axis=1, keepdims=True)
                for piece in range(PARTS):
                    high = part.astype(bf16).astype(f32)
                    row = row + jnp.where(lane == PARTS * index + piece, high, 0.0)
                    part = part - high
            row = jnp.broadcast_to(row, (own, kept))
            lane = lax.broadcasted_iota(jnp.int32, (own, kept), 1)
            for block in range(members * bands):
                out[block] = jnp.where(lane < lon_share, grad[block].astype(f32), row).astype(bf16)

        def hand_out(turn, first, second, *refs):
            blocks, outs = refs[: len(totals)], refs[len(totals) :]
            lane = lax.broadcasted_iota(jnp.int32, (1, kept), 1)
            ratio = closest(
                jnp.concatenate([first[t] for t in range(slots)], axis=0),
                jnp.concatenate([second[t] for t in range(slots)], axis=0),
            )
            rest = [
                jnp.where(lane < lon_share, second[t] - ratio * first[t], ratio) for t in range(slots)
            ]
            images = [first[t] for t in range(slots)] + rest
            pieces = []
            for band in range(bands):
                place = slice(band * own, (band + 1) * own)
                parts = [blocks[block][shift, place].astype(f32) for block, shift, _ in arrivals(0)]
                pieces.append(jnp.concatenate(parts + [image[place] for image in images], axis=0))
            deal(turn[:, :1], pieces, outs)

        def join(turn, own_static, pulling, *refs):
            blocks, (pulled, images) = refs[:-2], refs[-2:]
            if few:
                blocks = [block[...].astype(f32) for block in blocks]
            pieces = chosen(turn[:, :1], blocks, -1)
            size = slots * own
            for band in range(bands):
                place = slice(band * lon_share, (band + 1) * lon_share)
                piece = pieces[band].astype(f32)
                every = piece[:everything].astype(bf16)
                pulled[:, place] = parts_dot(pulling[...], every)[:, :lon_share]
                parts = piece[everything:]
                first = parts[:size]
                second = parts[size:] + parts[size : size + 1, lon_share : lon_share + 1] * first
                static = own_static[band]
                for t in range(slots):
                    at = slice(t * own, (t + 1) * own)
                    images[at, place] = (first[at] + static)[:, :lon_share]
                images[size:, place] = second[:, :lon_share]

        def finish(back, grad_first, pulled_first, pulled_second, images, *refs):
            (member_out, static_out, image_out), (member, static, image, sems) = refs[:3], refs[3:]

            def outgoing(index, source, target):
                return pltpu.make_async_copy(source, target, sems.at[index])

            def outgoing_member(index):
                place = pl.ds(index * level_share, level_share)
                return outgoing(index, member.at[place], member_out.at[0, place])

            static_copy = outgoing(members, static, static_out)
            image_copy = outgoing(members + 1, image, image_out)
            total = back[0, :1].astype(f32)
            for block in range(1, members * bands):
                total = total + back[block, :1].astype(f32)
            lane = lax.broadcasted_iota(jnp.int32, total.shape, 1) - lon_share
            first_norm, first_image, cross, second_image = [
                jnp.sum(
                    jnp.where((lane >= PARTS * index) & (lane < PARTS * (index + 1)), total, 0.0),
                    axis=1,
                    keepdims=True,
                )
                for index in range(SUMS)
            ]
            alpha = first_norm / (first_norm + first_image)
            ratio = first_image / first_norm
            next_norm = alpha * alpha * jnp.maximum(cross - ratio * first_image, 0.0)
            beta = next_norm / first_norm
            apart = second_image - 2.0 * ratio * cross + ratio * ratio * first_image
            curvature = next_norm + alpha * alpha * apart - beta * next_norm / alpha
            alpha_next = jnp.clip(next_norm / curvature, 0.0, 1.0)
            on_first = alpha + alpha_next * (1.0 - alpha + beta)
            on_second = -alpha * alpha_next
            values = on_first * pulled_first[...] + on_second * pulled_second[...]
            for level in range(levels):
                static[level] = values[level * rows : (level + 1) * rows]
            static_copy.start()
            half = slots * own
            values = on_first * images[:half] + on_second * images[half:]
            for t in range(slots):
                for level in range(level_share):
                    start = (t * level_share + level) * rows
                    image[t, level] = values[start : start + rows]
            image_copy.start()
            for source in range(members):
                parts = [
                    back[source * bands + band].astype(f32)[:, :lon_share] for band in range(bands)
                ]
                values = on_second * jnp.concatenate(parts, axis=1)
                values = values + on_first * grad_first[source * own : (source + 1) * own]
                for share in range(level_share):
                    member[source * level_share + share] = values[share * rows : (share + 1) * rows]
                outgoing_member(source).start()
            static_copy.wait()
            image_copy.wait()
            for source in range(members):
                outgoing_member(source).wait()

        def trade(blocks):
            if not few:
                return [lax.all_to_all(blocks[0], "band", 0, 0, tiled=True)]
            return [blocks[0]] + [
                lax.ppermute(
                    blocks[shift], "band", [(at, partner(at, shift, bands, 1)) for at in range(bands)]
                )
                for shift in range(1, bands)
            ]

        def around(block, beside):
            if not paired:
                return [lax.all_gather(block, "member")], beside
            here = [block] + [
                lax.ppermute(
                    block,
                    "member",
                    [(at, 2 * partner(at // 2, shift, members // 2, 1) + at % 2) for at in range(members)],
                )
                for shift in range(1, members // 2)
            ]
            here, beside = lax.optimization_barrier((jnp.stack(here), beside))
            return [here, lax.ppermute(here, "member", [(at, at ^ 1) for at in range(members)])], beside

        def arrivals(here):
            if not paired:
                return [(0, member, member) for member in range(members)]
            chip, core = lax.div(here, 2), lax.rem(here, 2)
            ring = (members // 2) & (members // 2 - 1)
            return [
                (
                    block,
                    shift,
                    2 * (lax.rem(chip + members // 2 - shift, members // 2) if ring else chip ^ shift) + side,
                )
                for block, side in enumerate((core, 1 - core))
                for shift in range(members // 2)
            ]

        def tradable(shape, kind):
            return [(shape, kind)] * bands if few else [((bands,) + shape, kind)]

        place = jnp.full((1, LANES), lax.axis_index("member"), jnp.int32)
        turn = jnp.full((1, LANES), lax.axis_index("band"), jnp.int32)
        here = lax.axis_index("member").astype(jnp.int32).reshape(1)

        block = (members * bands, slots * own, padded)
        pieces = pl.pallas_call(
            pack,
            out_shape=jax.ShapeDtypeStruct(block, bf16),
            in_specs=[pl.BlockSpec(memory_space=pltpu.HBM)] * 2,
            out_specs=pl.BlockSpec(memory_space=pltpu.HBM),
            scratch_shapes=[
                pltpu.SMEM((1,), jnp.int32),
                pltpu.VMEM((slots, levels, rows, lon), bf16),
                pltpu.VMEM(block, bf16),
                pltpu.SemaphoreType.DMA,
                pltpu.SemaphoreType.DMA((slots,)),
                pltpu.SemaphoreType.DMA((members,)),
            ],
            compiler_params=pltpu.CompilerParams(vmem_limit_bytes=60 * 2**20),
            name="pack",
        )(member_of_slot, ensemble)
        pieces, ensemble, innovation, precision, static_root = lax.optimization_barrier(
            (pieces, ensemble, innovation, precision, static_root)
        )
        stacked = lax.all_to_all(pieces, BOTH, 0, 0, tiled=True)

        of_level, same = row_levels(levels, rows)
        apart, level = row_apart(bands, level_share, rows, copies)
        every_level = np.tile(level, (members // copies, 1))
        block = (arrays * own, padded)
        between = [static_root] + [jnp.asarray(table) for table in (of_level, same)]
        results = call(
            observe,
            tradable(block, bf16) + [((bands, own, kept), f32), ((everything, lon), f32)],
            [],
            [place, turn, innovation, precision, *between],
        )
        blocks, (own_static, pulled) = trade(results[:-2]), results[-2:]
        own_static, between = lax.optimization_barrier((own_static, between))
        mixing, pulling, taper, factor, weights, own_weight, row_span = call(
            prepare,
            [
                ((own, everything), f32),
                ((everything, everything), f32),
                (apart.shape, bf16),
                (every_level.shape, f32),
                ((members, LANES), f32),
                ((1, LANES), f32),
                ((everything, LANES), f32),
            ],
            [here, halfwidth, member_weight, member_of_slot],
            [*between, jnp.asarray(apart), jnp.asarray(every_level)],
            scratch=[((levels, rows, everything), f32)] * 2,
        )
        blocks, ensemble, innovation, precision = lax.optimization_barrier(
            (blocks, ensemble, innovation, precision)
        )
        (smoothed,) = call(
            fold_smooth,
            [((everything, lon), bf16)],
            [],
            [own_weight, ensemble, innovation, precision, lon_kernel(LANES, 2 * LANES)],
        )
        pairs = [(at, at + 1) for at in range(bands - 1)]
        below, above = [
            lax.ppermute(smoothed, "band", pairs[start::2] + [(to, at) for at, to in pairs[start::2]])
            for start in range(2)
        ]
        ring = ring_kernel(width, padded)

        total, weighted, image_first, fields = call(
            first_half,
            [
                ((per_member, kept), bf16),
                ((slots, per_member, padded), f32),
                ((slots, per_member, kept), f32),
                ((arrays, per_member, kept), f32),
            ],
            [],
            [weights, turn, stacked, ring, taper, factor, *blocks],
        )
        grad, image_second = call(
            second_half,
            [((members * bands, own, kept), bf16), ((slots, per_member, kept), f32)],
            [],
            [weights, stacked, ring, taper, factor, weighted],
            flops=10**9,
        )
        totals, (image_second, below, above) = around(total, (image_second, below, above))

        grad, image_second = call(
            combine,
            [((members * bands, own, kept), bf16), ((slots, per_member, kept), f32)],
            [],
            [grad, image_first, image_second, fields, mixing, *totals],
        )
        back = lax.all_to_all(grad, BOTH, 0, 0, tiled=True)
        blocks = call(
            hand_out,
            tradable((traded, kept), bf16),
            [],
            [turn, image_first, image_second, *totals],
        )
        blocks = trade(blocks)
        pulled_second, images = call(
            join,
            [((everything, lon), f32), ((2 * slots * own, lon), f32)],
            [],
            [turn, own_static, pulling, *blocks],
        )
        (grad_first,) = call(
            first_gradient,
            [((everything, lon), f32)],
            [],
            [turn, row_span, below, smoothed, above, jnp.asarray(halo_apart(levels, rows))],
        )
        return pl.pallas_call(
            finish,
            out_shape=(
                jax.ShapeDtypeStruct((1, levels, rows, lon), f32),
                jax.ShapeDtypeStruct((levels, rows, lon), f32),
                jax.ShapeDtypeStruct((slots, level_share, rows, lon), f32),
            ),
            in_specs=[vmem] * 5,
            out_specs=(pl.BlockSpec(memory_space=pltpu.HBM),) * 3,
            scratch_shapes=[
                pltpu.VMEM((levels, rows, lon), f32),
                pltpu.VMEM((levels, rows, lon), f32),
                pltpu.VMEM((slots, level_share, rows, lon), f32),
                pltpu.SemaphoreType.DMA((members + 2,)),
            ],
            compiler_params=pltpu.CompilerParams(vmem_limit_bytes=limit),
            name="finish",
        )(back, grad_first, pulled, pulled_second, images)

    return jax.shard_map(
        shards,
        mesh=mesh,
        in_specs=(
            P("member", None, None, "band", None),
            P(),
            P("member"),
            P(),
            P(),
            P(None, None, "band", None),
            P(None, "band", None),
        ),
        out_specs=(
            P("member", None, "band", None),
            P(None, "band", None),
            P(None, "member", "band", None),
        ),
        check_vma=False,
    )
```

```python
import math

import jax
import jax.numpy as jnp
import numpy as np
from jax import lax
from jax.experimental import pallas as pl
from jax.experimental.pallas import tpu as pltpu
from jax.sharding import PartitionSpec as P

HMAX = 4
LREACH = 18
REACHES = 4
LANES = 128
FEW = 8
SUMS = 4
PARTS = 3
BOTH = ("member", "band")

ensemble_share = 0.8
static_share = 0.6
length_scale = 6.0


def round_up(value, step):
    return -(-value // step) * step


def lon_weights(distance):
    distance = distance.astype(np.float32)
    values = np.exp(np.float32(-0.5) * (distance / np.float32(length_scale)) ** 2)
    values = values / np.float32(length_scale * math.sqrt(2.0 * math.pi))
    return jnp.asarray(np.where(distance <= LREACH, values, 0.0), jnp.bfloat16)


def lon_kernel(reach, width):
    return lon_weights(np.abs(np.arange(width + 2 * reach)[:, None] - reach - np.arange(width)[None]))


def ring_kernel(width, padded):
    apart = np.abs(np.arange(padded)[:, None] - np.arange(padded)[None])
    inside = (np.arange(padded)[:, None] < width) & (np.arange(padded)[None] < width)
    return lon_weights(np.where(inside, np.minimum(apart, width - apart), 2 * LREACH))


def near(apart, spans):
    return jnp.maximum(spans - apart, 0.0).astype(jnp.bfloat16)


def row_apart(bands, held, rows, copies):
    index = np.arange(copies * bands * held * rows)
    latitude = index // (held * rows) % bands * rows + index % rows
    level = index // rows % held
    copy = index // (bands * held * rows)
    same = (copy[:, None] == copy[None]) & (level[:, None] == level[None])
    apart = np.where(same, np.abs(latitude[:, None] - latitude[None]), 1000)
    return apart.astype(np.float32), level[:, None].astype(np.float32)


def halo_apart(levels, rows):
    own = levels * rows
    target, source = np.arange(own)[:, None], np.arange(3 * own)[None]
    shift = (source // own - 1) * rows + source % rows - target % rows
    same = source // rows % levels == target // rows
    return np.where(same, np.abs(shift), 1000).astype(np.float32)


def row_levels(levels, rows):
    index = np.arange(levels * rows)
    level = index[:, None] // rows == np.arange(levels)[None]
    place = index[:, None] % rows == index[None] % rows
    return level.astype(np.float32), place.astype(np.float32)


def partner(at, step, count, sign):
    if count & (count - 1):
        return (at + sign * step) % count
    return at ^ step


def exact_dot(matrix, field):
    return jnp.dot(
        matrix, field, precision=lax.Precision.HIGHEST, preferred_element_type=jnp.float32
    )


def parts_dot(matrix, field):
    count, parts = matrix.shape[0], []
    for _ in range(PARTS):
        part = matrix.astype(jnp.bfloat16).astype(jnp.float32)
        parts.append(part)
        matrix = matrix - part
    stacked = jnp.concatenate(parts, axis=0).astype(jnp.bfloat16)
    products = jnp.dot(stacked, field, preferred_element_type=jnp.float32)
    total = products[:count]
    for index in range(1, PARTS):
        total = total + products[index * count : (index + 1) * count]
    return total


def window(values, band, share, halo, tail):
    lon = values.shape[1]
    start = band * share
    stop = start + share + halo
    parts = [values[:, start : min(lon, stop)]]
    if stop > lon:
        parts.append(values[:, : stop - lon])
    if start < halo:
        parts.append(values[:, lon - halo + start :])
    if start:
        parts.append(values[:, max(start - halo, 0) : start])
    return jnp.concatenate(parts + [tail], axis=1)


def spread(field, ring, taper, factor):
    copies = taper.shape[0]
    smoothed = jnp.dot(field.astype(jnp.bfloat16), ring, preferred_element_type=jnp.float32)
    smoothed = smoothed.astype(jnp.bfloat16)
    parts = []
    for start in range(0, field.shape[0], copies):
        part = smoothed[start : start + copies]
        parts.append(jnp.dot(taper, part, preferred_element_type=jnp.float32))
    return factor * (parts[0] if len(parts) == 1 else jnp.concatenate(parts, axis=0))


def solution(mesh):
    members, bands = mesh.shape["member"], mesh.shape["band"]
    few = bands <= FEW
    paired = members % 2 == 0 and members // 2 <= FEW

    def shards(ensemble, member_weight, member_of_slot, halfwidth, static_root, innovation, precision):
        _, slots, levels, rows, lon = ensemble.shape
        level_share, lon_share = levels // members, lon // bands
        own = level_share * rows
        halo = REACHES * LREACH
        width = lon_share + 2 * halo
        padded = round_up(width + 1, LANES)
        kept = round_up(lon_share + SUMS * PARTS, LANES)
        per_member = bands * own
        copies = members
        while copies > 1 and (copies * per_member > 256 or members % copies):
            copies -= 1
        arrays = slots + 2
        everything = levels * rows
        traded = everything + 2 * slots * own
        vmem = pl.BlockSpec(memory_space=pltpu.VMEM)
        smem = pl.BlockSpec(memory_space=pltpu.SMEM)
        limit = min(48, max(14, 24 * members * bands * slots * own * padded // 2**20)) * 2**20

        def call(body, shapes, scalars, operands, scratch=(), flops=0):
            return pl.pallas_call(
                body,
                out_shape=tuple(jax.ShapeDtypeStruct(shape, kind) for shape, kind in shapes),
                in_specs=[smem] * len(scalars) + [vmem] * len(operands),
                out_specs=(vmem,) * len(shapes),
                scratch_shapes=[pltpu.VMEM(shape, kind) for shape, kind in scratch],
                compiler_params=pltpu.CompilerParams(vmem_limit_bytes=limit),
                cost_estimate=pl.CostEstimate(flops=flops, bytes_accessed=0, transcendentals=0),
                name=body.__name__,
            )(*scalars, *operands)

        f32, bf16 = jnp.float32, jnp.bfloat16

        def fold_smooth(own_weight, ensemble, innovation, precision, kernel, out):
            total = []
            for at in range(levels):
                precise = precision[at].astype(f32)
                part = jnp.zeros((rows, lon), f32)
                for t in range(slots):
                    weighted = precise * innovation[t, at].astype(f32)
                    part = part + ensemble[0, t, at].astype(f32) * weighted
                total.append(part)
            total = own_weight[:, :1] * jnp.concatenate(total, axis=0)
            step = kernel.shape[1]
            margin = (kernel.shape[0] - step) // 2
            steps = -(-lon // step)
            after = steps * step + margin - lon
            ring = jnp.concatenate([total[:, lon - margin :], total, total[:, :after]], axis=1)
            ring = ring.astype(bf16)
            for start in range(0, lon, step):
                stop = min(lon, start + step)
                piece = jnp.dot(
                    ring[:, start : start + kernel.shape[0]], kernel[...], preferred_element_type=f32
                )
                out[:, start:stop] = piece[:, : stop - start].astype(bf16)

        def first_gradient(turn, row_span, below, middle, above, apart, grad):
            span = row_span[:, :1]
            odd = jnp.full((everything, 1), 1, jnp.int32) * lax.rem(turn[:, :1], 2) == 1
            even_pair, odd_pair = below[...].astype(f32), above[...].astype(f32)
            low = jnp.where(odd, even_pair, odd_pair).astype(bf16)
            high = jnp.where(odd, odd_pair, even_pair).astype(bf16)
            stacked = jnp.concatenate([low, middle[...], high], axis=0)
            summed = jnp.dot(near(apart[...], span), stacked, preferred_element_type=f32)
            grad[...] = ensemble_share / (span * span) * summed

        def chosen(turn, blocks, sign):
            if not few:
                return [blocks[0][band] for band in range(bands)]
            turned = []
            for band in range(bands):
                value = blocks[0]
                for shift in range(1, bands):
                    value = jnp.where(turn == partner(band, shift, bands, -sign), blocks[shift], value)
                turned.append(value)
            return turned

        def load_members(weights, stacked):
            shape = (members, per_member, padded)
            values = stacked[...].astype(f32)
            ensemble = [
                values[:, slot * own : (slot + 1) * own].reshape(shape) for slot in range(slots)
            ]
            which = ensemble[0][:, :1, width : width + 1]
            scale = jnp.zeros(which.shape, f32)
            for member in range(members):
                weight = weights[member : member + 1, :1].reshape(1, 1, 1)
                scale = scale + jnp.where(which == member, weight, 0.0)
            scale = jnp.broadcast_to(scale, (members, per_member, 1))
            return ensemble, scale.reshape(members * per_member, 1)

        def fold(ensemble, scale, weighted):
            total = ensemble[0] * weighted[0][None]
            for slot in range(1, slots):
                total = total + ensemble[slot] * weighted[slot][None]
            return scale * total.reshape(members * per_member, padded)

        def images_of(ensemble, grad, ring, taper, factor):
            local = spread(grad, ring, taper, factor).reshape(members, per_member, padded)
            return [jnp.sum(ensemble[t] * local, axis=0) for t in range(slots)]

        def pack(slot, ensemble, out, marks, arrived, packed, mark_sem, in_sems, out_sems):
            def incoming(t):
                return pltpu.make_async_copy(ensemble.at[0, t], arrived.at[t], in_sems.at[t])

            def outgoing(member):
                place = pl.ds(member * bands, bands)
                return pltpu.make_async_copy(packed.at[place], out.at[place], out_sems.at[member])

            mark = pltpu.make_async_copy(slot, marks, mark_sem)
            mark.start()
            for t in range(slots):
                incoming(t).start()
            mark.wait()
            tail = jnp.full((slots * own, padded - width), marks[0], jnp.int32).astype(f32).astype(bf16)
            for t in range(slots):
                incoming(t).wait()
            for member in range(members):
                picked = range(member * level_share, (member + 1) * level_share)
                values = [arrived[t, at].astype(f32) for t in range(slots) for at in picked]
                values = jnp.concatenate(values, axis=0).astype(bf16)
                for band in range(bands):
                    packed[member * bands + band] = window(values, band, lon_share, halo, tail)
                outgoing(member).start()
            for member in range(members):
                outgoing(member).wait()

        def rows_between(root, of_level, same):
            wide = lax.dot_general(
                exact_dot(of_level, static_share * root),
                of_level,
                (((1,), (1,)), ((), ())),
                precision=lax.Precision.HIGHEST,
                preferred_element_type=f32,
            )
            return wide * same

        def observe(place, turn, innovation, precision, root, of_level, same, *refs):
            outs, (own_static, pulled) = refs[:-2], refs[-2:]
            out_of = rows_between(root[...], of_level[...], same[...])
            row = lax.broadcasted_iota(jnp.int32, (own, everything), 0)
            column = lax.broadcasted_iota(jnp.int32, (own, everything), 1)
            picker = (column == place[:, :1] * own + row).astype(f32)
            out_of_own = exact_dot(picker, out_of)
            precise = jnp.concatenate([precision[at].astype(f32) for at in range(levels)], axis=0)
            innovations = [
                jnp.concatenate([innovation[t, at].astype(f32) for at in range(levels)], axis=0)
                for t in range(slots)
            ]
            total = precise * innovations[0]
            for t in range(1, slots):
                total = total + precise * innovations[t]
            high = total.astype(bf16)
            low = (total - high.astype(f32)).astype(bf16)
            into = out_of.T
            back = parts_dot(into, high) + jnp.dot(into.astype(bf16), low, preferred_element_type=f32)
            pulled[...] = back
            values = [
                jnp.dot(picker.astype(bf16), field.astype(bf16), preferred_element_type=f32)
                for field in innovations + [precise]
            ]
            values = jnp.concatenate(values + [exact_dot(out_of_own, back)], axis=0)
            tail = jnp.zeros((values.shape[0], padded - width), f32)
            pieces = [window(values, band, lon_share, halo, tail) for band in range(bands)]
            for band, piece in enumerate(pieces):
                own_static[band] = piece[(slots + 1) * own :, :kept]
            deal(turn[:, :1], pieces, outs)

        def prepare(here, widths, weight, marks, root, of_level, same, apart, level, *refs):
            mixing, pulling, taper, factor, weights, own_weight, row_span, mixed, pulls = refs
            for member in range(members):
                weights[member : member + 1] = jnp.full((1, LANES), weight[member], f32)
            own_weight[...] = jnp.full((1, LANES), weight[marks[0]], f32)
            for at in range(levels):
                row_span[at * rows : (at + 1) * rows] = jnp.full(
                    (rows, LANES), widths[at].astype(f32) + 1.0, f32
                )
            out_of = rows_between(root[...], of_level[...], same[...])
            both = exact_dot(out_of, out_of.T)
            for at in range(levels):
                mixed[at] = both[at * rows : (at + 1) * rows]
                pulls[at] = out_of[at * rows : (at + 1) * rows]
            arriving = [
                member * level_share + share
                for _, _, member in arrivals(here[0])
                for share in range(level_share)
            ]
            pulling[...] = jnp.concatenate([pulls[at] for at in arriving], axis=0).T
            column = lax.broadcasted_iota(jnp.int32, (everything, own), 0)
            own_column = here[0] * own + lax.broadcasted_iota(jnp.int32, (everything, own), 1)
            mixing[...] = exact_dot(
                jnp.concatenate([mixed[at] for at in arriving], axis=0), (column == own_column).astype(f32)
            ).T
            span = jnp.ones(level.shape, f32)
            for share in range(level_share):
                which = here[0] * level_share + share
                span = span + jnp.where(level[...] == share, widths[which].astype(f32), 0.0)
            taper[...] = near(apart[...], span[: apart.shape[0]])
            factor[...] = ensemble_share / (span * span)

        def first_half(weights, turn, stacked, ring, taper, factor, *refs):
            blocks, (total_out, weighted_out, image_out, fields) = refs[:-4], refs[-4:]
            if few:
                blocks = [block[...].astype(f32) for block in blocks]
            values = jnp.stack(chosen(turn[:, :1], blocks, -1)).astype(f32)
            field = []
            for index in range(arrays):
                piece = values[:, index * own : (index + 1) * own].reshape(per_member, padded)
                fields[index] = piece[:, :kept]
                field.append(piece)
            precise, static = field[slots], field[slots + 1]
            ensemble, scale = load_members(weights, stacked)
            weighted = [precise * field[t] for t in range(slots)]
            grad = spread(fold(ensemble, scale, weighted), ring[...], taper[...], factor[...])
            total = jnp.zeros((per_member, padded), f32)
            for t, image in enumerate(images_of(ensemble, grad, ring[...], taper[...], scale * factor[...])):
                image_out[t] = image[:, :kept]
                image = precise * (image + static)
                weighted_out[t] = image
                total = total + image
            total_out[...] = total[:, :kept].astype(bf16)

        def inner(first, second):
            inside = lax.broadcasted_iota(jnp.int32, first.shape, 1) < lon_share
            product = jnp.where(inside, first * second, 0.0)
            return jnp.sum(jnp.sum(product, axis=0, keepdims=True), axis=1, keepdims=True)

        def closest(first, second):
            norm = inner(first, first)
            ratio = inner(first, second) / jnp.where(norm > 0.0, norm, 1.0)
            return ratio.astype(bf16).astype(f32)

        def deal(turn, pieces, outs):
            if not few:
                for band, piece in enumerate(pieces):
                    outs[0][band] = piece.astype(bf16)
                return
            for shift in range(bands):
                value = pieces[0]
                for band in range(1, bands):
                    value = jnp.where(turn == partner(band, shift, bands, -1), pieces[band], value)
                outs[shift][...] = value.astype(bf16)

        def second_half(weights, stacked, ring, taper, factor, weighted, grad_out, image_out):
            ensemble, scale = load_members(weights, stacked)
            grad = fold(ensemble, scale, [weighted[t] for t in range(slots)])
            grad = spread(grad, ring[...], taper[...], factor[...])
            for t, image in enumerate(images_of(ensemble, grad, ring[...], taper[...], scale * factor[...])):
                image_out[t] = image[:, :kept]
            grad_out[...] = grad[:, :kept].reshape(members * bands, own, kept).astype(bf16)

        def combine(grad, first, second, fields, mixing, *refs):
            blocks, (out, image_out) = refs[:-2], refs[-2:]
            lane = lax.broadcasted_iota(jnp.int32, (1, kept), 1) - lon_share
            every = [
                jnp.concatenate(
                    [
                        blocks[block][shift, band * own : (band + 1) * own].astype(f32)
                        for block, shift, _ in arrivals(0)
                    ],
                    axis=0,
                )
                for band in range(bands)
            ]
            mixed = parts_dot(mixing[...], jnp.concatenate(every, axis=1).astype(bf16))
            mixed = jnp.concatenate(
                [mixed[:, band * kept : (band + 1) * kept] for band in range(bands)], axis=0
            )
            precise, static = fields[slots], fields[slots + 1]
            sums = [jnp.zeros((per_member, kept), f32) for _ in range(SUMS)]
            for t in range(slots):
                image = second[t] + mixed
                image_out[t] = image
                whole = first[t] + static
                weighted = precise * whole
                sums[0] = sums[0] + precise * fields[t] * whole
                sums[1] = sums[1] + weighted * whole
                sums[2] = sums[2] + weighted * image
                sums[3] = sums[3] + precise * image * image
            row = jnp.zeros((1, kept), f32)
            for index, part in enumerate(sums):
                part = jnp.sum(jnp.where(lane < 0, part, 0.0), axis=0, keepdims=True)
                part = jnp.sum(part, axis=1, keepdims=True)
                for piece in range(PARTS):
                    high = part.astype(bf16).astype(f32)
                    row = row + jnp.where(lane == PARTS * index + piece, high, 0.0)
                    part = part - high
            row = jnp.broadcast_to(row, (own, kept))
            lane = lax.broadcasted_iota(jnp.int32, (own, kept), 1)
            for block in range(members * bands):
                out[block] = jnp.where(lane < lon_share, grad[block].astype(f32), row).astype(bf16)

        def hand_out(turn, first, second, *refs):
            blocks, outs = refs[: len(totals)], refs[len(totals) :]
            lane = lax.broadcasted_iota(jnp.int32, (1, kept), 1)
            ratio = closest(
                jnp.concatenate([first[t] for t in range(slots)], axis=0),
                jnp.concatenate([second[t] for t in range(slots)], axis=0),
            )
            rest = [
                jnp.where(lane < lon_share, second[t] - ratio * first[t], ratio) for t in range(slots)
            ]
            images = [first[t] for t in range(slots)] + rest
            pieces = []
            for band in range(bands):
                place = slice(band * own, (band + 1) * own)
                parts = [blocks[block][shift, place].astype(f32) for block, shift, _ in arrivals(0)]
                pieces.append(jnp.concatenate(parts + [image[place] for image in images], axis=0))
            deal(turn[:, :1], pieces, outs)

        def join(turn, own_static, pulling, *refs):
            blocks, (pulled, images) = refs[:-2], refs[-2:]
            if few:
                blocks = [block[...].astype(f32) for block in blocks]
            pieces = chosen(turn[:, :1], blocks, -1)
            size = slots * own
            for band in range(bands):
                place = slice(band * lon_share, (band + 1) * lon_share)
                piece = pieces[band].astype(f32)
                every = piece[:everything].astype(bf16)
                pulled[:, place] = parts_dot(pulling[...], every)[:, :lon_share]
                parts = piece[everything:]
                first = parts[:size]
                second = parts[size:] + parts[size : size + 1, lon_share : lon_share + 1] * first
                static = own_static[band]
                for t in range(slots):
                    at = slice(t * own, (t + 1) * own)
                    images[at, place] = (first[at] + static)[:, :lon_share]
                images[size:, place] = second[:, :lon_share]

        def finish(back, grad_first, pulled_first, pulled_second, images, *refs):
            (member_out, static_out, image_out), (member, static, image, sems) = refs[:3], refs[3:]

            def outgoing(index, source, target):
                return pltpu.make_async_copy(source, target, sems.at[index])

            def outgoing_member(index):
                place = pl.ds(index * level_share, level_share)
                return outgoing(index, member.at[place], member_out.at[0, place])

            static_copy = outgoing(members, static, static_out)
            image_copy = outgoing(members + 1, image, image_out)
            total = back[0, :1].astype(f32)
            for block in range(1, members * bands):
                total = total + back[block, :1].astype(f32)
            lane = lax.broadcasted_iota(jnp.int32, total.shape, 1) - lon_share
            first_norm, first_image, cross, second_image = [
                jnp.sum(
                    jnp.where((lane >= PARTS * index) & (lane < PARTS * (index + 1)), total, 0.0),
                    axis=1,
                    keepdims=True,
                )
                for index in range(SUMS)
            ]
            alpha = first_norm / (first_norm + first_image)
            ratio = first_image / first_norm
            next_norm = alpha * alpha * jnp.maximum(cross - ratio * first_image, 0.0)
            beta = next_norm / first_norm
            apart = second_image - 2.0 * ratio * cross + ratio * ratio * first_image
            curvature = next_norm + alpha * alpha * apart - beta * next_norm / alpha
            alpha_next = jnp.clip(next_norm / curvature, 0.0, 1.0)
            on_first = alpha + alpha_next * (1.0 - alpha + beta)
            on_second = -alpha * alpha_next
            values = on_first * pulled_first[...] + on_second * pulled_second[...]
            for level in range(levels):
                static[level] = values[level * rows : (level + 1) * rows]
            static_copy.start()
            half = slots * own
            values = on_first * images[:half] + on_second * images[half:]
            for t in range(slots):
                for level in range(level_share):
                    start = (t * level_share + level) * rows
                    image[t, level] = values[start : start + rows]
            image_copy.start()
            for source in range(members):
                parts = [
                    back[source * bands + band].astype(f32)[:, :lon_share] for band in range(bands)
                ]
                values = on_second * jnp.concatenate(parts, axis=1)
                values = values + on_first * grad_first[source * own : (source + 1) * own]
                for share in range(level_share):
                    member[source * level_share + share] = values[share * rows : (share + 1) * rows]
                outgoing_member(source).start()
            static_copy.wait()
            image_copy.wait()
            for source in range(members):
                outgoing_member(source).wait()

        def trade(blocks):
            if not few:
                return [lax.all_to_all(blocks[0], "band", 0, 0, tiled=True)]
            return [blocks[0]] + [
                lax.ppermute(
                    blocks[shift], "band", [(at, partner(at, shift, bands, 1)) for at in range(bands)]
                )
                for shift in range(1, bands)
            ]

        def around(block, beside):
            if not paired:
                return [lax.all_gather(block, "member")], beside
            here = [block] + [
                lax.ppermute(
                    block,
                    "member",
                    [(at, 2 * partner(at // 2, shift, members // 2, 1) + at % 2) for at in range(members)],
                )
                for shift in range(1, members // 2)
            ]
            here, beside = lax.optimization_barrier((jnp.stack(here), beside))
            return [here, lax.ppermute(here, "member", [(at, at ^ 1) for at in range(members)])], beside

        def arrivals(here):
            if not paired:
                return [(0, member, member) for member in range(members)]
            chip, core = lax.div(here, 2), lax.rem(here, 2)
            ring = (members // 2) & (members // 2 - 1)
            return [
                (
                    block,
                    shift,
                    2 * (lax.rem(chip + members // 2 - shift, members // 2) if ring else chip ^ shift) + side,
                )
                for block, side in enumerate((core, 1 - core))
                for shift in range(members // 2)
            ]

        def tradable(shape, kind):
            return [(shape, kind)] * bands if few else [((bands,) + shape, kind)]

        place = jnp.full((1, LANES), lax.axis_index("member"), jnp.int32)
        turn = jnp.full((1, LANES), lax.axis_index("band"), jnp.int32)
        here = lax.axis_index("member").astype(jnp.int32).reshape(1)

        block = (members * bands, slots * own, padded)
        pieces = pl.pallas_call(
            pack,
            out_shape=jax.ShapeDtypeStruct(block, bf16),
            in_specs=[pl.BlockSpec(memory_space=pltpu.HBM)] * 2,
            out_specs=pl.BlockSpec(memory_space=pltpu.HBM),
            scratch_shapes=[
                pltpu.SMEM((1,), jnp.int32),
                pltpu.VMEM((slots, levels, rows, lon), bf16),
                pltpu.VMEM(block, bf16),
                pltpu.SemaphoreType.DMA,
                pltpu.SemaphoreType.DMA((slots,)),
                pltpu.SemaphoreType.DMA((members,)),
            ],
            compiler_params=pltpu.CompilerParams(vmem_limit_bytes=60 * 2**20),
            name="pack",
        )(member_of_slot, ensemble)
        pieces, ensemble, innovation, precision, static_root = lax.optimization_barrier(
            (pieces, ensemble, innovation, precision, static_root)
        )
        stacked = lax.all_to_all(pieces, BOTH, 0, 0, tiled=True)

        of_level, same = row_levels(levels, rows)
        apart, level = row_apart(bands, level_share, rows, copies)
        every_level = np.tile(level, (members // copies, 1))
        block = (arrays * own, padded)
        between = [static_root] + [jnp.asarray(table) for table in (of_level, same)]
        results = call(
            observe,
            tradable(block, bf16) + [((bands, own, kept), f32), ((everything, lon), f32)],
            [],
            [place, turn, innovation, precision, *between],
        )
        blocks, (own_static, pulled) = trade(results[:-2]), results[-2:]
        own_static, between = lax.optimization_barrier((own_static, between))
        mixing, pulling, taper, factor, weights, own_weight, row_span = call(
            prepare,
            [
                ((own, everything), f32),
                ((everything, everything), f32),
                (apart.shape, bf16),
                (every_level.shape, f32),
                ((members, LANES), f32),
                ((1, LANES), f32),
                ((everything, LANES), f32),
            ],
            [here, halfwidth, member_weight, member_of_slot],
            [*between, jnp.asarray(apart), jnp.asarray(every_level)],
            scratch=[((levels, rows, everything), f32)] * 2,
        )
        awaited = bands // 2 if few else 0
        blocks[awaited], ensemble, innovation, precision = lax.optimization_barrier(
            (blocks[awaited], ensemble, innovation, precision)
        )
        (smoothed,) = call(
            fold_smooth,
            [((everything, lon), bf16)],
            [],
            [own_weight, ensemble, innovation, precision, lon_kernel(LANES, 2 * LANES)],
        )
        pairs = [(at, at + 1) for at in range(bands - 1)]
        below, above = [
            lax.ppermute(smoothed, "band", pairs[start::2] + [(to, at) for at, to in pairs[start::2]])
            for start in range(2)
        ]
        ring = ring_kernel(width, padded)

        total, weighted, image_first, fields = call(
            first_half,
            [
                ((per_member, kept), bf16),
                ((slots, per_member, padded), f32),
                ((slots, per_member, kept), f32),
                ((arrays, per_member, kept), f32),
            ],
            [],
            [weights, turn, stacked, ring, taper, factor, *blocks],
        )
        grad, image_second = call(
            second_half,
            [((members * bands, own, kept), bf16), ((slots, per_member, kept), f32)],
            [],
            [weights, stacked, ring, taper, factor, weighted],
            flops=10**9,
        )
        totals, (image_second, below, above) = around(total, (image_second, below, above))

        grad, image_second = call(
            combine,
            [((members * bands, own, kept), bf16), ((slots, per_member, kept), f32)],
            [],
            [grad, image_first, image_second, fields, mixing, *totals],
        )
        back = lax.all_to_all(grad, BOTH, 0, 0, tiled=True)
        blocks = call(
            hand_out,
            tradable((traded, kept), bf16),
            [],
            [turn, image_first, image_second, *totals],
        )
        blocks = trade(blocks)
        pulled_second, images = call(
            join,
            [((everything, lon), f32), ((2 * slots * own, lon), f32)],
            [],
            [turn, own_static, pulling, *blocks],
        )
        (grad_first,) = call(
            first_gradient,
            [((everything, lon), f32)],
            [],
            [turn, row_span, below, smoothed, above, jnp.asarray(halo_apart(levels, rows))],
        )
        return pl.pallas_call(
            finish,
            out_shape=(
                jax.ShapeDtypeStruct((1, levels, rows, lon), f32),
                jax.ShapeDtypeStruct((levels, rows, lon), f32),
                jax.ShapeDtypeStruct((slots, level_share, rows, lon), f32),
            ),
            in_specs=[vmem] * 5,
            out_specs=(pl.BlockSpec(memory_space=pltpu.HBM),) * 3,
            scratch_shapes=[
                pltpu.VMEM((levels, rows, lon), f32),
                pltpu.VMEM((levels, rows, lon), f32),
                pltpu.VMEM((slots, level_share, rows, lon), f32),
                pltpu.SemaphoreType.DMA((members + 2,)),
            ],
            compiler_params=pltpu.CompilerParams(vmem_limit_bytes=limit),
            name="finish",
        )(back, grad_first, pulled, pulled_second, images)

    return jax.shard_map(
        shards,
        mesh=mesh,
        in_specs=(
            P("member", None, None, "band", None),
            P(),
            P("member"),
            P(),
            P(),
            P(None, None, "band", None),
            P(None, "band", None),
        ),
        out_specs=(
            P("member", None, "band", None),
            P(None, "band", None),
            P(None, "member", "band", None),
        ),
        check_vma=False,
    )
```

```python
import math

import jax
import jax.numpy as jnp
import numpy as np
from jax import lax
from jax.experimental import pallas as pl
from jax.experimental.pallas import tpu as pltpu
from jax.sharding import PartitionSpec as P

HMAX = 4
LREACH = 18
REACHES = 4
LANES = 128
FEW = 8
SUMS = 4
PARTS = 3
HALVES = 2
BOTH = ("member", "band")

ensemble_share = 0.8
static_share = 0.6
length_scale = 6.0


def round_up(value, step):
    return -(-value // step) * step


def lon_weights(distance):
    distance = distance.astype(np.float32)
    values = np.exp(np.float32(-0.5) * (distance / np.float32(length_scale)) ** 2)
    values = values / np.float32(length_scale * math.sqrt(2.0 * math.pi))
    return jnp.asarray(np.where(distance <= LREACH, values, 0.0), jnp.bfloat16)


def lon_kernel(reach, width):
    return lon_weights(np.abs(np.arange(width + 2 * reach)[:, None] - reach - np.arange(width)[None]))


def ring_kernel(width, padded):
    apart = np.abs(np.arange(padded)[:, None] - np.arange(padded)[None])
    inside = (np.arange(padded)[:, None] < width) & (np.arange(padded)[None] < width)
    return lon_weights(np.where(inside, np.minimum(apart, width - apart), 2 * LREACH))


def near(apart, spans):
    return jnp.maximum(spans - apart, 0.0).astype(jnp.bfloat16)


def row_apart(bands, held, rows, copies):
    index = np.arange(copies * bands * held * rows)
    latitude = index // (held * rows) % bands * rows + index % rows
    level = index // rows % held
    copy = index // (bands * held * rows)
    same = (copy[:, None] == copy[None]) & (level[:, None] == level[None])
    apart = np.where(same, np.abs(latitude[:, None] - latitude[None]), 1000)
    return apart.astype(np.float32), level[:, None].astype(np.float32)


def halo_apart(levels, rows):
    own = levels * rows
    target, source = np.arange(own)[:, None], np.arange(3 * own)[None]
    shift = (source // own - 1) * rows + source % rows - target % rows
    same = source // rows % levels == target // rows
    return np.where(same, np.abs(shift), 1000).astype(np.float32)


def row_levels(levels, rows):
    index = np.arange(levels * rows)
    level = index[:, None] // rows == np.arange(levels)[None]
    place = index[:, None] % rows == index[None] % rows
    return level.astype(np.float32), place.astype(np.float32)


def partner(at, step, count, sign):
    if count & (count - 1):
        return (at + sign * step) % count
    return at ^ step


def exact_dot(matrix, field):
    return jnp.dot(
        matrix, field, precision=lax.Precision.HIGHEST, preferred_element_type=jnp.float32
    )


def parts_dot(matrix, field):
    count, parts = matrix.shape[0], []
    for _ in range(HALVES):
        part = matrix.astype(jnp.bfloat16).astype(jnp.float32)
        parts.append(part)
        matrix = matrix - part
    stacked = jnp.concatenate(parts, axis=0).astype(jnp.bfloat16)
    products = jnp.dot(stacked, field, preferred_element_type=jnp.float32)
    total = products[:count]
    for index in range(1, HALVES):
        total = total + products[index * count : (index + 1) * count]
    return total


def window(values, band, share, halo, tail):
    lon = values.shape[1]
    start = band * share
    stop = start + share + halo
    parts = [values[:, start : min(lon, stop)]]
    if stop > lon:
        parts.append(values[:, : stop - lon])
    if start < halo:
        parts.append(values[:, lon - halo + start :])
    if start:
        parts.append(values[:, max(start - halo, 0) : start])
    return jnp.concatenate(parts + [tail], axis=1)


def spread(field, ring, taper, factor):
    copies = taper.shape[0]
    smoothed = jnp.dot(field.astype(jnp.bfloat16), ring, preferred_element_type=jnp.float32)
    smoothed = smoothed.astype(jnp.bfloat16)
    parts = []
    for start in range(0, field.shape[0], copies):
        part = smoothed[start : start + copies]
        parts.append(jnp.dot(taper, part, preferred_element_type=jnp.float32))
    return factor * (parts[0] if len(parts) == 1 else jnp.concatenate(parts, axis=0))


def solution(mesh):
    members, bands = mesh.shape["member"], mesh.shape["band"]
    few = bands <= FEW
    paired = members % 2 == 0 and members // 2 <= FEW

    def shards(ensemble, member_weight, member_of_slot, halfwidth, static_root, innovation, precision):
        _, slots, levels, rows, lon = ensemble.shape
        level_share, lon_share = levels // members, lon // bands
        own = level_share * rows
        halo = REACHES * LREACH
        width = lon_share + 2 * halo
        padded = round_up(width + 1, LANES)
        kept = round_up(lon_share + SUMS * PARTS, LANES)
        per_member = bands * own
        copies = members
        while copies > 1 and (copies * per_member > 256 or members % copies):
            copies -= 1
        arrays = slots + 2
        everything = levels * rows
        traded = everything + 2 * slots * own
        vmem = pl.BlockSpec(memory_space=pltpu.VMEM)
        smem = pl.BlockSpec(memory_space=pltpu.SMEM)
        limit = min(48, max(14, 24 * members * bands * slots * own * padded // 2**20)) * 2**20

        def call(body, shapes, scalars, operands, scratch=(), flops=0):
            return pl.pallas_call(
                body,
                out_shape=tuple(jax.ShapeDtypeStruct(shape, kind) for shape, kind in shapes),
                in_specs=[smem] * len(scalars) + [vmem] * len(operands),
                out_specs=(vmem,) * len(shapes),
                scratch_shapes=[pltpu.VMEM(shape, kind) for shape, kind in scratch],
                compiler_params=pltpu.CompilerParams(vmem_limit_bytes=limit),
                cost_estimate=pl.CostEstimate(flops=flops, bytes_accessed=0, transcendentals=0),
                name=body.__name__,
            )(*scalars, *operands)

        f32, bf16 = jnp.float32, jnp.bfloat16

        def fold_smooth(own_weight, ensemble, innovation, precision, kernel, out):
            total = []
            for at in range(levels):
                precise = precision[at].astype(f32)
                part = jnp.zeros((rows, lon), f32)
                for t in range(slots):
                    weighted = precise * innovation[t, at].astype(f32)
                    part = part + ensemble[0, t, at].astype(f32) * weighted
                total.append(part)
            total = own_weight[:, :1] * jnp.concatenate(total, axis=0)
            step = kernel.shape[1]
            margin = (kernel.shape[0] - step) // 2
            steps = -(-lon // step)
            after = steps * step + margin - lon
            ring = jnp.concatenate([total[:, lon - margin :], total, total[:, :after]], axis=1)
            ring = ring.astype(bf16)
            for start in range(0, lon, step):
                stop = min(lon, start + step)
                piece = jnp.dot(
                    ring[:, start : start + kernel.shape[0]], kernel[...], preferred_element_type=f32
                )
                out[:, start:stop] = piece[:, : stop - start].astype(bf16)

        def first_gradient(turn, row_span, below, middle, above, apart, grad):
            span = row_span[:, :1]
            odd = jnp.full((everything, 1), 1, jnp.int32) * lax.rem(turn[:, :1], 2) == 1
            even_pair, odd_pair = below[...].astype(f32), above[...].astype(f32)
            low = jnp.where(odd, even_pair, odd_pair).astype(bf16)
            high = jnp.where(odd, odd_pair, even_pair).astype(bf16)
            stacked = jnp.concatenate([low, middle[...], high], axis=0)
            summed = jnp.dot(near(apart[...], span), stacked, preferred_element_type=f32)
            grad[...] = ensemble_share / (span * span) * summed

        def chosen(turn, blocks, sign):
            if not few:
                return [blocks[0][band] for band in range(bands)]
            turned = []
            for band in range(bands):
                value = blocks[0]
                for shift in range(1, bands):
                    value = jnp.where(turn == partner(band, shift, bands, -sign), blocks[shift], value)
                turned.append(value)
            return turned

        def load_members(weights, stacked):
            shape = (members, per_member, padded)
            values = stacked[...].astype(f32)
            ensemble = [
                values[:, slot * own : (slot + 1) * own].reshape(shape) for slot in range(slots)
            ]
            which = ensemble[0][:, :1, width : width + 1]
            scale = jnp.zeros(which.shape, f32)
            for member in range(members):
                weight = weights[member : member + 1, :1].reshape(1, 1, 1)
                scale = scale + jnp.where(which == member, weight, 0.0)
            scale = jnp.broadcast_to(scale, (members, per_member, 1))
            return ensemble, scale.reshape(members * per_member, 1)

        def fold(ensemble, scale, weighted):
            total = ensemble[0] * weighted[0][None]
            for slot in range(1, slots):
                total = total + ensemble[slot] * weighted[slot][None]
            return scale * total.reshape(members * per_member, padded)

        def images_of(ensemble, grad, ring, taper, factor):
            local = spread(grad, ring, taper, factor).reshape(members, per_member, padded)
            return [jnp.sum(ensemble[t] * local, axis=0) for t in range(slots)]

        def pack(slot, ensemble, out, marks, arrived, packed, mark_sem, in_sems, out_sems):
            def incoming(t):
                return pltpu.make_async_copy(ensemble.at[0, t], arrived.at[t], in_sems.at[t])

            def outgoing(member):
                place = pl.ds(member * bands, bands)
                return pltpu.make_async_copy(packed.at[place], out.at[place], out_sems.at[member])

            mark = pltpu.make_async_copy(slot, marks, mark_sem)
            mark.start()
            for t in range(slots):
                incoming(t).start()
            mark.wait()
            tail = jnp.full((slots * own, padded - width), marks[0], jnp.int32).astype(f32).astype(bf16)
            for t in range(slots):
                incoming(t).wait()
            for member in range(members):
                picked = range(member * level_share, (member + 1) * level_share)
                values = [arrived[t, at].astype(f32) for t in range(slots) for at in picked]
                values = jnp.concatenate(values, axis=0).astype(bf16)
                for band in range(bands):
                    packed[member * bands + band] = window(values, band, lon_share, halo, tail)
                outgoing(member).start()
            for member in range(members):
                outgoing(member).wait()

        def rows_between(root, of_level, same):
            wide = lax.dot_general(
                exact_dot(of_level, static_share * root),
                of_level,
                (((1,), (1,)), ((), ())),
                precision=lax.Precision.HIGHEST,
                preferred_element_type=f32,
            )
            return wide * same

        def observe(place, turn, innovation, precision, root, of_level, same, *refs):
            outs, (own_static, pulled) = refs[:-2], refs[-2:]
            out_of = rows_between(root[...], of_level[...], same[...])
            row = lax.broadcasted_iota(jnp.int32, (own, everything), 0)
            column = lax.broadcasted_iota(jnp.int32, (own, everything), 1)
            picker = (column == place[:, :1] * own + row).astype(f32)
            out_of_own = exact_dot(picker, out_of)
            precise = jnp.concatenate([precision[at].astype(f32) for at in range(levels)], axis=0)
            innovations = [
                jnp.concatenate([innovation[t, at].astype(f32) for at in range(levels)], axis=0)
                for t in range(slots)
            ]
            total = precise * innovations[0]
            for t in range(1, slots):
                total = total + precise * innovations[t]
            high = total.astype(bf16)
            low = (total - high.astype(f32)).astype(bf16)
            into = out_of.T
            back = parts_dot(into, high) + jnp.dot(into.astype(bf16), low, preferred_element_type=f32)
            pulled[...] = back
            values = [
                jnp.dot(picker.astype(bf16), field.astype(bf16), preferred_element_type=f32)
                for field in innovations + [precise]
            ]
            values = jnp.concatenate(values + [exact_dot(out_of_own, back)], axis=0)
            tail = jnp.zeros((values.shape[0], padded - width), f32)
            pieces = [window(values, band, lon_share, halo, tail) for band in range(bands)]
            for band, piece in enumerate(pieces):
                own_static[band] = piece[(slots + 1) * own :, :kept]
            deal(turn[:, :1], pieces, outs)

        def prepare(here, widths, weight, marks, root, of_level, same, apart, level, *refs):
            mixing, pulling, taper, factor, weights, own_weight, row_span, mixed, pulls = refs
            for member in range(members):
                weights[member : member + 1] = jnp.full((1, LANES), weight[member], f32)
            own_weight[...] = jnp.full((1, LANES), weight[marks[0]], f32)
            for at in range(levels):
                row_span[at * rows : (at + 1) * rows] = jnp.full(
                    (rows, LANES), widths[at].astype(f32) + 1.0, f32
                )
            out_of = rows_between(root[...], of_level[...], same[...])
            both = exact_dot(out_of, out_of.T)
            for at in range(levels):
                mixed[at] = both[at * rows : (at + 1) * rows]
                pulls[at] = out_of[at * rows : (at + 1) * rows]
            arriving = [
                member * level_share + share
                for _, _, member in arrivals(here[0])
                for share in range(level_share)
            ]
            pulling[...] = jnp.concatenate([pulls[at] for at in arriving], axis=0).T
            column = lax.broadcasted_iota(jnp.int32, (everything, own), 0)
            own_column = here[0] * own + lax.broadcasted_iota(jnp.int32, (everything, own), 1)
            mixing[...] = exact_dot(
                jnp.concatenate([mixed[at] for at in arriving], axis=0), (column == own_column).astype(f32)
            ).T
            span = jnp.ones(level.shape, f32)
            for share in range(level_share):
                which = here[0] * level_share + share
                span = span + jnp.where(level[...] == share, widths[which].astype(f32), 0.0)
            taper[...] = near(apart[...], span[: apart.shape[0]])
            factor[...] = ensemble_share / (span * span)

        def first_half(weights, turn, stacked, ring, taper, factor, *refs):
            blocks, (total_out, weighted_out, image_out, fields) = refs[:-4], refs[-4:]
            if few:
                blocks = [block[...].astype(f32) for block in blocks]
            values = jnp.stack(chosen(turn[:, :1], blocks, -1)).astype(f32)
            field = []
            for index in range(arrays):
                piece = values[:, index * own : (index + 1) * own].reshape(per_member, padded)
                fields[index] = piece[:, :kept]
                field.append(piece)
            precise, static = field[slots], field[slots + 1]
            ensemble, scale = load_members(weights, stacked)
            weighted = [precise * field[t] for t in range(slots)]
            grad = spread(fold(ensemble, scale, weighted), ring[...], taper[...], factor[...])
            total = jnp.zeros((per_member, padded), f32)
            for t, image in enumerate(images_of(ensemble, grad, ring[...], taper[...], scale * factor[...])):
                image_out[t] = image[:, :kept]
                image = precise * (image + static)
                weighted_out[t] = image
                total = total + image
            total_out[...] = total[:, :kept].astype(bf16)

        def inner(first, second):
            inside = lax.broadcasted_iota(jnp.int32, first.shape, 1) < lon_share
            product = jnp.where(inside, first * second, 0.0)
            return jnp.sum(jnp.sum(product, axis=0, keepdims=True), axis=1, keepdims=True)

        def closest(first, second):
            norm = inner(first, first)
            ratio = inner(first, second) / jnp.where(norm > 0.0, norm, 1.0)
            return ratio.astype(bf16).astype(f32)

        def deal(turn, pieces, outs):
            if not few:
                for band, piece in enumerate(pieces):
                    outs[0][band] = piece.astype(bf16)
                return
            for shift in range(bands):
                value = pieces[0]
                for band in range(1, bands):
                    value = jnp.where(turn == partner(band, shift, bands, -1), pieces[band], value)
                outs[shift][...] = value.astype(bf16)

        def second_half(weights, stacked, ring, taper, factor, weighted, grad_out, image_out):
            ensemble, scale = load_members(weights, stacked)
            grad = fold(ensemble, scale, [weighted[t] for t in range(slots)])
            grad = spread(grad, ring[...], taper[...], factor[...])
            for t, image in enumerate(images_of(ensemble, grad, ring[...], taper[...], scale * factor[...])):
                image_out[t] = image[:, :kept]
            grad_out[...] = grad[:, :kept].reshape(members * bands, own, kept).astype(bf16)

        def combine(grad, first, second, fields, mixing, *refs):
            blocks, (out, image_out) = refs[:-2], refs[-2:]
            lane = lax.broadcasted_iota(jnp.int32, (1, kept), 1) - lon_share
            every = [
                jnp.concatenate(
                    [
                        blocks[block][shift, band * own : (band + 1) * own].astype(f32)
                        for block, shift, _ in arrivals(0)
                    ],
                    axis=0,
                )
                for band in range(bands)
            ]
            mixed = parts_dot(mixing[...], jnp.concatenate(every, axis=1).astype(bf16))
            mixed = jnp.concatenate(
                [mixed[:, band * kept : (band + 1) * kept] for band in range(bands)], axis=0
            )
            precise, static = fields[slots], fields[slots + 1]
            sums = [jnp.zeros((per_member, kept), f32) for _ in range(SUMS)]
            for t in range(slots):
                image = second[t] + mixed
                image_out[t] = image
                whole = first[t] + static
                weighted = precise * whole
                sums[0] = sums[0] + precise * fields[t] * whole
                sums[1] = sums[1] + weighted * whole
                sums[2] = sums[2] + weighted * image
                sums[3] = sums[3] + precise * image * image
            row = jnp.zeros((1, kept), f32)
            for index, part in enumerate(sums):
                part = jnp.sum(jnp.where(lane < 0, part, 0.0), axis=0, keepdims=True)
                part = jnp.sum(part, axis=1, keepdims=True)
                for piece in range(PARTS):
                    high = part.astype(bf16).astype(f32)
                    row = row + jnp.where(lane == PARTS * index + piece, high, 0.0)
                    part = part - high
            row = jnp.broadcast_to(row, (own, kept))
            lane = lax.broadcasted_iota(jnp.int32, (own, kept), 1)
            for block in range(members * bands):
                out[block] = jnp.where(lane < lon_share, grad[block].astype(f32), row).astype(bf16)

        def hand_out(turn, first, second, *refs):
            blocks, outs = refs[: len(totals)], refs[len(totals) :]
            lane = lax.broadcasted_iota(jnp.int32, (1, kept), 1)
            ratio = closest(
                jnp.concatenate([first[t] for t in range(slots)], axis=0),
                jnp.concatenate([second[t] for t in range(slots)], axis=0),
            )
            rest = [
                jnp.where(lane < lon_share, second[t] - ratio * first[t], ratio) for t in range(slots)
            ]
            images = [first[t] for t in range(slots)] + rest
            pieces = []
            for band in range(bands):
                place = slice(band * own, (band + 1) * own)
                parts = [blocks[block][shift, place].astype(f32) for block, shift, _ in arrivals(0)]
                pieces.append(jnp.concatenate(parts + [image[place] for image in images], axis=0))
            deal(turn[:, :1], pieces, outs)

        def join(turn, own_static, pulling, *refs):
            blocks, (pulled, images) = refs[:-2], refs[-2:]
            if few:
                blocks = [block[...].astype(f32) for block in blocks]
            pieces = chosen(turn[:, :1], blocks, -1)
            size = slots * own
            for band in range(bands):
                place = slice(band * lon_share, (band + 1) * lon_share)
                piece = pieces[band].astype(f32)
                every = piece[:everything].astype(bf16)
                pulled[:, place] = parts_dot(pulling[...], every)[:, :lon_share]
                parts = piece[everything:]
                first = parts[:size]
                second = parts[size:] + parts[size : size + 1, lon_share : lon_share + 1] * first
                static = own_static[band]
                for t in range(slots):
                    at = slice(t * own, (t + 1) * own)
                    images[at, place] = (first[at] + static)[:, :lon_share]
                images[size:, place] = second[:, :lon_share]

        def finish(back, grad_first, pulled_first, pulled_second, images, *refs):
            (member_out, static_out, image_out), (member, static, image, sems) = refs[:3], refs[3:]

            def outgoing(index, source, target):
                return pltpu.make_async_copy(source, target, sems.at[index])

            def outgoing_member(index):
                place = pl.ds(index * level_share, level_share)
                return outgoing(index, member.at[place], member_out.at[0, place])

            static_copy = outgoing(members, static, static_out)
            image_copy = outgoing(members + 1, image, image_out)
            tile = lon_share // LANES * LANES
            total = back[0, :1, tile:].astype(f32)
            for block in range(1, members * bands):
                total = total + back[block, :1, tile:].astype(f32)
            lane = lax.broadcasted_iota(jnp.int32, total.shape, 1) + tile - lon_share
            first_norm, first_image, cross, second_image = [
                jnp.sum(
                    jnp.where((lane >= PARTS * index) & (lane < PARTS * (index + 1)), total, 0.0),
                    axis=1,
                    keepdims=True,
                )
                for index in range(SUMS)
            ]
            alpha = first_norm / (first_norm + first_image)
            ratio = first_image / first_norm
            next_norm = alpha * alpha * jnp.maximum(cross - ratio * first_image, 0.0)
            beta = next_norm / first_norm
            apart = second_image - 2.0 * ratio * cross + ratio * ratio * first_image
            curvature = next_norm + alpha * alpha * apart - beta * next_norm / alpha
            alpha_next = jnp.clip(next_norm / curvature, 0.0, 1.0)
            on_first = alpha + alpha_next * (1.0 - alpha + beta)
            on_second = -alpha * alpha_next
            values = on_first * pulled_first[...] + on_second * pulled_second[...]
            for level in range(levels):
                static[level] = values[level * rows : (level + 1) * rows]
            static_copy.start()
            half = slots * own
            values = on_first * images[:half] + on_second * images[half:]
            for t in range(slots):
                for level in range(level_share):
                    start = (t * level_share + level) * rows
                    image[t, level] = values[start : start + rows]
            image_copy.start()
            for source in range(members):
                parts = [
                    back[source * bands + band].astype(f32)[:, :lon_share] for band in range(bands)
                ]
                values = on_second * jnp.concatenate(parts, axis=1)
                values = values + on_first * grad_first[source * own : (source + 1) * own]
                for share in range(level_share):
                    member[source * level_share + share] = values[share * rows : (share + 1) * rows]
                outgoing_member(source).start()
            static_copy.wait()
            image_copy.wait()
            for source in range(members):
                outgoing_member(source).wait()

        def trade(blocks):
            if not few:
                return [lax.all_to_all(blocks[0], "band", 0, 0, tiled=True)]
            return [blocks[0]] + [
                lax.ppermute(
                    blocks[shift], "band", [(at, partner(at, shift, bands, 1)) for at in range(bands)]
                )
                for shift in range(1, bands)
            ]

        def around(block, beside):
            if not paired:
                return [lax.all_gather(block, "member")], beside
            here = [block] + [
                lax.ppermute(
                    block,
                    "member",
                    [(at, 2 * partner(at // 2, shift, members // 2, 1) + at % 2) for at in range(members)],
                )
                for shift in range(1, members // 2)
            ]
            here, beside = lax.optimization_barrier((jnp.stack(here), beside))
            return [here, lax.ppermute(here, "member", [(at, at ^ 1) for at in range(members)])], beside

        def arrivals(here):
            if not paired:
                return [(0, member, member) for member in range(members)]
            chip, core = lax.div(here, 2), lax.rem(here, 2)
            ring = (members // 2) & (members // 2 - 1)
            return [
                (
                    block,
                    shift,
                    2 * (lax.rem(chip + members // 2 - shift, members // 2) if ring else chip ^ shift) + side,
                )
                for block, side in enumerate((core, 1 - core))
                for shift in range(members // 2)
            ]

        def tradable(shape, kind):
            return [(shape, kind)] * bands if few else [((bands,) + shape, kind)]

        place = jnp.full((1, LANES), lax.axis_index("member"), jnp.int32)
        turn = jnp.full((1, LANES), lax.axis_index("band"), jnp.int32)
        here = lax.axis_index("member").astype(jnp.int32).reshape(1)

        block = (members * bands, slots * own, padded)
        pieces = pl.pallas_call(
            pack,
            out_shape=jax.ShapeDtypeStruct(block, bf16),
            in_specs=[pl.BlockSpec(memory_space=pltpu.HBM)] * 2,
            out_specs=pl.BlockSpec(memory_space=pltpu.HBM),
            scratch_shapes=[
                pltpu.SMEM((1,), jnp.int32),
                pltpu.VMEM((slots, levels, rows, lon), bf16),
                pltpu.VMEM(block, bf16),
                pltpu.SemaphoreType.DMA,
                pltpu.SemaphoreType.DMA((slots,)),
                pltpu.SemaphoreType.DMA((members,)),
            ],
            compiler_params=pltpu.CompilerParams(vmem_limit_bytes=60 * 2**20),
            name="pack",
        )(member_of_slot, ensemble)
        pieces, ensemble, innovation, precision, static_root = lax.optimization_barrier(
            (pieces, ensemble, innovation, precision, static_root)
        )
        stacked = lax.all_to_all(pieces, BOTH, 0, 0, tiled=True)

        of_level, same = row_levels(levels, rows)
        apart, level = row_apart(bands, level_share, rows, copies)
        every_level = np.tile(level, (members // copies, 1))
        block = (arrays * own, padded)
        between = [static_root] + [jnp.asarray(table) for table in (of_level, same)]
        results = call(
            observe,
            tradable(block, bf16) + [((bands, own, kept), f32), ((everything, lon), f32)],
            [],
            [place, turn, innovation, precision, *between],
        )
        blocks, (own_static, pulled) = trade(results[:-2]), results[-2:]
        own_static, between = lax.optimization_barrier((own_static, between))
        mixing, pulling, taper, factor, weights, own_weight, row_span = call(
            prepare,
            [
                ((own, everything), f32),
                ((everything, everything), f32),
                (apart.shape, bf16),
                (every_level.shape, f32),
                ((members, LANES), f32),
                ((1, LANES), f32),
                ((everything, LANES), f32),
            ],
            [here, halfwidth, member_weight, member_of_slot],
            [*between, jnp.asarray(apart), jnp.asarray(every_level)],
            scratch=[((levels, rows, everything), f32)] * 2,
        )
        awaited = bands // 2 if few else 0
        blocks[awaited], ensemble, innovation, precision = lax.optimization_barrier(
            (blocks[awaited], ensemble, innovation, precision)
        )
        (smoothed,) = call(
            fold_smooth,
            [((everything, lon), bf16)],
            [],
            [own_weight, ensemble, innovation, precision, lon_kernel(LANES, 2 * LANES)],
        )
        pairs = [(at, at + 1) for at in range(bands - 1)]
        below, above = [
            lax.ppermute(smoothed, "band", pairs[start::2] + [(to, at) for at, to in pairs[start::2]])
            for start in range(2)
        ]
        ring = ring_kernel(width, padded)

        total, weighted, image_first, fields = call(
            first_half,
            [
                ((per_member, kept), bf16),
                ((slots, per_member, padded), f32),
                ((slots, per_member, kept), f32),
                ((arrays, per_member, kept), f32),
            ],
            [],
            [weights, turn, stacked, ring, taper, factor, *blocks],
        )
        grad, image_second = call(
            second_half,
            [((members * bands, own, kept), bf16), ((slots, per_member, kept), f32)],
            [],
            [weights, stacked, ring, taper, factor, weighted],
            flops=10**9,
        )
        totals, (image_second, below, above) = around(total, (image_second, below, above))

        grad, image_second = call(
            combine,
            [((members * bands, own, kept), bf16), ((slots, per_member, kept), f32)],
            [],
            [grad, image_first, image_second, fields, mixing, *totals],
        )
        back = lax.all_to_all(grad, BOTH, 0, 0, tiled=True)
        blocks = call(
            hand_out,
            tradable((traded, kept), bf16),
            [],
            [turn, image_first, image_second, *totals],
        )
        blocks = trade(blocks)
        pulled_second, images = call(
            join,
            [((everything, lon), f32), ((2 * slots * own, lon), f32)],
            [],
            [turn, own_static, pulling, *blocks],
        )
        (grad_first,) = call(
            first_gradient,
            [((everything, lon), f32)],
            [],
            [turn, row_span, below, smoothed, above, jnp.asarray(halo_apart(levels, rows))],
        )
        return pl.pallas_call(
            finish,
            out_shape=(
                jax.ShapeDtypeStruct((1, levels, rows, lon), f32),
                jax.ShapeDtypeStruct((levels, rows, lon), f32),
                jax.ShapeDtypeStruct((slots, level_share, rows, lon), f32),
            ),
            in_specs=[vmem] * 5,
            out_specs=(pl.BlockSpec(memory_space=pltpu.HBM),) * 3,
            scratch_shapes=[
                pltpu.VMEM((levels, rows, lon), f32),
                pltpu.VMEM((levels, rows, lon), f32),
                pltpu.VMEM((slots, level_share, rows, lon), f32),
                pltpu.SemaphoreType.DMA((members + 2,)),
            ],
            compiler_params=pltpu.CompilerParams(vmem_limit_bytes=limit),
            name="finish",
        )(back, grad_first, pulled, pulled_second, images)

    return jax.shard_map(
        shards,
        mesh=mesh,
        in_specs=(
            P("member", None, None, "band", None),
            P(),
            P("member"),
            P(),
            P(),
            P(None, None, "band", None),
            P(None, "band", None),
        ),
        out_specs=(
            P("member", None, "band", None),
            P(None, "band", None),
            P(None, "member", "band", None),
        ),
        check_vma=False,
    )
```

```python
import math

import jax
import jax.numpy as jnp
import numpy as np
from jax import lax
from jax.experimental import pallas as pl
from jax.experimental.pallas import tpu as pltpu
from jax.sharding import PartitionSpec as P

HMAX = 4
LREACH = 18
REACHES = 4
LANES = 128
FEW = 8
SUMS = 4
PARTS = 3
HALVES = 2
BOTH = ("member", "band")

ensemble_share = 0.8
static_share = 0.6
length_scale = 6.0


def round_up(value, step):
    return -(-value // step) * step


def lon_weights(distance):
    distance = distance.astype(np.float32)
    values = np.exp(np.float32(-0.5) * (distance / np.float32(length_scale)) ** 2)
    values = values / np.float32(length_scale * math.sqrt(2.0 * math.pi))
    return jnp.asarray(np.where(distance <= LREACH, values, 0.0), jnp.bfloat16)


def lon_kernel(reach, width):
    return lon_weights(np.abs(np.arange(width + 2 * reach)[:, None] - reach - np.arange(width)[None]))


def ring_kernel(width, padded):
    apart = np.abs(np.arange(padded)[:, None] - np.arange(padded)[None])
    inside = (np.arange(padded)[:, None] < width) & (np.arange(padded)[None] < width)
    return lon_weights(np.where(inside, np.minimum(apart, width - apart), 2 * LREACH))


def near(apart, spans):
    return jnp.maximum(spans - apart, 0.0).astype(jnp.bfloat16)


def row_apart(bands, held, rows, copies):
    index = np.arange(copies * bands * held * rows)
    latitude = index // (held * rows) % bands * rows + index % rows
    level = index // rows % held
    copy = index // (bands * held * rows)
    same = (copy[:, None] == copy[None]) & (level[:, None] == level[None])
    apart = np.where(same, np.abs(latitude[:, None] - latitude[None]), 1000)
    return apart.astype(np.float32), level[:, None].astype(np.float32)


def halo_apart(levels, rows):
    own = levels * rows
    target, source = np.arange(own)[:, None], np.arange(3 * own)[None]
    shift = (source // own - 1) * rows + source % rows - target % rows
    same = source // rows % levels == target // rows
    return np.where(same, np.abs(shift), 1000).astype(np.float32)


def row_levels(levels, rows):
    index = np.arange(levels * rows)
    level = index[:, None] // rows == np.arange(levels)[None]
    place = index[:, None] % rows == index[None] % rows
    return level.astype(np.float32), place.astype(np.float32)


def partner(at, step, count, sign):
    if count & (count - 1):
        return (at + sign * step) % count
    return at ^ step


def exact_dot(matrix, field):
    return jnp.dot(
        matrix, field, precision=lax.Precision.HIGHEST, preferred_element_type=jnp.float32
    )


def parts_dot(matrix, field):
    count, parts = matrix.shape[0], []
    for _ in range(HALVES):
        part = matrix.astype(jnp.bfloat16).astype(jnp.float32)
        parts.append(part)
        matrix = matrix - part
    stacked = jnp.concatenate(parts, axis=0).astype(jnp.bfloat16)
    products = jnp.dot(stacked, field, preferred_element_type=jnp.float32)
    total = products[:count]
    for index in range(1, HALVES):
        total = total + products[index * count : (index + 1) * count]
    return total


def window(values, band, share, halo, tail):
    lon = values.shape[1]
    start = band * share
    stop = start + share + halo
    parts = [values[:, start : min(lon, stop)]]
    if stop > lon:
        parts.append(values[:, : stop - lon])
    if start < halo:
        parts.append(values[:, lon - halo + start :])
    if start:
        parts.append(values[:, max(start - halo, 0) : start])
    return jnp.concatenate(parts + [tail], axis=1)


def spread(field, ring, taper, factor):
    copies = taper.shape[0]
    smoothed = jnp.dot(field.astype(jnp.bfloat16), ring, preferred_element_type=jnp.float32)
    smoothed = smoothed.astype(jnp.bfloat16)
    parts = []
    for start in range(0, field.shape[0], copies):
        part = smoothed[start : start + copies]
        parts.append(jnp.dot(taper, part, preferred_element_type=jnp.float32))
    return factor * (parts[0] if len(parts) == 1 else jnp.concatenate(parts, axis=0))


def solution(mesh):
    members, bands = mesh.shape["member"], mesh.shape["band"]
    few = bands <= FEW
    paired = members % 2 == 0 and members // 2 <= FEW

    def shards(ensemble, member_weight, member_of_slot, halfwidth, static_root, innovation, precision):
        _, slots, levels, rows, lon = ensemble.shape
        level_share, lon_share = levels // members, lon // bands
        own = level_share * rows
        halo = REACHES * LREACH
        width = lon_share + 2 * halo
        padded = round_up(width + 1, LANES)
        kept = round_up(lon_share + SUMS * PARTS, LANES)
        per_member = bands * own
        copies = members
        while copies > 1 and (copies * per_member > 256 or members % copies):
            copies -= 1
        arrays = slots + 2
        everything = levels * rows
        traded = everything + 2 * slots * own
        vmem = pl.BlockSpec(memory_space=pltpu.VMEM)
        smem = pl.BlockSpec(memory_space=pltpu.SMEM)
        limit = min(48, max(14, 24 * members * bands * slots * own * padded // 2**20)) * 2**20

        def call(body, shapes, scalars, operands, scratch=(), flops=0):
            return pl.pallas_call(
                body,
                out_shape=tuple(jax.ShapeDtypeStruct(shape, kind) for shape, kind in shapes),
                in_specs=[smem] * len(scalars) + [vmem] * len(operands),
                out_specs=(vmem,) * len(shapes),
                scratch_shapes=[pltpu.VMEM(shape, kind) for shape, kind in scratch],
                compiler_params=pltpu.CompilerParams(vmem_limit_bytes=limit),
                cost_estimate=pl.CostEstimate(flops=flops, bytes_accessed=0, transcendentals=0),
                name=body.__name__,
            )(*scalars, *operands)

        f32, bf16 = jnp.float32, jnp.bfloat16

        def fold_smooth(own_weight, ensemble, innovation, precision, kernel, out):
            total = []
            for at in range(levels):
                precise = precision[at].astype(f32)
                part = jnp.zeros((rows, lon), f32)
                for t in range(slots):
                    weighted = precise * innovation[t, at].astype(f32)
                    part = part + ensemble[0, t, at].astype(f32) * weighted
                total.append(part)
            total = own_weight[:, :1] * jnp.concatenate(total, axis=0)
            step = kernel.shape[1]
            margin = (kernel.shape[0] - step) // 2
            steps = -(-lon // step)
            after = steps * step + margin - lon
            ring = jnp.concatenate([total[:, lon - margin :], total, total[:, :after]], axis=1)
            ring = ring.astype(bf16)
            for start in range(0, lon, step):
                stop = min(lon, start + step)
                piece = jnp.dot(
                    ring[:, start : start + kernel.shape[0]], kernel[...], preferred_element_type=f32
                )
                out[:, start:stop] = piece[:, : stop - start].astype(bf16)

        def first_gradient(turn, row_span, below, middle, above, apart, grad):
            span = row_span[:, :1]
            odd = jnp.full((everything, 1), 1, jnp.int32) * lax.rem(turn[:, :1], 2) == 1
            even_pair, odd_pair = below[...].astype(f32), above[...].astype(f32)
            low = jnp.where(odd, even_pair, odd_pair).astype(bf16)
            high = jnp.where(odd, odd_pair, even_pair).astype(bf16)
            stacked = jnp.concatenate([low, middle[...], high], axis=0)
            summed = jnp.dot(near(apart[...], span), stacked, preferred_element_type=f32)
            grad[...] = ensemble_share / (span * span) * summed

        def chosen(turn, blocks, sign):
            if not few:
                return [blocks[0][band] for band in range(bands)]
            turned = []
            for band in range(bands):
                value = blocks[0]
                for shift in range(1, bands):
                    value = jnp.where(turn == partner(band, shift, bands, -sign), blocks[shift], value)
                turned.append(value)
            return turned

        def load_members(weights, stacked):
            shape = (members, per_member, padded)
            values = stacked[...].astype(f32)
            ensemble = [
                values[:, slot * own : (slot + 1) * own].reshape(shape) for slot in range(slots)
            ]
            which = ensemble[0][:, :1, width : width + 1]
            scale = jnp.zeros(which.shape, f32)
            for member in range(members):
                weight = weights[member : member + 1, :1].reshape(1, 1, 1)
                scale = scale + jnp.where(which == member, weight, 0.0)
            scale = jnp.broadcast_to(scale, (members, per_member, 1))
            return ensemble, scale.reshape(members * per_member, 1)

        def fold(ensemble, scale, weighted):
            total = ensemble[0] * weighted[0][None]
            for slot in range(1, slots):
                total = total + ensemble[slot] * weighted[slot][None]
            return scale * total.reshape(members * per_member, padded)

        def images_of(ensemble, grad, ring, taper, factor):
            local = spread(grad, ring, taper, factor).reshape(members, per_member, padded)
            return [jnp.sum(ensemble[t] * local, axis=0) for t in range(slots)]

        def pack(slot, ensemble, out, marks, arrived, packed, mark_sem, in_sems, out_sems):
            def incoming(t):
                return pltpu.make_async_copy(ensemble.at[0, t], arrived.at[t], in_sems.at[t])

            def outgoing(member):
                place = pl.ds(member * bands, bands)
                return pltpu.make_async_copy(packed.at[place], out.at[place], out_sems.at[member])

            mark = pltpu.make_async_copy(slot, marks, mark_sem)
            mark.start()
            for t in range(slots):
                incoming(t).start()
            mark.wait()
            tail = jnp.full((slots * own, padded - width), marks[0], jnp.int32).astype(f32).astype(bf16)
            for t in range(slots):
                incoming(t).wait()
            for member in range(members):
                picked = range(member * level_share, (member + 1) * level_share)
                values = [arrived[t, at].astype(f32) for t in range(slots) for at in picked]
                values = jnp.concatenate(values, axis=0).astype(bf16)
                for band in range(bands):
                    packed[member * bands + band] = window(values, band, lon_share, halo, tail)
                outgoing(member).start()
            for member in range(members):
                outgoing(member).wait()

        def rows_between(root, of_level, same):
            wide = lax.dot_general(
                exact_dot(of_level, static_share * root),
                of_level,
                (((1,), (1,)), ((), ())),
                precision=lax.Precision.HIGHEST,
                preferred_element_type=f32,
            )
            return wide * same

        def observe(place, turn, innovation, precision, root, of_level, same, *refs):
            outs, (own_static, pulled) = refs[:-2], refs[-2:]
            out_of = rows_between(root[...], of_level[...], same[...])
            row = lax.broadcasted_iota(jnp.int32, (own, everything), 0)
            column = lax.broadcasted_iota(jnp.int32, (own, everything), 1)
            picker = (column == place[:, :1] * own + row).astype(f32)
            out_of_own = exact_dot(picker, out_of)
            precise = jnp.concatenate([precision[at].astype(f32) for at in range(levels)], axis=0)
            innovations = [
                jnp.concatenate([innovation[t, at].astype(f32) for at in range(levels)], axis=0)
                for t in range(slots)
            ]
            total = precise * innovations[0]
            for t in range(1, slots):
                total = total + precise * innovations[t]
            high = total.astype(bf16)
            low = (total - high.astype(f32)).astype(bf16)
            into = out_of.T
            back = parts_dot(into, high) + jnp.dot(into.astype(bf16), low, preferred_element_type=f32)
            pulled[...] = back
            values = [
                jnp.dot(picker.astype(bf16), field.astype(bf16), preferred_element_type=f32)
                for field in innovations + [precise]
            ]
            values = jnp.concatenate(values + [exact_dot(out_of_own, back)], axis=0)
            tail = jnp.zeros((values.shape[0], padded - width), f32)
            pieces = [window(values, band, lon_share, halo, tail) for band in range(bands)]
            for band, piece in enumerate(pieces):
                own_static[band] = piece[(slots + 1) * own :, :kept]
            deal(turn[:, :1], pieces, outs)

        def prepare(here, widths, weight, marks, root, of_level, same, apart, level, *refs):
            mixing, pulling, taper, factor, weights, own_weight, row_span, mixed, pulls = refs
            for member in range(members):
                weights[member : member + 1] = jnp.full((1, LANES), weight[member], f32)
            own_weight[...] = jnp.full((1, LANES), weight[marks[0]], f32)
            for at in range(levels):
                row_span[at * rows : (at + 1) * rows] = jnp.full(
                    (rows, LANES), widths[at].astype(f32) + 1.0, f32
                )
            out_of = rows_between(root[...], of_level[...], same[...])
            both = exact_dot(out_of, out_of.T)
            for at in range(levels):
                mixed[at] = both[at * rows : (at + 1) * rows]
                pulls[at] = out_of[at * rows : (at + 1) * rows]
            arriving = [
                member * level_share + share
                for _, _, member in arrivals(here[0])
                for share in range(level_share)
            ]
            pulling[...] = jnp.concatenate([pulls[at] for at in arriving], axis=0).T
            column = lax.broadcasted_iota(jnp.int32, (everything, own), 0)
            own_column = here[0] * own + lax.broadcasted_iota(jnp.int32, (everything, own), 1)
            mixing[...] = exact_dot(
                jnp.concatenate([mixed[at] for at in arriving], axis=0), (column == own_column).astype(f32)
            ).T
            span = jnp.ones(level.shape, f32)
            for share in range(level_share):
                which = here[0] * level_share + share
                span = span + jnp.where(level[...] == share, widths[which].astype(f32), 0.0)
            taper[...] = near(apart[...], span[: apart.shape[0]])
            factor[...] = ensemble_share / (span * span)

        def arrange(turn, *refs):
            blocks, (fields, kept_fields, weighted) = refs[:-3], refs[-3:]
            if few:
                blocks = [block[...].astype(f32) for block in blocks]
            values = jnp.stack(chosen(turn[:, :1], blocks, -1)).astype(f32)
            field = []
            for index in range(arrays):
                piece = values[:, index * own : (index + 1) * own].reshape(per_member, padded)
                kept_fields[index] = piece[:, :kept]
                field.append(piece)
            for index in range(slots, arrays):
                fields[index - slots] = field[index]
            for t in range(slots):
                weighted[t] = field[slots] * field[t]

        def first_half(weights, stacked, ring, taper, factor, fields, ready, total_out, weighted_out, image_out):
            precise, static = fields[0], fields[1]
            ensemble, scale = load_members(weights, stacked)
            weighted = [ready[t] for t in range(slots)]
            grad = spread(fold(ensemble, scale, weighted), ring[...], taper[...], factor[...])
            total = jnp.zeros((per_member, padded), f32)
            for t, image in enumerate(images_of(ensemble, grad, ring[...], taper[...], scale * factor[...])):
                image_out[t] = image[:, :kept]
                image = precise * (image + static)
                weighted_out[t] = image
                total = total + image
            total_out[...] = total[:, :kept].astype(bf16)

        def inner(first, second):
            inside = lax.broadcasted_iota(jnp.int32, first.shape, 1) < lon_share
            product = jnp.where(inside, first * second, 0.0)
            return jnp.sum(jnp.sum(product, axis=0, keepdims=True), axis=1, keepdims=True)

        def closest(first, second):
            norm = inner(first, first)
            ratio = inner(first, second) / jnp.where(norm > 0.0, norm, 1.0)
            return ratio.astype(bf16).astype(f32)

        def deal(turn, pieces, outs):
            if not few:
                for band, piece in enumerate(pieces):
                    outs[0][band] = piece.astype(bf16)
                return
            for shift in range(bands):
                value = pieces[0]
                for band in range(1, bands):
                    value = jnp.where(turn == partner(band, shift, bands, -1), pieces[band], value)
                outs[shift][...] = value.astype(bf16)

        def second_half(weights, stacked, ring, taper, factor, weighted, grad_out, image_out):
            ensemble, scale = load_members(weights, stacked)
            grad = fold(ensemble, scale, [weighted[t] for t in range(slots)])
            grad = spread(grad, ring[...], taper[...], factor[...])
            for t, image in enumerate(images_of(ensemble, grad, ring[...], taper[...], scale * factor[...])):
                image_out[t] = image[:, :kept]
            grad_out[...] = grad[:, :kept].reshape(members * bands, own, kept).astype(bf16)

        def combine(grad, first, second, fields, mixing, *refs):
            blocks, (out, image_out) = refs[:-2], refs[-2:]
            lane = lax.broadcasted_iota(jnp.int32, (1, kept), 1) - lon_share
            every = [
                jnp.concatenate(
                    [
                        blocks[block][shift, band * own : (band + 1) * own].astype(f32)
                        for block, shift, _ in arrivals(0)
                    ],
                    axis=0,
                )
                for band in range(bands)
            ]
            mixed = parts_dot(mixing[...], jnp.concatenate(every, axis=1).astype(bf16))
            mixed = jnp.concatenate(
                [mixed[:, band * kept : (band + 1) * kept] for band in range(bands)], axis=0
            )
            precise, static = fields[slots], fields[slots + 1]
            sums = [jnp.zeros((per_member, kept), f32) for _ in range(SUMS)]
            for t in range(slots):
                image = second[t] + mixed
                image_out[t] = image
                whole = first[t] + static
                weighted = precise * whole
                sums[0] = sums[0] + precise * fields[t] * whole
                sums[1] = sums[1] + weighted * whole
                sums[2] = sums[2] + weighted * image
                sums[3] = sums[3] + precise * image * image
            row = jnp.zeros((1, kept), f32)
            for index, part in enumerate(sums):
                part = jnp.sum(jnp.where(lane < 0, part, 0.0), axis=0, keepdims=True)
                part = jnp.sum(part, axis=1, keepdims=True)
                for piece in range(PARTS):
                    high = part.astype(bf16).astype(f32)
                    row = row + jnp.where(lane == PARTS * index + piece, high, 0.0)
                    part = part - high
            row = jnp.broadcast_to(row, (own, kept))
            lane = lax.broadcasted_iota(jnp.int32, (own, kept), 1)
            for block in range(members * bands):
                out[block] = jnp.where(lane < lon_share, grad[block].astype(f32), row).astype(bf16)

        def hand_out(turn, first, second, *refs):
            blocks, outs = refs[: len(totals)], refs[len(totals) :]
            lane = lax.broadcasted_iota(jnp.int32, (1, kept), 1)
            ratio = closest(
                jnp.concatenate([first[t] for t in range(slots)], axis=0),
                jnp.concatenate([second[t] for t in range(slots)], axis=0),
            )
            rest = [
                jnp.where(lane < lon_share, second[t] - ratio * first[t], ratio) for t in range(slots)
            ]
            images = [first[t] for t in range(slots)] + rest
            pieces = []
            for band in range(bands):
                place = slice(band * own, (band + 1) * own)
                parts = [blocks[block][shift, place].astype(f32) for block, shift, _ in arrivals(0)]
                pieces.append(jnp.concatenate(parts + [image[place] for image in images], axis=0))
            deal(turn[:, :1], pieces, outs)

        def join(turn, own_static, pulling, *refs):
            blocks, (pulled, images) = refs[:-2], refs[-2:]
            if few:
                blocks = [block[...].astype(f32) for block in blocks]
            pieces = chosen(turn[:, :1], blocks, -1)
            size = slots * own
            for band in range(bands):
                place = slice(band * lon_share, (band + 1) * lon_share)
                piece = pieces[band].astype(f32)
                every = piece[:everything].astype(bf16)
                pulled[:, place] = parts_dot(pulling[...], every)[:, :lon_share]
                parts = piece[everything:]
                first = parts[:size]
                second = parts[size:] + parts[size : size + 1, lon_share : lon_share + 1] * first
                static = own_static[band]
                for t in range(slots):
                    at = slice(t * own, (t + 1) * own)
                    images[at, place] = (first[at] + static)[:, :lon_share]
                images[size:, place] = second[:, :lon_share]

        def finish(back, grad_first, pulled_first, pulled_second, images, *refs):
            (member_out, static_out, image_out), (member, static, image, sems) = refs[:3], refs[3:]

            def outgoing(index, source, target):
                return pltpu.make_async_copy(source, target, sems.at[index])

            def outgoing_member(index):
                place = pl.ds(index * level_share, level_share)
                return outgoing(index, member.at[place], member_out.at[0, place])

            static_copy = outgoing(members, static, static_out)
            image_copy = outgoing(members + 1, image, image_out)
            tile = lon_share // LANES * LANES
            total = back[0, :1, tile:].astype(f32)
            for block in range(1, members * bands):
                total = total + back[block, :1, tile:].astype(f32)
            lane = lax.broadcasted_iota(jnp.int32, total.shape, 1) + tile - lon_share
            first_norm, first_image, cross, second_image = [
                jnp.sum(
                    jnp.where((lane >= PARTS * index) & (lane < PARTS * (index + 1)), total, 0.0),
                    axis=1,
                    keepdims=True,
                )
                for index in range(SUMS)
            ]
            alpha = first_norm / (first_norm + first_image)
            ratio = first_image / first_norm
            next_norm = alpha * alpha * jnp.maximum(cross - ratio * first_image, 0.0)
            beta = next_norm / first_norm
            apart = second_image - 2.0 * ratio * cross + ratio * ratio * first_image
            curvature = next_norm + alpha * alpha * apart - beta * next_norm / alpha
            alpha_next = jnp.clip(next_norm / curvature, 0.0, 1.0)
            on_first = alpha + alpha_next * (1.0 - alpha + beta)
            on_second = -alpha * alpha_next
            values = on_first * pulled_first[...] + on_second * pulled_second[...]
            for level in range(levels):
                static[level] = values[level * rows : (level + 1) * rows]
            static_copy.start()
            half = slots * own
            values = on_first * images[:half] + on_second * images[half:]
            for t in range(slots):
                for level in range(level_share):
                    start = (t * level_share + level) * rows
                    image[t, level] = values[start : start + rows]
            image_copy.start()
            for source in range(members):
                parts = [
                    back[source * bands + band].astype(f32)[:, :lon_share] for band in range(bands)
                ]
                values = on_second * jnp.concatenate(parts, axis=1)
                values = values + on_first * grad_first[source * own : (source + 1) * own]
                for share in range(level_share):
                    member[source * level_share + share] = values[share * rows : (share + 1) * rows]
                outgoing_member(source).start()
            static_copy.wait()
            image_copy.wait()
            for source in range(members):
                outgoing_member(source).wait()

        def trade(blocks):
            if not few:
                return [lax.all_to_all(blocks[0], "band", 0, 0, tiled=True)]
            return [blocks[0]] + [
                lax.ppermute(
                    blocks[shift], "band", [(at, partner(at, shift, bands, 1)) for at in range(bands)]
                )
                for shift in range(1, bands)
            ]

        def around(block, beside):
            if not paired:
                return [lax.all_gather(block, "member")], beside
            here = [block] + [
                lax.ppermute(
                    block,
                    "member",
                    [(at, 2 * partner(at // 2, shift, members // 2, 1) + at % 2) for at in range(members)],
                )
                for shift in range(1, members // 2)
            ]
            here, beside = lax.optimization_barrier((jnp.stack(here), beside))
            return [here, lax.ppermute(here, "member", [(at, at ^ 1) for at in range(members)])], beside

        def arrivals(here):
            if not paired:
                return [(0, member, member) for member in range(members)]
            chip, core = lax.div(here, 2), lax.rem(here, 2)
            ring = (members // 2) & (members // 2 - 1)
            return [
                (
                    block,
                    shift,
                    2 * (lax.rem(chip + members // 2 - shift, members // 2) if ring else chip ^ shift) + side,
                )
                for block, side in enumerate((core, 1 - core))
                for shift in range(members // 2)
            ]

        def tradable(shape, kind):
            return [(shape, kind)] * bands if few else [((bands,) + shape, kind)]

        place = jnp.full((1, LANES), lax.axis_index("member"), jnp.int32)
        turn = jnp.full((1, LANES), lax.axis_index("band"), jnp.int32)
        here = lax.axis_index("member").astype(jnp.int32).reshape(1)

        block = (members * bands, slots * own, padded)
        pieces = pl.pallas_call(
            pack,
            out_shape=jax.ShapeDtypeStruct(block, bf16),
            in_specs=[pl.BlockSpec(memory_space=pltpu.HBM)] * 2,
            out_specs=pl.BlockSpec(memory_space=pltpu.HBM),
            scratch_shapes=[
                pltpu.SMEM((1,), jnp.int32),
                pltpu.VMEM((slots, levels, rows, lon), bf16),
                pltpu.VMEM(block, bf16),
                pltpu.SemaphoreType.DMA,
                pltpu.SemaphoreType.DMA((slots,)),
                pltpu.SemaphoreType.DMA((members,)),
            ],
            compiler_params=pltpu.CompilerParams(vmem_limit_bytes=60 * 2**20),
            name="pack",
        )(member_of_slot, ensemble)
        pieces, ensemble, innovation, precision, static_root = lax.optimization_barrier(
            (pieces, ensemble, innovation, precision, static_root)
        )
        stacked = lax.all_to_all(pieces, BOTH, 0, 0, tiled=True)

        of_level, same = row_levels(levels, rows)
        apart, level = row_apart(bands, level_share, rows, copies)
        every_level = np.tile(level, (members // copies, 1))
        block = (arrays * own, padded)
        between = [static_root] + [jnp.asarray(table) for table in (of_level, same)]
        results = call(
            observe,
            tradable(block, bf16) + [((bands, own, kept), f32), ((everything, lon), f32)],
            [],
            [place, turn, innovation, precision, *between],
        )
        blocks, (own_static, pulled) = trade(results[:-2]), results[-2:]
        own_static, between = lax.optimization_barrier((own_static, between))
        mixing, pulling, taper, factor, weights, own_weight, row_span = call(
            prepare,
            [
                ((own, everything), f32),
                ((everything, everything), f32),
                (apart.shape, bf16),
                (every_level.shape, f32),
                ((members, LANES), f32),
                ((1, LANES), f32),
                ((everything, LANES), f32),
            ],
            [here, halfwidth, member_weight, member_of_slot],
            [*between, jnp.asarray(apart), jnp.asarray(every_level)],
            scratch=[((levels, rows, everything), f32)] * 2,
        )
        awaited = bands // 2 if few else 0
        blocks[awaited], ensemble, innovation, precision = lax.optimization_barrier(
            (blocks[awaited], ensemble, innovation, precision)
        )
        (smoothed,) = call(
            fold_smooth,
            [((everything, lon), bf16)],
            [],
            [own_weight, ensemble, innovation, precision, lon_kernel(LANES, 2 * LANES)],
        )
        pairs = [(at, at + 1) for at in range(bands - 1)]
        below, above = [
            lax.ppermute(smoothed, "band", pairs[start::2] + [(to, at) for at, to in pairs[start::2]])
            for start in range(2)
        ]
        ring = ring_kernel(width, padded)

        fields, kept_fields, ready = call(
            arrange,
            [
                ((arrays - slots, per_member, padded), f32),
                ((arrays, per_member, kept), f32),
                ((slots, per_member, padded), f32),
            ],
            [],
            [turn, *blocks],
        )
        total, weighted, image_first = call(
            first_half,
            [
                ((per_member, kept), bf16),
                ((slots, per_member, padded), f32),
                ((slots, per_member, kept), f32),
            ],
            [],
            [weights, stacked, ring, taper, factor, fields, ready],
        )
        fields = kept_fields
        grad, image_second = call(
            second_half,
            [((members * bands, own, kept), bf16), ((slots, per_member, kept), f32)],
            [],
            [weights, stacked, ring, taper, factor, weighted],
            flops=10**9,
        )
        totals, (image_second, below, above) = around(total, (image_second, below, above))

        grad, image_second = call(
            combine,
            [((members * bands, own, kept), bf16), ((slots, per_member, kept), f32)],
            [],
            [grad, image_first, image_second, fields, mixing, *totals],
        )
        back = lax.all_to_all(grad, BOTH, 0, 0, tiled=True)
        blocks = call(
            hand_out,
            tradable((traded, kept), bf16),
            [],
            [turn, image_first, image_second, *totals],
        )
        blocks = trade(blocks)
        pulled_second, images = call(
            join,
            [((everything, lon), f32), ((2 * slots * own, lon), f32)],
            [],
            [turn, own_static, pulling, *blocks],
        )
        (grad_first,) = call(
            first_gradient,
            [((everything, lon), f32)],
            [],
            [turn, row_span, below, smoothed, above, jnp.asarray(halo_apart(levels, rows))],
        )
        return pl.pallas_call(
            finish,
            out_shape=(
                jax.ShapeDtypeStruct((1, levels, rows, lon), f32),
                jax.ShapeDtypeStruct((levels, rows, lon), f32),
                jax.ShapeDtypeStruct((slots, level_share, rows, lon), f32),
            ),
            in_specs=[vmem] * 5,
            out_specs=(pl.BlockSpec(memory_space=pltpu.HBM),) * 3,
            scratch_shapes=[
                pltpu.VMEM((levels, rows, lon), f32),
                pltpu.VMEM((levels, rows, lon), f32),
                pltpu.VMEM((slots, level_share, rows, lon), f32),
                pltpu.SemaphoreType.DMA((members + 2,)),
            ],
            compiler_params=pltpu.CompilerParams(vmem_limit_bytes=limit),
            name="finish",
        )(back, grad_first, pulled, pulled_second, images)

    return jax.shard_map(
        shards,
        mesh=mesh,
        in_specs=(
            P("member", None, None, "band", None),
            P(),
            P("member"),
            P(),
            P(),
            P(None, None, "band", None),
            P(None, "band", None),
        ),
        out_specs=(
            P("member", None, "band", None),
            P(None, "band", None),
            P(None, "member", "band", None),
        ),
        check_vma=False,
    )
```

```python
import math

import jax
import jax.numpy as jnp
import numpy as np
from jax import lax
from jax.experimental import pallas as pl
from jax.experimental.pallas import tpu as pltpu
from jax.sharding import PartitionSpec as P

HMAX = 4
LREACH = 18
REACHES = 4
LANES = 128
FEW = 8
SUMS = 4
PARTS = 3
HALVES = 2
BOTH = ("member", "band")

ensemble_share = 0.8
static_share = 0.6
length_scale = 6.0


def round_up(value, step):
    return -(-value // step) * step


def lon_weights(distance):
    distance = distance.astype(np.float32)
    values = np.exp(np.float32(-0.5) * (distance / np.float32(length_scale)) ** 2)
    values = values / np.float32(length_scale * math.sqrt(2.0 * math.pi))
    return jnp.asarray(np.where(distance <= LREACH, values, 0.0), jnp.bfloat16)


def lon_kernel(reach, width):
    return lon_weights(np.abs(np.arange(width + 2 * reach)[:, None] - reach - np.arange(width)[None]))


def ring_kernel(width, padded):
    apart = np.abs(np.arange(padded)[:, None] - np.arange(padded)[None])
    inside = (np.arange(padded)[:, None] < width) & (np.arange(padded)[None] < width)
    return lon_weights(np.where(inside, np.minimum(apart, width - apart), 2 * LREACH))


def near(apart, spans):
    return jnp.maximum(spans - apart, 0.0).astype(jnp.bfloat16)


def row_apart(bands, held, rows, copies):
    index = np.arange(copies * bands * held * rows)
    latitude = index // (held * rows) % bands * rows + index % rows
    level = index // rows % held
    copy = index // (bands * held * rows)
    same = (copy[:, None] == copy[None]) & (level[:, None] == level[None])
    apart = np.where(same, np.abs(latitude[:, None] - latitude[None]), 1000)
    return apart.astype(np.float32), level[:, None].astype(np.float32)


def halo_apart(levels, rows):
    own = levels * rows
    target, source = np.arange(own)[:, None], np.arange(3 * own)[None]
    shift = (source // own - 1) * rows + source % rows - target % rows
    same = source // rows % levels == target // rows
    return np.where(same, np.abs(shift), 1000).astype(np.float32)


def row_levels(levels, rows):
    index = np.arange(levels * rows)
    level = index[:, None] // rows == np.arange(levels)[None]
    place = index[:, None] % rows == index[None] % rows
    return level.astype(np.float32), place.astype(np.float32)


def partner(at, step, count, sign):
    if count & (count - 1):
        return (at + sign * step) % count
    return at ^ step


def exact_dot(matrix, field):
    return jnp.dot(
        matrix, field, precision=lax.Precision.HIGHEST, preferred_element_type=jnp.float32
    )


def parts_dot(matrix, field):
    count, parts = matrix.shape[0], []
    for _ in range(HALVES):
        part = matrix.astype(jnp.bfloat16).astype(jnp.float32)
        parts.append(part)
        matrix = matrix - part
    stacked = jnp.concatenate(parts, axis=0).astype(jnp.bfloat16)
    products = jnp.dot(stacked, field, preferred_element_type=jnp.float32)
    total = products[:count]
    for index in range(1, HALVES):
        total = total + products[index * count : (index + 1) * count]
    return total


def window(values, band, share, halo, tail):
    lon = values.shape[1]
    start = band * share
    stop = start + share + halo
    parts = [values[:, start : min(lon, stop)]]
    if stop > lon:
        parts.append(values[:, : stop - lon])
    if start < halo:
        parts.append(values[:, lon - halo + start :])
    if start:
        parts.append(values[:, max(start - halo, 0) : start])
    return jnp.concatenate(parts + [tail], axis=1)


def spread(field, ring, taper, factor):
    copies = taper.shape[0]
    smoothed = jnp.dot(field.astype(jnp.bfloat16), ring, preferred_element_type=jnp.float32)
    smoothed = smoothed.astype(jnp.bfloat16)
    parts = []
    for start in range(0, field.shape[0], copies):
        part = smoothed[start : start + copies]
        parts.append(jnp.dot(taper, part, preferred_element_type=jnp.float32))
    return factor * (parts[0] if len(parts) == 1 else jnp.concatenate(parts, axis=0))


def solution(mesh):
    members, bands = mesh.shape["member"], mesh.shape["band"]
    few = bands <= FEW
    paired = members % 2 == 0 and members // 2 <= FEW

    def shards(ensemble, member_weight, member_of_slot, halfwidth, static_root, innovation, precision):
        _, slots, levels, rows, lon = ensemble.shape
        level_share, lon_share = levels // members, lon // bands
        own = level_share * rows
        halo = REACHES * LREACH
        width = lon_share + 2 * halo
        padded = round_up(width + 1, LANES)
        kept = round_up(lon_share + SUMS * PARTS, LANES)
        per_member = bands * own
        copies = members
        while copies > 1 and (copies * per_member > 256 or members % copies):
            copies -= 1
        arrays = slots + 2
        everything = levels * rows
        traded = everything + 2 * slots * own
        vmem = pl.BlockSpec(memory_space=pltpu.VMEM)
        smem = pl.BlockSpec(memory_space=pltpu.SMEM)
        limit = min(48, max(14, 24 * members * bands * slots * own * padded // 2**20)) * 2**20

        def call(body, shapes, scalars, operands, scratch=(), flops=0):
            return pl.pallas_call(
                body,
                out_shape=tuple(jax.ShapeDtypeStruct(shape, kind) for shape, kind in shapes),
                in_specs=[smem] * len(scalars) + [vmem] * len(operands),
                out_specs=(vmem,) * len(shapes),
                scratch_shapes=[pltpu.VMEM(shape, kind) for shape, kind in scratch],
                compiler_params=pltpu.CompilerParams(vmem_limit_bytes=limit),
                cost_estimate=pl.CostEstimate(flops=flops, bytes_accessed=0, transcendentals=0),
                name=body.__name__,
            )(*scalars, *operands)

        f32, bf16 = jnp.float32, jnp.bfloat16

        def fold_smooth(own_weight, ensemble, innovation, precision, kernel, out):
            total = []
            for at in range(levels):
                precise = precision[at].astype(f32)
                part = jnp.zeros((rows, lon), f32)
                for t in range(slots):
                    weighted = precise * innovation[t, at].astype(f32)
                    part = part + ensemble[0, t, at].astype(f32) * weighted
                total.append(part)
            total = own_weight[:, :1] * jnp.concatenate(total, axis=0)
            step = kernel.shape[1]
            margin = (kernel.shape[0] - step) // 2
            steps = -(-lon // step)
            after = steps * step + margin - lon
            ring = jnp.concatenate([total[:, lon - margin :], total, total[:, :after]], axis=1)
            ring = ring.astype(bf16)
            for start in range(0, lon, step):
                stop = min(lon, start + step)
                piece = jnp.dot(
                    ring[:, start : start + kernel.shape[0]], kernel[...], preferred_element_type=f32
                )
                out[:, start:stop] = piece[:, : stop - start].astype(bf16)

        def first_gradient(turn, row_span, below, middle, above, apart, grad):
            span = row_span[:, :1]
            odd = jnp.full((everything, 1), 1, jnp.int32) * lax.rem(turn[:, :1], 2) == 1
            even_pair, odd_pair = below[...].astype(f32), above[...].astype(f32)
            low = jnp.where(odd, even_pair, odd_pair).astype(bf16)
            high = jnp.where(odd, odd_pair, even_pair).astype(bf16)
            stacked = jnp.concatenate([low, middle[...], high], axis=0)
            summed = jnp.dot(near(apart[...], span), stacked, preferred_element_type=f32)
            grad[...] = ensemble_share / (span * span) * summed

        def chosen(turn, blocks, sign):
            if not few:
                return [blocks[0][band] for band in range(bands)]
            turned = []
            for band in range(bands):
                value = blocks[0]
                for shift in range(1, bands):
                    value = jnp.where(turn == partner(band, shift, bands, -sign), blocks[shift], value)
                turned.append(value)
            return turned

        def load_members(weights, stacked):
            shape = (members, per_member, padded)
            values = stacked[...].astype(f32)
            ensemble = [
                values[:, slot * own : (slot + 1) * own].reshape(shape) for slot in range(slots)
            ]
            which = ensemble[0][:, :1, width : width + 1]
            scale = jnp.zeros(which.shape, f32)
            for member in range(members):
                weight = weights[member : member + 1, :1].reshape(1, 1, 1)
                scale = scale + jnp.where(which == member, weight, 0.0)
            scale = jnp.broadcast_to(scale, (members, per_member, 1))
            return ensemble, scale.reshape(members * per_member, 1)

        def fold(ensemble, scale, weighted):
            total = ensemble[0] * weighted[0][None]
            for slot in range(1, slots):
                total = total + ensemble[slot] * weighted[slot][None]
            return scale * total.reshape(members * per_member, padded)

        def images_of(ensemble, grad, ring, taper, factor):
            local = spread(grad, ring, taper, factor).reshape(members, per_member, padded)
            return [jnp.sum(ensemble[t] * local, axis=0) for t in range(slots)]

        def pack(slot, ensemble, out, marks, arrived, packed, mark_sem, in_sems, out_sems):
            def incoming(t):
                return pltpu.make_async_copy(ensemble.at[0, t], arrived.at[t], in_sems.at[t])

            def outgoing(member):
                place = pl.ds(member * bands, bands)
                return pltpu.make_async_copy(packed.at[place], out.at[place], out_sems.at[member])

            mark = pltpu.make_async_copy(slot, marks, mark_sem)
            mark.start()
            for t in range(slots):
                incoming(t).start()
            mark.wait()
            tail = jnp.full((slots * own, padded - width), marks[0], jnp.int32).astype(f32).astype(bf16)
            for t in range(slots):
                incoming(t).wait()
            for member in range(members):
                picked = range(member * level_share, (member + 1) * level_share)
                values = [arrived[t, at].astype(f32) for t in range(slots) for at in picked]
                values = jnp.concatenate(values, axis=0).astype(bf16)
                for band in range(bands):
                    packed[member * bands + band] = window(values, band, lon_share, halo, tail)
                outgoing(member).start()
            for member in range(members):
                outgoing(member).wait()

        def rows_between(root, of_level, same):
            wide = lax.dot_general(
                exact_dot(of_level, static_share * root),
                of_level,
                (((1,), (1,)), ((), ())),
                precision=lax.Precision.HIGHEST,
                preferred_element_type=f32,
            )
            return wide * same

        def observe(place, turn, innovation, precision, root, of_level, same, *refs):
            outs, (own_static, pulled) = refs[:-2], refs[-2:]
            out_of = rows_between(root[...], of_level[...], same[...])
            row = lax.broadcasted_iota(jnp.int32, (own, everything), 0)
            column = lax.broadcasted_iota(jnp.int32, (own, everything), 1)
            picker = (column == place[:, :1] * own + row).astype(f32)
            out_of_own = exact_dot(picker, out_of)
            precise = jnp.concatenate([precision[at].astype(f32) for at in range(levels)], axis=0)
            innovations = [
                jnp.concatenate([innovation[t, at].astype(f32) for at in range(levels)], axis=0)
                for t in range(slots)
            ]
            total = precise * innovations[0]
            for t in range(1, slots):
                total = total + precise * innovations[t]
            high = total.astype(bf16)
            low = (total - high.astype(f32)).astype(bf16)
            into = out_of.T
            back = parts_dot(into, high) + jnp.dot(into.astype(bf16), low, preferred_element_type=f32)
            pulled[...] = back
            values = [
                jnp.dot(picker.astype(bf16), field.astype(bf16), preferred_element_type=f32)
                for field in innovations + [precise]
            ]
            values = jnp.concatenate(values + [exact_dot(out_of_own, back)], axis=0)
            tail = jnp.zeros((values.shape[0], padded - width), f32)
            pieces = [window(values, band, lon_share, halo, tail) for band in range(bands)]
            for band, piece in enumerate(pieces):
                own_static[band] = piece[(slots + 1) * own :, :kept]
            deal(turn[:, :1], pieces, outs)

        def prepare(here, widths, weight, marks, root, of_level, same, apart, level, *refs):
            mixing, pulling, taper, factor, weights, own_weight, row_span, mixed, pulls = refs
            for member in range(members):
                weights[member : member + 1] = jnp.full((1, LANES), weight[member], f32)
            own_weight[...] = jnp.full((1, LANES), weight[marks[0]], f32)
            for at in range(levels):
                row_span[at * rows : (at + 1) * rows] = jnp.full(
                    (rows, LANES), widths[at].astype(f32) + 1.0, f32
                )
            out_of = rows_between(root[...], of_level[...], same[...])
            both = exact_dot(out_of, out_of.T)
            for at in range(levels):
                mixed[at] = both[at * rows : (at + 1) * rows]
                pulls[at] = out_of[at * rows : (at + 1) * rows]
            arriving = [
                member * level_share + share
                for _, _, member in arrivals(here[0])
                for share in range(level_share)
            ]
            pulling[...] = jnp.concatenate([pulls[at] for at in arriving], axis=0).T
            column = lax.broadcasted_iota(jnp.int32, (everything, own), 0)
            own_column = here[0] * own + lax.broadcasted_iota(jnp.int32, (everything, own), 1)
            mixing[...] = exact_dot(
                jnp.concatenate([mixed[at] for at in arriving], axis=0), (column == own_column).astype(f32)
            ).T
            span = jnp.ones(level.shape, f32)
            for share in range(level_share):
                which = here[0] * level_share + share
                span = span + jnp.where(level[...] == share, widths[which].astype(f32), 0.0)
            taper[...] = near(apart[...], span[: apart.shape[0]])
            factor[...] = ensemble_share / (span * span)

        def first_half(weights, turn, stacked, ring, taper, factor, *refs):
            blocks, (total_out, weighted_out, image_out, fields) = refs[:-4], refs[-4:]
            if few:
                blocks = [block[...].astype(f32) for block in blocks]
            values = jnp.stack(chosen(turn[:, :1], blocks, -1)).astype(f32)
            field = []
            for index in range(arrays):
                piece = values[:, index * own : (index + 1) * own].reshape(per_member, padded)
                fields[index] = piece[:, :kept]
                field.append(piece)
            precise, static = field[slots], field[slots + 1]
            ensemble, scale = load_members(weights, stacked)
            weighted = [precise * field[t] for t in range(slots)]
            grad = spread(fold(ensemble, scale, weighted), ring[...], taper[...], factor[...])
            total = jnp.zeros((per_member, padded), f32)
            for t, image in enumerate(images_of(ensemble, grad, ring[...], taper[...], scale * factor[...])):
                image_out[t] = image[:, :kept]
                image = precise * (image + static)
                weighted_out[t] = image
                total = total + image
            total_out[...] = total[:, :kept].astype(bf16)

        def inner(first, second):
            inside = lax.broadcasted_iota(jnp.int32, first.shape, 1) < lon_share
            product = jnp.where(inside, first * second, 0.0)
            return jnp.sum(jnp.sum(product, axis=0, keepdims=True), axis=1, keepdims=True)

        def closest(first, second):
            norm = inner(first, first)
            ratio = inner(first, second) / jnp.where(norm > 0.0, norm, 1.0)
            return ratio.astype(bf16).astype(f32)

        def deal(turn, pieces, outs):
            if not few:
                for band, piece in enumerate(pieces):
                    outs[0][band] = piece.astype(bf16)
                return
            for shift in range(bands):
                value = pieces[0]
                for band in range(1, bands):
                    value = jnp.where(turn == partner(band, shift, bands, -1), pieces[band], value)
                outs[shift][...] = value.astype(bf16)

        def second_half(weights, stacked, ring, taper, factor, weighted, grad_out, image_out):
            ensemble, scale = load_members(weights, stacked)
            grad = fold(ensemble, scale, [weighted[t] for t in range(slots)])
            grad = spread(grad, ring[...], taper[...], factor[...])
            for t, image in enumerate(images_of(ensemble, grad, ring[...], taper[...], scale * factor[...])):
                image_out[t] = image[:, :kept]
            grad_out[...] = grad[:, :kept].reshape(members * bands, own, kept).astype(bf16)

        def combine(grad, first, second, fields, mixing, *refs):
            blocks, (out, image_out) = refs[:-2], refs[-2:]
            lane = lax.broadcasted_iota(jnp.int32, (1, kept), 1) - lon_share
            every = [
                jnp.concatenate(
                    [
                        blocks[block][shift, band * own : (band + 1) * own].astype(f32)
                        for block, shift, _ in arrivals(0)
                    ],
                    axis=0,
                )
                for band in range(bands)
            ]
            mixed = parts_dot(mixing[...], jnp.concatenate(every, axis=1).astype(bf16))
            mixed = jnp.concatenate(
                [mixed[:, band * kept : (band + 1) * kept] for band in range(bands)], axis=0
            )
            precise, static = fields[slots], fields[slots + 1]
            sums = [jnp.zeros((per_member, kept), f32) for _ in range(SUMS)]
            for t in range(slots):
                image = second[t] + mixed
                image_out[t] = image
                whole = first[t] + static
                weighted = precise * whole
                sums[0] = sums[0] + precise * fields[t] * whole
                sums[1] = sums[1] + weighted * whole
                sums[2] = sums[2] + weighted * image
                sums[3] = sums[3] + precise * image * image
            row = jnp.zeros((1, kept), f32)
            for index, part in enumerate(sums):
                part = jnp.sum(jnp.where(lane < 0, part, 0.0), axis=0, keepdims=True)
                part = jnp.sum(part, axis=1, keepdims=True)
                for piece in range(PARTS):
                    high = part.astype(bf16).astype(f32)
                    row = row + jnp.where(lane == PARTS * index + piece, high, 0.0)
                    part = part - high
            tile = lon_share // LANES * LANES
            row = jnp.broadcast_to(row, (own, kept))[:, tile:]
            lane = lax.broadcasted_iota(jnp.int32, (own, kept - tile), 1) + tile
            for block in range(members * bands):
                last = jnp.where(lane < lon_share, grad[block, :, tile:].astype(f32), row)
                if tile:
                    out[block, :, :tile] = grad[block, :, :tile]
                out[block, :, tile:] = last.astype(bf16)

        def hand_out(turn, first, second, *refs):
            blocks, outs = refs[: len(totals)], refs[len(totals) :]
            lane = lax.broadcasted_iota(jnp.int32, (1, kept), 1)
            ratio = closest(
                jnp.concatenate([first[t] for t in range(slots)], axis=0),
                jnp.concatenate([second[t] for t in range(slots)], axis=0),
            )
            rest = [
                jnp.where(lane < lon_share, second[t] - ratio * first[t], ratio) for t in range(slots)
            ]
            images = [first[t] for t in range(slots)] + rest
            pieces = []
            for band in range(bands):
                place = slice(band * own, (band + 1) * own)
                parts = [blocks[block][shift, place].astype(f32) for block, shift, _ in arrivals(0)]
                pieces.append(jnp.concatenate(parts + [image[place] for image in images], axis=0))
            deal(turn[:, :1], pieces, outs)

        def join(turn, own_static, pulling, *refs):
            blocks, (pulled, images) = refs[:-2], refs[-2:]
            if few:
                blocks = [block[...].astype(f32) for block in blocks]
            pieces = chosen(turn[:, :1], blocks, -1)
            size = slots * own
            for band in range(bands):
                place = slice(band * lon_share, (band + 1) * lon_share)
                piece = pieces[band].astype(f32)
                every = piece[:everything].astype(bf16)
                pulled[:, place] = parts_dot(pulling[...], every)[:, :lon_share]
                parts = piece[everything:]
                first = parts[:size]
                second = parts[size:] + parts[size : size + 1, lon_share : lon_share + 1] * first
                static = own_static[band]
                for t in range(slots):
                    at = slice(t * own, (t + 1) * own)
                    images[at, place] = (first[at] + static)[:, :lon_share]
                images[size:, place] = second[:, :lon_share]

        def finish(back, grad_first, pulled_first, pulled_second, images, *refs):
            (member_out, static_out, image_out), (member, static, image, sems) = refs[:3], refs[3:]

            def outgoing(index, source, target):
                return pltpu.make_async_copy(source, target, sems.at[index])

            def outgoing_member(index):
                place = pl.ds(index * level_share, level_share)
                return outgoing(index, member.at[place], member_out.at[0, place])

            static_copy = outgoing(members, static, static_out)
            image_copy = outgoing(members + 1, image, image_out)
            tile = lon_share // LANES * LANES
            total = back[0, :1, tile:].astype(f32)
            for block in range(1, members * bands):
                total = total + back[block, :1, tile:].astype(f32)
            lane = lax.broadcasted_iota(jnp.int32, total.shape, 1) + tile - lon_share
            first_norm, first_image, cross, second_image = [
                jnp.sum(
                    jnp.where((lane >= PARTS * index) & (lane < PARTS * (index + 1)), total, 0.0),
                    axis=1,
                    keepdims=True,
                )
                for index in range(SUMS)
            ]
            alpha = first_norm / (first_norm + first_image)
            ratio = first_image / first_norm
            next_norm = alpha * alpha * jnp.maximum(cross - ratio * first_image, 0.0)
            beta = next_norm / first_norm
            apart = second_image - 2.0 * ratio * cross + ratio * ratio * first_image
            curvature = next_norm + alpha * alpha * apart - beta * next_norm / alpha
            alpha_next = jnp.clip(next_norm / curvature, 0.0, 1.0)
            on_first = alpha + alpha_next * (1.0 - alpha + beta)
            on_second = -alpha * alpha_next
            values = on_first * pulled_first[...] + on_second * pulled_second[...]
            for level in range(levels):
                static[level] = values[level * rows : (level + 1) * rows]
            static_copy.start()
            half = slots * own
            values = on_first * images[:half] + on_second * images[half:]
            for t in range(slots):
                for level in range(level_share):
                    start = (t * level_share + level) * rows
                    image[t, level] = values[start : start + rows]
            image_copy.start()
            for source in range(members):
                parts = [
                    back[source * bands + band].astype(f32)[:, :lon_share] for band in range(bands)
                ]
                values = on_second * jnp.concatenate(parts, axis=1)
                values = values + on_first * grad_first[source * own : (source + 1) * own]
                for share in range(level_share):
                    member[source * level_share + share] = values[share * rows : (share + 1) * rows]
                outgoing_member(source).start()
            static_copy.wait()
            image_copy.wait()
            for source in range(members):
                outgoing_member(source).wait()

        def trade(blocks):
            if not few:
                return [lax.all_to_all(blocks[0], "band", 0, 0, tiled=True)]
            return [blocks[0]] + [
                lax.ppermute(
                    blocks[shift], "band", [(at, partner(at, shift, bands, 1)) for at in range(bands)]
                )
                for shift in range(1, bands)
            ]

        def around(block, beside):
            if not paired:
                return [lax.all_gather(block, "member")], beside
            here = [block] + [
                lax.ppermute(
                    block,
                    "member",
                    [(at, 2 * partner(at // 2, shift, members // 2, 1) + at % 2) for at in range(members)],
                )
                for shift in range(1, members // 2)
            ]
            here, beside = lax.optimization_barrier((jnp.stack(here), beside))
            return [here, lax.ppermute(here, "member", [(at, at ^ 1) for at in range(members)])], beside

        def arrivals(here):
            if not paired:
                return [(0, member, member) for member in range(members)]
            chip, core = lax.div(here, 2), lax.rem(here, 2)
            ring = (members // 2) & (members // 2 - 1)
            return [
                (
                    block,
                    shift,
                    2 * (lax.rem(chip + members // 2 - shift, members // 2) if ring else chip ^ shift) + side,
                )
                for block, side in enumerate((core, 1 - core))
                for shift in range(members // 2)
            ]

        def tradable(shape, kind):
            return [(shape, kind)] * bands if few else [((bands,) + shape, kind)]

        place = jnp.full((1, LANES), lax.axis_index("member"), jnp.int32)
        turn = jnp.full((1, LANES), lax.axis_index("band"), jnp.int32)
        here = lax.axis_index("member").astype(jnp.int32).reshape(1)

        block = (members * bands, slots * own, padded)
        pieces = pl.pallas_call(
            pack,
            out_shape=jax.ShapeDtypeStruct(block, bf16),
            in_specs=[pl.BlockSpec(memory_space=pltpu.HBM)] * 2,
            out_specs=pl.BlockSpec(memory_space=pltpu.HBM),
            scratch_shapes=[
                pltpu.SMEM((1,), jnp.int32),
                pltpu.VMEM((slots, levels, rows, lon), bf16),
                pltpu.VMEM(block, bf16),
                pltpu.SemaphoreType.DMA,
                pltpu.SemaphoreType.DMA((slots,)),
                pltpu.SemaphoreType.DMA((members,)),
            ],
            compiler_params=pltpu.CompilerParams(vmem_limit_bytes=60 * 2**20),
            name="pack",
        )(member_of_slot, ensemble)
        pieces, ensemble, innovation, precision, static_root = lax.optimization_barrier(
            (pieces, ensemble, innovation, precision, static_root)
        )
        stacked = lax.all_to_all(pieces, BOTH, 0, 0, tiled=True)

        of_level, same = row_levels(levels, rows)
        apart, level = row_apart(bands, level_share, rows, copies)
        every_level = np.tile(level, (members // copies, 1))
        block = (arrays * own, padded)
        between = [static_root] + [jnp.asarray(table) for table in (of_level, same)]
        results = call(
            observe,
            tradable(block, bf16) + [((bands, own, kept), f32), ((everything, lon), f32)],
            [],
            [place, turn, innovation, precision, *between],
        )
        blocks, (own_static, pulled) = trade(results[:-2]), results[-2:]
        own_static, between = lax.optimization_barrier((own_static, between))
        mixing, pulling, taper, factor, weights, own_weight, row_span = call(
            prepare,
            [
                ((own, everything), f32),
                ((everything, everything), f32),
                (apart.shape, bf16),
                (every_level.shape, f32),
                ((members, LANES), f32),
                ((1, LANES), f32),
                ((everything, LANES), f32),
            ],
            [here, halfwidth, member_weight, member_of_slot],
            [*between, jnp.asarray(apart), jnp.asarray(every_level)],
            scratch=[((levels, rows, everything), f32)] * 2,
        )
        awaited = bands // 2 if few else 0
        blocks[awaited], ensemble, innovation, precision = lax.optimization_barrier(
            (blocks[awaited], ensemble, innovation, precision)
        )
        (smoothed,) = call(
            fold_smooth,
            [((everything, lon), bf16)],
            [],
            [own_weight, ensemble, innovation, precision, lon_kernel(LANES, 2 * LANES)],
        )
        pairs = [(at, at + 1) for at in range(bands - 1)]
        below, above = [
            lax.ppermute(smoothed, "band", pairs[start::2] + [(to, at) for at, to in pairs[start::2]])
            for start in range(2)
        ]
        ring = ring_kernel(width, padded)

        total, weighted, image_first, fields = call(
            first_half,
            [
                ((per_member, kept), bf16),
                ((slots, per_member, padded), f32),
                ((slots, per_member, kept), f32),
                ((arrays, per_member, kept), f32),
            ],
            [],
            [weights, turn, stacked, ring, taper, factor, *blocks],
        )
        grad, image_second = call(
            second_half,
            [((members * bands, own, kept), bf16), ((slots, per_member, kept), f32)],
            [],
            [weights, stacked, ring, taper, factor, weighted],
            flops=10**9,
        )
        totals, (image_second, below, above) = around(total, (image_second, below, above))

        grad, image_second = call(
            combine,
            [((members * bands, own, kept), bf16), ((slots, per_member, kept), f32)],
            [],
            [grad, image_first, image_second, fields, mixing, *totals],
        )
        back = lax.all_to_all(grad, BOTH, 0, 0, tiled=True)
        blocks = call(
            hand_out,
            tradable((traded, kept), bf16),
            [],
            [turn, image_first, image_second, *totals],
        )
        blocks = trade(blocks)
        pulled_second, images = call(
            join,
            [((everything, lon), f32), ((2 * slots * own, lon), f32)],
            [],
            [turn, own_static, pulling, *blocks],
        )
        (grad_first,) = call(
            first_gradient,
            [((everything, lon), f32)],
            [],
            [turn, row_span, below, smoothed, above, jnp.asarray(halo_apart(levels, rows))],
        )
        return pl.pallas_call(
            finish,
            out_shape=(
                jax.ShapeDtypeStruct((1, levels, rows, lon), f32),
                jax.ShapeDtypeStruct((levels, rows, lon), f32),
                jax.ShapeDtypeStruct((slots, level_share, rows, lon), f32),
            ),
            in_specs=[vmem] * 5,
            out_specs=(pl.BlockSpec(memory_space=pltpu.HBM),) * 3,
            scratch_shapes=[
                pltpu.VMEM((levels, rows, lon), f32),
                pltpu.VMEM((levels, rows, lon), f32),
                pltpu.VMEM((slots, level_share, rows, lon), f32),
                pltpu.SemaphoreType.DMA((members + 2,)),
            ],
            compiler_params=pltpu.CompilerParams(vmem_limit_bytes=limit),
            name="finish",
        )(back, grad_first, pulled, pulled_second, images)

    return jax.shard_map(
        shards,
        mesh=mesh,
        in_specs=(
            P("member", None, None, "band", None),
            P(),
            P("member"),
            P(),
            P(),
            P(None, None, "band", None),
            P(None, "band", None),
        ),
        out_specs=(
            P("member", None, "band", None),
            P(None, "band", None),
            P(None, "member", "band", None),
        ),
        check_vma=False,
    )
```

```python
import math

import jax
import jax.numpy as jnp
import numpy as np
from jax import lax
from jax.experimental import pallas as pl
from jax.experimental.pallas import tpu as pltpu
from jax.sharding import PartitionSpec as P

HMAX = 4
LREACH = 18
REACHES = 4
LANES = 128
FEW = 8
SUMS = 4
PARTS = 3
HALVES = 2
BOTH = ("member", "band")

ensemble_share = 0.8
static_share = 0.6
length_scale = 6.0


def round_up(value, step):
    return -(-value // step) * step


def lon_weights(distance):
    distance = distance.astype(np.float32)
    values = np.exp(np.float32(-0.5) * (distance / np.float32(length_scale)) ** 2)
    values = values / np.float32(length_scale * math.sqrt(2.0 * math.pi))
    return jnp.asarray(np.where(distance <= LREACH, values, 0.0), jnp.bfloat16)


def lon_kernel(reach, width):
    return lon_weights(np.abs(np.arange(width + 2 * reach)[:, None] - reach - np.arange(width)[None]))


def ring_kernel(width, padded):
    apart = np.abs(np.arange(padded)[:, None] - np.arange(padded)[None])
    inside = (np.arange(padded)[:, None] < width) & (np.arange(padded)[None] < width)
    return lon_weights(np.where(inside, np.minimum(apart, width - apart), 2 * LREACH))


def near(apart, spans):
    return jnp.maximum(spans - apart, 0.0).astype(jnp.bfloat16)


def row_apart(bands, held, rows, copies):
    index = np.arange(copies * bands * held * rows)
    latitude = index // (held * rows) % bands * rows + index % rows
    level = index // rows % held
    copy = index // (bands * held * rows)
    same = (copy[:, None] == copy[None]) & (level[:, None] == level[None])
    apart = np.where(same, np.abs(latitude[:, None] - latitude[None]), 1000)
    return apart.astype(np.float32), level[:, None].astype(np.float32)


def halo_apart(levels, rows):
    own = levels * rows
    target, source = np.arange(own)[:, None], np.arange(3 * own)[None]
    shift = (source // own - 1) * rows + source % rows - target % rows
    same = source // rows % levels == target // rows
    return np.where(same, np.abs(shift), 1000).astype(np.float32)


def row_levels(levels, rows):
    index = np.arange(levels * rows)
    level = index[:, None] // rows == np.arange(levels)[None]
    place = index[:, None] % rows == index[None] % rows
    return level.astype(np.float32), place.astype(np.float32)


def partner(at, step, count, sign):
    if count & (count - 1):
        return (at + sign * step) % count
    return at ^ step


def exact_dot(matrix, field):
    return jnp.dot(
        matrix, field, precision=lax.Precision.HIGHEST, preferred_element_type=jnp.float32
    )


def parts_dot(matrix, field):
    count, parts = matrix.shape[0], []
    for _ in range(HALVES):
        part = matrix.astype(jnp.bfloat16).astype(jnp.float32)
        parts.append(part)
        matrix = matrix - part
    stacked = jnp.concatenate(parts, axis=0).astype(jnp.bfloat16)
    products = jnp.dot(stacked, field, preferred_element_type=jnp.float32)
    total = products[:count]
    for index in range(1, HALVES):
        total = total + products[index * count : (index + 1) * count]
    return total


def window(values, band, share, halo, tail):
    lon = values.shape[1]
    start = band * share
    stop = start + share + halo
    parts = [values[:, start : min(lon, stop)]]
    if stop > lon:
        parts.append(values[:, : stop - lon])
    if start < halo:
        parts.append(values[:, lon - halo + start :])
    if start:
        parts.append(values[:, max(start - halo, 0) : start])
    return jnp.concatenate(parts + [tail], axis=1)


def spread(field, ring, taper, factor):
    copies = taper.shape[0]
    smoothed = jnp.dot(field.astype(jnp.bfloat16), ring, preferred_element_type=jnp.float32)
    smoothed = smoothed.astype(jnp.bfloat16)
    parts = []
    for start in range(0, field.shape[0], copies):
        part = smoothed[start : start + copies]
        parts.append(jnp.dot(taper, part, preferred_element_type=jnp.float32))
    return factor * (parts[0] if len(parts) == 1 else jnp.concatenate(parts, axis=0))


def solution(mesh):
    members, bands = mesh.shape["member"], mesh.shape["band"]
    few = bands <= FEW
    paired = members % 2 == 0 and members // 2 <= FEW

    def shards(ensemble, member_weight, member_of_slot, halfwidth, static_root, innovation, precision):
        _, slots, levels, rows, lon = ensemble.shape
        level_share, lon_share = levels // members, lon // bands
        own = level_share * rows
        halo = REACHES * LREACH
        width = lon_share + 2 * halo
        padded = round_up(width + 1, LANES)
        kept = round_up(lon_share + SUMS * PARTS, LANES)
        per_member = bands * own
        copies = members
        while copies > 1 and (copies * per_member > 256 or members % copies):
            copies -= 1
        arrays = slots + 2
        everything = levels * rows
        traded = everything + 2 * slots * own
        vmem = pl.BlockSpec(memory_space=pltpu.VMEM)
        smem = pl.BlockSpec(memory_space=pltpu.SMEM)
        limit = min(48, max(14, 24 * members * bands * slots * own * padded // 2**20)) * 2**20

        def call(body, shapes, scalars, operands, scratch=(), flops=0):
            return pl.pallas_call(
                body,
                out_shape=tuple(jax.ShapeDtypeStruct(shape, kind) for shape, kind in shapes),
                in_specs=[smem] * len(scalars) + [vmem] * len(operands),
                out_specs=(vmem,) * len(shapes),
                scratch_shapes=[pltpu.VMEM(shape, kind) for shape, kind in scratch],
                compiler_params=pltpu.CompilerParams(vmem_limit_bytes=limit),
                cost_estimate=pl.CostEstimate(flops=flops, bytes_accessed=0, transcendentals=0),
                name=body.__name__,
            )(*scalars, *operands)

        f32, bf16 = jnp.float32, jnp.bfloat16

        def fold_smooth(slot, weight, ensemble, innovation, precision, kernel, out):
            total = []
            for at in range(levels):
                precise = precision[at].astype(f32)
                part = jnp.zeros((rows, lon), f32)
                for t in range(slots):
                    weighted = precise * innovation[t, at].astype(f32)
                    part = part + ensemble[0, t, at].astype(f32) * weighted
                total.append(part)
            chosen_weight = jnp.where(
                lax.broadcasted_iota(jnp.int32, weight.shape, 1) == slot[...], weight[...], 0.0
            )
            total = jnp.sum(chosen_weight, axis=1, keepdims=True) * jnp.concatenate(total, axis=0)
            step = kernel.shape[1]
            margin = (kernel.shape[0] - step) // 2
            steps = -(-lon // step)
            after = steps * step + margin - lon
            ring = jnp.concatenate([total[:, lon - margin :], total, total[:, :after]], axis=1)
            ring = ring.astype(bf16)
            for start in range(0, lon, step):
                stop = min(lon, start + step)
                piece = jnp.dot(
                    ring[:, start : start + kernel.shape[0]], kernel[...], preferred_element_type=f32
                )
                out[:, start:stop] = piece[:, : stop - start].astype(bf16)

        def first_gradient(turn, row_span, below, middle, above, apart, grad):
            span = row_span[:, :1]
            odd = jnp.full((everything, 1), 1, jnp.int32) * lax.rem(turn[:, :1], 2) == 1
            even_pair, odd_pair = below[...].astype(f32), above[...].astype(f32)
            low = jnp.where(odd, even_pair, odd_pair).astype(bf16)
            high = jnp.where(odd, odd_pair, even_pair).astype(bf16)
            stacked = jnp.concatenate([low, middle[...], high], axis=0)
            summed = jnp.dot(near(apart[...], span), stacked, preferred_element_type=f32)
            grad[...] = ensemble_share / (span * span) * summed

        def chosen(turn, blocks, sign):
            if not few:
                return [blocks[0][band] for band in range(bands)]
            turned = []
            for band in range(bands):
                value = blocks[0]
                for shift in range(1, bands):
                    value = jnp.where(turn == partner(band, shift, bands, -sign), blocks[shift], value)
                turned.append(value)
            return turned

        def load_members(weights, stacked):
            shape = (members, per_member, padded)
            values = stacked[...].astype(f32)
            ensemble = [
                values[:, slot * own : (slot + 1) * own].reshape(shape) for slot in range(slots)
            ]
            which = ensemble[0][:, :1, width : width + 1]
            scale = jnp.zeros(which.shape, f32)
            for member in range(members):
                weight = weights[member : member + 1, :1].reshape(1, 1, 1)
                scale = scale + jnp.where(which == member, weight, 0.0)
            scale = jnp.broadcast_to(scale, (members, per_member, 1))
            return ensemble, scale.reshape(members * per_member, 1)

        def fold(ensemble, scale, weighted):
            total = ensemble[0] * weighted[0][None]
            for slot in range(1, slots):
                total = total + ensemble[slot] * weighted[slot][None]
            return scale * total.reshape(members * per_member, padded)

        def images_of(ensemble, grad, ring, taper, factor):
            local = spread(grad, ring, taper, factor).reshape(members, per_member, padded)
            return [jnp.sum(ensemble[t] * local, axis=0) for t in range(slots)]

        def pack(slot, ensemble, out, marks, arrived, packed, mark_sem, in_sems, out_sems):
            def incoming(t):
                return pltpu.make_async_copy(ensemble.at[0, t], arrived.at[t], in_sems.at[t])

            def outgoing(member):
                place = pl.ds(member * bands, bands)
                return pltpu.make_async_copy(packed.at[place], out.at[place], out_sems.at[member])

            mark = pltpu.make_async_copy(slot, marks, mark_sem)
            mark.start()
            for t in range(slots):
                incoming(t).start()
            mark.wait()
            tail = jnp.full((slots * own, padded - width), marks[0], jnp.int32).astype(f32).astype(bf16)
            for t in range(slots):
                incoming(t).wait()
            for member in range(members):
                picked = range(member * level_share, (member + 1) * level_share)
                values = [arrived[t, at].astype(f32) for t in range(slots) for at in picked]
                values = jnp.concatenate(values, axis=0).astype(bf16)
                for band in range(bands):
                    packed[member * bands + band] = window(values, band, lon_share, halo, tail)
                outgoing(member).start()
            for member in range(members):
                outgoing(member).wait()

        def rows_between(root, of_level, same):
            wide = lax.dot_general(
                exact_dot(of_level, static_share * root),
                of_level,
                (((1,), (1,)), ((), ())),
                precision=lax.Precision.HIGHEST,
                preferred_element_type=f32,
            )
            return wide * same

        def observe(place, turn, innovation, precision, root, of_level, same, *refs):
            outs, (own_static, pulled) = refs[:-2], refs[-2:]
            out_of = rows_between(root[...], of_level[...], same[...])
            row = lax.broadcasted_iota(jnp.int32, (own, everything), 0)
            column = lax.broadcasted_iota(jnp.int32, (own, everything), 1)
            picker = (column == place[:, :1] * own + row).astype(f32)
            out_of_own = exact_dot(picker, out_of)
            precise = jnp.concatenate([precision[at].astype(f32) for at in range(levels)], axis=0)
            innovations = [
                jnp.concatenate([innovation[t, at].astype(f32) for at in range(levels)], axis=0)
                for t in range(slots)
            ]
            total = precise * innovations[0]
            for t in range(1, slots):
                total = total + precise * innovations[t]
            high = total.astype(bf16)
            low = (total - high.astype(f32)).astype(bf16)
            into = out_of.T
            back = parts_dot(into, high) + jnp.dot(into.astype(bf16), low, preferred_element_type=f32)
            pulled[...] = back
            values = [
                jnp.dot(picker.astype(bf16), field.astype(bf16), preferred_element_type=f32)
                for field in innovations + [precise]
            ]
            values = jnp.concatenate(values + [exact_dot(out_of_own, back)], axis=0)
            tail = jnp.zeros((values.shape[0], padded - width), f32)
            pieces = [window(values, band, lon_share, halo, tail) for band in range(bands)]
            for band, piece in enumerate(pieces):
                own_static[band] = piece[(slots + 1) * own :, :kept]
            deal(turn[:, :1], pieces, outs)

        def prepare(here, widths, weight, root, of_level, same, apart, level, *refs):
            mixing, pulling, taper, factor, weights, row_span, mixed, pulls = refs
            for member in range(members):
                weights[member : member + 1] = jnp.full((1, LANES), weight[member], f32)
            for at in range(levels):
                row_span[at * rows : (at + 1) * rows] = jnp.full(
                    (rows, LANES), widths[at].astype(f32) + 1.0, f32
                )
            out_of = rows_between(root[...], of_level[...], same[...])
            both = exact_dot(out_of, out_of.T)
            for at in range(levels):
                mixed[at] = both[at * rows : (at + 1) * rows]
                pulls[at] = out_of[at * rows : (at + 1) * rows]
            arriving = [
                member * level_share + share
                for _, _, member in arrivals(here[0])
                for share in range(level_share)
            ]
            pulling[...] = jnp.concatenate([pulls[at] for at in arriving], axis=0).T
            column = lax.broadcasted_iota(jnp.int32, (everything, own), 0)
            own_column = here[0] * own + lax.broadcasted_iota(jnp.int32, (everything, own), 1)
            mixing[...] = exact_dot(
                jnp.concatenate([mixed[at] for at in arriving], axis=0), (column == own_column).astype(f32)
            ).T
            span = jnp.ones(level.shape, f32)
            for share in range(level_share):
                which = here[0] * level_share + share
                span = span + jnp.where(level[...] == share, widths[which].astype(f32), 0.0)
            taper[...] = near(apart[...], span[: apart.shape[0]])
            factor[...] = ensemble_share / (span * span)

        def first_half(weights, turn, stacked, ring, taper, factor, *refs):
            blocks, (total_out, weighted_out, image_out, fields) = refs[:-4], refs[-4:]
            if few:
                blocks = [block[...].astype(f32) for block in blocks]
            values = jnp.stack(chosen(turn[:, :1], blocks, -1)).astype(f32)
            field = []
            for index in range(arrays):
                piece = values[:, index * own : (index + 1) * own].reshape(per_member, padded)
                fields[index] = piece[:, :kept]
                field.append(piece)
            precise, static = field[slots], field[slots + 1]
            ensemble, scale = load_members(weights, stacked)
            weighted = [precise * field[t] for t in range(slots)]
            grad = spread(fold(ensemble, scale, weighted), ring[...], taper[...], factor[...])
            total = jnp.zeros((per_member, padded), f32)
            for t, image in enumerate(images_of(ensemble, grad, ring[...], taper[...], scale * factor[...])):
                image_out[t] = image[:, :kept]
                image = precise * (image + static)
                weighted_out[t] = image
                total = total + image
            total_out[...] = total[:, :kept].astype(bf16)

        def inner(first, second):
            inside = lax.broadcasted_iota(jnp.int32, first.shape, 1) < lon_share
            product = jnp.where(inside, first * second, 0.0)
            return jnp.sum(jnp.sum(product, axis=0, keepdims=True), axis=1, keepdims=True)

        def closest(first, second):
            norm = inner(first, first)
            ratio = inner(first, second) / jnp.where(norm > 0.0, norm, 1.0)
            return ratio.astype(bf16).astype(f32)

        def deal(turn, pieces, outs):
            if not few:
                for band, piece in enumerate(pieces):
                    outs[0][band] = piece.astype(bf16)
                return
            for shift in range(bands):
                value = pieces[0]
                for band in range(1, bands):
                    value = jnp.where(turn == partner(band, shift, bands, -1), pieces[band], value)
                outs[shift][...] = value.astype(bf16)

        def second_half(weights, stacked, ring, taper, factor, weighted, grad_out, image_out):
            ensemble, scale = load_members(weights, stacked)
            grad = fold(ensemble, scale, [weighted[t] for t in range(slots)])
            grad = spread(grad, ring[...], taper[...], factor[...])
            for t, image in enumerate(images_of(ensemble, grad, ring[...], taper[...], scale * factor[...])):
                image_out[t] = image[:, :kept]
            grad_out[...] = grad[:, :kept].reshape(members * bands, own, kept).astype(bf16)

        def combine(grad, first, second, fields, mixing, *refs):
            blocks, (out, image_out) = refs[:-2], refs[-2:]
            lane = lax.broadcasted_iota(jnp.int32, (1, kept), 1) - lon_share
            every = [
                jnp.concatenate(
                    [
                        blocks[block][shift, band * own : (band + 1) * own].astype(f32)
                        for block, shift, _ in arrivals(0)
                    ],
                    axis=0,
                )
                for band in range(bands)
            ]
            mixed = parts_dot(mixing[...], jnp.concatenate(every, axis=1).astype(bf16))
            mixed = jnp.concatenate(
                [mixed[:, band * kept : (band + 1) * kept] for band in range(bands)], axis=0
            )
            precise, static = fields[slots], fields[slots + 1]
            sums = [jnp.zeros((per_member, kept), f32) for _ in range(SUMS)]
            for t in range(slots):
                image = second[t] + mixed
                image_out[t] = image
                whole = first[t] + static
                weighted = precise * whole
                sums[0] = sums[0] + precise * fields[t] * whole
                sums[1] = sums[1] + weighted * whole
                sums[2] = sums[2] + weighted * image
                sums[3] = sums[3] + precise * image * image
            row = jnp.zeros((1, kept), f32)
            for index, part in enumerate(sums):
                part = jnp.sum(jnp.where(lane < 0, part, 0.0), axis=0, keepdims=True)
                part = jnp.sum(part, axis=1, keepdims=True)
                for piece in range(PARTS):
                    high = part.astype(bf16).astype(f32)
                    row = row + jnp.where(lane == PARTS * index + piece, high, 0.0)
                    part = part - high
            row = jnp.broadcast_to(row, (own, kept))
            lane = lax.broadcasted_iota(jnp.int32, (own, kept), 1)
            for block in range(members * bands):
                out[block] = jnp.where(lane < lon_share, grad[block].astype(f32), row).astype(bf16)

        def hand_out(turn, first, second, *refs):
            blocks, outs = refs[: len(totals)], refs[len(totals) :]
            lane = lax.broadcasted_iota(jnp.int32, (1, kept), 1)
            ratio = closest(
                jnp.concatenate([first[t] for t in range(slots)], axis=0),
                jnp.concatenate([second[t] for t in range(slots)], axis=0),
            )
            rest = [
                jnp.where(lane < lon_share, second[t] - ratio * first[t], ratio) for t in range(slots)
            ]
            images = [first[t] for t in range(slots)] + rest
            pieces = []
            for band in range(bands):
                place = slice(band * own, (band + 1) * own)
                parts = [blocks[block][shift, place].astype(f32) for block, shift, _ in arrivals(0)]
                pieces.append(jnp.concatenate(parts + [image[place] for image in images], axis=0))
            deal(turn[:, :1], pieces, outs)

        def join(turn, own_static, pulling, *refs):
            blocks, (pulled, images) = refs[:-2], refs[-2:]
            if few:
                blocks = [block[...].astype(f32) for block in blocks]
            pieces = chosen(turn[:, :1], blocks, -1)
            size = slots * own
            for band in range(bands):
                place = slice(band * lon_share, (band + 1) * lon_share)
                piece = pieces[band].astype(f32)
                every = piece[:everything].astype(bf16)
                pulled[:, place] = parts_dot(pulling[...], every)[:, :lon_share]
                parts = piece[everything:]
                first = parts[:size]
                second = parts[size:] + parts[size : size + 1, lon_share : lon_share + 1] * first
                static = own_static[band]
                for t in range(slots):
                    at = slice(t * own, (t + 1) * own)
                    images[at, place] = (first[at] + static)[:, :lon_share]
                images[size:, place] = second[:, :lon_share]

        def finish(back, grad_first, pulled_first, pulled_second, images, *refs):
            (member_out, static_out, image_out), (member, static, image, sems) = refs[:3], refs[3:]

            def outgoing(index, source, target):
                return pltpu.make_async_copy(source, target, sems.at[index])

            def outgoing_member(index):
                place = pl.ds(index * level_share, level_share)
                return outgoing(index, member.at[place], member_out.at[0, place])

            static_copy = outgoing(members, static, static_out)
            image_copy = outgoing(members + 1, image, image_out)
            tile = lon_share // LANES * LANES
            total = back[0, :1, tile:].astype(f32)
            for block in range(1, members * bands):
                total = total + back[block, :1, tile:].astype(f32)
            lane = lax.broadcasted_iota(jnp.int32, total.shape, 1) + tile - lon_share
            first_norm, first_image, cross, second_image = [
                jnp.sum(
                    jnp.where((lane >= PARTS * index) & (lane < PARTS * (index + 1)), total, 0.0),
                    axis=1,
                    keepdims=True,
                )
                for index in range(SUMS)
            ]
            alpha = first_norm / (first_norm + first_image)
            ratio = first_image / first_norm
            next_norm = alpha * alpha * jnp.maximum(cross - ratio * first_image, 0.0)
            beta = next_norm / first_norm
            apart = second_image - 2.0 * ratio * cross + ratio * ratio * first_image
            curvature = next_norm + alpha * alpha * apart - beta * next_norm / alpha
            alpha_next = jnp.clip(next_norm / curvature, 0.0, 1.0)
            on_first = alpha + alpha_next * (1.0 - alpha + beta)
            on_second = -alpha * alpha_next
            values = on_first * pulled_first[...] + on_second * pulled_second[...]
            for level in range(levels):
                static[level] = values[level * rows : (level + 1) * rows]
            static_copy.start()
            half = slots * own
            values = on_first * images[:half] + on_second * images[half:]
            for t in range(slots):
                for level in range(level_share):
                    start = (t * level_share + level) * rows
                    image[t, level] = values[start : start + rows]
            image_copy.start()
            for source in range(members):
                parts = [
                    back[source * bands + band].astype(f32)[:, :lon_share] for band in range(bands)
                ]
                values = on_second * jnp.concatenate(parts, axis=1)
                values = values + on_first * grad_first[source * own : (source + 1) * own]
                for share in range(level_share):
                    member[source * level_share + share] = values[share * rows : (share + 1) * rows]
                outgoing_member(source).start()
            static_copy.wait()
            image_copy.wait()
            for source in range(members):
                outgoing_member(source).wait()

        def trade(blocks):
            if not few:
                return [lax.all_to_all(blocks[0], "band", 0, 0, tiled=True)]
            return [blocks[0]] + [
                lax.ppermute(
                    blocks[shift], "band", [(at, partner(at, shift, bands, 1)) for at in range(bands)]
                )
                for shift in range(1, bands)
            ]

        def around(block, beside):
            if not paired:
                return [lax.all_gather(block, "member")], beside
            here = [block] + [
                lax.ppermute(
                    block,
                    "member",
                    [(at, 2 * partner(at // 2, shift, members // 2, 1) + at % 2) for at in range(members)],
                )
                for shift in range(1, members // 2)
            ]
            here, beside = lax.optimization_barrier((jnp.stack(here), beside))
            return [here, lax.ppermute(here, "member", [(at, at ^ 1) for at in range(members)])], beside

        def arrivals(here):
            if not paired:
                return [(0, member, member) for member in range(members)]
            chip, core = lax.div(here, 2), lax.rem(here, 2)
            ring = (members // 2) & (members // 2 - 1)
            return [
                (
                    block,
                    shift,
                    2 * (lax.rem(chip + members // 2 - shift, members // 2) if ring else chip ^ shift) + side,
                )
                for block, side in enumerate((core, 1 - core))
                for shift in range(members // 2)
            ]

        def tradable(shape, kind):
            return [(shape, kind)] * bands if few else [((bands,) + shape, kind)]

        place = jnp.full((1, LANES), lax.axis_index("member"), jnp.int32)
        turn = jnp.full((1, LANES), lax.axis_index("band"), jnp.int32)
        here = lax.axis_index("member").astype(jnp.int32).reshape(1)

        block = (members * bands, slots * own, padded)
        pieces = pl.pallas_call(
            pack,
            out_shape=jax.ShapeDtypeStruct(block, bf16),
            in_specs=[pl.BlockSpec(memory_space=pltpu.HBM)] * 2,
            out_specs=pl.BlockSpec(memory_space=pltpu.HBM),
            scratch_shapes=[
                pltpu.SMEM((1,), jnp.int32),
                pltpu.VMEM((slots, levels, rows, lon), bf16),
                pltpu.VMEM(block, bf16),
                pltpu.SemaphoreType.DMA,
                pltpu.SemaphoreType.DMA((slots,)),
                pltpu.SemaphoreType.DMA((members,)),
            ],
            compiler_params=pltpu.CompilerParams(vmem_limit_bytes=60 * 2**20),
            name="pack",
        )(member_of_slot, ensemble)
        pieces, ensemble, innovation, precision, static_root = lax.optimization_barrier(
            (pieces, ensemble, innovation, precision, static_root)
        )
        stacked = lax.all_to_all(pieces, BOTH, 0, 0, tiled=True)

        of_level, same = row_levels(levels, rows)
        apart, level = row_apart(bands, level_share, rows, copies)
        every_level = np.tile(level, (members // copies, 1))
        block = (arrays * own, padded)
        between = [static_root] + [jnp.asarray(table) for table in (of_level, same)]
        results = call(
            observe,
            tradable(block, bf16) + [((bands, own, kept), f32), ((everything, lon), f32)],
            [],
            [place, turn, innovation, precision, *between],
        )
        blocks, (own_static, pulled) = trade(results[:-2]), results[-2:]
        own_static, between = lax.optimization_barrier((own_static, between))
        mixing, pulling, taper, factor, weights, row_span = call(
            prepare,
            [
                ((own, everything), f32),
                ((everything, everything), f32),
                (apart.shape, bf16),
                (every_level.shape, f32),
                ((members, LANES), f32),
                ((everything, LANES), f32),
            ],
            [here, halfwidth, member_weight],
            [*between, jnp.asarray(apart), jnp.asarray(every_level)],
            scratch=[((levels, rows, everything), f32)] * 2,
        )
        awaited = bands // 2 if few else 0
        blocks[awaited], ensemble, innovation, precision = lax.optimization_barrier(
            (blocks[awaited], ensemble, innovation, precision)
        )
        (smoothed,) = call(
            fold_smooth,
            [((everything, lon), bf16)],
            [],
            [member_of_slot[None], member_weight[None], ensemble, innovation, precision, lon_kernel(LANES, 2 * LANES)],
        )
        pairs = [(at, at + 1) for at in range(bands - 1)]
        below, above = [
            lax.ppermute(smoothed, "band", pairs[start::2] + [(to, at) for at, to in pairs[start::2]])
            for start in range(2)
        ]
        ring = ring_kernel(width, padded)

        total, weighted, image_first, fields = call(
            first_half,
            [
                ((per_member, kept), bf16),
                ((slots, per_member, padded), f32),
                ((slots, per_member, kept), f32),
                ((arrays, per_member, kept), f32),
            ],
            [],
            [weights, turn, stacked, ring, taper, factor, *blocks],
        )
        grad, image_second = call(
            second_half,
            [((members * bands, own, kept), bf16), ((slots, per_member, kept), f32)],
            [],
            [weights, stacked, ring, taper, factor, weighted],
            flops=10**9,
        )
        totals, (image_second, below, above) = around(total, (image_second, below, above))

        grad, image_second = call(
            combine,
            [((members * bands, own, kept), bf16), ((slots, per_member, kept), f32)],
            [],
            [grad, image_first, image_second, fields, mixing, *totals],
        )
        back = lax.all_to_all(grad, BOTH, 0, 0, tiled=True)
        blocks = call(
            hand_out,
            tradable((traded, kept), bf16),
            [],
            [turn, image_first, image_second, *totals],
        )
        blocks = trade(blocks)
        pulled_second, images = call(
            join,
            [((everything, lon), f32), ((2 * slots * own, lon), f32)],
            [],
            [turn, own_static, pulling, *blocks],
        )
        (grad_first,) = call(
            first_gradient,
            [((everything, lon), f32)],
            [],
            [turn, row_span, below, smoothed, above, jnp.asarray(halo_apart(levels, rows))],
        )
        return pl.pallas_call(
            finish,
            out_shape=(
                jax.ShapeDtypeStruct((1, levels, rows, lon), f32),
                jax.ShapeDtypeStruct((levels, rows, lon), f32),
                jax.ShapeDtypeStruct((slots, level_share, rows, lon), f32),
            ),
            in_specs=[vmem] * 5,
            out_specs=(pl.BlockSpec(memory_space=pltpu.HBM),) * 3,
            scratch_shapes=[
                pltpu.VMEM((levels, rows, lon), f32),
                pltpu.VMEM((levels, rows, lon), f32),
                pltpu.VMEM((slots, level_share, rows, lon), f32),
                pltpu.SemaphoreType.DMA((members + 2,)),
            ],
            compiler_params=pltpu.CompilerParams(vmem_limit_bytes=limit),
            name="finish",
        )(back, grad_first, pulled, pulled_second, images)

    return jax.shard_map(
        shards,
        mesh=mesh,
        in_specs=(
            P("member", None, None, "band", None),
            P(),
            P("member"),
            P(),
            P(),
            P(None, None, "band", None),
            P(None, "band", None),
        ),
        out_specs=(
            P("member", None, "band", None),
            P(None, "band", None),
            P(None, "member", "band", None),
        ),
        check_vma=False,
    )
```
